32 devices in a mesh: groups: 2 (over y), tensor: 4 (over z), section: 4 (over x, core).
Axes of the slice: x: 2, y: 2, z: 4, core: 2. Of those that a mesh axis runs over, the one named last changes fastest.
Arguments:
- prefill_x: bfloat16 [4096, 8192], P(('groups', 'section'), 'tensor'), parts along dimension 0, may hold values from -6 to 6
- norm_gain: float32 [8192], replicated, may hold values from 0.5 to 2
- w_q: bfloat16 [8192, 8192], P(None, 'tensor'), may hold values from -127 to 127, as said below
- q_scale: float32 [8192], P('tensor'), may hold values from 7.7339806e-05 to 0.00030935922
- key_value_weight: bfloat16 [8192, 2048], P(None, 'tensor'), may hold values from -127 to 127, as said below
- key_value_scale: float32 [2048], P('tensor'), may hold values from 7.7339806e-05 to 0.00030935922
- w_o: bfloat16 [8192, 8192], P('tensor'), may hold values from -127 to 127, as said below
- o_scale: float32 [8192], P('tensor'), may hold values from 0.0022097088 to 0.008838835
- prefix_cache: bfloat16 [4, 32, 2048, 512], P('tensor', ('groups', 'section')), parts along dimension 1, may hold values from -2048 to 2048, as said below
- prefix_len: int32 [32], P(('groups', 'section')), parts along dimension 0, may hold values from 512 to 2048, as said below
- dec_x: bfloat16 [2, 256, 8192], P(None, ('groups', 'section'), 'tensor'), parts along dimension 1, may hold values from -6 to 6
- dec_cache: bfloat16 [4, 256, 64, 512], P('tensor', ('groups', 'section')), parts along dimension 1, may hold values from -2048 to 2048, as said below
- dec_len: int32 [256], P(('groups', 'section')), parts along dimension 0, may hold values from 16 to 64, as said below
- place: int32 [32], P('groups'), parts along dimension 0, may hold values from 0 to 127, as said below
Outputs:
- prefill_out: bfloat16 [4096, 8192], P(('groups', 'section'), 'tensor'), parts along dimension 0
- decode_out: bfloat16 [2, 256, 8192], P(None, ('groups', 'section'), 'tensor'), parts along dimension 1
The draws below stay inside these ranges and needn't reach their ends.
There are 2 independent parts, one for each index of `groups`. The reference program is written for one: setup_inputs(seed, part) draws one part's arguments, and reference() takes and returns one part's arrays. A program takes and returns all parts, laid end to end along the dimension named above; an argument that names none is the same for every part. Nothing has to cross between parts.
Inputs may be any that keep to these rules, and one draw needn't show every extreme that they name: `w_q`: integers, int8 weight values. `key_value_weight`: integers, int8 weight values. `w_o`: integers, int8 weight values. `prefix_cache`: copies of one kv head on different tensor indices are equal. `dec_cache`: copies of one kv head on different tensor indices are equal. `prefix_len`: some prompt has exactly 2048 live positions. `dec_len`: some decode row has exactly 64 live positions. place[s * 4 + p] = o * 32 + r sends prompt p of section index s to decode row r of owner section index o; no two prompts share a decode row; one section index sends at most 2 prompts to one owner, and in every draw some owner receives 2 prompts from every section index.
All inputs are finite; a program needn't handle non-finite values.
Results may differ from the reference program's by a relative error of at most 0.024.
Values may be sent and summed in bfloat16 or wider, within the bound.
No kernel may reach another device: no remote copies, remote signals or barrier semaphores. Data moves between devices by JAX's collectives and lax.ppermute only.
A program may use at most 192 MiB of HBM per device.

```python
import math
import jax
import jax.numpy as jnp
from jax import lax

MODEL_WIDTH = 8192
HQ = 64
KEY_VALUE_HEADS = 8
HEAD_SIZE = 128
PROMPT_TOKENS = 128
PROMPTS = 4
PREFIX = 2048
DROWS = 32
DCTX = 64
CAP = 2
HQD = 16
KVH_DEV = 2
N_TENSOR = 4
N_SECTION = 4


def integer_matrix(key, row_count, column_count):
    return jax.random.randint(key, (row_count, column_count), -127, 128).astype(jnp.float32).astype(jnp.bfloat16)


def draw_w_q(key, part):
    return integer_matrix(jax.random.fold_in(key, 21), MODEL_WIDTH, HQ * HEAD_SIZE)


def draw_key_value_weight(key, part):
    return integer_matrix(jax.random.fold_in(key, 22), MODEL_WIDTH, 2 * KEY_VALUE_HEADS * HEAD_SIZE)


def draw_w_o(key, part):
    return integer_matrix(jax.random.fold_in(key, 23), HQ * HEAD_SIZE, MODEL_WIDTH)


def head_cache(key, entries_count, length_total):
    starting_key = jax.random.fold_in(key, 0)
    cached_value_rows = jax.random.truncated_normal(starting_key, -5.0, 5.0, (entries_count, length_total, KEY_VALUE_HEADS, 2 * HEAD_SIZE), jnp.float32)
    return cached_value_rows.astype(jnp.bfloat16)


def tensor_copies(cached_value_rows):
    device = jnp.arange(N_TENSOR)
    head_index = device[:, None] * HQD // 8 + jnp.arange(KVH_DEV)[None, :]
    picked = cached_value_rows[:, :, head_index]
    picked = jnp.transpose(picked, (2, 0, 1, 3, 4))
    return picked.reshape(N_TENSOR, cached_value_rows.shape[0], cached_value_rows.shape[1], KVH_DEV * 2 * HEAD_SIZE)


def draw_prefix_cache(key, part):
    return tensor_copies(head_cache(jax.random.fold_in(key, 11), N_SECTION * PROMPTS, PREFIX))


def draw_dec_cache(key, part):
    return tensor_copies(head_cache(jax.random.fold_in(key, 12), N_SECTION * DROWS, DCTX))


def ragged(key, entries_count, longest):
    value_key, chosen_key = jax.random.split(key)
    values = jax.random.randint(value_key, (entries_count,), longest // 4, longest + 1)
    chosen = jax.random.randint(chosen_key, (), 0, entries_count)
    return jnp.where(jnp.arange(entries_count) == chosen, longest, values).astype(jnp.int32)


def draw_prefix_len(key, part):
    return ragged(jax.random.fold_in(key, 31), N_SECTION * PROMPTS, PREFIX)


def draw_dec_len(key, part):
    return ragged(jax.random.fold_in(key, 32), N_SECTION * DROWS, DCTX)


def draw_place(key, part):
    starting_key = jax.random.fold_in(key, 41)
    heavy_key, offset_key, order_key, row_key = jax.random.split(starting_key, 4)
    heavy_owner = jax.random.randint(heavy_key, (), 0, N_SECTION)
    offset = jax.random.randint(offset_key, (N_SECTION,), 1, N_SECTION)
    other_owner = (heavy_owner + offset) % N_SECTION
    prompt_order = jax.vmap(lambda sub: jax.random.permutation(sub, PROMPTS))(jax.random.split(order_key, N_SECTION))
    owner_section = jnp.where(prompt_order < CAP, heavy_owner, other_owner[:, None]).reshape(-1)
    owner_hits = (owner_section[:, None] == jnp.arange(N_SECTION)[None, :]).astype(jnp.int32)
    arrival_rank = jnp.sum((jnp.cumsum(owner_hits, axis=0) - owner_hits) * owner_hits, axis=1)
    row_orders = jax.vmap(lambda sub: jax.random.permutation(sub, DROWS))(jax.random.split(row_key, N_SECTION))
    decode_row = row_orders[owner_section, arrival_rank]
    return (owner_section * DROWS + decode_row).astype(jnp.int32)


def level_of(stream_key, extent, cuts, low, high):
    gain, own = 1.0, jax.random.fold_in(stream_key, 6)
    for axis_at, parts in cuts:
        steps = jnp.exp(jax.random.uniform(jax.random.fold_in(own, axis_at), (parts,), jnp.float32, low / len(cuts), high / len(cuts)))
        gain = gain * jnp.repeat(steps, extent[axis_at] // parts).reshape([-1 if axis == axis_at else 1 for axis in range(len(extent))])
    return gain


def centred(own_key, extent, width, limit, pieces=(), kind=jnp.bfloat16):
    array = width * jax.random.normal(own_key, extent, jnp.float32)
    if pieces:
        array = array * level_of(own_key, extent, pieces, -0.22, 0.18)
    return jnp.clip(array, -limit, limit).astype(kind)


def setup_inputs(seed: int = 0, part: int = 0) -> dict:
    seeds = jax.random.split(jax.random.key(seed), 15)
    part_splits = jax.random.split(jax.random.fold_in(seeds[14], part), 15)
    prefill_x = centred(part_splits[0], (N_SECTION * PROMPTS * PROMPT_TOKENS, MODEL_WIDTH), 1.0, 6.0, ((0, 4), (1, 4)))
    norm_gain = jnp.clip(jnp.exp(jax.random.uniform(seeds[1], (MODEL_WIDTH,), jnp.float32, math.log(0.5), math.log(2.0))), 0.5, 2.0)
    w_q = draw_w_q(jax.random.fold_in(seeds[14], 71), part)
    q_scale = jnp.clip(jnp.exp(math.log(0.00030935922) - 1.3862944 * jax.random.uniform(seeds[3], (HQ * HEAD_SIZE,), jnp.float32) ** level_of(seeds[3], (HQ * HEAD_SIZE,), ((0, 4),), -0.2, 0.2)), 7.733980601187795e-05, 0.00030935922)
    key_value_weight = draw_key_value_weight(jax.random.fold_in(seeds[14], 71), part)
    key_value_scale = jnp.clip(jnp.exp(math.log(0.00030935922) - 1.3862944 * jax.random.uniform(seeds[5], (2 * KEY_VALUE_HEADS * HEAD_SIZE,), jnp.float32) ** level_of(seeds[5], (2 * KEY_VALUE_HEADS * HEAD_SIZE,), ((0, 4),), -0.2, 0.2)), 7.733980601187795e-05, 0.00030935922)
    w_o = draw_w_o(jax.random.fold_in(seeds[14], 71), part)
    o_scale = jnp.clip(jnp.exp(math.log(0.008838835) - 1.3862944 * jax.random.uniform(seeds[7], (MODEL_WIDTH,), jnp.float32) ** level_of(seeds[7], (MODEL_WIDTH,), ((0, 4),), -0.2, 0.2)), 0.0022097088, 0.008838835)
    prefix_cache = draw_prefix_cache(jax.random.fold_in(jax.random.fold_in(seeds[14], part), 71), part)
    prefix_len = draw_prefix_len(jax.random.fold_in(jax.random.fold_in(seeds[14], part), 71), part)
    dec_x = centred(part_splits[10], (2, N_SECTION * DROWS, MODEL_WIDTH), 1.0, 6.0, ((1, 4), (2, 4)))
    dec_cache = draw_dec_cache(jax.random.fold_in(jax.random.fold_in(seeds[14], part), 71), part)
    dec_len = draw_dec_len(jax.random.fold_in(jax.random.fold_in(seeds[14], part), 71), part)
    place = draw_place(jax.random.fold_in(jax.random.fold_in(seeds[14], part), 71), part)
    return {"prefill_x": prefill_x, "norm_gain": norm_gain, "w_q": w_q, "q_scale": q_scale, "key_value_weight": key_value_weight, "key_value_scale": key_value_scale, "w_o": w_o, "o_scale": o_scale, "prefix_cache": prefix_cache, "prefix_len": prefix_len, "dec_x": dec_x, "dec_cache": dec_cache, "dec_len": dec_len, "place": place}


def rms_norm(activations, norm_gain):
    values = activations.astype(jnp.float32)
    mean_square = lax.optimization_barrier(jnp.mean(values * values, axis=-1, keepdims=True))
    return (values * lax.rsqrt(mean_square + 1e-05) * norm_gain).astype(jnp.bfloat16)

def project_rows(normalized_input, weight, channel_scale):
    return (jnp.dot(normalized_input, weight, preferred_element_type=jnp.float32) * channel_scale).astype(jnp.bfloat16)

def prefill_attention(queries, prefix_pages, recent_pages, live_len):
    factor = 1.0 / math.sqrt(HEAD_SIZE)
    q_float = queries.astype(jnp.float32)
    distant = jnp.einsum('pcagd,plad->pagcl', q_float, prefix_pages[:, :, :, 0].astype(jnp.float32)) * factor
    nearby = jnp.einsum('pcagd,pkad->pagck', q_float, recent_pages[:, :, :, 0].astype(jnp.float32)) * factor
    distant_live = jnp.arange(prefix_pages.shape[1])[None, :] < live_len[:, None]
    steps_new = jnp.arange(recent_pages.shape[1])
    nearby_live = steps_new[None, :] <= steps_new[:, None]
    distant = jnp.where(distant_live[:, None, None, None, :], distant, -1e+30)
    nearby = jnp.where(nearby_live[None, None, None], nearby, -1e+30)
    peak = jnp.maximum(lax.optimization_barrier(jnp.max(distant, -1, keepdims=True)), lax.optimization_barrier(jnp.max(nearby, -1, keepdims=True)))
    distant_exp = jnp.exp(distant - peak)
    nearby_exp = jnp.exp(nearby - peak)
    denominator = lax.optimization_barrier(jnp.sum(distant_exp, -1, keepdims=True)) + lax.optimization_barrier(jnp.sum(nearby_exp, -1, keepdims=True))
    distant_w = (distant_exp / denominator).astype(jnp.bfloat16).astype(jnp.float32)
    nearby_w = (nearby_exp / denominator).astype(jnp.bfloat16).astype(jnp.float32)
    attended = jnp.einsum('pagcl,plad->pcagd', distant_w, prefix_pages[:, :, :, 1].astype(jnp.float32))
    attended = attended + jnp.einsum('pagck,pkad->pcagd', nearby_w, recent_pages[:, :, :, 1].astype(jnp.float32))
    return attended.astype(jnp.bfloat16).reshape(queries.shape[0] * queries.shape[1], -1)

def decode_attention(queries, cache_pages, live_len, landed_pages, landed, fresh_pages):
    factor = 1.0 / math.sqrt(HEAD_SIZE)
    q_float = queries.astype(jnp.float32)
    distant = jnp.einsum('ragd,rlad->ragl', q_float, cache_pages[:, :, :, 0].astype(jnp.float32)) * factor
    arrival = jnp.einsum('ragd,rkad->ragk', q_float, landed_pages[:, :, :, 0].astype(jnp.float32)) * factor
    recent = jnp.einsum('ragd,rmad->ragm', q_float, fresh_pages[:, :, :, 0].astype(jnp.float32)) * factor
    distant_live = jnp.arange(cache_pages.shape[1])[None, :] < live_len[:, None]
    distant = jnp.where(distant_live[:, None, None, :], distant, -1e+30)
    arrival = jnp.where(landed[:, None, None, None], arrival, -1e+30)
    peak = jnp.maximum(lax.optimization_barrier(jnp.max(distant, -1, keepdims=True)), lax.optimization_barrier(jnp.max(arrival, -1, keepdims=True)))
    peak = jnp.maximum(peak, lax.optimization_barrier(jnp.max(recent, -1, keepdims=True)))
    distant_exp = jnp.exp(distant - peak)
    arrival_exp = jnp.exp(arrival - peak)
    recent_exp = jnp.exp(recent - peak)
    denominator = lax.optimization_barrier(jnp.sum(distant_exp, -1, keepdims=True)) + lax.optimization_barrier(jnp.sum(arrival_exp, -1, keepdims=True)) + lax.optimization_barrier(jnp.sum(recent_exp, -1, keepdims=True))
    distant_w = (distant_exp / denominator).astype(jnp.bfloat16).astype(jnp.float32)
    arrival_w = (arrival_exp / denominator).astype(jnp.bfloat16).astype(jnp.float32)
    recent_w = (recent_exp / denominator).astype(jnp.bfloat16).astype(jnp.float32)
    attended = jnp.einsum('ragl,rlad->ragd', distant_w, cache_pages[:, :, :, 1].astype(jnp.float32))
    attended = attended + jnp.einsum('ragk,rkad->ragd', arrival_w, landed_pages[:, :, :, 1].astype(jnp.float32))
    attended = attended + jnp.einsum('ragm,rmad->ragd', recent_w, fresh_pages[:, :, :, 1].astype(jnp.float32))
    return attended.astype(jnp.bfloat16).reshape(queries.shape[0], -1)

def reference(prefill_x, norm_gain, w_q, q_scale, key_value_weight, key_value_scale, w_o, o_scale, prefix_cache, prefix_len, dec_x, dec_cache, dec_len, place):
    prompts_total = N_SECTION * PROMPTS
    row_count = N_SECTION * DROWS
    page_width = KVH_DEV * 2 * HEAD_SIZE
    group_size = HQD // KVH_DEV
    normalized_input = rms_norm(prefill_x, norm_gain)
    queries = project_rows(normalized_input, w_q, q_scale).reshape(prompts_total, PROMPT_TOKENS, N_TENSOR, KVH_DEV, group_size, HEAD_SIZE)
    block_key_value = project_rows(normalized_input, key_value_weight, key_value_scale).reshape(prompts_total, PROMPT_TOKENS, 2 * KEY_VALUE_HEADS * HEAD_SIZE)
    dec_normed = rms_norm(dec_x, norm_gain)
    dec_queries = project_rows(dec_normed, w_q, q_scale).reshape(2, row_count, N_TENSOR, KVH_DEV, group_size, HEAD_SIZE)
    dec_kv = project_rows(dec_normed, key_value_weight, key_value_scale)
    arrival_hits = (place[None, :] == jnp.arange(row_count, dtype=jnp.int32)[:, None]).astype(jnp.float32)
    landed = lax.optimization_barrier(jnp.sum(arrival_hits, axis=1)) > 0.5
    out_rows = w_o.reshape(N_TENSOR, HQD * HEAD_SIZE, MODEL_WIDTH)

    def shard_terms(totals, inputs):
        device, weight_rows, prefix_pages, cache_pages = inputs
        column_start = (device * HQD // 8 * (2 * HEAD_SIZE)).astype(jnp.int32)
        own_block = lax.dynamic_slice_in_dim(block_key_value, column_start, page_width, 2)
        arrived = jnp.einsum('gp,pcw->gcw', arrival_hits, own_block.astype(jnp.float32)).astype(jnp.bfloat16)
        fresh_kv = lax.dynamic_slice_in_dim(dec_kv, column_start, page_width, 2)
        fresh_rows = jnp.transpose(fresh_kv, (1, 0, 2)).reshape(row_count, 2, KVH_DEV, 2, HEAD_SIZE)
        shard_queries = lax.dynamic_index_in_dim(queries, device, 2, keepdims=False)
        attended = prefill_attention(shard_queries, prefix_pages.reshape(prompts_total, PREFIX, KVH_DEV, 2, HEAD_SIZE), own_block.reshape(prompts_total, PROMPT_TOKENS, KVH_DEV, 2, HEAD_SIZE), prefix_len)
        shard_dec = lax.dynamic_index_in_dim(dec_queries, device, 2, keepdims=False)
        cache_rows = cache_pages.reshape(row_count, DCTX, KVH_DEV, 2, HEAD_SIZE)
        landed_rows = arrived.reshape(row_count, PROMPT_TOKENS, KVH_DEV, 2, HEAD_SIZE)
        first_step = decode_attention(shard_dec[0], cache_rows, dec_len, landed_rows, landed, fresh_rows[:, :1])
        second = decode_attention(shard_dec[1], cache_rows, dec_len, landed_rows, landed, fresh_rows)
        dec_attended = jnp.stack([first_step, second])
        prefill_term = lax.optimization_barrier(jnp.dot(attended, weight_rows, preferred_element_type=jnp.float32).astype(jnp.bfloat16)).astype(jnp.float32)
        decode_term = lax.optimization_barrier(jnp.dot(dec_attended, weight_rows, preferred_element_type=jnp.float32).astype(jnp.bfloat16)).astype(jnp.float32)
        return ((totals[0] + prefill_term, totals[1] + decode_term), None)
    initial = (jnp.zeros((prompts_total * PROMPT_TOKENS, MODEL_WIDTH), jnp.float32), jnp.zeros((2, row_count, MODEL_WIDTH), jnp.float32))
    devices = jnp.arange(N_TENSOR, dtype=jnp.int32)
    totals, unused = lax.scan(shard_terms, initial, (devices, out_rows, prefix_cache, dec_cache))
    prefill_out = (prefill_x.astype(jnp.float32) + totals[0] * o_scale).astype(jnp.bfloat16)
    decode_out = (dec_x.astype(jnp.float32) + totals[1] * o_scale).astype(jnp.bfloat16)
    return (prefill_out, decode_out)
```

```python
import functools
import math

import jax
import jax.numpy as jnp
from jax import lax
from jax.experimental import pallas as pl
from jax.experimental.pallas import tpu as pltpu
from jax.sharding import PartitionSpec as P

HEAD_SIZE = 128
PROMPT_TOKENS = 128
MIB = 1 << 20
LINE_LIMIT = 8
EXP2_FACTOR = math.log2(math.e) / math.sqrt(HEAD_SIZE)
MASKED = -1e30


def partner_2(block, axis, distance):
    count = lax.axis_size(axis)
    route = []
    for low in range(count):
        high = low | 1 << distance
        if high != low and high < count:
            route += [(low, high), (high, low)]
    return lax.ppermute(block, axis, route)


def joined(portion, partner, bit_number, concat_dim, tensor_index):
    upper_half = tensor_index // 2**bit_number % 2 == 1
    lower_first = jnp.concatenate([portion, partner], axis=concat_dim)
    upper_first = jnp.concatenate([partner, portion], axis=concat_dim)
    return jnp.where(upper_half, upper_first, lower_first)


def tile_of(extent, most):
    tile = extent
    while tile > most and tile % 2 == 0:
        tile //= 2
    return tile


def after(value, *others):
    return lax.optimization_barrier((value,) + others)[0]


def line_gather(block, axis, index):
    count = lax.axis_size(axis)
    if count == 1:
        return block[None], [block]
    if count > LINE_LIMIT:
        gathered = lax.all_gather(block, axis, axis=0, tiled=False)
        return gathered, [block] * 2
    up, down = [block], [block]
    for hop in range(1, count):
        up.append(lax.ppermute(up[-1], axis, [(j, j + 1) for j in range(hop - 1, count - 1)]))
        down.append(lax.ppermute(down[-1], axis, [(j, j - 1) for j in range(1, count - hop + 1)]))
    pieces = [block] + [
        jnp.where(index + k < count, down[k], up[count - k]) for k in range(1, count)
    ]
    return jnp.stack(pieces), up + down


def line_scatter(partial, axis, index):
    count = lax.axis_size(axis)
    own = lax.dynamic_index_in_dim(partial, index, 0, keepdims=False).astype(jnp.float32)
    if count == 1:
        return own
    if count > LINE_LIMIT:
        return lax.psum_scatter(partial, axis, scatter_dimension=0, tiled=False).astype(jnp.float32)
    up = down = None
    for step in range(1, count):
        reach = count - step
        up_own = lax.dynamic_index_in_dim(
            partial, jnp.minimum(index + reach, count - 1), 0, keepdims=False
        )
        down_own = lax.dynamic_index_in_dim(
            partial, jnp.maximum(index - reach, 0), 0, keepdims=False
        )
        if up is not None:
            up_own = (up_own.astype(jnp.float32) + up.astype(jnp.float32)).astype(partial.dtype)
            down_own = (down_own.astype(jnp.float32) + down.astype(jnp.float32)).astype(
                partial.dtype
            )
        up = lax.ppermute(up_own, axis, [(j, j + 1) for j in range(step)])
        down = lax.ppermute(down_own, axis, [(j, j - 1) for j in range(reach, count)])
    return own + up.astype(jnp.float32) + down.astype(jnp.float32)


def qkv_kernel(
    rotation, x_ref, gain_ref, wq_ref, wkv_ref, qs_ref, kvs_ref, q_ref, kv_ref, accq, acckv, squares
):
    step = pl.program_id(0)

    @pl.when(step == 0)
    def _():
        accq[...] = jnp.zeros_like(accq)
        acckv[...] = jnp.zeros_like(acckv)
        squares[...] = jnp.zeros_like(squares)

    values = x_ref[0].astype(jnp.float32)
    squares[...] += jnp.sum(values * values, axis=-1, keepdims=True)
    scaled = (values * gain_ref[...]).astype(jnp.bfloat16)
    accq[...] += jnp.dot(scaled, wq_ref[...], preferred_element_type=jnp.float32)
    acckv[...] += jnp.dot(scaled, wkv_ref[...], preferred_element_type=jnp.float32)

    @pl.when(step == pl.num_programs(0) - 1)
    def _():
        width = x_ref.shape[2] * pl.num_programs(0)
        root = lax.rsqrt(squares[...] / width + 1e-05)
        q_ref[...] = (accq[...] * root * qs_ref[...]).astype(q_ref.dtype)
        kv_ref[...] = (acckv[...] * root * kvs_ref[...]).astype(kv_ref.dtype)


def project_qkv(pieces, rotation, norm_gain, w_q, q_scale, kv_weight, kv_scale):
    count, rows, depth = pieces.shape
    width = count * depth
    tile = tile_of(depth, 1024)
    per = depth // tile
    q_cols, kv_cols = w_q.shape[1], kv_weight.shape[1]

    def place(g, rot):
        return lax.rem(g // per + rot[0], count) * per + lax.rem(g, per)

    return pl.pallas_call(
        qkv_kernel,
        grid_spec=pltpu.PrefetchScalarGridSpec(
            num_scalar_prefetch=1,
            grid=(count * per,),
            in_specs=[
                pl.BlockSpec((1, rows, tile), lambda g, rot: (g // per, 0, lax.rem(g, per))),
                pl.BlockSpec((1, tile), lambda g, rot: (0, place(g, rot))),
                pl.BlockSpec((tile, q_cols), lambda g, rot: (place(g, rot), 0)),
                pl.BlockSpec((tile, kv_cols), lambda g, rot: (place(g, rot), 0)),
                pl.BlockSpec((1, q_cols), lambda g, rot: (0, 0)),
                pl.BlockSpec((1, kv_cols), lambda g, rot: (0, 0)),
            ],
            out_specs=[
                pl.BlockSpec((rows, q_cols), lambda g, rot: (0, 0)),
                pl.BlockSpec((rows, kv_cols), lambda g, rot: (0, 0)),
            ],
            scratch_shapes=[
                pltpu.VMEM((rows, q_cols), jnp.float32),
                pltpu.VMEM((rows, kv_cols), jnp.float32),
                pltpu.VMEM((rows, 1), jnp.float32),
            ],
        ),
        out_shape=[
            jax.ShapeDtypeStruct((rows, q_cols), jnp.bfloat16),
            jax.ShapeDtypeStruct((rows, kv_cols), jnp.bfloat16),
        ],
        compiler_params=pltpu.CompilerParams(vmem_limit_bytes=32 * MIB),
        cost_estimate=pl.CostEstimate(
            flops=2 * rows * width * (q_cols + kv_cols),
            bytes_accessed=2 * width * (q_cols + kv_cols + rows),
            transcendentals=0,
        ),
        name="norm_qkv",
    )(
        rotation,
        pieces,
        norm_gain.reshape(1, -1),
        w_q,
        kv_weight,
        q_scale.reshape(1, -1),
        kv_scale.reshape(1, -1),
    )


def out_kernel(x_ref, w_ref, o_ref):
    o_ref[0] = jnp.dot(x_ref[...], w_ref[...], preferred_element_type=jnp.float32).astype(
        o_ref.dtype
    )


def project_out(attended, w_o, count):
    rows, depth = attended.shape
    block = w_o.shape[1] // count
    tile = tile_of(block, 1024)
    per = block // tile
    return pl.pallas_call(
        out_kernel,
        grid=(count * per,),
        in_specs=[
            pl.BlockSpec((rows, depth), lambda g: (0, 0)),
            pl.BlockSpec((depth, tile), lambda g: (0, g)),
        ],
        out_specs=pl.BlockSpec((1, rows, tile), lambda g: (g // per, 0, lax.rem(g, per))),
        out_shape=jax.ShapeDtypeStruct((count, rows, block), jnp.bfloat16),
        compiler_params=pltpu.CompilerParams(vmem_limit_bytes=32 * MIB),
        cost_estimate=pl.CostEstimate(
            flops=2 * rows * depth * w_o.shape[1],
            bytes_accessed=2 * depth * w_o.shape[1],
            transcendentals=0,
        ),
        name="project_out",
    )(attended, w_o)


def with_ones(values):
    return jnp.concatenate([values, jnp.ones_like(values)], axis=1)


def scores_of(queries, keys):
    return lax.dot_general(
        queries, keys, (((1,), (1,)), ((), ())), preferred_element_type=jnp.float32
    )


def prefill_kernel(kv_heads, group, span, len_ref, q_ref, cache_ref, new_ref, o_ref, acc, peak):
    tokens = q_ref.shape[0]
    rows = group * tokens
    live = len_ref[0]
    steps = (live + span - 1) // span
    query_token = lax.rem(lax.broadcasted_iota(jnp.int32, (rows, tokens), 0), tokens)
    key_token = lax.broadcasted_iota(jnp.int32, (rows, tokens), 1)
    causal = key_token <= query_token
    lane = lax.broadcasted_iota(jnp.int32, (1, span), 1)
    for a in range(kv_heads):
        key_at, value_at = 2 * a * HEAD_SIZE, (2 * a + 1) * HEAD_SIZE
        queries = jnp.concatenate(
            [
                q_ref[:, (a * group + h) * HEAD_SIZE : (a * group + h + 1) * HEAD_SIZE]
                for h in range(group)
            ],
            axis=0,
        )
        scores = scores_of(queries, new_ref[:, key_at : key_at + HEAD_SIZE])
        scores = jnp.where(causal, scores, MASKED)
        top = jnp.max(scores, axis=-1, keepdims=True)
        weights = jnp.exp2((scores - top) * EXP2_FACTOR).astype(jnp.bfloat16)
        acc[...] = jnp.dot(
            weights,
            with_ones(new_ref[:, value_at : value_at + HEAD_SIZE]),
            preferred_element_type=jnp.float32,
        )
        peak[...] = top

        def step(s, carry):
            at = pl.multiple_of(s * span, span)
            keys = cache_ref[0, 0, pl.ds(at, span), key_at : key_at + HEAD_SIZE]
            values = cache_ref[0, 0, pl.ds(at, span), value_at : value_at + HEAD_SIZE]
            bias = jnp.where(lane + at < live, 0.0, MASKED)
            scores = scores_of(queries, keys) + bias
            top = jnp.maximum(peak[...], jnp.max(scores, axis=-1, keepdims=True))
            weights = jnp.exp2((scores - top) * EXP2_FACTOR).astype(jnp.bfloat16)
            fade = jnp.exp2((peak[...] - top) * EXP2_FACTOR)
            acc[...] = acc[...] * fade + jnp.dot(
                weights, with_ones(values), preferred_element_type=jnp.float32
            )
            peak[...] = top
            return carry

        lax.fori_loop(0, steps, step, 0)
        result = acc[:, :HEAD_SIZE] / acc[:, HEAD_SIZE:]
        for h in range(group):
            o_ref[:, (a * group + h) * HEAD_SIZE : (a * group + h + 1) * HEAD_SIZE] = result[
                h * tokens : (h + 1) * tokens
            ].astype(o_ref.dtype)


def prefill_attention(queries, prefix_cache, prompt, new_kv, live_len):
    tokens, width = queries.shape
    positions, page = prefix_cache.shape[2:]
    kv_heads = page // (2 * HEAD_SIZE)
    group = width // HEAD_SIZE // kv_heads
    span = tile_of(positions, 512)
    rows = group * tokens
    return pl.pallas_call(
        functools.partial(prefill_kernel, kv_heads, group, span),
        grid_spec=pltpu.PrefetchScalarGridSpec(
            num_scalar_prefetch=1,
            grid=(1,),
            in_specs=[
                pl.BlockSpec((tokens, width), lambda g, n: (0, 0)),
                pl.BlockSpec((1, 1, positions, page), lambda g, n: (0, prompt, 0, 0)),
                pl.BlockSpec((tokens, page), lambda g, n: (0, 0)),
            ],
            out_specs=pl.BlockSpec((tokens, width), lambda g, n: (0, 0)),
            scratch_shapes=[
                pltpu.VMEM((rows, 2 * HEAD_SIZE), jnp.float32),
                pltpu.VMEM((rows, 1), jnp.float32),
            ],
        ),
        out_shape=jax.ShapeDtypeStruct((tokens, width), jnp.bfloat16),
        compiler_params=pltpu.CompilerParams(vmem_limit_bytes=32 * MIB),
        cost_estimate=pl.CostEstimate(
            flops=8 * rows * kv_heads * (positions + tokens) * HEAD_SIZE,
            bytes_accessed=2 * positions * page,
            transcendentals=rows * kv_heads * (positions + tokens),
        ),
        name="prefill_attention",
    )(live_len, queries, prefix_cache, new_kv)


def decode_kernel(
    kv_heads, batch, len_ref, row_ref, q_ref, cache_ref, landed_ref, fresh_ref, o_ref, acc, peak
):
    row_count, context = cache_ref.shape[1], cache_ref.shape[2]
    per_row = q_ref.shape[2]
    steps = fresh_ref.shape[1]
    rows = batch * per_row
    row_of = lax.broadcasted_iota(jnp.int32, (rows, batch * context), 0) // per_row
    key_row = lax.broadcasted_iota(jnp.int32, (rows, batch * context), 1) // context
    key_at = lax.rem(lax.broadcasted_iota(jnp.int32, (rows, batch * context), 1), context)
    fresh_query = lax.broadcasted_iota(jnp.int32, (rows, batch * steps), 0)
    fresh_key = lax.broadcasted_iota(jnp.int32, (rows, batch * steps), 1)
    fresh_live = (fresh_key // steps == fresh_query // per_row) & (
        lax.rem(fresh_key, steps) <= lax.rem(fresh_query, per_row) // (per_row // steps)
    )

    def cached(b, carry):
        first = b * batch
        live = jnp.zeros_like(key_row)
        for r in range(batch):
            live = jnp.where(key_row == r, len_ref[first + r], live)
        cache_live = (row_of == key_row) & (key_at < live)
        pages = cache_ref[0, pl.ds(first, batch)].reshape(batch * context, cache_ref.shape[3])
        fresh = fresh_ref[pl.ds(first, batch)].reshape(batch * steps, fresh_ref.shape[2])
        for a in range(kv_heads):
            queries = q_ref[pl.ds(first, batch), a].reshape(rows, HEAD_SIZE).astype(jnp.bfloat16)
            k_at, v_at = 2 * a * HEAD_SIZE, (2 * a + 1) * HEAD_SIZE
            scores = scores_of(queries, pages[:, k_at : k_at + HEAD_SIZE])
            scores = jnp.where(cache_live, scores, MASKED)
            recent = scores_of(queries, fresh[:, k_at : k_at + HEAD_SIZE].astype(jnp.bfloat16))
            recent = jnp.where(fresh_live, recent, MASKED)
            top = jnp.maximum(
                jnp.max(scores, axis=-1, keepdims=True), jnp.max(recent, axis=-1, keepdims=True)
            )
            weights = jnp.exp2((scores - top) * EXP2_FACTOR).astype(jnp.bfloat16)
            recent = jnp.exp2((recent - top) * EXP2_FACTOR).astype(jnp.bfloat16)
            total = jnp.dot(
                weights,
                with_ones(pages[:, v_at : v_at + HEAD_SIZE]),
                preferred_element_type=jnp.float32,
            ) + jnp.dot(
                recent,
                with_ones(fresh[:, v_at : v_at + HEAD_SIZE].astype(jnp.bfloat16)),
                preferred_element_type=jnp.float32,
            )
            acc[pl.ds(first, batch), a] = total.reshape(batch, per_row, 2 * HEAD_SIZE)
            peak[pl.ds(first, batch), a] = jnp.broadcast_to(top, (rows, HEAD_SIZE)).reshape(
                batch, per_row, HEAD_SIZE
            )
        return carry

    lax.fori_loop(0, row_count // batch, cached, 0)

    def arrival(slot, carry):
        row = row_ref[slot]

        @pl.when(row >= 0)
        def _():
            for a in range(kv_heads):
                queries = q_ref[row, a].astype(jnp.bfloat16)
                k_at, v_at = 2 * a * HEAD_SIZE, (2 * a + 1) * HEAD_SIZE
                scores = scores_of(queries, landed_ref[slot, :, k_at : k_at + HEAD_SIZE])
                before = peak[row, a]
                top = jnp.maximum(before, jnp.max(scores, axis=-1, keepdims=True))
                weights = jnp.exp2((scores - top[:, :1]) * EXP2_FACTOR).astype(jnp.bfloat16)
                fade = jnp.exp2((before - top) * EXP2_FACTOR)
                acc[row, a] = acc[row, a] * jnp.concatenate([fade, fade], axis=1) + jnp.dot(
                    weights,
                    with_ones(landed_ref[slot, :, v_at : v_at + HEAD_SIZE]),
                    preferred_element_type=jnp.float32,
                )

        return carry

    lax.fori_loop(0, row_ref.shape[0], arrival, 0)
    o_ref[...] = (acc[:, :, :, :HEAD_SIZE] / acc[:, :, :, HEAD_SIZE:]).astype(o_ref.dtype)


def decode_attention(queries, dec_cache, dec_len, landed, slot_rows, fresh):
    row_count, kv_heads, per_row = queries.shape[:3]
    context = dec_cache.shape[2]
    batch = max(1, min(row_count, 2 * HEAD_SIZE // context))
    whole = lambda array: pl.BlockSpec(array.shape, lambda g, *_: (0,) * array.ndim)
    return pl.pallas_call(
        functools.partial(decode_kernel, kv_heads, batch),
        grid_spec=pltpu.PrefetchScalarGridSpec(
            num_scalar_prefetch=2,
            grid=(1,),
            in_specs=[whole(queries), whole(dec_cache), whole(landed), whole(fresh)],
            out_specs=whole(queries),
            scratch_shapes=[
                pltpu.VMEM((row_count, kv_heads, per_row, 2 * HEAD_SIZE), jnp.float32),
                pltpu.VMEM((row_count, kv_heads, per_row, HEAD_SIZE), jnp.float32),
            ],
        ),
        out_shape=jax.ShapeDtypeStruct(queries.shape, jnp.float32),
        compiler_params=pltpu.CompilerParams(vmem_limit_bytes=32 * MIB),
        cost_estimate=pl.CostEstimate(
            flops=8 * queries.size * batch * context,
            bytes_accessed=2 * dec_cache.size + 2 * landed.size,
            transcendentals=queries.size * batch * context // HEAD_SIZE,
        ),
        name="decode_attention",
    )(dec_len, slot_rows, queries, dec_cache, landed, fresh)


def shards(
    prefill_x,
    norm_gain,
    w_q,
    q_scale,
    key_value_weight,
    key_value_scale,
    w_o,
    o_scale,
    prefix_cache,
    prefix_len,
    dec_x,
    dec_cache,
    dec_len,
    place,
):
    prompts_total = prefix_cache.shape[1]
    row_count = dec_cache.shape[1]
    page_width = prefix_cache.shape[3]
    kv_heads = page_width // (2 * HEAD_SIZE)
    query_heads = w_q.shape[1] // HEAD_SIZE
    group_size = query_heads // kv_heads
    steps = dec_x.shape[0]
    section_count = lax.axis_size("section")
    section_index = lax.axis_index("section")
    tensor_count = lax.axis_size("tensor")
    tensor_index = lax.axis_index("tensor")
    head_span = max(1, 8 // query_heads)
    span_bits = head_span.bit_length() - 1
    on_line = tensor_count <= LINE_LIMIT
    rotation = (tensor_index if on_line else 0 * tensor_index).astype(jnp.int32).reshape(1)

    def project(pieces):
        queries, stacked = project_qkv(
            pieces, rotation, norm_gain, w_q, q_scale, key_value_weight, key_value_scale
        )
        for bit_number in range(span_bits):
            partner = partner_2(stacked, "tensor", bit_number)
            stacked = joined(stacked, partner, bit_number, 1, tensor_index)
        return queries, stacked

    chunks = [
        prefill_x[p * PROMPT_TOKENS : (p + 1) * PROMPT_TOKENS] for p in range(prompts_total)
    ] + [dec_x.reshape(steps * row_count, -1)]
    gathered = []
    gate = None
    for chunk in chunks:
        if gate is not None:
            chunk = after(chunk, *gate)
        pieces, hops = line_gather(chunk, "tensor", tensor_index)
        gathered.append(pieces)
        half = len(hops) // 2
        gate = (hops[min(2, half - 1)], hops[half + min(2, half - 1)])

    pages = []
    summed = []
    for p in range(prompts_total):
        queries, new_kv = project(gathered[p])
        pages.append(new_kv)
        attended = prefill_attention(queries, prefix_cache, p, new_kv, prefix_len[p : p + 1])
        summed.append(
            line_scatter(project_out(attended, w_o, tensor_count), "tensor", tensor_index)
        )

    own_block = jnp.stack(pages)
    owners = (place // row_count).reshape(section_count, prompts_total)
    targets = (place % row_count).reshape(section_count, prompts_total)
    owner_hits = (owners[:, :, None] == jnp.arange(section_count)[None, None, :]).astype(jnp.int32)
    slot_ranks = jnp.sum((jnp.cumsum(owner_hits, axis=1) - owner_hits) * owner_hits, axis=2)
    capacity = prompts_total // 2
    slot_ids = jnp.arange(capacity)
    sending = lax.dynamic_index_in_dim(owner_hits, section_index, 0, keepdims=False)
    my_ranks = lax.dynamic_index_in_dim(slot_ranks, section_index, 0, keepdims=False)
    selector = (
        jnp.transpose(sending)[:, None, :] * (my_ranks[None, None, :] == slot_ids[None, :, None])
    ).astype(jnp.bfloat16)
    here = (owners == section_index)[:, None, :] & (
        slot_ranks[:, None, :] == slot_ids[None, :, None]
    )
    slot_rows = jnp.sum(jnp.where(here, targets[:, None, :] + 1, 0), axis=2) - 1
    outgoing = jnp.einsum(
        "skp,pcw->skcw", selector, own_block, preferred_element_type=jnp.float32
    ).astype(jnp.bfloat16)
    received = lax.all_to_all(outgoing, "section", split_axis=0, concat_axis=0, tiled=True)
    landed = received.reshape(section_count * capacity, PROMPT_TOKENS, page_width)

    dec_queries, fresh_kv = project(gathered[-1])
    dec_queries = jnp.transpose(
        dec_queries.reshape(steps, row_count, kv_heads, group_size, HEAD_SIZE), (1, 2, 0, 3, 4)
    ).reshape(row_count, kv_heads, steps * group_size, HEAD_SIZE)
    fresh = jnp.transpose(fresh_kv.reshape(steps, row_count, page_width), (1, 0, 2))
    dec_attended = decode_attention(
        dec_queries.astype(jnp.float32),
        dec_cache,
        dec_len,
        landed,
        slot_rows.reshape(-1).astype(jnp.int32),
        fresh.astype(jnp.float32),
    )
    dec_attended = (
        jnp.transpose(
            dec_attended.reshape(row_count, kv_heads, steps, group_size, HEAD_SIZE), (2, 0, 1, 3, 4)
        )
        .reshape(steps * row_count, -1)
        .astype(jnp.bfloat16)
    )
    dec_summed = line_scatter(
        project_out(dec_attended, w_o, tensor_count), "tensor", tensor_index
    ).reshape(dec_x.shape)
    prefill_out = (
        prefill_x.astype(jnp.float32) + jnp.concatenate(summed, axis=0) * o_scale
    ).astype(jnp.bfloat16)
    decode_out = (dec_x.astype(jnp.float32) + dec_summed * o_scale).astype(jnp.bfloat16)
    return (prefill_out, decode_out)


def solution(mesh):
    in_specs = (
        P(("groups", "section"), "tensor"),
        P(),
        P(None, "tensor"),
        P("tensor"),
        P(None, "tensor"),
        P("tensor"),
        P("tensor", None),
        P("tensor"),
        P("tensor", ("groups", "section"), None, None),
        P(("groups", "section")),
        P(None, ("groups", "section"), "tensor"),
        P("tensor", ("groups", "section"), None, None),
        P(("groups", "section")),
        P("groups"),
    )
    out_specs = (P(("groups", "section"), "tensor"), P(None, ("groups", "section"), "tensor"))
    return jax.shard_map(shards, mesh=mesh, in_specs=in_specs, out_specs=out_specs, check_vma=False)
```

```python
import functools
import math

import jax
import jax.numpy as jnp
from jax import lax
from jax.experimental import pallas as pl
from jax.experimental.pallas import tpu as pltpu
from jax.sharding import PartitionSpec as P

HEAD_SIZE = 128
PROMPT_TOKENS = 128
MIB = 1 << 20
EXP2_FACTOR = math.log2(math.e) / math.sqrt(HEAD_SIZE)
MASKED = -1e30


def partner_2(block, axis, distance):
    count = lax.axis_size(axis)
    route = []
    for low in range(count):
        high = low | 1 << distance
        if high != low and high < count:
            route += [(low, high), (high, low)]
    return lax.ppermute(block, axis, route)


def joined(portion, partner, bit_number, concat_dim, tensor_index):
    upper_half = tensor_index // 2**bit_number % 2 == 1
    lower_first = jnp.concatenate([portion, partner], axis=concat_dim)
    upper_first = jnp.concatenate([partner, portion], axis=concat_dim)
    return jnp.where(upper_half, upper_first, lower_first)


def tile_of(extent, most):
    tile = extent
    while tile > most and tile % 2 == 0:
        tile //= 2
    return tile


def after(value, *others):
    return lax.optimization_barrier((value,) + others)[0]


def after_all(values, *others):
    return lax.optimization_barrier(tuple(values) + others)[: len(values)]


def line_order(index):
    low = index < 2
    return [index, index ^ 1, jnp.where(low, 2, 1), jnp.where(low, 3, 0)]


OUTER = [(0, 1), (1, 0), (2, 3), (3, 2)]
MIDDLE = [(1, 2), (2, 1)]
INWARD = [(0, 1), (3, 2)]
OUTWARD = [(1, 0), (2, 3)]


class LineGather:
    def __init__(self, block, axis):
        self.block, self.axis = block, axis
        self.partner = lax.ppermute(block, axis, OUTER)
        self.middle = lax.ppermute(block, axis, MIDDLE)

    def second(self, *held):
        partner, middle = after_all((self.partner, self.middle), *held)
        self.outer = lax.ppermute(middle, self.axis, OUTWARD)
        self.middle_far = lax.ppermute(partner, self.axis, MIDDLE)

    def third(self, *held):
        self.outer_far = lax.ppermute(after(self.middle_far, *held), self.axis, OUTWARD)

    def slots_begun(self):
        return [[self.block], [self.partner]]

    def slots_ended(self):
        return [[self.middle, self.outer], [self.middle_far, self.outer_far]]


def added(*terms):
    total = sum(term.astype(jnp.float32) for term in terms)
    return total.astype(terms[0].dtype)


class LineScatter:
    def __init__(self, far, near, axis):
        self.near, self.axis = near, axis
        self.far, self.far_in = far, lax.ppermute(far, axis, INWARD)

    def second(self, own, partner, *held):
        self.own, self.partner = own, partner
        far, near = after_all((added(self.far, self.far_in), self.near), *held)
        self.first_hop = (far,)
        self.near_in = lax.ppermute(near, self.axis, INWARD)
        self.far_out = lax.ppermute(far, self.axis, MIDDLE)

    def third(self, *held):
        near, partner = after_all(
            (added(self.near, self.near_in), added(self.partner, self.far_out)), *held
        )
        self.second_hop = (near, partner)
        near = lax.ppermute(near, self.axis, MIDDLE)
        partner = lax.ppermute(partner, self.axis, OUTER)
        self.terms = [self.own, near, partner]


def qkv_kernel(counts, begun, ended, order, *refs):
    refs = list(refs)
    xs = [[refs.pop(0) for _ in range(count)] for count in counts]
    gain_ref, wq_ref, wkv_ref = (refs.pop(0) for _ in range(3))
    if begun:
        accq_in, acckv_in, squares_in = (refs.pop(0) for _ in range(3))
    if ended:
        qs_ref, kvs_ref, q_ref, kv_ref, accq, acckv, squares = refs
    else:
        accq, acckv, squares = refs
    step = pl.program_id(0)
    per = pl.num_programs(0) // len(counts)

    @pl.when(step == 0)
    def _():
        if begun:
            accq[...] = accq_in[...]
            acckv[...] = acckv_in[...]
            squares[...] = squares_in[...]
        else:
            accq[...] = jnp.zeros_like(accq)
            acckv[...] = jnp.zeros_like(acckv)
            squares[...] = jnp.zeros_like(squares)

    slot = step // per
    values = None
    for s, slot_refs in enumerate(xs):
        total = sum(ref[...].astype(jnp.float32) for ref in slot_refs)
        values = total if values is None else jnp.where(slot == s, total, values)
    squares[...] += jnp.broadcast_to(
        jnp.sum(values * values, axis=-1, keepdims=True), squares.shape
    )
    scaled = (values * gain_ref[...]).astype(jnp.bfloat16)
    accq[...] += jnp.dot(scaled, wq_ref[...], preferred_element_type=jnp.float32)
    acckv[...] += jnp.dot(scaled, wkv_ref[...], preferred_element_type=jnp.float32)
    if ended:

        @pl.when(step == pl.num_programs(0) - 1)
        def _():
            root = lax.rsqrt(squares[:, :1] / ended + 1e-05)
            q_ref[...] = (accq[...] * root * qs_ref[...]).astype(q_ref.dtype)
            kv_ref[...] = (acckv[...] * root * kvs_ref[...]).astype(kv_ref.dtype)


def project_part(slots, order, norm_gain, w_q, kv_weight, begun, scales):
    rows, depth = slots[0][0].shape
    tile = tile_of(depth, 512)
    per = depth // tile
    q_cols, kv_cols = w_q.shape[1], kv_weight.shape[1]

    def place(g, order):
        return order[g // per] * per + lax.rem(g, per)

    def whole(shape):
        return pl.BlockSpec(shape, lambda g, order: (0,) * len(shape))

    def of_slot(s):
        return pl.BlockSpec(
            (rows, tile), lambda g, order: (0, jnp.clip(g - s * per, 0, per - 1))
        )

    operands = [array for slot in slots for array in slot]
    in_specs = [of_slot(s) for s, slot in enumerate(slots) for _ in slot]
    operands += [norm_gain.reshape(1, -1), w_q, kv_weight]
    in_specs += [
        pl.BlockSpec((1, tile), lambda g, order: (0, place(g, order))),
        pl.BlockSpec((tile, q_cols), lambda g, order: (place(g, order), 0)),
        pl.BlockSpec((tile, kv_cols), lambda g, order: (place(g, order), 0)),
    ]
    sums = [(rows, q_cols), (rows, kv_cols), (rows, HEAD_SIZE)]
    if begun is not None:
        operands += list(begun)
        in_specs += [whole(shape) for shape in sums]
    if scales is not None:
        operands += [scale.reshape(1, -1) for scale in scales]
        in_specs += [whole((1, q_cols)), whole((1, kv_cols))]
        out_shapes = [jax.ShapeDtypeStruct(shape, jnp.bfloat16) for shape in sums[:2]]
        scratch = [pltpu.VMEM(shape, jnp.float32) for shape in sums]
    else:
        out_shapes = [jax.ShapeDtypeStruct(shape, jnp.float32) for shape in sums]
        scratch = []
    return pl.pallas_call(
        functools.partial(
            qkv_kernel,
            [len(slot) for slot in slots],
            begun is not None,
            0 if scales is None else w_q.shape[0],
        ),
        grid_spec=pltpu.PrefetchScalarGridSpec(
            num_scalar_prefetch=1,
            grid=(len(slots) * per,),
            in_specs=in_specs,
            out_specs=[whole(out.shape) for out in out_shapes],
            scratch_shapes=scratch,
        ),
        out_shape=out_shapes,
        compiler_params=pltpu.CompilerParams(vmem_limit_bytes=40 * MIB),
        cost_estimate=pl.CostEstimate(
            flops=2 * rows * depth * len(slots) * (q_cols + kv_cols),
            bytes_accessed=2 * depth * len(slots) * (q_cols + kv_cols),
            transcendentals=0,
        ),
        name="norm_qkv",
    )(order, *operands)


def out_kernel(order, x_ref, w_ref, *o_refs):
    step = pl.program_id(0)
    per = pl.num_programs(0) // len(o_refs)
    product = jnp.dot(x_ref[...], w_ref[...], preferred_element_type=jnp.float32)
    for s, o_ref in enumerate(o_refs):

        @pl.when(step // per == s)
        def _(o_ref=o_ref):
            o_ref[...] = product.astype(o_ref.dtype)


def project_out(attended, w_o, order, block):
    rows, depth = attended.shape
    tile = tile_of(block, 512)
    per = block // tile
    count = order.shape[0]

    def of_block(s):
        return pl.BlockSpec(
            (rows, tile), lambda g, order: (0, jnp.clip(g - s * per, 0, per - 1))
        )

    return pl.pallas_call(
        out_kernel,
        grid_spec=pltpu.PrefetchScalarGridSpec(
            num_scalar_prefetch=1,
            grid=(count * per,),
            in_specs=[
                pl.BlockSpec((rows, depth), lambda g, order: (0, 0)),
                pl.BlockSpec(
                    (depth, tile), lambda g, order: (0, order[g // per] * per + lax.rem(g, per))
                ),
            ],
            out_specs=[of_block(s) for s in range(count)],
        ),
        out_shape=[jax.ShapeDtypeStruct((rows, block), jnp.bfloat16)] * count,
        compiler_params=pltpu.CompilerParams(vmem_limit_bytes=40 * MIB),
        cost_estimate=pl.CostEstimate(
            flops=2 * rows * depth * count * block,
            bytes_accessed=2 * depth * count * block,
            transcendentals=0,
        ),
        name="project_out",
    )(order, attended, w_o)


def with_ones(values):
    return jnp.concatenate([values, jnp.ones_like(values)], axis=1)


def scores_of(queries, keys):
    return lax.dot_general(
        queries, keys, (((1,), (1,)), ((), ())), preferred_element_type=jnp.float32
    )


def prefill_kernel(kv_heads, group, span, first, len_ref, q_ref, cache_ref, new_ref, o_ref, *scratch):
    accs, peaks = scratch[:kv_heads], scratch[kv_heads:]
    tokens = q_ref.shape[0]
    rows = group * tokens
    live = len_ref[first + pl.program_id(0)]
    full = live // span
    query_token = lax.rem(lax.broadcasted_iota(jnp.int32, (rows, tokens), 0), tokens)
    key_token = lax.broadcasted_iota(jnp.int32, (rows, tokens), 1)
    causal = key_token <= query_token
    lane = lax.broadcasted_iota(jnp.int32, (1, span), 1)

    def queries_of(a):
        return jnp.concatenate(
            [
                q_ref[:, (a * group + h) * HEAD_SIZE : (a * group + h + 1) * HEAD_SIZE]
                for h in range(group)
            ],
            axis=0,
        )

    def columns(a, part):
        return pl.ds((2 * a + part) * HEAD_SIZE, HEAD_SIZE)

    for a in range(kv_heads):
        scores = jnp.where(causal, scores_of(queries_of(a), new_ref[:, columns(a, 0)]), MASKED)
        top = jnp.broadcast_to(jnp.max(scores, axis=-1, keepdims=True), (rows, HEAD_SIZE))
        weights = jnp.exp2(scores - top[:, :tokens]).astype(jnp.bfloat16)
        accs[a][...] = jnp.dot(
            weights, with_ones(new_ref[:, columns(a, 1)]), preferred_element_type=jnp.float32
        )
        peaks[a][...] = top

    def block(s, bias):
        at = pl.multiple_of(s * span, span)
        scores = [
            scores_of(queries_of(a), cache_ref[0, 0, pl.ds(at, span), columns(a, 0)])
            for a in range(kv_heads)
        ]
        for a in range(kv_heads):
            here = scores[a] if bias is None else scores[a] + bias
            before = peaks[a][...]
            top = jnp.maximum(before, jnp.max(here, axis=-1, keepdims=True))
            weights = jnp.exp2(
                here - jnp.concatenate([top] * (span // HEAD_SIZE), axis=1)
            ).astype(jnp.bfloat16)
            fade = jnp.exp2(before - top)
            values = cache_ref[0, 0, pl.ds(at, span), columns(a, 1)]
            accs[a][...] = accs[a][...] * jnp.concatenate([fade, fade], axis=1) + jnp.dot(
                weights, with_ones(values), preferred_element_type=jnp.float32
            )
            peaks[a][...] = top

    def step(s, carry):
        block(s, None)
        return carry

    lax.fori_loop(0, full, step, 0)

    @pl.when(full * span < live)
    def _():
        block(full, jnp.where(lane + full * span < live, 0.0, MASKED))

    for a in range(kv_heads):
        result = accs[a][:, :HEAD_SIZE] / accs[a][:, HEAD_SIZE:]
        for h in range(group):
            o_ref[:, (a * group + h) * HEAD_SIZE : (a * group + h + 1) * HEAD_SIZE] = result[
                h * tokens : (h + 1) * tokens
            ].astype(o_ref.dtype)


def prefill_attention(queries, prefix_cache, first, count, new_kv, prefix_len):
    width = queries.shape[1]
    positions, page = prefix_cache.shape[2:]
    kv_heads = page // (2 * HEAD_SIZE)
    group = width // HEAD_SIZE // kv_heads
    span = tile_of(positions, 512)
    rows = group * PROMPT_TOKENS
    return pl.pallas_call(
        functools.partial(prefill_kernel, kv_heads, group, span, first),
        grid_spec=pltpu.PrefetchScalarGridSpec(
            num_scalar_prefetch=1,
            grid=(count,),
            in_specs=[
                pl.BlockSpec((PROMPT_TOKENS, width), lambda g, n: (g, 0)),
                pl.BlockSpec((1, 1, positions, page), lambda g, n: (0, first + g, 0, 0)),
                pl.BlockSpec((PROMPT_TOKENS, page), lambda g, n: (g, 0)),
            ],
            out_specs=pl.BlockSpec((PROMPT_TOKENS, width), lambda g, n: (g, 0)),
            scratch_shapes=[pltpu.VMEM((rows, 2 * HEAD_SIZE), jnp.float32)] * kv_heads
            + [pltpu.VMEM((rows, HEAD_SIZE), jnp.float32)] * kv_heads,
        ),
        out_shape=jax.ShapeDtypeStruct((count * PROMPT_TOKENS, width), jnp.bfloat16),
        compiler_params=pltpu.CompilerParams(vmem_limit_bytes=40 * MIB),
        cost_estimate=pl.CostEstimate(
            flops=8 * count * rows * kv_heads * (positions + PROMPT_TOKENS) * HEAD_SIZE,
            bytes_accessed=2 * count * positions * page,
            transcendentals=count * rows * kv_heads * (positions + PROMPT_TOKENS),
        ),
        name="prefill_attention",
    )(prefix_len, queries, prefix_cache, new_kv)


def decode_kernel(
    kv_heads, batch, len_ref, row_ref, q_ref, cache_ref, landed_ref, fresh_ref, o_ref, acc, peak
):
    row_count, context = cache_ref.shape[1], cache_ref.shape[2]
    per_row = q_ref.shape[2]
    steps = fresh_ref.shape[1]
    rows = batch * per_row
    row_of = lax.broadcasted_iota(jnp.int32, (rows, batch * context), 0) // per_row
    key_row = lax.broadcasted_iota(jnp.int32, (rows, batch * context), 1) // context
    key_at = lax.rem(lax.broadcasted_iota(jnp.int32, (rows, batch * context), 1), context)
    fresh_query = lax.broadcasted_iota(jnp.int32, (rows, batch * steps), 0)
    fresh_key = lax.broadcasted_iota(jnp.int32, (rows, batch * steps), 1)
    fresh_live = (fresh_key // steps == fresh_query // per_row) & (
        lax.rem(fresh_key, steps) <= lax.rem(fresh_query, per_row) // (per_row // steps)
    )

    def cached(b, carry):
        first = b * batch
        live = jnp.zeros_like(key_row)
        for r in range(batch):
            live = jnp.where(key_row == r, len_ref[first + r], live)
        cache_live = (row_of == key_row) & (key_at < live)
        pages = cache_ref[0, pl.ds(first, batch)].reshape(batch * context, cache_ref.shape[3])
        fresh = fresh_ref[pl.ds(first, batch)].reshape(batch * steps, fresh_ref.shape[2])
        for a in range(kv_heads):
            queries = q_ref[pl.ds(first, batch), a].reshape(rows, HEAD_SIZE).astype(jnp.bfloat16)
            k_at, v_at = 2 * a * HEAD_SIZE, (2 * a + 1) * HEAD_SIZE
            scores = scores_of(queries, pages[:, k_at : k_at + HEAD_SIZE])
            scores = jnp.where(cache_live, scores, MASKED)
            recent = scores_of(queries, fresh[:, k_at : k_at + HEAD_SIZE].astype(jnp.bfloat16))
            recent = jnp.where(fresh_live, recent, MASKED)
            top = jnp.maximum(
                jnp.max(scores, axis=-1, keepdims=True), jnp.max(recent, axis=-1, keepdims=True)
            )
            weights = jnp.exp2(scores - top).astype(jnp.bfloat16)
            recent = jnp.exp2(recent - top).astype(jnp.bfloat16)
            total = jnp.dot(
                weights,
                with_ones(pages[:, v_at : v_at + HEAD_SIZE]),
                preferred_element_type=jnp.float32,
            ) + jnp.dot(
                recent,
                with_ones(fresh[:, v_at : v_at + HEAD_SIZE].astype(jnp.bfloat16)),
                preferred_element_type=jnp.float32,
            )
            acc[pl.ds(first, batch), a] = total.reshape(batch, per_row, 2 * HEAD_SIZE)
            peak[pl.ds(first, batch), a] = jnp.broadcast_to(top, (rows, HEAD_SIZE)).reshape(
                batch, per_row, HEAD_SIZE
            )
        return carry

    lax.fori_loop(0, row_count // batch, cached, 0)

    def arrival(slot, carry):
        row = row_ref[slot]

        @pl.when(row >= 0)
        def _():
            for a in range(kv_heads):
                queries = q_ref[row, a].astype(jnp.bfloat16)
                k_at, v_at = 2 * a * HEAD_SIZE, (2 * a + 1) * HEAD_SIZE
                scores = scores_of(queries, landed_ref[slot, :, k_at : k_at + HEAD_SIZE])
                before = peak[row, a]
                top = jnp.maximum(before, jnp.max(scores, axis=-1, keepdims=True))
                weights = jnp.exp2(scores - top[:, :1]).astype(jnp.bfloat16)
                fade = jnp.exp2(before - top)
                acc[row, a] = acc[row, a] * jnp.concatenate([fade, fade], axis=1) + jnp.dot(
                    weights,
                    with_ones(landed_ref[slot, :, v_at : v_at + HEAD_SIZE]),
                    preferred_element_type=jnp.float32,
                )

        return carry

    lax.fori_loop(0, row_ref.shape[0], arrival, 0)
    o_ref[...] = (acc[:, :, :, :HEAD_SIZE] / acc[:, :, :, HEAD_SIZE:]).astype(o_ref.dtype)


def decode_attention(queries, dec_cache, dec_len, landed, slot_rows, fresh):
    row_count, kv_heads, per_row = queries.shape[:3]
    context = dec_cache.shape[2]
    batch = max(1, min(row_count, 2 * HEAD_SIZE // context))
    whole = lambda array: pl.BlockSpec(array.shape, lambda g, *_: (0,) * array.ndim)
    return pl.pallas_call(
        functools.partial(decode_kernel, kv_heads, batch),
        grid_spec=pltpu.PrefetchScalarGridSpec(
            num_scalar_prefetch=2,
            grid=(1,),
            in_specs=[whole(queries), whole(dec_cache), whole(landed), whole(fresh)],
            out_specs=whole(queries),
            scratch_shapes=[
                pltpu.VMEM((row_count, kv_heads, per_row, 2 * HEAD_SIZE), jnp.float32),
                pltpu.VMEM((row_count, kv_heads, per_row, HEAD_SIZE), jnp.float32),
            ],
        ),
        out_shape=jax.ShapeDtypeStruct(queries.shape, jnp.float32),
        compiler_params=pltpu.CompilerParams(vmem_limit_bytes=32 * MIB),
        cost_estimate=pl.CostEstimate(
            flops=8 * queries.size * batch * context,
            bytes_accessed=2 * dec_cache.size + 2 * landed.size,
            transcendentals=queries.size * batch * context // HEAD_SIZE,
        ),
        name="decode_attention",
    )(dec_len, slot_rows, queries, dec_cache, landed, fresh)


def shards(
    prefill_x,
    norm_gain,
    w_q,
    q_scale,
    key_value_weight,
    key_value_scale,
    w_o,
    o_scale,
    prefix_cache,
    prefix_len,
    dec_x,
    dec_cache,
    dec_len,
    place,
):
    prompts_total = prefix_cache.shape[1]
    row_count = dec_cache.shape[1]
    page_width = prefix_cache.shape[3]
    kv_heads = page_width // (2 * HEAD_SIZE)
    query_heads = w_q.shape[1] // HEAD_SIZE
    group_size = query_heads // kv_heads
    steps = dec_x.shape[0]
    section_count = lax.axis_size("section")
    section_index = lax.axis_index("section")
    tensor_count = lax.axis_size("tensor")
    tensor_index = lax.axis_index("tensor")
    head_span = max(1, 8 // query_heads)
    span_bits = head_span.bit_length() - 1
    on_line = tensor_count == 4
    block_width = w_o.shape[1] // tensor_count
    order = jnp.stack(
        line_order(tensor_index) if on_line else list(range(tensor_count))
    ).astype(jnp.int32)
    scales = (q_scale * EXP2_FACTOR, key_value_scale)

    weights = (norm_gain, w_q, key_value_weight)

    def kv_of_head(new_kv):
        for bit_number in range(span_bits):
            partner = partner_2(new_kv, "tensor", bit_number)
            new_kv = joined(new_kv, partner, bit_number, 1, tensor_index)
        return new_kv

    def finished(x, terms):
        total = sum(term.astype(jnp.float32) for term in terms)
        return (x.astype(jnp.float32) + total * o_scale).astype(jnp.bfloat16)

    dec_rows = dec_x.reshape(steps * row_count, -1)
    bounds = sorted({0, 1, max(1, prompts_total - 1), prompts_total})
    spans = list(zip(bounds[:-1], bounds[1:]))
    chunks = [prefill_x[first * PROMPT_TOKENS : last * PROMPT_TOKENS] for first, last in spans]
    blocks = chunks[:-1] + [jnp.concatenate([chunks[-1], dec_rows], axis=0)]
    pages, queries_of, kv_of = [], [], []

    def attention(k, queries):
        first, last = spans[k]
        return prefill_attention(
            queries, prefix_cache, first, last - first, pages[k], prefix_len
        )

    def keep(k, queries, new_kv):
        new_kv = kv_of_head(new_kv)
        pages.append(new_kv[: chunks[k].shape[0]])
        queries_of.append(queries)
        kv_of.append(new_kv)

    def back(attended):
        far, near = project_out(attended, w_o, order[:1:-1], block_width)
        scatter = LineScatter(far, near, "tensor")
        partner, own = project_out(after(attended, far), w_o, order[1::-1], block_width)
        return scatter, own, partner

    if on_line:
        last = len(spans) - 1
        gather = LineGather(blocks[0], "tensor")
        gather.second()
        scatters = []
        for k in range(last + 1):
            slots = gather.slots_begun()
            if k == 0:
                slots[0][0] = after(slots[0][0], gather.middle)
            elif k == 1:
                slots[0][0] = after(slots[0][0], *scatters[0].first_hop, gather.outer)
            else:
                slots[0][0] = after(slots[0][0], own)
            begun = project_part(slots, order[:2], *weights, None, None)
            if k == 0:
                gather.third(begun[2])
            elif k == 1:
                scatters[0].third(begun[2])
            else:
                scatters[k - 1].second(own, partner, begun[2])
            if k < last and k == 0:
                following = LineGather(
                    after(blocks[1], gather.outer, gather.middle_far, begun[2]), "tensor"
                )
            slots = gather.slots_ended()
            if k == 1:
                slots[1][0] = after(slots[1][0], *scatters[0].second_hop)
            elif k > 1:
                slots[1][0] = after(slots[1][0], *scatters[k - 1].first_hop)
            queries, new_kv = project_part(slots, order[2:], *weights, begun, scales)
            keep(k, queries, new_kv)
            if 0 < k < last:
                following.second(queries)
                queries = after(queries, following.partner, following.middle)
            attended = attention(k, queries)
            if k > 1:
                scatters[k - 1].third(attended)
                attended = after(attended, *scatters[k - 1].second_hop)
            if k < last:
                if k == 0:
                    following.second(attended)
                    attended = after(attended, following.partner, following.middle)
                else:
                    following.third(attended)
                    attended = after(
                        attended, following.outer, following.middle_far, *scatters[k - 1].terms
                    )
            scatter, own, partner = back(attended)
            scatters.append(scatter)
            if k == 0:
                scatter.second(own, partner, own)
                if last:
                    following.third(own)
            if k < last:
                gather = following
                if k + 2 <= last:
                    following = LineGather(
                        after(blocks[k + 2], gather.outer, gather.middle_far, own), "tensor"
                    )
        if last:
            scatters[last].second(own, partner, own)
        else:
            scatters[last].third()
        dec_hold = scatters[last].first_hop
        if last:
            dec_hold += tuple(scatters[last - 1].terms)
        queries, new_kv = queries_of[last], kv_of[last]
    else:
        terms_of = []
        for k, block in enumerate(blocks):
            whole = lax.all_gather(block, "tensor", axis=1, tiled=True)
            queries, new_kv = project_part([[whole]], order[:1], *weights, None, scales)
            keep(k, queries, new_kv)
            partial = project_out(attention(k, queries), w_o, order[:1], w_o.shape[1])[0]
            terms_of.append(
                [lax.psum_scatter(partial, "tensor", scatter_dimension=1, tiled=True)]
            )
        dec_hold = ()
    tokens = chunks[-1].shape[0]
    dec_queries, fresh_kv = queries_of[-1][tokens:], kv_of[-1][tokens:]

    own_block = jnp.concatenate(pages, axis=0).reshape(prompts_total, PROMPT_TOKENS, page_width)
    owners = (place // row_count).reshape(section_count, prompts_total)
    targets = (place % row_count).reshape(section_count, prompts_total)
    owner_hits = (owners[:, :, None] == jnp.arange(section_count)[None, None, :]).astype(jnp.int32)
    slot_ranks = jnp.sum((jnp.cumsum(owner_hits, axis=1) - owner_hits) * owner_hits, axis=2)
    capacity = prompts_total // 2
    slot_ids = jnp.arange(capacity)
    sending = lax.dynamic_index_in_dim(owner_hits, section_index, 0, keepdims=False)
    my_ranks = lax.dynamic_index_in_dim(slot_ranks, section_index, 0, keepdims=False)
    selector = (
        jnp.transpose(sending)[:, None, :] * (my_ranks[None, None, :] == slot_ids[None, :, None])
    ).astype(jnp.bfloat16)
    here = (owners == section_index)[:, None, :] & (
        slot_ranks[:, None, :] == slot_ids[None, :, None]
    )
    slot_rows = jnp.sum(jnp.where(here, targets[:, None, :] + 1, 0), axis=2) - 1
    outgoing = jnp.einsum(
        "skp,pcw->skcw", selector, own_block, preferred_element_type=jnp.float32
    ).astype(jnp.bfloat16)
    received = lax.all_to_all(outgoing, "section", split_axis=0, concat_axis=0, tiled=True)
    landed = received.reshape(section_count * capacity, PROMPT_TOKENS, page_width)

    dec_queries = jnp.transpose(
        dec_queries.reshape(steps, row_count, kv_heads, group_size, HEAD_SIZE), (1, 2, 0, 3, 4)
    ).reshape(row_count, kv_heads, steps * group_size, HEAD_SIZE)
    fresh = jnp.transpose(fresh_kv.reshape(steps, row_count, page_width), (1, 0, 2))
    dec_attended = decode_attention(
        after(dec_queries.astype(jnp.float32), *dec_hold),
        dec_cache,
        dec_len,
        landed,
        slot_rows.reshape(-1).astype(jnp.int32),
        fresh.astype(jnp.float32),
    )
    dec_attended = (
        jnp.transpose(
            dec_attended.reshape(row_count, kv_heads, steps, group_size, HEAD_SIZE), (2, 0, 1, 3, 4)
        )
        .reshape(steps * row_count, -1)
        .astype(jnp.bfloat16)
    )
    if on_line:
        if last:
            scatters[last].third(dec_attended)
        scatter, own, partner = back(after(dec_attended, *scatters[last].second_hop))
        scatter.second(own, partner)
        scatter.third()
        terms_of = [other.terms for other in scatters]
        dec_terms = scatter.terms
    else:
        partial = project_out(dec_attended, w_o, order[:1], w_o.shape[1])[0]
        dec_terms = [lax.psum_scatter(partial, "tensor", scatter_dimension=1, tiled=True)]
    prefill_out = jnp.concatenate(
        [finished(x, terms) for x, terms in zip(chunks, terms_of)], axis=0
    )
    decode_out = finished(dec_rows, dec_terms).reshape(dec_x.shape)
    return (prefill_out, decode_out)


def solution(mesh):
    in_specs = (
        P(("groups", "section"), "tensor"),
        P(),
        P(None, "tensor"),
        P("tensor"),
        P(None, "tensor"),
        P("tensor"),
        P("tensor", None),
        P("tensor"),
        P("tensor", ("groups", "section"), None, None),
        P(("groups", "section")),
        P(None, ("groups", "section"), "tensor"),
        P("tensor", ("groups", "section"), None, None),
        P(("groups", "section")),
        P("groups"),
    )
    out_specs = (P(("groups", "section"), "tensor"), P(None, ("groups", "section"), "tensor"))
    return jax.shard_map(shards, mesh=mesh, in_specs=in_specs, out_specs=out_specs, check_vma=False)
```

```python
import functools
import math

import jax
import jax.numpy as jnp
from jax import lax
from jax.experimental import pallas as pl
from jax.experimental.pallas import tpu as pltpu
from jax.sharding import PartitionSpec as P

HEAD_SIZE = 128
PROMPT_TOKENS = 128
KERNEL_VMEM = 46 << 20
WEIGHT_BUFFERS = 8
EXP2_FACTOR = math.log2(math.e) / math.sqrt(HEAD_SIZE)
MASKED = -1e30


def partner_2(block, axis, distance):
    count = lax.axis_size(axis)
    route = []
    for low in range(count):
        high = low | 1 << distance
        if high != low and high < count:
            route += [(low, high), (high, low)]
    return lax.ppermute(block, axis, route)


def joined(portion, partner, bit_number, concat_dim, tensor_index):
    upper_half = tensor_index // 2**bit_number % 2 == 1
    lower_first = jnp.concatenate([portion, partner], axis=concat_dim)
    upper_first = jnp.concatenate([partner, portion], axis=concat_dim)
    return jnp.where(upper_half, upper_first, lower_first)


def tile_of(extent, most):
    tile = extent
    while tile > most and tile % 2 == 0:
        tile //= 2
    return tile


def after(value, *others):
    return lax.optimization_barrier((value,) + others)[0]


def after_all(values, *others):
    return lax.optimization_barrier(tuple(values) + others)[: len(values)]


def line_order(index):
    low = index < 2
    return [index, index ^ 1, jnp.where(low, 2, 1), jnp.where(low, 3, 0)]


OUTER = [(0, 1), (1, 0), (2, 3), (3, 2)]
MIDDLE = [(1, 2), (2, 1)]
INWARD = [(0, 1), (3, 2)]
OUTWARD = [(1, 0), (2, 3)]


class LineGather:
    def __init__(self, block, axis, outer_held=(), middle_held=()):
        self.block, self.axis = block, axis
        self.partner = lax.ppermute(after(block, *outer_held), axis, OUTER)
        self.middle = lax.ppermute(after(block, *middle_held), axis, MIDDLE)

    def second(self, *held):
        partner, middle = after_all((self.partner, self.middle), *held)
        self.outer = lax.ppermute(middle, self.axis, OUTWARD)
        self.middle_far = lax.ppermute(partner, self.axis, MIDDLE)

    def third(self, *held):
        self.outer_far = lax.ppermute(after(self.middle_far, *held), self.axis, OUTWARD)

    def slots(self):
        return [
            [self.block],
            [self.partner],
            [self.middle, self.outer],
            [self.middle_far, self.outer_far],
        ]


def added(*terms):
    total = sum(term.astype(jnp.float32) for term in terms)
    return total.astype(terms[0].dtype)


class LineScatter:
    def __init__(self, own, partner, near, far, axis):
        self.own, self.partner, self.near, self.far = own, partner, near, far
        self.axis = axis
        self.far_in = lax.ppermute(far, axis, INWARD)

    def second(self, *held):
        far, near = after_all((added(self.far, self.far_in), self.near), *held)
        self.first_hop = (far,)
        self.near_in = lax.ppermute(near, self.axis, INWARD)
        self.far_out = lax.ppermute(far, self.axis, MIDDLE)

    def third(self, *held):
        near, partner = after_all(
            (added(self.near, self.near_in), added(self.partner, self.far_out)), *held
        )
        self.second_hop = (near, partner)
        near = lax.ppermute(near, self.axis, MIDDLE)
        partner = lax.ppermute(partner, self.axis, OUTER)
        self.terms = [self.own, near, partner]


def qkv_kernel(counts, begun, ended, tile, order, *refs):
    refs = list(refs)
    arrays = sum(counts)
    xs = [refs.pop(0) for _ in range(arrays)]
    gain_ref, wq_ref, wkv_ref = (refs.pop(0) for _ in range(3))
    sums_in = [refs.pop(0) for _ in range(3)] if begun else []
    if ended:
        qs_ref, kvs_ref, q_ref, kv_ref, accq, acckv, squares = (refs.pop(0) for _ in range(7))
    else:
        accq, acckv, squares = (refs.pop(0) for _ in range(3))
    x_bufs = [refs.pop(0) for _ in range(arrays)]
    wq_buf, wkv_buf, x_sem, w_sem, sum_sem = refs
    per = x_bufs[0].shape[1] // tile
    steps = len(counts) * per
    ahead = min(steps, wq_buf.shape[0])

    def weight_copies(step):
        buffer = lax.rem(step, ahead)
        at = pl.multiple_of((order[step // per] * per + lax.rem(step, per)) * tile, tile)
        return [
            pltpu.make_async_copy(ref.at[pl.ds(at, tile)], buf.at[buffer], w_sem.at[w, buffer])
            for w, (ref, buf) in enumerate([(wq_ref, wq_buf), (wkv_ref, wkv_buf)])
        ]

    x_copies = [
        pltpu.make_async_copy(ref, buf, x_sem.at[a]) for a, (ref, buf) in enumerate(zip(xs, x_bufs))
    ]
    sum_copies = [
        pltpu.make_async_copy(ref, acc, sum_sem.at[a])
        for a, (ref, acc) in enumerate(zip(sums_in, (accq, acckv, squares)))
    ]
    for copy in x_copies[: counts[0]] + sum_copies:
        copy.start()
    for step in range(ahead):
        for copy in weight_copies(step):
            copy.start()
    for copy in x_copies[counts[0] :]:
        copy.start()
    for copy in sum_copies:
        copy.wait()
    if not begun:
        accq[...] = jnp.zeros_like(accq)
        acckv[...] = jnp.zeros_like(acckv)
        squares[...] = jnp.zeros_like(squares)

    taken = 0
    for s, count in enumerate(counts):
        for copy in x_copies[taken : taken + count]:
            copy.wait()
        bufs = x_bufs[taken : taken + count]
        taken += count

        def body(j, carry, s=s, bufs=bufs):
            step = s * per + j
            for copy in weight_copies(step):
                copy.wait()
            at = pl.multiple_of(j * tile, tile)
            values = sum(buf[:, pl.ds(at, tile)].astype(jnp.float32) for buf in bufs)
            gain = gain_ref[:, pl.ds(pl.multiple_of((order[s] * per + j) * tile, tile), tile)]
            squares[...] += jnp.broadcast_to(
                jnp.sum(values * values, axis=-1, keepdims=True), squares.shape
            )
            scaled = (values * gain).astype(jnp.bfloat16)
            buffer = lax.rem(step, ahead)
            accq[...] += jnp.dot(scaled, wq_buf[buffer], preferred_element_type=jnp.float32)
            acckv[...] += jnp.dot(scaled, wkv_buf[buffer], preferred_element_type=jnp.float32)

            @pl.when(step + ahead < steps)
            def _():
                for copy in weight_copies(step + ahead):
                    copy.start()

            return carry

        lax.fori_loop(0, per, body, 0)
    if ended:
        root = lax.rsqrt(squares[:, :1] / ended + 1e-05)
        q_ref[...] = (accq[...] * root * qs_ref[...]).astype(q_ref.dtype)
        kv_ref[...] = (acckv[...] * root * kvs_ref[...]).astype(kv_ref.dtype)


def project_part(slots, order, norm_gain, w_q, kv_weight, begun, scales):
    rows, depth = slots[0][0].shape
    tile = tile_of(depth, 512)
    q_cols, kv_cols = w_q.shape[1], kv_weight.shape[1]
    arrays = [array for slot in slots for array in slot]

    def whole(shape):
        return pl.BlockSpec(shape, lambda g, order: (0,) * len(shape))

    anywhere = pl.BlockSpec(memory_space=pl.ANY)
    operands = arrays + [norm_gain.reshape(1, -1), w_q, kv_weight]
    in_specs = [anywhere] * len(arrays) + [whole((1, norm_gain.shape[0])), anywhere, anywhere]
    sums = [(rows, q_cols), (rows, kv_cols), (rows, HEAD_SIZE)]
    if begun is not None:
        operands += list(begun)
        in_specs += [anywhere] * 3
    if scales is not None:
        operands += [scale.reshape(1, -1) for scale in scales]
        in_specs += [whole((1, q_cols)), whole((1, kv_cols))]
        out_shapes = [jax.ShapeDtypeStruct(shape, jnp.bfloat16) for shape in sums[:2]]
        scratch = [pltpu.VMEM(shape, jnp.float32) for shape in sums]
    else:
        out_shapes = [jax.ShapeDtypeStruct(shape, jnp.float32) for shape in sums]
        scratch = []
    return pl.pallas_call(
        functools.partial(
            qkv_kernel,
            [len(slot) for slot in slots],
            begun is not None,
            0 if scales is None else w_q.shape[0],
            tile,
        ),
        grid_spec=pltpu.PrefetchScalarGridSpec(
            num_scalar_prefetch=1,
            grid=(1,),
            in_specs=in_specs,
            out_specs=[whole(out.shape) for out in out_shapes],
            scratch_shapes=scratch
            + [pltpu.VMEM((rows, depth), jnp.bfloat16) for _ in arrays]
            + [
                pltpu.VMEM((WEIGHT_BUFFERS, tile, q_cols), jnp.bfloat16),
                pltpu.VMEM((WEIGHT_BUFFERS, tile, kv_cols), jnp.bfloat16),
                pltpu.SemaphoreType.DMA((len(arrays),)),
                pltpu.SemaphoreType.DMA((2, WEIGHT_BUFFERS)),
                pltpu.SemaphoreType.DMA((3,)),
            ],
        ),
        out_shape=out_shapes,
        compiler_params=pltpu.CompilerParams(vmem_limit_bytes=KERNEL_VMEM),
        cost_estimate=pl.CostEstimate(
            flops=2 * rows * depth * len(slots) * (q_cols + kv_cols),
            bytes_accessed=2 * depth * len(slots) * (q_cols + kv_cols),
            transcendentals=0,
        ),
        name="norm_qkv",
    )(order, *operands)


def out_kernel(count, tile, order, x_ref, w_ref, *refs):
    outs = refs[:count]
    x_buf, w_buf, x_sem, w_sem, o_sem = refs[count : count + 5]
    o_bufs = refs[count + 5 :]
    per = outs[0].shape[1] // tile
    steps = count * per
    ahead = min(steps, w_buf.shape[0])

    def weight_copy(step):
        at = pl.multiple_of((order[step // per] * per + lax.rem(step, per)) * tile, tile)
        buffer = lax.rem(step, ahead)
        return pltpu.make_async_copy(
            w_ref.at[:, pl.ds(at, tile)], w_buf.at[buffer], w_sem.at[buffer]
        )

    x_copy = pltpu.make_async_copy(x_ref, x_buf, x_sem)
    x_copy.start()
    for step in range(ahead):
        weight_copy(step).start()
    x_copy.wait()
    o_copies = []
    for s, (out, o_buf) in enumerate(zip(outs, o_bufs)):

        def body(j, carry, s=s, o_buf=o_buf):
            step = s * per + j
            weight_copy(step).wait()
            o_buf[:, pl.ds(pl.multiple_of(j * tile, tile), tile)] = jnp.dot(
                x_buf[...], w_buf[lax.rem(step, ahead)], preferred_element_type=jnp.float32
            ).astype(o_buf.dtype)

            @pl.when(step + ahead < steps)
            def _():
                weight_copy(step + ahead).start()

            return carry

        lax.fori_loop(0, per, body, 0)
        o_copies.append(pltpu.make_async_copy(o_buf, out, o_sem.at[s]))
        o_copies[-1].start()
    for copy in o_copies:
        copy.wait()


def project_out(attended, w_o, order, block):
    rows, depth = attended.shape
    tile = tile_of(block, 512)
    count = order.shape[0]
    anywhere = pl.BlockSpec(memory_space=pl.ANY)
    return pl.pallas_call(
        functools.partial(out_kernel, count, tile),
        grid_spec=pltpu.PrefetchScalarGridSpec(
            num_scalar_prefetch=1,
            grid=(1,),
            in_specs=[anywhere, anywhere],
            out_specs=[anywhere] * count,
            scratch_shapes=[
                pltpu.VMEM((rows, depth), jnp.bfloat16),
                pltpu.VMEM((WEIGHT_BUFFERS, depth, tile), jnp.bfloat16),
                pltpu.SemaphoreType.DMA,
                pltpu.SemaphoreType.DMA((WEIGHT_BUFFERS,)),
                pltpu.SemaphoreType.DMA((count,)),
            ]
            + [pltpu.VMEM((rows, block), jnp.bfloat16)] * count,
        ),
        out_shape=[jax.ShapeDtypeStruct((rows, block), jnp.bfloat16)] * count,
        compiler_params=pltpu.CompilerParams(vmem_limit_bytes=KERNEL_VMEM),
        cost_estimate=pl.CostEstimate(
            flops=2 * rows * depth * count * block,
            bytes_accessed=2 * depth * count * block,
            transcendentals=0,
        ),
        name="project_out",
    )(order, attended, w_o)


def with_ones(values):
    return jnp.concatenate([values, jnp.ones_like(values)], axis=1)


def scores_of(queries, keys):
    return lax.dot_general(
        queries, keys, (((1,), (1,)), ((), ())), preferred_element_type=jnp.float32
    )


def prefill_kernel(kv_heads, group, span, first, len_ref, q_ref, cache_ref, new_ref, o_ref, *scratch):
    accs, peaks = scratch[:kv_heads], scratch[kv_heads:]
    tokens = q_ref.shape[0]
    rows = group * tokens
    live = len_ref[first + pl.program_id(0)]
    full = live // span
    query_token = lax.rem(lax.broadcasted_iota(jnp.int32, (rows, tokens), 0), tokens)
    key_token = lax.broadcasted_iota(jnp.int32, (rows, tokens), 1)
    causal = key_token <= query_token
    lane = lax.broadcasted_iota(jnp.int32, (1, span), 1)

    def queries_of(a):
        return jnp.concatenate(
            [
                q_ref[:, (a * group + h) * HEAD_SIZE : (a * group + h + 1) * HEAD_SIZE]
                for h in range(group)
            ],
            axis=0,
        )

    def columns(a, part):
        return pl.ds((2 * a + part) * HEAD_SIZE, HEAD_SIZE)

    for a in range(kv_heads):
        scores = jnp.where(causal, scores_of(queries_of(a), new_ref[:, columns(a, 0)]), MASKED)
        top = jnp.broadcast_to(jnp.max(scores, axis=-1, keepdims=True), (rows, HEAD_SIZE))
        weights = jnp.exp2(scores - top[:, :tokens]).astype(jnp.bfloat16)
        accs[a][...] = jnp.dot(
            weights, with_ones(new_ref[:, columns(a, 1)]), preferred_element_type=jnp.float32
        )
        peaks[a][...] = top

    def block(s, bias):
        at = pl.multiple_of(s * span, span)
        scores = [
            scores_of(queries_of(a), cache_ref[0, 0, pl.ds(at, span), columns(a, 0)])
            for a in range(kv_heads)
        ]
        for a in range(kv_heads):
            here = scores[a] if bias is None else scores[a] + bias
            before = peaks[a][...]
            top = jnp.maximum(before, jnp.max(here, axis=-1, keepdims=True))
            weights = jnp.exp2(
                here - jnp.concatenate([top] * (span // HEAD_SIZE), axis=1)
            ).astype(jnp.bfloat16)
            fade = jnp.exp2(before - top)
            values = cache_ref[0, 0, pl.ds(at, span), columns(a, 1)]
            accs[a][...] = accs[a][...] * jnp.concatenate([fade, fade], axis=1) + jnp.dot(
                weights, with_ones(values), preferred_element_type=jnp.float32
            )
            peaks[a][...] = top

    def step(s, carry):
        block(s, None)
        return carry

    lax.fori_loop(0, full, step, 0)

    @pl.when(full * span < live)
    def _():
        block(full, jnp.where(lane + full * span < live, 0.0, MASKED))

    for a in range(kv_heads):
        result = accs[a][:, :HEAD_SIZE] / accs[a][:, HEAD_SIZE:]
        for h in range(group):
            o_ref[:, (a * group + h) * HEAD_SIZE : (a * group + h + 1) * HEAD_SIZE] = result[
                h * tokens : (h + 1) * tokens
            ].astype(o_ref.dtype)


def prefill_attention(queries, prefix_cache, first, count, new_kv, prefix_len):
    width = queries.shape[1]
    positions, page = prefix_cache.shape[2:]
    kv_heads = page // (2 * HEAD_SIZE)
    group = width // HEAD_SIZE // kv_heads
    span = tile_of(positions, 512)
    rows = group * PROMPT_TOKENS
    return pl.pallas_call(
        functools.partial(prefill_kernel, kv_heads, group, span, first),
        grid_spec=pltpu.PrefetchScalarGridSpec(
            num_scalar_prefetch=1,
            grid=(count,),
            in_specs=[
                pl.BlockSpec((PROMPT_TOKENS, width), lambda g, n: (g, 0)),
                pl.BlockSpec((1, 1, positions, page), lambda g, n: (0, first + g, 0, 0)),
                pl.BlockSpec((PROMPT_TOKENS, page), lambda g, n: (g, 0)),
            ],
            out_specs=pl.BlockSpec((PROMPT_TOKENS, width), lambda g, n: (g, 0)),
            scratch_shapes=[pltpu.VMEM((rows, 2 * HEAD_SIZE), jnp.float32)] * kv_heads
            + [pltpu.VMEM((rows, HEAD_SIZE), jnp.float32)] * kv_heads,
        ),
        out_shape=jax.ShapeDtypeStruct((count * PROMPT_TOKENS, width), jnp.bfloat16),
        compiler_params=pltpu.CompilerParams(vmem_limit_bytes=KERNEL_VMEM),
        cost_estimate=pl.CostEstimate(
            flops=8 * count * rows * kv_heads * (positions + PROMPT_TOKENS) * HEAD_SIZE,
            bytes_accessed=2 * count * positions * page,
            transcendentals=count * rows * kv_heads * (positions + PROMPT_TOKENS),
        ),
        name="prefill_attention",
    )(prefix_len, queries, prefix_cache, new_kv)


def decode_kernel(
    kv_heads, batch, len_ref, row_ref, q_ref, cache_ref, landed_ref, fresh_ref, o_ref, acc, peak
):
    row_count, context = cache_ref.shape[1], cache_ref.shape[2]
    per_row = q_ref.shape[2]
    steps = fresh_ref.shape[1]
    rows = batch * per_row
    row_of = lax.broadcasted_iota(jnp.int32, (rows, batch * context), 0) // per_row
    key_row = lax.broadcasted_iota(jnp.int32, (rows, batch * context), 1) // context
    key_at = lax.rem(lax.broadcasted_iota(jnp.int32, (rows, batch * context), 1), context)
    fresh_query = lax.broadcasted_iota(jnp.int32, (rows, batch * steps), 0)
    fresh_key = lax.broadcasted_iota(jnp.int32, (rows, batch * steps), 1)
    fresh_live = (fresh_key // steps == fresh_query // per_row) & (
        lax.rem(fresh_key, steps) <= lax.rem(fresh_query, per_row) // (per_row // steps)
    )

    def cached(b, carry):
        first = b * batch
        live = jnp.zeros_like(key_row)
        for r in range(batch):
            live = jnp.where(key_row == r, len_ref[first + r], live)
        cache_live = (row_of == key_row) & (key_at < live)
        pages = cache_ref[0, pl.ds(first, batch)].reshape(batch * context, cache_ref.shape[3])
        fresh = fresh_ref[pl.ds(first, batch)].reshape(batch * steps, fresh_ref.shape[2])
        for a in range(kv_heads):
            queries = q_ref[pl.ds(first, batch), a].reshape(rows, HEAD_SIZE).astype(jnp.bfloat16)
            k_at, v_at = 2 * a * HEAD_SIZE, (2 * a + 1) * HEAD_SIZE
            scores = scores_of(queries, pages[:, k_at : k_at + HEAD_SIZE])
            scores = jnp.where(cache_live, scores, MASKED)
            recent = scores_of(queries, fresh[:, k_at : k_at + HEAD_SIZE].astype(jnp.bfloat16))
            recent = jnp.where(fresh_live, recent, MASKED)
            top = jnp.maximum(
                jnp.max(scores, axis=-1, keepdims=True), jnp.max(recent, axis=-1, keepdims=True)
            )
            weights = jnp.exp2(scores - top).astype(jnp.bfloat16)
            recent = jnp.exp2(recent - top).astype(jnp.bfloat16)
            total = jnp.dot(
                weights,
                with_ones(pages[:, v_at : v_at + HEAD_SIZE]),
                preferred_element_type=jnp.float32,
            ) + jnp.dot(
                recent,
                with_ones(fresh[:, v_at : v_at + HEAD_SIZE].astype(jnp.bfloat16)),
                preferred_element_type=jnp.float32,
            )
            acc[pl.ds(first, batch), a] = total.reshape(batch, per_row, 2 * HEAD_SIZE)
            peak[pl.ds(first, batch), a] = jnp.broadcast_to(top, (rows, HEAD_SIZE)).reshape(
                batch, per_row, HEAD_SIZE
            )
        return carry

    lax.fori_loop(0, row_count // batch, cached, 0)

    def arrival(slot, carry):
        row = row_ref[slot]

        @pl.when(row >= 0)
        def _():
            for a in range(kv_heads):
                queries = q_ref[row, a].astype(jnp.bfloat16)
                k_at, v_at = 2 * a * HEAD_SIZE, (2 * a + 1) * HEAD_SIZE
                scores = scores_of(queries, landed_ref[slot, :, k_at : k_at + HEAD_SIZE])
                before = peak[row, a]
                top = jnp.maximum(before, jnp.max(scores, axis=-1, keepdims=True))
                weights = jnp.exp2(scores - top[:, :1]).astype(jnp.bfloat16)
                fade = jnp.exp2(before - top)
                acc[row, a] = acc[row, a] * jnp.concatenate([fade, fade], axis=1) + jnp.dot(
                    weights,
                    with_ones(landed_ref[slot, :, v_at : v_at + HEAD_SIZE]),
                    preferred_element_type=jnp.float32,
                )

        return carry

    lax.fori_loop(0, row_ref.shape[0], arrival, 0)
    o_ref[...] = (acc[:, :, :, :HEAD_SIZE] / acc[:, :, :, HEAD_SIZE:]).astype(o_ref.dtype)


def decode_attention(queries, dec_cache, dec_len, landed, slot_rows, fresh):
    row_count, kv_heads, per_row = queries.shape[:3]
    context = dec_cache.shape[2]
    batch = max(1, min(row_count, 2 * HEAD_SIZE // context))
    whole = lambda array: pl.BlockSpec(array.shape, lambda g, *_: (0,) * array.ndim)
    return pl.pallas_call(
        functools.partial(decode_kernel, kv_heads, batch),
        grid_spec=pltpu.PrefetchScalarGridSpec(
            num_scalar_prefetch=2,
            grid=(1,),
            in_specs=[whole(queries), whole(dec_cache), whole(landed), whole(fresh)],
            out_specs=whole(queries),
            scratch_shapes=[
                pltpu.VMEM((row_count, kv_heads, per_row, 2 * HEAD_SIZE), jnp.float32),
                pltpu.VMEM((row_count, kv_heads, per_row, HEAD_SIZE), jnp.float32),
            ],
        ),
        out_shape=jax.ShapeDtypeStruct(queries.shape, jnp.float32),
        compiler_params=pltpu.CompilerParams(vmem_limit_bytes=KERNEL_VMEM),
        cost_estimate=pl.CostEstimate(
            flops=8 * queries.size * batch * context,
            bytes_accessed=2 * dec_cache.size + 2 * landed.size,
            transcendentals=queries.size * batch * context // HEAD_SIZE,
        ),
        name="decode_attention",
    )(dec_len, slot_rows, queries, dec_cache, landed, fresh)


def shards(
    prefill_x,
    norm_gain,
    w_q,
    q_scale,
    key_value_weight,
    key_value_scale,
    w_o,
    o_scale,
    prefix_cache,
    prefix_len,
    dec_x,
    dec_cache,
    dec_len,
    place,
):
    prompts_total = prefix_cache.shape[1]
    row_count = dec_cache.shape[1]
    page_width = prefix_cache.shape[3]
    kv_heads = page_width // (2 * HEAD_SIZE)
    query_heads = w_q.shape[1] // HEAD_SIZE
    group_size = query_heads // kv_heads
    steps = dec_x.shape[0]
    section_count = lax.axis_size("section")
    section_index = lax.axis_index("section")
    tensor_count = lax.axis_size("tensor")
    tensor_index = lax.axis_index("tensor")
    head_span = max(1, 8 // query_heads)
    span_bits = head_span.bit_length() - 1
    block_width = w_o.shape[1] // tensor_count
    scales = (q_scale * EXP2_FACTOR, key_value_scale)

    weights = (norm_gain, w_q, key_value_weight)

    def kv_of_head(new_kv):
        for bit_number in range(span_bits):
            partner = partner_2(new_kv, "tensor", bit_number)
            new_kv = joined(new_kv, partner, bit_number, 1, tensor_index)
        return new_kv

    def finished(x, terms):
        total = sum(term.astype(jnp.float32) for term in terms)
        return (x.astype(jnp.float32) + total * o_scale).astype(jnp.bfloat16)

    dec_rows = dec_x.reshape(steps * row_count, -1)
    bounds = sorted({0, max(0, prompts_total - 2), prompts_total - 1, prompts_total})
    spans = list(zip(bounds[:-1], bounds[1:]))
    on_line = tensor_count == 4 and len(spans) == 3
    order = jnp.stack(
        line_order(tensor_index) if on_line else list(range(tensor_count))
    ).astype(jnp.int32)
    chunks = [prefill_x[first * PROMPT_TOKENS : last * PROMPT_TOKENS] for first, last in spans]
    blocks = chunks[:-1] + [jnp.concatenate([chunks[-1], dec_rows], axis=0)]
    pages = []

    def attention(k, queries):
        first, last = spans[k]
        return prefill_attention(queries, prefix_cache, first, last - first, pages[k], prefix_len)

    def keep(new_kv):
        new_kv = kv_of_head(new_kv)
        pages.append(new_kv[: chunks[len(pages)].shape[0]])
        return new_kv

    def back(attended):
        far, near, partner, own = project_out(attended, w_o, order[::-1], block_width)
        return LineScatter(own, partner, near, far, "tensor")

    if on_line:
        first = LineGather(blocks[0], "tensor")
        first.second()
        slots = [[after(first.block, first.middle)], [first.partner]]
        begun = project_part(slots, order[:2], *weights, None, None)
        first.third(begun[2])
        second = LineGather(
            blocks[1], "tensor", (first.outer_far,), (first.outer, first.middle_far, begun[2])
        )
        queries, new_kv = project_part(first.slots()[2:], order[2:], *weights, begun, scales)
        keep(new_kv)
        second.second(queries)
        attended = attention(0, after(queries, second.partner, second.middle))
        second.third(attended)
        sums = [back(after(attended, second.outer, second.middle_far))]
        third = LineGather(
            blocks[2], "tensor", (second.outer_far,), (second.outer, second.middle_far)
        )

        queries, new_kv = project_part(second.slots(), order, *weights, None, scales)
        keep(new_kv)
        sums[0].second(queries)
        third.second(queries)
        attended = attention(1, after(queries, *sums[0].first_hop, third.partner, third.middle))
        sums.append(back(attended))
        third.third(sums[1].own)

        slots = third.slots()
        slots[0][0] = after(slots[0][0], sums[1].own)
        begun = project_part(slots[:2], order[:2], *weights, None, None)
        sums[0].third(begun[2])
        slots[3][0] = after(slots[3][0], *sums[0].second_hop)
        queries, new_kv = project_part(slots[2:], order[2:], *weights, begun, scales)
        new_kv = keep(new_kv)
        sums[1].second(queries)
        attended = attention(2, after(queries, *sums[1].first_hop))
        sums[1].third(attended)
        sums.append(back(after(attended, *sums[1].second_hop)))
        dec_hold = (sums[2].own, *sums[0].terms)
    else:
        terms_of = []
        for k, block in enumerate(blocks):
            whole = lax.all_gather(block, "tensor", axis=1, tiled=True)
            queries, new_kv = project_part([[whole]], order[:1], *weights, None, scales)
            new_kv = keep(new_kv)
            partial = project_out(attention(k, queries), w_o, order[:1], w_o.shape[1])[0]
            terms_of.append(
                [lax.psum_scatter(partial, "tensor", scatter_dimension=1, tiled=True)]
            )
        dec_hold = ()
    tokens = chunks[-1].shape[0]
    dec_queries, fresh_kv = queries[tokens:], new_kv[tokens:]

    own_block = jnp.concatenate(pages, axis=0).reshape(prompts_total, PROMPT_TOKENS, page_width)
    owners = (place // row_count).reshape(section_count, prompts_total)
    targets = (place % row_count).reshape(section_count, prompts_total)
    owner_hits = (owners[:, :, None] == jnp.arange(section_count)[None, None, :]).astype(jnp.int32)
    slot_ranks = jnp.sum((jnp.cumsum(owner_hits, axis=1) - owner_hits) * owner_hits, axis=2)
    capacity = prompts_total // 2
    slot_ids = jnp.arange(capacity)
    sending = lax.dynamic_index_in_dim(owner_hits, section_index, 0, keepdims=False)
    my_ranks = lax.dynamic_index_in_dim(slot_ranks, section_index, 0, keepdims=False)
    selector = (
        jnp.transpose(sending)[:, None, :] * (my_ranks[None, None, :] == slot_ids[None, :, None])
    ).astype(jnp.bfloat16)
    here = (owners == section_index)[:, None, :] & (
        slot_ranks[:, None, :] == slot_ids[None, :, None]
    )
    slot_rows = jnp.sum(jnp.where(here, targets[:, None, :] + 1, 0), axis=2) - 1
    outgoing = jnp.einsum(
        "skp,pcw->skcw", selector, own_block, preferred_element_type=jnp.float32
    ).astype(jnp.bfloat16)
    received = lax.all_to_all(outgoing, "section", split_axis=0, concat_axis=0, tiled=True)
    landed = received.reshape(section_count * capacity, PROMPT_TOKENS, page_width)

    dec_queries = jnp.transpose(
        dec_queries.reshape(steps, row_count, kv_heads, group_size, HEAD_SIZE), (1, 2, 0, 3, 4)
    ).reshape(row_count, kv_heads, steps * group_size, HEAD_SIZE)
    fresh = jnp.transpose(fresh_kv.reshape(steps, row_count, page_width), (1, 0, 2))
    dec_attended = decode_attention(
        after(dec_queries.astype(jnp.float32), *dec_hold),
        dec_cache,
        dec_len,
        landed,
        slot_rows.reshape(-1).astype(jnp.int32),
        fresh.astype(jnp.float32),
    )
    dec_attended = (
        jnp.transpose(
            dec_attended.reshape(row_count, kv_heads, steps, group_size, HEAD_SIZE), (2, 0, 1, 3, 4)
        )
        .reshape(steps * row_count, -1)
        .astype(jnp.bfloat16)
    )
    if on_line:
        sums[2].second(dec_attended)
        dec_sum = back(after(dec_attended, *sums[2].first_hop, *sums[1].terms))
        sums[2].third(dec_sum.own)
        dec_sum.second()
        dec_sum.third()
        terms_of = [each.terms for each in sums]
        dec_terms = dec_sum.terms
    else:
        partial = project_out(dec_attended, w_o, order[:1], w_o.shape[1])[0]
        dec_terms = [lax.psum_scatter(partial, "tensor", scatter_dimension=1, tiled=True)]
    prefill_out = jnp.concatenate(
        [finished(x, terms) for x, terms in zip(chunks, terms_of)], axis=0
    )
    decode_out = finished(dec_rows, dec_terms).reshape(dec_x.shape)
    return (prefill_out, decode_out)


def solution(mesh):
    in_specs = (
        P(("groups", "section"), "tensor"),
        P(),
        P(None, "tensor"),
        P("tensor"),
        P(None, "tensor"),
        P("tensor"),
        P("tensor", None),
        P("tensor"),
        P("tensor", ("groups", "section"), None, None),
        P(("groups", "section")),
        P(None, ("groups", "section"), "tensor"),
        P("tensor", ("groups", "section"), None, None),
        P(("groups", "section")),
        P("groups"),
    )
    out_specs = (P(("groups", "section"), "tensor"), P(None, ("groups", "section"), "tensor"))
    return jax.shard_map(shards, mesh=mesh, in_specs=in_specs, out_specs=out_specs, check_vma=False)
```

```python
import functools
import math

import jax
import jax.numpy as jnp
from jax import lax
from jax.experimental import pallas as pl
from jax.experimental.pallas import tpu as pltpu
from jax.sharding import PartitionSpec as P

HEAD_SIZE = 128
PROMPT_TOKENS = 128
KERNEL_VMEM = 46 << 20
WEIGHT_BUFFERS = 8
EXP2_FACTOR = math.log2(math.e) / math.sqrt(HEAD_SIZE)
MASKED = -1e30


def partner_2(block, axis, distance):
    count = lax.axis_size(axis)
    route = []
    for low in range(count):
        high = low | 1 << distance
        if high != low and high < count:
            route += [(low, high), (high, low)]
    return lax.ppermute(block, axis, route)


def joined(portion, partner, bit_number, concat_dim, tensor_index):
    upper_half = tensor_index // 2**bit_number % 2 == 1
    lower_first = jnp.concatenate([portion, partner], axis=concat_dim)
    upper_first = jnp.concatenate([partner, portion], axis=concat_dim)
    return jnp.where(upper_half, upper_first, lower_first)


def tile_of(extent, most):
    tile = extent
    while tile > most and tile % 2 == 0:
        tile //= 2
    return tile


def after(value, *others):
    return lax.optimization_barrier((value,) + others)[0]


def after_all(values, *others):
    return lax.optimization_barrier(tuple(values) + others)[: len(values)]


def line_order(index):
    low = index < 2
    return [index, index ^ 1, jnp.where(low, 2, 1), jnp.where(low, 3, 0)]


OUTER = [(0, 1), (1, 0), (2, 3), (3, 2)]
MIDDLE = [(1, 2), (2, 1)]
INWARD = [(0, 1), (3, 2)]


def added(*terms):
    total = sum(term.astype(jnp.float32) for term in terms)
    return total.astype(terms[0].dtype)


class LineScatter:
    def __init__(self, own, partner, near, far, axis):
        self.own, self.partner, self.near, self.far = own, partner, near, far
        self.axis = axis
        self.far_in = lax.ppermute(far, axis, INWARD)

    def second(self, *held):
        far, near = after_all((added(self.far, self.far_in), self.near), *held)
        self.first_hop = (far,)
        self.near_in = lax.ppermute(near, self.axis, INWARD)
        self.far_out = lax.ppermute(far, self.axis, MIDDLE)

    def third(self, *held):
        near, partner = after_all(
            (added(self.near, self.near_in), added(self.partner, self.far_out)), *held
        )
        self.second_hop = (near, partner)
        near = lax.ppermute(near, self.axis, MIDDLE)
        partner = lax.ppermute(partner, self.axis, OUTER)
        self.terms = [self.own, near, partner]


def qkv_kernel(
    tile,
    x_ref,
    gain_ref,
    wq_ref,
    wkv_ref,
    qs_ref,
    kvs_ref,
    q_ref,
    kv_ref,
    accq,
    acckv,
    squares,
    x_buf,
    wq_buf,
    wkv_buf,
    x_sem,
    w_sem,
):
    count, rows, depth = x_buf.shape
    per = depth // tile
    steps = count * per
    ahead = min(steps, wq_buf.shape[0])

    def weight_copies(step):
        buffer = lax.rem(step, ahead)
        at = pl.multiple_of(step * tile, tile)
        return [
            pltpu.make_async_copy(ref.at[pl.ds(at, tile)], buf.at[buffer], w_sem.at[w, buffer])
            for w, (ref, buf) in enumerate([(wq_ref, wq_buf), (wkv_ref, wkv_buf)])
        ]

    x_copies = [
        pltpu.make_async_copy(x_ref.at[s], x_buf.at[s], x_sem.at[s]) for s in range(count)
    ]
    x_copies[0].start()
    for step in range(ahead):
        for copy in weight_copies(step):
            copy.start()
    for copy in x_copies[1:]:
        copy.start()
    accq[...] = jnp.zeros_like(accq)
    acckv[...] = jnp.zeros_like(acckv)
    squares[...] = jnp.zeros_like(squares)
    for s in range(count):
        x_copies[s].wait()

        def body(j, carry, s=s):
            step = s * per + j
            for copy in weight_copies(step):
                copy.wait()
            values = x_buf[s, :, pl.ds(pl.multiple_of(j * tile, tile), tile)].astype(jnp.float32)
            gain = gain_ref[:, pl.ds(pl.multiple_of(step * tile, tile), tile)]
            squares[...] += jnp.broadcast_to(
                jnp.sum(values * values, axis=-1, keepdims=True), squares.shape
            )
            scaled = (values * gain).astype(jnp.bfloat16)
            buffer = lax.rem(step, ahead)
            accq[...] += jnp.dot(scaled, wq_buf[buffer], preferred_element_type=jnp.float32)
            acckv[...] += jnp.dot(scaled, wkv_buf[buffer], preferred_element_type=jnp.float32)

            @pl.when(step + ahead < steps)
            def _():
                for copy in weight_copies(step + ahead):
                    copy.start()

            return carry

        lax.fori_loop(0, per, body, 0)
    root = lax.rsqrt(squares[:, :1] / (count * depth) + 1e-05)
    q_ref[...] = (accq[...] * root * qs_ref[...]).astype(q_ref.dtype)
    kv_ref[...] = (acckv[...] * root * kvs_ref[...]).astype(kv_ref.dtype)


def project_qkv(pieces, norm_gain, w_q, kv_weight, q_scale, kv_scale):
    count, rows, depth = pieces.shape
    tile = tile_of(depth, 512)
    width = count * depth
    q_cols, kv_cols = w_q.shape[1], kv_weight.shape[1]
    anywhere = pl.BlockSpec(memory_space=pl.ANY)
    whole = lambda shape: pl.BlockSpec(shape, lambda g: (0,) * len(shape))
    return pl.pallas_call(
        functools.partial(qkv_kernel, tile),
        grid=(1,),
        in_specs=[
            anywhere,
            whole((1, width)),
            anywhere,
            anywhere,
            whole((1, q_cols)),
            whole((1, kv_cols)),
        ],
        out_specs=[whole((rows, q_cols)), whole((rows, kv_cols))],
        scratch_shapes=[
            pltpu.VMEM((rows, q_cols), jnp.float32),
            pltpu.VMEM((rows, kv_cols), jnp.float32),
            pltpu.VMEM((rows, HEAD_SIZE), jnp.float32),
            pltpu.VMEM((count, rows, depth), jnp.bfloat16),
            pltpu.VMEM((WEIGHT_BUFFERS, tile, q_cols), jnp.bfloat16),
            pltpu.VMEM((WEIGHT_BUFFERS, tile, kv_cols), jnp.bfloat16),
            pltpu.SemaphoreType.DMA((count,)),
            pltpu.SemaphoreType.DMA((2, WEIGHT_BUFFERS)),
        ],
        out_shape=[
            jax.ShapeDtypeStruct((rows, q_cols), jnp.bfloat16),
            jax.ShapeDtypeStruct((rows, kv_cols), jnp.bfloat16),
        ],
        compiler_params=pltpu.CompilerParams(vmem_limit_bytes=KERNEL_VMEM),
        cost_estimate=pl.CostEstimate(
            flops=2 * rows * width * (q_cols + kv_cols),
            bytes_accessed=2 * width * (q_cols + kv_cols),
            transcendentals=0,
        ),
        name="norm_qkv",
    )(
        pieces,
        norm_gain.reshape(1, -1),
        w_q,
        kv_weight,
        q_scale.reshape(1, -1),
        kv_scale.reshape(1, -1),
    )


def out_kernel(count, tile, order, x_ref, w_ref, *refs):
    outs = refs[:count]
    x_buf, w_buf, x_sem, w_sem, o_sem = refs[count : count + 5]
    o_bufs = refs[count + 5 :]
    per = outs[0].shape[1] // tile
    steps = count * per
    ahead = min(steps, w_buf.shape[0])

    def weight_copy(step):
        at = pl.multiple_of((order[step // per] * per + lax.rem(step, per)) * tile, tile)
        buffer = lax.rem(step, ahead)
        return pltpu.make_async_copy(
            w_ref.at[:, pl.ds(at, tile)], w_buf.at[buffer], w_sem.at[buffer]
        )

    x_copy = pltpu.make_async_copy(x_ref, x_buf, x_sem)
    x_copy.start()
    for step in range(ahead):
        weight_copy(step).start()
    x_copy.wait()
    o_copies = []
    for s, (out, o_buf) in enumerate(zip(outs, o_bufs)):

        def body(j, carry, s=s, o_buf=o_buf):
            step = s * per + j
            weight_copy(step).wait()
            o_buf[:, pl.ds(pl.multiple_of(j * tile, tile), tile)] = jnp.dot(
                x_buf[...], w_buf[lax.rem(step, ahead)], preferred_element_type=jnp.float32
            ).astype(o_buf.dtype)

            @pl.when(step + ahead < steps)
            def _():
                weight_copy(step + ahead).start()

            return carry

        lax.fori_loop(0, per, body, 0)
        o_copies.append(pltpu.make_async_copy(o_buf, out, o_sem.at[s]))
        o_copies[-1].start()
    for copy in o_copies:
        copy.wait()


def project_out(attended, w_o, order, block):
    rows, depth = attended.shape
    tile = tile_of(block, 512)
    count = order.shape[0]
    anywhere = pl.BlockSpec(memory_space=pl.ANY)
    return pl.pallas_call(
        functools.partial(out_kernel, count, tile),
        grid_spec=pltpu.PrefetchScalarGridSpec(
            num_scalar_prefetch=1,
            grid=(1,),
            in_specs=[anywhere, anywhere],
            out_specs=[anywhere] * count,
            scratch_shapes=[
                pltpu.VMEM((rows, depth), jnp.bfloat16),
                pltpu.VMEM((WEIGHT_BUFFERS, depth, tile), jnp.bfloat16),
                pltpu.SemaphoreType.DMA,
                pltpu.SemaphoreType.DMA((WEIGHT_BUFFERS,)),
                pltpu.SemaphoreType.DMA((count,)),
            ]
            + [pltpu.VMEM((rows, block), jnp.bfloat16)] * count,
        ),
        out_shape=[jax.ShapeDtypeStruct((rows, block), jnp.bfloat16)] * count,
        compiler_params=pltpu.CompilerParams(vmem_limit_bytes=KERNEL_VMEM),
        cost_estimate=pl.CostEstimate(
            flops=2 * rows * depth * count * block,
            bytes_accessed=2 * depth * count * block,
            transcendentals=0,
        ),
        name="project_out",
    )(order, attended, w_o)


def with_ones(values):
    return jnp.concatenate([values, jnp.ones_like(values)], axis=1)


def scores_of(queries, keys):
    return lax.dot_general(
        queries, keys, (((1,), (1,)), ((), ())), preferred_element_type=jnp.float32
    )


def prefill_kernel(kv_heads, group, span, first, len_ref, q_ref, cache_ref, new_ref, o_ref, *scratch):
    accs, peaks = scratch[:kv_heads], scratch[kv_heads:]
    tokens = q_ref.shape[0]
    rows = group * tokens
    live = len_ref[first + pl.program_id(0)]
    full = live // span
    query_token = lax.rem(lax.broadcasted_iota(jnp.int32, (rows, tokens), 0), tokens)
    key_token = lax.broadcasted_iota(jnp.int32, (rows, tokens), 1)
    causal = key_token <= query_token
    lane = lax.broadcasted_iota(jnp.int32, (1, span), 1)

    def queries_of(a):
        return jnp.concatenate(
            [
                q_ref[:, (a * group + h) * HEAD_SIZE : (a * group + h + 1) * HEAD_SIZE]
                for h in range(group)
            ],
            axis=0,
        )

    def columns(a, part):
        return pl.ds((2 * a + part) * HEAD_SIZE, HEAD_SIZE)

    for a in range(kv_heads):
        scores = jnp.where(causal, scores_of(queries_of(a), new_ref[:, columns(a, 0)]), MASKED)
        top = jnp.broadcast_to(jnp.max(scores, axis=-1, keepdims=True), (rows, HEAD_SIZE))
        weights = jnp.exp2(scores - top[:, :tokens]).astype(jnp.bfloat16)
        accs[a][...] = jnp.dot(
            weights, with_ones(new_ref[:, columns(a, 1)]), preferred_element_type=jnp.float32
        )
        peaks[a][...] = top

    def block(s, bias):
        at = pl.multiple_of(s * span, span)
        scores = [
            scores_of(queries_of(a), cache_ref[0, 0, pl.ds(at, span), columns(a, 0)])
            for a in range(kv_heads)
        ]
        for a in range(kv_heads):
            here = scores[a] if bias is None else scores[a] + bias
            before = peaks[a][...]
            top = jnp.maximum(before, jnp.max(here, axis=-1, keepdims=True))
            weights = jnp.exp2(
                here - jnp.concatenate([top] * (span // HEAD_SIZE), axis=1)
            ).astype(jnp.bfloat16)
            fade = jnp.exp2(before - top)
            values = cache_ref[0, 0, pl.ds(at, span), columns(a, 1)]
            accs[a][...] = accs[a][...] * jnp.concatenate([fade, fade], axis=1) + jnp.dot(
                weights, with_ones(values), preferred_element_type=jnp.float32
            )
            peaks[a][...] = top

    def step(s, carry):
        block(s, None)
        return carry

    lax.fori_loop(0, full, step, 0)

    @pl.when(full * span < live)
    def _():
        block(full, jnp.where(lane + full * span < live, 0.0, MASKED))

    for a in range(kv_heads):
        result = accs[a][:, :HEAD_SIZE] / accs[a][:, HEAD_SIZE:]
        for h in range(group):
            o_ref[:, (a * group + h) * HEAD_SIZE : (a * group + h + 1) * HEAD_SIZE] = result[
                h * tokens : (h + 1) * tokens
            ].astype(o_ref.dtype)


def prefill_attention(queries, prefix_cache, first, count, new_kv, prefix_len):
    width = queries.shape[1]
    positions, page = prefix_cache.shape[2:]
    kv_heads = page // (2 * HEAD_SIZE)
    group = width // HEAD_SIZE // kv_heads
    span = tile_of(positions, 512)
    rows = group * PROMPT_TOKENS
    return pl.pallas_call(
        functools.partial(prefill_kernel, kv_heads, group, span, first),
        grid_spec=pltpu.PrefetchScalarGridSpec(
            num_scalar_prefetch=1,
            grid=(count,),
            in_specs=[
                pl.BlockSpec((PROMPT_TOKENS, width), lambda g, n: (g, 0)),
                pl.BlockSpec((1, 1, positions, page), lambda g, n: (0, first + g, 0, 0)),
                pl.BlockSpec((PROMPT_TOKENS, page), lambda g, n: (g, 0)),
            ],
            out_specs=pl.BlockSpec((PROMPT_TOKENS, width), lambda g, n: (g, 0)),
            scratch_shapes=[pltpu.VMEM((rows, 2 * HEAD_SIZE), jnp.float32)] * kv_heads
            + [pltpu.VMEM((rows, HEAD_SIZE), jnp.float32)] * kv_heads,
        ),
        out_shape=jax.ShapeDtypeStruct((count * PROMPT_TOKENS, width), jnp.bfloat16),
        compiler_params=pltpu.CompilerParams(vmem_limit_bytes=KERNEL_VMEM),
        cost_estimate=pl.CostEstimate(
            flops=8 * count * rows * kv_heads * (positions + PROMPT_TOKENS) * HEAD_SIZE,
            bytes_accessed=2 * count * positions * page,
            transcendentals=count * rows * kv_heads * (positions + PROMPT_TOKENS),
        ),
        name="prefill_attention",
    )(prefix_len, queries, prefix_cache, new_kv)


def decode_kernel(
    kv_heads, batch, len_ref, row_ref, q_ref, cache_ref, landed_ref, fresh_ref, o_ref, acc, peak
):
    row_count, context = cache_ref.shape[1], cache_ref.shape[2]
    per_row = q_ref.shape[2]
    steps = fresh_ref.shape[1]
    rows = batch * per_row
    row_of = lax.broadcasted_iota(jnp.int32, (rows, batch * context), 0) // per_row
    key_row = lax.broadcasted_iota(jnp.int32, (rows, batch * context), 1) // context
    key_at = lax.rem(lax.broadcasted_iota(jnp.int32, (rows, batch * context), 1), context)
    fresh_query = lax.broadcasted_iota(jnp.int32, (rows, batch * steps), 0)
    fresh_key = lax.broadcasted_iota(jnp.int32, (rows, batch * steps), 1)
    fresh_live = (fresh_key // steps == fresh_query // per_row) & (
        lax.rem(fresh_key, steps) <= lax.rem(fresh_query, per_row) // (per_row // steps)
    )

    def cached(b, carry):
        first = b * batch
        live = jnp.zeros_like(key_row)
        for r in range(batch):
            live = jnp.where(key_row == r, len_ref[first + r], live)
        cache_live = (row_of == key_row) & (key_at < live)
        pages = cache_ref[0, pl.ds(first, batch)].reshape(batch * context, cache_ref.shape[3])
        fresh = fresh_ref[pl.ds(first, batch)].reshape(batch * steps, fresh_ref.shape[2])
        for a in range(kv_heads):
            queries = q_ref[pl.ds(first, batch), a].reshape(rows, HEAD_SIZE).astype(jnp.bfloat16)
            k_at, v_at = 2 * a * HEAD_SIZE, (2 * a + 1) * HEAD_SIZE
            scores = scores_of(queries, pages[:, k_at : k_at + HEAD_SIZE])
            scores = jnp.where(cache_live, scores, MASKED)
            recent = scores_of(queries, fresh[:, k_at : k_at + HEAD_SIZE].astype(jnp.bfloat16))
            recent = jnp.where(fresh_live, recent, MASKED)
            top = jnp.maximum(
                jnp.max(scores, axis=-1, keepdims=True), jnp.max(recent, axis=-1, keepdims=True)
            )
            weights = jnp.exp2(scores - top).astype(jnp.bfloat16)
            recent = jnp.exp2(recent - top).astype(jnp.bfloat16)
            total = jnp.dot(
                weights,
                with_ones(pages[:, v_at : v_at + HEAD_SIZE]),
                preferred_element_type=jnp.float32,
            ) + jnp.dot(
                recent,
                with_ones(fresh[:, v_at : v_at + HEAD_SIZE].astype(jnp.bfloat16)),
                preferred_element_type=jnp.float32,
            )
            acc[pl.ds(first, batch), a] = total.reshape(batch, per_row, 2 * HEAD_SIZE)
            peak[pl.ds(first, batch), a] = jnp.broadcast_to(top, (rows, HEAD_SIZE)).reshape(
                batch, per_row, HEAD_SIZE
            )
        return carry

    lax.fori_loop(0, row_count // batch, cached, 0)

    def arrival(slot, carry):
        row = row_ref[slot]

        @pl.when(row >= 0)
        def _():
            for a in range(kv_heads):
                queries = q_ref[row, a].astype(jnp.bfloat16)
                k_at, v_at = 2 * a * HEAD_SIZE, (2 * a + 1) * HEAD_SIZE
                scores = scores_of(queries, landed_ref[slot, :, k_at : k_at + HEAD_SIZE])
                before = peak[row, a]
                top = jnp.maximum(before, jnp.max(scores, axis=-1, keepdims=True))
                weights = jnp.exp2(scores - top[:, :1]).astype(jnp.bfloat16)
                fade = jnp.exp2(before - top)
                acc[row, a] = acc[row, a] * jnp.concatenate([fade, fade], axis=1) + jnp.dot(
                    weights,
                    with_ones(landed_ref[slot, :, v_at : v_at + HEAD_SIZE]),
                    preferred_element_type=jnp.float32,
                )

        return carry

    lax.fori_loop(0, row_ref.shape[0], arrival, 0)
    o_ref[...] = (acc[:, :, :, :HEAD_SIZE] / acc[:, :, :, HEAD_SIZE:]).astype(o_ref.dtype)


def decode_attention(queries, dec_cache, dec_len, landed, slot_rows, fresh):
    row_count, kv_heads, per_row = queries.shape[:3]
    context = dec_cache.shape[2]
    batch = max(1, min(row_count, 2 * HEAD_SIZE // context))
    whole = lambda array: pl.BlockSpec(array.shape, lambda g, *_: (0,) * array.ndim)
    return pl.pallas_call(
        functools.partial(decode_kernel, kv_heads, batch),
        grid_spec=pltpu.PrefetchScalarGridSpec(
            num_scalar_prefetch=2,
            grid=(1,),
            in_specs=[whole(queries), whole(dec_cache), whole(landed), whole(fresh)],
            out_specs=whole(queries),
            scratch_shapes=[
                pltpu.VMEM((row_count, kv_heads, per_row, 2 * HEAD_SIZE), jnp.float32),
                pltpu.VMEM((row_count, kv_heads, per_row, HEAD_SIZE), jnp.float32),
            ],
        ),
        out_shape=jax.ShapeDtypeStruct(queries.shape, jnp.float32),
        compiler_params=pltpu.CompilerParams(vmem_limit_bytes=KERNEL_VMEM),
        cost_estimate=pl.CostEstimate(
            flops=8 * queries.size * batch * context,
            bytes_accessed=2 * dec_cache.size + 2 * landed.size,
            transcendentals=queries.size * batch * context // HEAD_SIZE,
        ),
        name="decode_attention",
    )(dec_len, slot_rows, queries, dec_cache, landed, fresh)


def shards(
    prefill_x,
    norm_gain,
    w_q,
    q_scale,
    key_value_weight,
    key_value_scale,
    w_o,
    o_scale,
    prefix_cache,
    prefix_len,
    dec_x,
    dec_cache,
    dec_len,
    place,
):
    prompts_total = prefix_cache.shape[1]
    row_count = dec_cache.shape[1]
    page_width = prefix_cache.shape[3]
    kv_heads = page_width // (2 * HEAD_SIZE)
    query_heads = w_q.shape[1] // HEAD_SIZE
    group_size = query_heads // kv_heads
    steps = dec_x.shape[0]
    section_count = lax.axis_size("section")
    section_index = lax.axis_index("section")
    tensor_count = lax.axis_size("tensor")
    tensor_index = lax.axis_index("tensor")
    head_span = max(1, 8 // query_heads)
    span_bits = head_span.bit_length() - 1
    block_width = w_o.shape[1] // tensor_count

    scores_scale = q_scale * EXP2_FACTOR

    def kv_of_head(new_kv):
        for bit_number in range(span_bits):
            partner = partner_2(new_kv, "tensor", bit_number)
            new_kv = joined(new_kv, partner, bit_number, 1, tensor_index)
        return new_kv

    def finished(x, terms):
        total = sum(term.astype(jnp.float32) for term in terms)
        return (x.astype(jnp.float32) + total * o_scale).astype(jnp.bfloat16)

    dec_rows = dec_x.reshape(steps * row_count, -1)
    bounds = sorted({0, min(1, prompts_total - 1), prompts_total - 1, prompts_total})
    spans = list(zip(bounds[:-1], bounds[1:]))
    on_line = tensor_count == 4 and len(spans) == 3
    order = jnp.stack(
        line_order(tensor_index) if on_line else list(range(tensor_count))
    ).astype(jnp.int32)
    chunks = [prefill_x[first * PROMPT_TOKENS : last * PROMPT_TOKENS] for first, last in spans]
    blocks = chunks[:-1] + [jnp.concatenate([chunks[-1], dec_rows], axis=0)]
    pages = []

    def attention(k, queries):
        first, last = spans[k]
        return prefill_attention(queries, prefix_cache, first, last - first, pages[k], prefix_len)

    def keep(new_kv):
        new_kv = kv_of_head(new_kv)
        pages.append(new_kv[: chunks[len(pages)].shape[0]])
        return new_kv

    def back(attended):
        far, near, partner, own = project_out(attended, w_o, order[::-1], block_width)
        return LineScatter(own, partner, near, far, "tensor")

    def project(pieces):
        queries, new_kv = project_qkv(
            pieces, norm_gain, w_q, key_value_weight, scores_scale, key_value_scale
        )
        return queries, keep(new_kv)

    if on_line:
        pieces = lax.all_gather(blocks[0], "tensor")
        later = lax.all_gather(after(blocks[1], pieces), "tensor")
        queries, new_kv = project(pieces)
        last = lax.all_gather(after(blocks[2], queries), "tensor")
        sums = [back(attention(0, queries))]
        sums[0].second()
        sums[0].third()

        queries, new_kv = project(after(later, *sums[0].second_hop))
        sums.append(back(after(attention(1, queries), *sums[0].terms)))

        queries, new_kv = project(after(last, sums[1].own))
        sums[1].second(queries)
        attended = attention(2, after(queries, *sums[1].first_hop))
        sums.append(back(attended))
        sums[1].third(sums[2].own)
        a2a_hold = (sums[2].own,)
        dec_hold = sums[1].second_hop
    else:
        terms_of = []
        for k, block in enumerate(blocks):
            queries, new_kv = project(lax.all_gather(block, "tensor"))
            partial = project_out(attention(k, queries), w_o, order[:1], w_o.shape[1])[0]
            terms_of.append(
                [lax.psum_scatter(partial, "tensor", scatter_dimension=1, tiled=True)]
            )
        a2a_hold = dec_hold = ()
    tokens = chunks[-1].shape[0]
    dec_queries, fresh_kv = queries[tokens:], new_kv[tokens:]

    own_block = after(jnp.concatenate(pages, axis=0), *a2a_hold).reshape(
        prompts_total, PROMPT_TOKENS, page_width
    )
    owners = (place // row_count).reshape(section_count, prompts_total)
    targets = (place % row_count).reshape(section_count, prompts_total)
    owner_hits = (owners[:, :, None] == jnp.arange(section_count)[None, None, :]).astype(jnp.int32)
    slot_ranks = jnp.sum((jnp.cumsum(owner_hits, axis=1) - owner_hits) * owner_hits, axis=2)
    capacity = prompts_total // 2
    slot_ids = jnp.arange(capacity)
    sending = lax.dynamic_index_in_dim(owner_hits, section_index, 0, keepdims=False)
    my_ranks = lax.dynamic_index_in_dim(slot_ranks, section_index, 0, keepdims=False)
    selector = (
        jnp.transpose(sending)[:, None, :] * (my_ranks[None, None, :] == slot_ids[None, :, None])
    ).astype(jnp.bfloat16)
    here = (owners == section_index)[:, None, :] & (
        slot_ranks[:, None, :] == slot_ids[None, :, None]
    )
    slot_rows = jnp.sum(jnp.where(here, targets[:, None, :] + 1, 0), axis=2) - 1
    outgoing = jnp.einsum(
        "skp,pcw->skcw", selector, own_block, preferred_element_type=jnp.float32
    ).astype(jnp.bfloat16)
    received = lax.all_to_all(outgoing, "section", split_axis=0, concat_axis=0, tiled=True)
    landed = received.reshape(section_count * capacity, PROMPT_TOKENS, page_width)

    dec_queries = jnp.transpose(
        dec_queries.reshape(steps, row_count, kv_heads, group_size, HEAD_SIZE), (1, 2, 0, 3, 4)
    ).reshape(row_count, kv_heads, steps * group_size, HEAD_SIZE)
    fresh = jnp.transpose(fresh_kv.reshape(steps, row_count, page_width), (1, 0, 2))
    dec_attended = decode_attention(
        after(dec_queries.astype(jnp.float32), *dec_hold),
        dec_cache,
        dec_len,
        landed,
        slot_rows.reshape(-1).astype(jnp.int32),
        fresh.astype(jnp.float32),
    )
    dec_attended = (
        jnp.transpose(
            dec_attended.reshape(row_count, kv_heads, steps, group_size, HEAD_SIZE), (2, 0, 1, 3, 4)
        )
        .reshape(steps * row_count, -1)
        .astype(jnp.bfloat16)
    )
    if on_line:
        sums[2].second(dec_attended)
        dec_sum = back(after(dec_attended, *sums[2].first_hop))
        sums[2].third(dec_sum.own, *sums[1].terms)
        dec_sum.second()
        dec_sum.third()
        terms_of = [each.terms for each in sums]
        dec_terms = dec_sum.terms
    else:
        partial = project_out(dec_attended, w_o, order[:1], w_o.shape[1])[0]
        dec_terms = [lax.psum_scatter(partial, "tensor", scatter_dimension=1, tiled=True)]
    prefill_out = jnp.concatenate(
        [finished(x, terms) for x, terms in zip(chunks, terms_of)], axis=0
    )
    decode_out = finished(dec_rows, dec_terms).reshape(dec_x.shape)
    return (prefill_out, decode_out)


def solution(mesh):
    in_specs = (
        P(("groups", "section"), "tensor"),
        P(),
        P(None, "tensor"),
        P("tensor"),
        P(None, "tensor"),
        P("tensor"),
        P("tensor", None),
        P("tensor"),
        P("tensor", ("groups", "section"), None, None),
        P(("groups", "section")),
        P(None, ("groups", "section"), "tensor"),
        P("tensor", ("groups", "section"), None, None),
        P(("groups", "section")),
        P("groups"),
    )
    out_specs = (P(("groups", "section"), "tensor"), P(None, ("groups", "section"), "tensor"))
    return jax.shard_map(shards, mesh=mesh, in_specs=in_specs, out_specs=out_specs, check_vma=False)
```

```python
import functools
import math

import jax
import jax.numpy as jnp
from jax import lax
from jax.experimental import pallas as pl
from jax.experimental.pallas import tpu as pltpu
from jax.sharding import PartitionSpec as P

HEAD_SIZE = 128
PROMPT_TOKENS = 128
KERNEL_VMEM = 46 << 20
WEIGHT_BUFFERS = 8
EXP2_FACTOR = math.log2(math.e) / math.sqrt(HEAD_SIZE)
MASKED = -1e30


def partner_2(block, axis, distance):
    count = lax.axis_size(axis)
    route = []
    for low in range(count):
        high = low | 1 << distance
        if high != low and high < count:
            route += [(low, high), (high, low)]
    return lax.ppermute(block, axis, route)


def joined(portion, partner, bit_number, concat_dim, tensor_index):
    upper_half = tensor_index // 2**bit_number % 2 == 1
    lower_first = jnp.concatenate([portion, partner], axis=concat_dim)
    upper_first = jnp.concatenate([partner, portion], axis=concat_dim)
    return jnp.where(upper_half, upper_first, lower_first)


def tile_of(extent, most):
    tile = extent
    while tile > most and tile % 2 == 0:
        tile //= 2
    return tile


def after(value, *others):
    return lax.optimization_barrier((value,) + others)[0]


def after_all(values, *others):
    return lax.optimization_barrier(tuple(values) + others)[: len(values)]


def line_order(index):
    low = index < 2
    return [index, index ^ 1, jnp.where(low, 2, 1), jnp.where(low, 3, 0)]


OUTER = [(0, 1), (1, 0), (2, 3), (3, 2)]
MIDDLE = [(1, 2), (2, 1)]
INWARD = [(0, 1), (3, 2)]
OUTWARD = [(1, 0), (2, 3)]


class LineGather:
    def __init__(self, block, axis, outer_held=(), middle_held=()):
        self.block, self.axis = block, axis
        self.partner = lax.ppermute(after(block, *outer_held), axis, OUTER)
        self.middle = lax.ppermute(after(block, *middle_held), axis, MIDDLE)

    def second(self, *held):
        partner, middle = after_all((self.partner, self.middle), *held)
        self.outer = lax.ppermute(middle, self.axis, OUTWARD)
        self.middle_far = lax.ppermute(partner, self.axis, MIDDLE)

    def third(self, *held):
        self.outer_far = lax.ppermute(after(self.middle_far, *held), self.axis, OUTWARD)

    def slots(self):
        return [
            [self.block],
            [self.partner],
            [self.middle, self.outer],
            [self.middle_far, self.outer_far],
        ]


def added(*terms):
    total = sum(term.astype(jnp.float32) for term in terms)
    return total.astype(terms[0].dtype)


class LineScatter:
    def __init__(self, own, partner, near, far, axis):
        self.own, self.partner, self.near, self.far = own, partner, near, far
        self.axis = axis
        self.far_in = lax.ppermute(far, axis, INWARD)

    def second(self, *held):
        far, near = after_all((added(self.far, self.far_in), self.near), *held)
        self.first_hop = (far,)
        self.near_in = lax.ppermute(near, self.axis, INWARD)
        self.far_out = lax.ppermute(far, self.axis, MIDDLE)

    def third(self, *held):
        near, partner = after_all(
            (added(self.near, self.near_in), added(self.partner, self.far_out)), *held
        )
        self.second_hop = (near, partner)
        near = lax.ppermute(near, self.axis, MIDDLE)
        partner = lax.ppermute(partner, self.axis, OUTER)
        self.terms = [self.own, near, partner]


def qkv_kernel(counts, begun, ended, tile, order, *refs):
    refs = list(refs)
    arrays = sum(counts)
    xs = [refs.pop(0) for _ in range(arrays)]
    gain_ref, wq_ref, wkv_ref = (refs.pop(0) for _ in range(3))
    sums_in = [refs.pop(0) for _ in range(3)] if begun else []
    if ended:
        qs_ref, kvs_ref, q_ref, kv_ref, accq, acckv, squares = (refs.pop(0) for _ in range(7))
    else:
        accq, acckv, squares = (refs.pop(0) for _ in range(3))
    x_bufs = [refs.pop(0) for _ in range(arrays)]
    wq_buf, wkv_buf, x_sem, w_sem, sum_sem = refs
    per = x_bufs[0].shape[1] // tile
    steps = len(counts) * per
    ahead = min(steps, wq_buf.shape[0])

    def weight_copies(step):
        buffer = lax.rem(step, ahead)
        at = pl.multiple_of((order[step // per] * per + lax.rem(step, per)) * tile, tile)
        return [
            pltpu.make_async_copy(ref.at[pl.ds(at, tile)], buf.at[buffer], w_sem.at[w, buffer])
            for w, (ref, buf) in enumerate([(wq_ref, wq_buf), (wkv_ref, wkv_buf)])
        ]

    x_copies = [
        pltpu.make_async_copy(ref, buf, x_sem.at[a]) for a, (ref, buf) in enumerate(zip(xs, x_bufs))
    ]
    sum_copies = [
        pltpu.make_async_copy(ref, acc, sum_sem.at[a])
        for a, (ref, acc) in enumerate(zip(sums_in, (accq, acckv, squares)))
    ]
    for copy in x_copies[: counts[0]] + sum_copies:
        copy.start()
    for step in range(ahead):
        for copy in weight_copies(step):
            copy.start()
    for copy in x_copies[counts[0] :]:
        copy.start()
    for copy in sum_copies:
        copy.wait()
    if not begun:
        accq[...] = jnp.zeros_like(accq)
        acckv[...] = jnp.zeros_like(acckv)
        squares[...] = jnp.zeros_like(squares)

    taken = 0
    for s, count in enumerate(counts):
        for copy in x_copies[taken : taken + count]:
            copy.wait()
        bufs = x_bufs[taken : taken + count]
        taken += count

        def body(j, carry, s=s, bufs=bufs):
            step = s * per + j
            for copy in weight_copies(step):
                copy.wait()
            at = pl.multiple_of(j * tile, tile)
            values = sum(buf[:, pl.ds(at, tile)].astype(jnp.float32) for buf in bufs)
            gain = gain_ref[:, pl.ds(pl.multiple_of((order[s] * per + j) * tile, tile), tile)]
            squares[...] += jnp.broadcast_to(
                jnp.sum(values * values, axis=-1, keepdims=True), squares.shape
            )
            scaled = (values * gain).astype(jnp.bfloat16)
            buffer = lax.rem(step, ahead)
            accq[...] += jnp.dot(scaled, wq_buf[buffer], preferred_element_type=jnp.float32)
            acckv[...] += jnp.dot(scaled, wkv_buf[buffer], preferred_element_type=jnp.float32)

            @pl.when(step + ahead < steps)
            def _():
                for copy in weight_copies(step + ahead):
                    copy.start()

            return carry

        lax.fori_loop(0, per, body, 0)
    if ended:
        root = lax.rsqrt(squares[:, :1] / ended + 1e-05)
        q_ref[...] = (accq[...] * root * qs_ref[...]).astype(q_ref.dtype)
        kv_ref[...] = (acckv[...] * root * kvs_ref[...]).astype(kv_ref.dtype)


def project_part(slots, order, norm_gain, w_q, kv_weight, begun, scales):
    rows, depth = slots[0][0].shape
    tile = tile_of(depth, 512)
    q_cols, kv_cols = w_q.shape[1], kv_weight.shape[1]
    arrays = [array for slot in slots for array in slot]

    def whole(shape):
        return pl.BlockSpec(shape, lambda g, order: (0,) * len(shape))

    anywhere = pl.BlockSpec(memory_space=pl.ANY)
    operands = arrays + [norm_gain.reshape(1, -1), w_q, kv_weight]
    in_specs = [anywhere] * len(arrays) + [whole((1, norm_gain.shape[0])), anywhere, anywhere]
    sums = [(rows, q_cols), (rows, kv_cols), (rows, HEAD_SIZE)]
    if begun is not None:
        operands += list(begun)
        in_specs += [anywhere] * 3
    if scales is not None:
        operands += [scale.reshape(1, -1) for scale in scales]
        in_specs += [whole((1, q_cols)), whole((1, kv_cols))]
        out_shapes = [jax.ShapeDtypeStruct(shape, jnp.bfloat16) for shape in sums[:2]]
        scratch = [pltpu.VMEM(shape, jnp.float32) for shape in sums]
    else:
        out_shapes = [jax.ShapeDtypeStruct(shape, jnp.float32) for shape in sums]
        scratch = []
    return pl.pallas_call(
        functools.partial(
            qkv_kernel,
            [len(slot) for slot in slots],
            begun is not None,
            0 if scales is None else w_q.shape[0],
            tile,
        ),
        grid_spec=pltpu.PrefetchScalarGridSpec(
            num_scalar_prefetch=1,
            grid=(1,),
            in_specs=in_specs,
            out_specs=[whole(out.shape) for out in out_shapes],
            scratch_shapes=scratch
            + [pltpu.VMEM((rows, depth), jnp.bfloat16) for _ in arrays]
            + [
                pltpu.VMEM((WEIGHT_BUFFERS, tile, q_cols), jnp.bfloat16),
                pltpu.VMEM((WEIGHT_BUFFERS, tile, kv_cols), jnp.bfloat16),
                pltpu.SemaphoreType.DMA((len(arrays),)),
                pltpu.SemaphoreType.DMA((2, WEIGHT_BUFFERS)),
                pltpu.SemaphoreType.DMA((3,)),
            ],
        ),
        out_shape=out_shapes,
        compiler_params=pltpu.CompilerParams(vmem_limit_bytes=KERNEL_VMEM),
        cost_estimate=pl.CostEstimate(
            flops=2 * rows * depth * len(slots) * (q_cols + kv_cols),
            bytes_accessed=2 * depth * len(slots) * (q_cols + kv_cols),
            transcendentals=0,
        ),
        name="norm_qkv",
    )(order, *operands)


def out_kernel(count, stacked, tile, order, x_ref, w_ref, *refs):
    if stacked:
        outs, refs = [refs[0].at[s] for s in range(count)], refs[1:]
    else:
        outs, refs = refs[:count], refs[count:]
    x_buf, w_buf, x_sem, w_sem, o_sem = refs[:5]
    o_bufs = refs[5:]
    per = o_bufs[0].shape[1] // tile
    steps = count * per
    ahead = min(steps, w_buf.shape[0])

    def weight_copy(step):
        at = pl.multiple_of((order[step // per] * per + lax.rem(step, per)) * tile, tile)
        buffer = lax.rem(step, ahead)
        return pltpu.make_async_copy(
            w_ref.at[:, pl.ds(at, tile)], w_buf.at[buffer], w_sem.at[buffer]
        )

    x_copy = pltpu.make_async_copy(x_ref, x_buf, x_sem)
    x_copy.start()
    for step in range(ahead):
        weight_copy(step).start()
    x_copy.wait()
    o_copies = []
    for s, (out, o_buf) in enumerate(zip(outs, o_bufs)):

        def body(j, carry, s=s, o_buf=o_buf):
            step = s * per + j
            weight_copy(step).wait()
            o_buf[:, pl.ds(pl.multiple_of(j * tile, tile), tile)] = jnp.dot(
                x_buf[...], w_buf[lax.rem(step, ahead)], preferred_element_type=jnp.float32
            ).astype(o_buf.dtype)

            @pl.when(step + ahead < steps)
            def _():
                weight_copy(step + ahead).start()

            return carry

        lax.fori_loop(0, per, body, 0)
        o_copies.append(pltpu.make_async_copy(o_buf, out, o_sem.at[s]))
        o_copies[-1].start()
    for copy in o_copies:
        copy.wait()


def without(kernel, first, count):
    return lambda *refs: kernel(*refs[:first], *refs[first + count :])


def project_out(attended, w_o, order, block, stacked=False, held=()):
    rows, depth = attended.shape
    tile = tile_of(block, 512)
    count = order.shape[0]
    anywhere = pl.BlockSpec(memory_space=pl.ANY)
    return pl.pallas_call(
        without(functools.partial(out_kernel, count, stacked, tile), 3, len(held)),
        grid_spec=pltpu.PrefetchScalarGridSpec(
            num_scalar_prefetch=1,
            grid=(1,),
            in_specs=[anywhere] * (2 + len(held)),
            out_specs=anywhere if stacked else [anywhere] * count,
            scratch_shapes=[
                pltpu.VMEM((rows, depth), jnp.bfloat16),
                pltpu.VMEM((WEIGHT_BUFFERS, depth, tile), jnp.bfloat16),
                pltpu.SemaphoreType.DMA,
                pltpu.SemaphoreType.DMA((WEIGHT_BUFFERS,)),
                pltpu.SemaphoreType.DMA((count,)),
            ]
            + [pltpu.VMEM((rows, block), jnp.bfloat16)] * count,
        ),
        out_shape=jax.ShapeDtypeStruct((count, rows, block), jnp.bfloat16)
        if stacked
        else [jax.ShapeDtypeStruct((rows, block), jnp.bfloat16)] * count,
        compiler_params=pltpu.CompilerParams(vmem_limit_bytes=KERNEL_VMEM),
        cost_estimate=pl.CostEstimate(
            flops=2 * rows * depth * count * block,
            bytes_accessed=2 * depth * count * block,
            transcendentals=0,
        ),
        name="project_out",
    )(order, attended, w_o, *held)


def with_ones(values):
    return jnp.concatenate([values, jnp.ones_like(values)], axis=1)


def scores_of(queries, keys):
    return lax.dot_general(
        queries, keys, (((1,), (1,)), ((), ())), preferred_element_type=jnp.float32
    )


def prefill_kernel(kv_heads, group, span, first, len_ref, q_ref, cache_ref, new_ref, o_ref, *scratch):
    accs, peaks = scratch[:kv_heads], scratch[kv_heads:]
    tokens = q_ref.shape[0]
    rows = group * tokens
    live = len_ref[first + pl.program_id(0)]
    full = live // span
    query_token = lax.rem(lax.broadcasted_iota(jnp.int32, (rows, tokens), 0), tokens)
    key_token = lax.broadcasted_iota(jnp.int32, (rows, tokens), 1)
    causal = key_token <= query_token
    lane = lax.broadcasted_iota(jnp.int32, (1, span), 1)

    def queries_of(a):
        return jnp.concatenate(
            [
                q_ref[:, (a * group + h) * HEAD_SIZE : (a * group + h + 1) * HEAD_SIZE]
                for h in range(group)
            ],
            axis=0,
        )

    def columns(a, part):
        return pl.ds((2 * a + part) * HEAD_SIZE, HEAD_SIZE)

    for a in range(kv_heads):
        scores = jnp.where(causal, scores_of(queries_of(a), new_ref[:, columns(a, 0)]), MASKED)
        top = jnp.broadcast_to(jnp.max(scores, axis=-1, keepdims=True), (rows, HEAD_SIZE))
        weights = jnp.exp2(scores - top[:, :tokens]).astype(jnp.bfloat16)
        accs[a][...] = jnp.dot(
            weights, with_ones(new_ref[:, columns(a, 1)]), preferred_element_type=jnp.float32
        )
        peaks[a][...] = top

    def block(s, bias):
        at = pl.multiple_of(s * span, span)
        scores = [
            scores_of(queries_of(a), cache_ref[0, 0, pl.ds(at, span), columns(a, 0)])
            for a in range(kv_heads)
        ]
        for a in range(kv_heads):
            here = scores[a] if bias is None else scores[a] + bias
            before = peaks[a][...]
            top = jnp.maximum(before, jnp.max(here, axis=-1, keepdims=True))
            weights = jnp.exp2(
                here - jnp.concatenate([top] * (span // HEAD_SIZE), axis=1)
            ).astype(jnp.bfloat16)
            fade = jnp.exp2(before - top)
            values = cache_ref[0, 0, pl.ds(at, span), columns(a, 1)]
            accs[a][...] = accs[a][...] * jnp.concatenate([fade, fade], axis=1) + jnp.dot(
                weights, with_ones(values), preferred_element_type=jnp.float32
            )
            peaks[a][...] = top

    def step(s, carry):
        block(s, None)
        return carry

    lax.fori_loop(0, full, step, 0)

    @pl.when(full * span < live)
    def _():
        block(full, jnp.where(lane + full * span < live, 0.0, MASKED))

    for a in range(kv_heads):
        result = accs[a][:, :HEAD_SIZE] / accs[a][:, HEAD_SIZE:]
        for h in range(group):
            o_ref[:, (a * group + h) * HEAD_SIZE : (a * group + h + 1) * HEAD_SIZE] = result[
                h * tokens : (h + 1) * tokens
            ].astype(o_ref.dtype)


def prefill_attention(queries, prefix_cache, first, count, new_kv, prefix_len):
    width = queries.shape[1]
    positions, page = prefix_cache.shape[2:]
    kv_heads = page // (2 * HEAD_SIZE)
    group = width // HEAD_SIZE // kv_heads
    span = tile_of(positions, 512)
    rows = group * PROMPT_TOKENS
    return pl.pallas_call(
        functools.partial(prefill_kernel, kv_heads, group, span, first),
        grid_spec=pltpu.PrefetchScalarGridSpec(
            num_scalar_prefetch=1,
            grid=(count,),
            in_specs=[
                pl.BlockSpec((PROMPT_TOKENS, width), lambda g, n: (g, 0)),
                pl.BlockSpec((1, 1, positions, page), lambda g, n: (0, first + g, 0, 0)),
                pl.BlockSpec((PROMPT_TOKENS, page), lambda g, n: (g, 0)),
            ],
            out_specs=pl.BlockSpec((PROMPT_TOKENS, width), lambda g, n: (g, 0)),
            scratch_shapes=[pltpu.VMEM((rows, 2 * HEAD_SIZE), jnp.float32)] * kv_heads
            + [pltpu.VMEM((rows, HEAD_SIZE), jnp.float32)] * kv_heads,
        ),
        out_shape=jax.ShapeDtypeStruct((count * PROMPT_TOKENS, width), jnp.bfloat16),
        compiler_params=pltpu.CompilerParams(vmem_limit_bytes=KERNEL_VMEM),
        cost_estimate=pl.CostEstimate(
            flops=8 * count * rows * kv_heads * (positions + PROMPT_TOKENS) * HEAD_SIZE,
            bytes_accessed=2 * count * positions * page,
            transcendentals=count * rows * kv_heads * (positions + PROMPT_TOKENS),
        ),
        name="prefill_attention",
    )(prefix_len, queries, prefix_cache, new_kv)


def decode_kernel(
    kv_heads, batch, len_ref, row_ref, q_ref, cache_ref, landed_ref, fresh_ref, o_ref, acc, peak
):
    row_count, context = cache_ref.shape[1], cache_ref.shape[2]
    per_row = q_ref.shape[2]
    steps = fresh_ref.shape[1]
    rows = batch * per_row
    row_of = lax.broadcasted_iota(jnp.int32, (rows, batch * context), 0) // per_row
    key_row = lax.broadcasted_iota(jnp.int32, (rows, batch * context), 1) // context
    key_at = lax.rem(lax.broadcasted_iota(jnp.int32, (rows, batch * context), 1), context)
    fresh_query = lax.broadcasted_iota(jnp.int32, (rows, batch * steps), 0)
    fresh_key = lax.broadcasted_iota(jnp.int32, (rows, batch * steps), 1)
    fresh_live = (fresh_key // steps == fresh_query // per_row) & (
        lax.rem(fresh_key, steps) <= lax.rem(fresh_query, per_row) // (per_row // steps)
    )

    def cached(b, carry):
        first = b * batch
        live = jnp.zeros_like(key_row)
        for r in range(batch):
            live = jnp.where(key_row == r, len_ref[first + r], live)
        cache_live = (row_of == key_row) & (key_at < live)
        pages = cache_ref[0, pl.ds(first, batch)].reshape(batch * context, cache_ref.shape[3])
        fresh = fresh_ref[pl.ds(first, batch)].reshape(batch * steps, fresh_ref.shape[2])
        for a in range(kv_heads):
            queries = q_ref[pl.ds(first, batch), a].reshape(rows, HEAD_SIZE).astype(jnp.bfloat16)
            k_at, v_at = 2 * a * HEAD_SIZE, (2 * a + 1) * HEAD_SIZE
            scores = scores_of(queries, pages[:, k_at : k_at + HEAD_SIZE])
            scores = jnp.where(cache_live, scores, MASKED)
            recent = scores_of(queries, fresh[:, k_at : k_at + HEAD_SIZE].astype(jnp.bfloat16))
            recent = jnp.where(fresh_live, recent, MASKED)
            top = jnp.maximum(
                jnp.max(scores, axis=-1, keepdims=True), jnp.max(recent, axis=-1, keepdims=True)
            )
            weights = jnp.exp2(scores - top).astype(jnp.bfloat16)
            recent = jnp.exp2(recent - top).astype(jnp.bfloat16)
            total = jnp.dot(
                weights,
                with_ones(pages[:, v_at : v_at + HEAD_SIZE]),
                preferred_element_type=jnp.float32,
            ) + jnp.dot(
                recent,
                with_ones(fresh[:, v_at : v_at + HEAD_SIZE].astype(jnp.bfloat16)),
                preferred_element_type=jnp.float32,
            )
            acc[pl.ds(first, batch), a] = total.reshape(batch, per_row, 2 * HEAD_SIZE)
            peak[pl.ds(first, batch), a] = jnp.broadcast_to(top, (rows, HEAD_SIZE)).reshape(
                batch, per_row, HEAD_SIZE
            )
        return carry

    lax.fori_loop(0, row_count // batch, cached, 0)

    def arrival(slot, carry):
        row = row_ref[slot]

        @pl.when(row >= 0)
        def _():
            for a in range(kv_heads):
                queries = q_ref[row, a].astype(jnp.bfloat16)
                k_at, v_at = 2 * a * HEAD_SIZE, (2 * a + 1) * HEAD_SIZE
                scores = scores_of(queries, landed_ref[slot, :, k_at : k_at + HEAD_SIZE])
                before = peak[row, a]
                top = jnp.maximum(before, jnp.max(scores, axis=-1, keepdims=True))
                weights = jnp.exp2(scores - top[:, :1]).astype(jnp.bfloat16)
                fade = jnp.exp2(before - top)
                acc[row, a] = acc[row, a] * jnp.concatenate([fade, fade], axis=1) + jnp.dot(
                    weights,
                    with_ones(landed_ref[slot, :, v_at : v_at + HEAD_SIZE]),
                    preferred_element_type=jnp.float32,
                )

        return carry

    lax.fori_loop(0, row_ref.shape[0], arrival, 0)
    o_ref[...] = (acc[:, :, :, :HEAD_SIZE] / acc[:, :, :, HEAD_SIZE:]).astype(o_ref.dtype)


def decode_attention(queries, dec_cache, dec_len, landed, slot_rows, fresh):
    row_count, kv_heads, per_row = queries.shape[:3]
    context = dec_cache.shape[2]
    batch = max(1, min(row_count, 2 * HEAD_SIZE // context))
    whole = lambda array: pl.BlockSpec(array.shape, lambda g, *_: (0,) * array.ndim)
    return pl.pallas_call(
        functools.partial(decode_kernel, kv_heads, batch),
        grid_spec=pltpu.PrefetchScalarGridSpec(
            num_scalar_prefetch=2,
            grid=(1,),
            in_specs=[whole(queries), whole(dec_cache), whole(landed), whole(fresh)],
            out_specs=whole(queries),
            scratch_shapes=[
                pltpu.VMEM((row_count, kv_heads, per_row, 2 * HEAD_SIZE), jnp.float32),
                pltpu.VMEM((row_count, kv_heads, per_row, HEAD_SIZE), jnp.float32),
            ],
        ),
        out_shape=jax.ShapeDtypeStruct(queries.shape, jnp.float32),
        compiler_params=pltpu.CompilerParams(vmem_limit_bytes=KERNEL_VMEM),
        cost_estimate=pl.CostEstimate(
            flops=8 * queries.size * batch * context,
            bytes_accessed=2 * dec_cache.size + 2 * landed.size,
            transcendentals=queries.size * batch * context // HEAD_SIZE,
        ),
        name="decode_attention",
    )(dec_len, slot_rows, queries, dec_cache, landed, fresh)


def shards(
    prefill_x,
    norm_gain,
    w_q,
    q_scale,
    key_value_weight,
    key_value_scale,
    w_o,
    o_scale,
    prefix_cache,
    prefix_len,
    dec_x,
    dec_cache,
    dec_len,
    place,
):
    prompts_total = prefix_cache.shape[1]
    row_count = dec_cache.shape[1]
    page_width = prefix_cache.shape[3]
    kv_heads = page_width // (2 * HEAD_SIZE)
    query_heads = w_q.shape[1] // HEAD_SIZE
    group_size = query_heads // kv_heads
    steps = dec_x.shape[0]
    section_count = lax.axis_size("section")
    section_index = lax.axis_index("section")
    tensor_count = lax.axis_size("tensor")
    tensor_index = lax.axis_index("tensor")
    head_span = max(1, 8 // query_heads)
    span_bits = head_span.bit_length() - 1
    block_width = w_o.shape[1] // tensor_count
    scales = (q_scale * EXP2_FACTOR, key_value_scale)

    weights = (norm_gain, w_q, key_value_weight)

    def kv_of_head(new_kv):
        for bit_number in range(span_bits):
            partner = partner_2(new_kv, "tensor", bit_number)
            new_kv = joined(new_kv, partner, bit_number, 1, tensor_index)
        return new_kv

    def finished(x, terms):
        total = sum(term.astype(jnp.float32) for term in terms)
        return (x.astype(jnp.float32) + total * o_scale).astype(jnp.bfloat16)

    dec_rows = dec_x.reshape(steps * row_count, -1)
    bounds = sorted({0, max(0, prompts_total - 2), prompts_total - 1, prompts_total})
    spans = list(zip(bounds[:-1], bounds[1:]))
    on_line = tensor_count == 4 and len(spans) == 3
    order = jnp.stack(
        line_order(tensor_index) if on_line else list(range(tensor_count))
    ).astype(jnp.int32)
    chunks = [prefill_x[first * PROMPT_TOKENS : last * PROMPT_TOKENS] for first, last in spans]
    blocks = chunks[:-1] + [jnp.concatenate([chunks[-1], dec_rows], axis=0)]
    pages = []

    def attention(k, queries):
        first, last = spans[k]
        return prefill_attention(queries, prefix_cache, first, last - first, pages[k], prefix_len)

    def keep(new_kv):
        new_kv = kv_of_head(new_kv)
        pages.append(new_kv[: chunks[len(pages)].shape[0]])
        return new_kv

    def back(attended, held=()):
        far, near, partner, own = project_out(
            attended, w_o, order[::-1], block_width, held=held
        )
        return LineScatter(own, partner, near, far, "tensor")

    def back_whole(attended):
        return project_out(
            attended, w_o, jnp.arange(tensor_count, dtype=jnp.int32), block_width, stacked=True
        )

    def summed(partial):
        return [lax.psum_scatter(partial, "tensor", scatter_dimension=0, tiled=False)]

    if on_line:
        first = LineGather(blocks[0], "tensor")
        first.second()
        slots = [[after(first.block, first.middle)], [first.partner]]
        begun = project_part(slots, order[:2], *weights, None, None)
        first.third(begun[2])
        second = LineGather(
            blocks[1], "tensor", (first.outer_far,), (first.outer, first.middle_far, begun[2])
        )
        queries, new_kv = project_part(first.slots()[2:], order[2:], *weights, begun, scales)
        keep(new_kv)
        second.second(queries)
        attended = attention(0, after(queries, second.partner, second.middle))
        second.third(attended)
        third = LineGather(
            after(blocks[2], second.outer, second.middle_far, attended), "tensor"
        )
        scatter = back(after(attended, second.outer, second.middle_far))

        queries, new_kv = project_part(second.slots(), order, *weights, None, scales)
        keep(new_kv)
        third.second(queries)
        attended = attention(1, after(queries, third.partner, third.middle))
        scatter.second(attended)
        partial = back_whole(after(attended, *scatter.first_hop))
        third.third(partial)
        middle_terms = summed(partial)

        slots = third.slots()
        slots[0][0] = after(slots[0][0], partial, third.outer, third.middle_far)
        begun = project_part(slots[:2], order[:2], *weights, None, None)
        queries, new_kv = project_part(slots[2:], order[2:], *weights, begun, scales)
        new_kv = keep(new_kv)
        scatter.third(queries)
        last_sum = back(attention(2, after(queries, *scatter.second_hop)), middle_terms)
        hold = (last_sum.own,)
    else:
        terms_of = []
        for k, block in enumerate(blocks):
            whole = lax.all_gather(block, "tensor", axis=1, tiled=True)
            queries, new_kv = project_part([[whole]], order[:1], *weights, None, scales)
            new_kv = keep(new_kv)
            terms_of.append(summed(back_whole(attention(k, queries))))
        hold = ()
    tokens = chunks[-1].shape[0]
    dec_queries, fresh_kv = queries[tokens:], new_kv[tokens:]

    own_block = after(jnp.concatenate(pages, axis=0), *hold).reshape(
        prompts_total, PROMPT_TOKENS, page_width
    )
    owners = (place // row_count).reshape(section_count, prompts_total)
    targets = (place % row_count).reshape(section_count, prompts_total)
    owner_hits = (owners[:, :, None] == jnp.arange(section_count)[None, None, :]).astype(jnp.int32)
    slot_ranks = jnp.sum((jnp.cumsum(owner_hits, axis=1) - owner_hits) * owner_hits, axis=2)
    capacity = prompts_total // 2
    slot_ids = jnp.arange(capacity)
    sending = lax.dynamic_index_in_dim(owner_hits, section_index, 0, keepdims=False)
    my_ranks = lax.dynamic_index_in_dim(slot_ranks, section_index, 0, keepdims=False)
    selector = (
        jnp.transpose(sending)[:, None, :] * (my_ranks[None, None, :] == slot_ids[None, :, None])
    ).astype(jnp.bfloat16)
    here = (owners == section_index)[:, None, :] & (
        slot_ranks[:, None, :] == slot_ids[None, :, None]
    )
    slot_rows = jnp.sum(jnp.where(here, targets[:, None, :] + 1, 0), axis=2) - 1
    outgoing = jnp.einsum(
        "skp,pcw->skcw", selector, own_block, preferred_element_type=jnp.float32
    ).astype(jnp.bfloat16)
    received = lax.all_to_all(outgoing, "section", split_axis=0, concat_axis=0, tiled=True)
    if on_line:
        last_sum.second(received)
        dec_queries = after(dec_queries, *last_sum.first_hop, *scatter.terms)
    landed = received.reshape(section_count * capacity, PROMPT_TOKENS, page_width)

    dec_queries = jnp.transpose(
        dec_queries.reshape(steps, row_count, kv_heads, group_size, HEAD_SIZE), (1, 2, 0, 3, 4)
    ).reshape(row_count, kv_heads, steps * group_size, HEAD_SIZE)
    fresh = jnp.transpose(fresh_kv.reshape(steps, row_count, page_width), (1, 0, 2))
    dec_attended = decode_attention(
        dec_queries.astype(jnp.float32),
        dec_cache,
        dec_len,
        landed,
        slot_rows.reshape(-1).astype(jnp.int32),
        fresh.astype(jnp.float32),
    )
    dec_attended = (
        jnp.transpose(
            dec_attended.reshape(row_count, kv_heads, steps, group_size, HEAD_SIZE), (2, 0, 1, 3, 4)
        )
        .reshape(steps * row_count, -1)
        .astype(jnp.bfloat16)
    )
    partial = back_whole(dec_attended)
    dec_terms = summed(partial)
    if on_line:
        last_sum.third(partial)
        terms_of = [scatter.terms, middle_terms, last_sum.terms]
    prefill_out = jnp.concatenate(
        [finished(x, terms) for x, terms in zip(chunks, terms_of)], axis=0
    )
    decode_out = finished(dec_rows, dec_terms).reshape(dec_x.shape)
    return (prefill_out, decode_out)


def solution(mesh):
    in_specs = (
        P(("groups", "section"), "tensor"),
        P(),
        P(None, "tensor"),
        P("tensor"),
        P(None, "tensor"),
        P("tensor"),
        P("tensor", None),
        P("tensor"),
        P("tensor", ("groups", "section"), None, None),
        P(("groups", "section")),
        P(None, ("groups", "section"), "tensor"),
        P("tensor", ("groups", "section"), None, None),
        P(("groups", "section")),
        P("groups"),
    )
    out_specs = (P(("groups", "section"), "tensor"), P(None, ("groups", "section"), "tensor"))
    return jax.shard_map(shards, mesh=mesh, in_specs=in_specs, out_specs=out_specs, check_vma=False)
```

```python
import functools
import math

import jax
import jax.numpy as jnp
from jax import lax
from jax.experimental import pallas as pl
from jax.experimental.pallas import tpu as pltpu
from jax.sharding import PartitionSpec as P

HEAD_SIZE = 128
PROMPT_TOKENS = 128
KERNEL_VMEM = 46 << 20
WEIGHT_BUFFERS = 8
COST_SHARE = 8
EXP2_FACTOR = math.log2(math.e) / math.sqrt(HEAD_SIZE)
MASKED = -1e30


def partner_2(block, axis, distance):
    count = lax.axis_size(axis)
    route = []
    for low in range(count):
        high = low | 1 << distance
        if high != low and high < count:
            route += [(low, high), (high, low)]
    return lax.ppermute(block, axis, route)


def joined(portion, partner, bit_number, concat_dim, tensor_index):
    upper_half = tensor_index // 2**bit_number % 2 == 1
    lower_first = jnp.concatenate([portion, partner], axis=concat_dim)
    upper_first = jnp.concatenate([partner, portion], axis=concat_dim)
    return jnp.where(upper_half, upper_first, lower_first)


def tile_of(extent, most):
    tile = extent
    while tile > most and tile % 2 == 0:
        tile //= 2
    return tile


def after(value, *others):
    return lax.optimization_barrier((value,) + others)[0]


def after_all(values, *others):
    return lax.optimization_barrier(tuple(values) + others)[: len(values)]


def line_order(index):
    low = index < 2
    return [index, index ^ 1, jnp.where(low, 2, 1), jnp.where(low, 3, 0)]


OUTER = [(0, 1), (1, 0), (2, 3), (3, 2)]
MIDDLE = [(1, 2), (2, 1)]
INWARD = [(0, 1), (3, 2)]
OUTWARD = [(1, 0), (2, 3)]


class LineGather:
    def __init__(self, block, axis, outer_held=(), middle_held=()):
        self.block, self.axis = block, axis
        self.partner = lax.ppermute(after(block, *outer_held), axis, OUTER)
        self.middle = lax.ppermute(after(block, *middle_held), axis, MIDDLE)

    def second(self, *held):
        partner, middle = after_all((self.partner, self.middle), *held)
        self.outer = lax.ppermute(middle, self.axis, OUTWARD)
        self.middle_far = lax.ppermute(partner, self.axis, MIDDLE)

    def third(self, *held):
        self.outer_far = lax.ppermute(after(self.middle_far, *held), self.axis, OUTWARD)

    def slots(self):
        return [
            [self.block],
            [self.partner],
            [self.middle, self.outer],
            [self.middle_far, self.outer_far],
        ]


def added(*terms):
    total = sum(term.astype(jnp.float32) for term in terms)
    return total.astype(terms[0].dtype)


class LineScatter:
    def __init__(self, own, partner, near, far, axis):
        self.own, self.partner, self.near, self.far = own, partner, near, far
        self.axis = axis
        self.far_in = lax.ppermute(far, axis, INWARD)

    def second(self, *held):
        far, near = after_all((added(self.far, self.far_in), self.near), *held)
        self.first_hop = (far,)
        self.near_in = lax.ppermute(near, self.axis, INWARD)
        self.far_out = lax.ppermute(far, self.axis, MIDDLE)

    def third(self, *held):
        near, partner = after_all(
            (added(self.near, self.near_in), added(self.partner, self.far_out)), *held
        )
        self.second_hop = (near, partner)
        near = lax.ppermute(near, self.axis, MIDDLE)
        partner = lax.ppermute(partner, self.axis, OUTER)
        self.terms = [self.own, near, partner]


def without(kernel, first, count):
    return lambda *refs: kernel(*refs[:first], *refs[first + count :])


def qkv_kernel(counts, begun, ended, tile, order, *refs):
    refs = list(refs)
    arrays = sum(counts)
    xs = [refs.pop(0) for _ in range(arrays)]
    gain_ref, wq_ref, wkv_ref = (refs.pop(0) for _ in range(3))
    sums_in = [refs.pop(0) for _ in range(3)] if begun else []
    if ended:
        qs_ref, kvs_ref, q_ref, kv_ref, accq, acckv, squares = (refs.pop(0) for _ in range(7))
    else:
        accq, acckv, squares = (refs.pop(0) for _ in range(3))
    x_bufs = [refs.pop(0) for _ in range(arrays)]
    wq_buf, wkv_buf, x_sem, w_sem, sum_sem = refs
    per = x_bufs[0].shape[1] // tile
    steps = len(counts) * per
    ahead = min(steps, wq_buf.shape[0])

    def weight_copies(step):
        buffer = lax.rem(step, ahead)
        at = pl.multiple_of((order[step // per] * per + lax.rem(step, per)) * tile, tile)
        return [
            pltpu.make_async_copy(ref.at[pl.ds(at, tile)], buf.at[buffer], w_sem.at[w, buffer])
            for w, (ref, buf) in enumerate([(wq_ref, wq_buf), (wkv_ref, wkv_buf)])
        ]

    x_copies = [
        pltpu.make_async_copy(ref, buf, x_sem.at[a]) for a, (ref, buf) in enumerate(zip(xs, x_bufs))
    ]
    sum_copies = [
        pltpu.make_async_copy(ref, acc, sum_sem.at[a])
        for a, (ref, acc) in enumerate(zip(sums_in, (accq, acckv, squares)))
    ]
    for copy in x_copies[: counts[0]] + sum_copies:
        copy.start()
    for step in range(ahead):
        for copy in weight_copies(step):
            copy.start()
    for copy in x_copies[counts[0] :]:
        copy.start()
    for copy in sum_copies:
        copy.wait()
    if not begun:
        accq[...] = jnp.zeros_like(accq)
        acckv[...] = jnp.zeros_like(acckv)
        squares[...] = jnp.zeros_like(squares)

    taken = 0
    for s, count in enumerate(counts):
        for copy in x_copies[taken : taken + count]:
            copy.wait()
        bufs = x_bufs[taken : taken + count]
        taken += count

        def body(j, carry, s=s, bufs=bufs):
            step = s * per + j
            for copy in weight_copies(step):
                copy.wait()
            at = pl.multiple_of(j * tile, tile)
            values = sum(buf[:, pl.ds(at, tile)].astype(jnp.float32) for buf in bufs)
            gain = gain_ref[:, pl.ds(pl.multiple_of((order[s] * per + j) * tile, tile), tile)]
            squares[...] += jnp.broadcast_to(
                jnp.sum(values * values, axis=-1, keepdims=True), squares.shape
            )
            scaled = (values * gain).astype(jnp.bfloat16)
            buffer = lax.rem(step, ahead)
            accq[...] += jnp.dot(scaled, wq_buf[buffer], preferred_element_type=jnp.float32)
            acckv[...] += jnp.dot(scaled, wkv_buf[buffer], preferred_element_type=jnp.float32)

            @pl.when(step + ahead < steps)
            def _():
                for copy in weight_copies(step + ahead):
                    copy.start()

            return carry

        lax.fori_loop(0, per, body, 0)
    if ended:
        root = lax.rsqrt(squares[:, :1] / ended + 1e-05)
        q_ref[...] = (accq[...] * root * qs_ref[...]).astype(q_ref.dtype)
        kv_ref[...] = (acckv[...] * root * kvs_ref[...]).astype(kv_ref.dtype)


def project_part(slots, order, norm_gain, w_q, kv_weight, begun, scales, held=()):
    rows, depth = slots[0][0].shape
    tile = tile_of(depth, 512)
    q_cols, kv_cols = w_q.shape[1], kv_weight.shape[1]
    arrays = [array for slot in slots for array in slot]

    def whole(shape):
        return pl.BlockSpec(shape, lambda g, order: (0,) * len(shape))

    anywhere = pl.BlockSpec(memory_space=pl.ANY)
    operands = arrays + [norm_gain.reshape(1, -1), w_q, kv_weight]
    in_specs = [anywhere] * len(arrays) + [whole((1, norm_gain.shape[0])), anywhere, anywhere]
    sums = [(rows, q_cols), (rows, kv_cols), (rows, HEAD_SIZE)]
    if begun is not None:
        operands += list(begun)
        in_specs += [anywhere] * 3
    if scales is not None:
        operands += [scale.reshape(1, -1) for scale in scales]
        in_specs += [whole((1, q_cols)), whole((1, kv_cols))]
        out_shapes = [jax.ShapeDtypeStruct(shape, jnp.bfloat16) for shape in sums[:2]]
        scratch = [pltpu.VMEM(shape, jnp.float32) for shape in sums]
    else:
        out_shapes = [jax.ShapeDtypeStruct(shape, jnp.float32) for shape in sums]
        scratch = []
    kernel = functools.partial(
        qkv_kernel,
        [len(slot) for slot in slots],
        begun is not None,
        0 if scales is None else w_q.shape[0],
        tile,
    )
    return pl.pallas_call(
        without(kernel, 1 + len(operands), len(held)),
        grid_spec=pltpu.PrefetchScalarGridSpec(
            num_scalar_prefetch=1,
            grid=(1,),
            in_specs=in_specs + [anywhere] * len(held),
            out_specs=[whole(out.shape) for out in out_shapes],
            scratch_shapes=scratch
            + [pltpu.VMEM((rows, depth), jnp.bfloat16) for _ in arrays]
            + [
                pltpu.VMEM((WEIGHT_BUFFERS, tile, q_cols), jnp.bfloat16),
                pltpu.VMEM((WEIGHT_BUFFERS, tile, kv_cols), jnp.bfloat16),
                pltpu.SemaphoreType.DMA((len(arrays),)),
                pltpu.SemaphoreType.DMA((2, WEIGHT_BUFFERS)),
                pltpu.SemaphoreType.DMA((3,)),
            ],
        ),
        out_shape=out_shapes,
        compiler_params=pltpu.CompilerParams(vmem_limit_bytes=KERNEL_VMEM),
        cost_estimate=pl.CostEstimate(
            flops=2 * rows * depth * len(slots) * (q_cols + kv_cols) // COST_SHARE,
            bytes_accessed=(2 * depth * len(slots) * (q_cols + kv_cols)) // COST_SHARE,
            transcendentals=0,
        ),
        name="norm_qkv",
    )(order, *operands, *held)


def out_kernel(count, stacked, tile, order, x_ref, w_ref, *refs):
    if stacked:
        outs, refs = [refs[0].at[s] for s in range(count)], refs[1:]
    else:
        outs, refs = refs[:count], refs[count:]
    x_buf, w_buf, x_sem, w_sem, o_sem = refs[:5]
    o_bufs = refs[5:]
    per = o_bufs[0].shape[1] // tile
    steps = count * per
    ahead = min(steps, w_buf.shape[0])

    def weight_copy(step):
        at = pl.multiple_of((order[step // per] * per + lax.rem(step, per)) * tile, tile)
        buffer = lax.rem(step, ahead)
        return pltpu.make_async_copy(
            w_ref.at[:, pl.ds(at, tile)], w_buf.at[buffer], w_sem.at[buffer]
        )

    x_copy = pltpu.make_async_copy(x_ref, x_buf, x_sem)
    x_copy.start()
    for step in range(ahead):
        weight_copy(step).start()
    x_copy.wait()
    o_copies = []
    for s, (out, o_buf) in enumerate(zip(outs, o_bufs)):

        def body(j, carry, s=s, o_buf=o_buf):
            step = s * per + j
            weight_copy(step).wait()
            o_buf[:, pl.ds(pl.multiple_of(j * tile, tile), tile)] = jnp.dot(
                x_buf[...], w_buf[lax.rem(step, ahead)], preferred_element_type=jnp.float32
            ).astype(o_buf.dtype)

            @pl.when(step + ahead < steps)
            def _():
                weight_copy(step + ahead).start()

            return carry

        lax.fori_loop(0, per, body, 0)
        o_copies.append(pltpu.make_async_copy(o_buf, out, o_sem.at[s]))
        o_copies[-1].start()
    for copy in o_copies:
        copy.wait()


def project_out(attended, w_o, order, block, stacked=False, held=()):
    rows, depth = attended.shape
    tile = tile_of(block, 512)
    count = order.shape[0]
    anywhere = pl.BlockSpec(memory_space=pl.ANY)
    return pl.pallas_call(
        without(functools.partial(out_kernel, count, stacked, tile), 3, len(held)),
        grid_spec=pltpu.PrefetchScalarGridSpec(
            num_scalar_prefetch=1,
            grid=(1,),
            in_specs=[anywhere] * (2 + len(held)),
            out_specs=anywhere if stacked else [anywhere] * count,
            scratch_shapes=[
                pltpu.VMEM((rows, depth), jnp.bfloat16),
                pltpu.VMEM((WEIGHT_BUFFERS, depth, tile), jnp.bfloat16),
                pltpu.SemaphoreType.DMA,
                pltpu.SemaphoreType.DMA((WEIGHT_BUFFERS,)),
                pltpu.SemaphoreType.DMA((count,)),
            ]
            + [pltpu.VMEM((rows, block), jnp.bfloat16)] * count,
        ),
        out_shape=jax.ShapeDtypeStruct((count, rows, block), jnp.bfloat16)
        if stacked
        else [jax.ShapeDtypeStruct((rows, block), jnp.bfloat16)] * count,
        compiler_params=pltpu.CompilerParams(vmem_limit_bytes=KERNEL_VMEM),
        cost_estimate=pl.CostEstimate(
            flops=2 * rows * depth * count * block // COST_SHARE,
            bytes_accessed=(2 * depth * count * block) // COST_SHARE,
            transcendentals=0,
        ),
        name="project_out",
    )(order, attended, w_o, *held)


def with_ones(values):
    return jnp.concatenate([values, jnp.ones_like(values)], axis=1)


def scores_of(queries, keys):
    return lax.dot_general(
        queries, keys, (((1,), (1,)), ((), ())), preferred_element_type=jnp.float32
    )


def prefill_kernel(kv_heads, group, span, first, len_ref, q_ref, cache_ref, new_ref, o_ref, *scratch):
    accs, peaks = scratch[:kv_heads], scratch[kv_heads:]
    tokens = q_ref.shape[0]
    rows = group * tokens
    live = len_ref[first + pl.program_id(0)]
    full = live // span
    query_token = lax.rem(lax.broadcasted_iota(jnp.int32, (rows, tokens), 0), tokens)
    key_token = lax.broadcasted_iota(jnp.int32, (rows, tokens), 1)
    causal = key_token <= query_token
    lane = lax.broadcasted_iota(jnp.int32, (1, span), 1)

    def queries_of(a):
        return jnp.concatenate(
            [
                q_ref[:, (a * group + h) * HEAD_SIZE : (a * group + h + 1) * HEAD_SIZE]
                for h in range(group)
            ],
            axis=0,
        )

    def columns(a, part):
        return pl.ds((2 * a + part) * HEAD_SIZE, HEAD_SIZE)

    for a in range(kv_heads):
        scores = jnp.where(causal, scores_of(queries_of(a), new_ref[:, columns(a, 0)]), MASKED)
        top = jnp.broadcast_to(jnp.max(scores, axis=-1, keepdims=True), (rows, HEAD_SIZE))
        weights = jnp.exp2(scores - top[:, :tokens]).astype(jnp.bfloat16)
        accs[a][...] = jnp.dot(
            weights, with_ones(new_ref[:, columns(a, 1)]), preferred_element_type=jnp.float32
        )
        peaks[a][...] = top

    def block(s, bias):
        at = pl.multiple_of(s * span, span)
        scores = [
            scores_of(queries_of(a), cache_ref[0, 0, pl.ds(at, span), columns(a, 0)])
            for a in range(kv_heads)
        ]
        for a in range(kv_heads):
            here = scores[a] if bias is None else scores[a] + bias
            before = peaks[a][...]
            top = jnp.maximum(before, jnp.max(here, axis=-1, keepdims=True))
            weights = jnp.exp2(
                here - jnp.concatenate([top] * (span // HEAD_SIZE), axis=1)
            ).astype(jnp.bfloat16)
            fade = jnp.exp2(before - top)
            values = cache_ref[0, 0, pl.ds(at, span), columns(a, 1)]
            accs[a][...] = accs[a][...] * jnp.concatenate([fade, fade], axis=1) + jnp.dot(
                weights, with_ones(values), preferred_element_type=jnp.float32
            )
            peaks[a][...] = top

    def step(s, carry):
        block(s, None)
        return carry

    lax.fori_loop(0, full, step, 0)

    @pl.when(full * span < live)
    def _():
        block(full, jnp.where(lane + full * span < live, 0.0, MASKED))

    for a in range(kv_heads):
        result = accs[a][:, :HEAD_SIZE] / accs[a][:, HEAD_SIZE:]
        for h in range(group):
            o_ref[:, (a * group + h) * HEAD_SIZE : (a * group + h + 1) * HEAD_SIZE] = result[
                h * tokens : (h + 1) * tokens
            ].astype(o_ref.dtype)


def prefill_attention(queries, prefix_cache, first, count, new_kv, prefix_len):
    width = queries.shape[1]
    positions, page = prefix_cache.shape[2:]
    kv_heads = page // (2 * HEAD_SIZE)
    group = width // HEAD_SIZE // kv_heads
    span = tile_of(positions, 512)
    rows = group * PROMPT_TOKENS
    return pl.pallas_call(
        functools.partial(prefill_kernel, kv_heads, group, span, first),
        grid_spec=pltpu.PrefetchScalarGridSpec(
            num_scalar_prefetch=1,
            grid=(count,),
            in_specs=[
                pl.BlockSpec((PROMPT_TOKENS, width), lambda g, n: (g, 0)),
                pl.BlockSpec((1, 1, positions, page), lambda g, n: (0, first + g, 0, 0)),
                pl.BlockSpec((PROMPT_TOKENS, page), lambda g, n: (g, 0)),
            ],
            out_specs=pl.BlockSpec((PROMPT_TOKENS, width), lambda g, n: (g, 0)),
            scratch_shapes=[pltpu.VMEM((rows, 2 * HEAD_SIZE), jnp.float32)] * kv_heads
            + [pltpu.VMEM((rows, HEAD_SIZE), jnp.float32)] * kv_heads,
        ),
        out_shape=jax.ShapeDtypeStruct((count * PROMPT_TOKENS, width), jnp.bfloat16),
        compiler_params=pltpu.CompilerParams(vmem_limit_bytes=KERNEL_VMEM),
        cost_estimate=pl.CostEstimate(
            flops=8 * count * rows * kv_heads * (positions + PROMPT_TOKENS) * HEAD_SIZE // COST_SHARE,
            bytes_accessed=(2 * count * positions * page) // COST_SHARE,
            transcendentals=count * rows * kv_heads * (positions + PROMPT_TOKENS),
        ),
        name="prefill_attention",
    )(prefix_len, queries, prefix_cache, new_kv)


def decode_kernel(
    kv_heads, batch, len_ref, row_ref, q_ref, cache_ref, landed_ref, fresh_ref, o_ref, acc, peak
):
    row_count, context = cache_ref.shape[1], cache_ref.shape[2]
    per_row = q_ref.shape[2]
    steps = fresh_ref.shape[1]
    rows = batch * per_row
    row_of = lax.broadcasted_iota(jnp.int32, (rows, batch * context), 0) // per_row
    key_row = lax.broadcasted_iota(jnp.int32, (rows, batch * context), 1) // context
    key_at = lax.rem(lax.broadcasted_iota(jnp.int32, (rows, batch * context), 1), context)
    fresh_query = lax.broadcasted_iota(jnp.int32, (rows, batch * steps), 0)
    fresh_key = lax.broadcasted_iota(jnp.int32, (rows, batch * steps), 1)
    fresh_live = (fresh_key // steps == fresh_query // per_row) & (
        lax.rem(fresh_key, steps) <= lax.rem(fresh_query, per_row) // (per_row // steps)
    )

    def cached(b, carry):
        first = b * batch
        live = jnp.zeros_like(key_row)
        for r in range(batch):
            live = jnp.where(key_row == r, len_ref[first + r], live)
        cache_live = (row_of == key_row) & (key_at < live)
        pages = cache_ref[0, pl.ds(first, batch)].reshape(batch * context, cache_ref.shape[3])
        fresh = fresh_ref[pl.ds(first, batch)].reshape(batch * steps, fresh_ref.shape[2])
        for a in range(kv_heads):
            queries = q_ref[pl.ds(first, batch), a].reshape(rows, HEAD_SIZE).astype(jnp.bfloat16)
            k_at, v_at = 2 * a * HEAD_SIZE, (2 * a + 1) * HEAD_SIZE
            scores = scores_of(queries, pages[:, k_at : k_at + HEAD_SIZE])
            scores = jnp.where(cache_live, scores, MASKED)
            recent = scores_of(queries, fresh[:, k_at : k_at + HEAD_SIZE].astype(jnp.bfloat16))
            recent = jnp.where(fresh_live, recent, MASKED)
            top = jnp.maximum(
                jnp.max(scores, axis=-1, keepdims=True), jnp.max(recent, axis=-1, keepdims=True)
            )
            weights = jnp.exp2(scores - top).astype(jnp.bfloat16)
            recent = jnp.exp2(recent - top).astype(jnp.bfloat16)
            total = jnp.dot(
                weights,
                with_ones(pages[:, v_at : v_at + HEAD_SIZE]),
                preferred_element_type=jnp.float32,
            ) + jnp.dot(
                recent,
                with_ones(fresh[:, v_at : v_at + HEAD_SIZE].astype(jnp.bfloat16)),
                preferred_element_type=jnp.float32,
            )
            acc[pl.ds(first, batch), a] = total.reshape(batch, per_row, 2 * HEAD_SIZE)
            peak[pl.ds(first, batch), a] = jnp.broadcast_to(top, (rows, HEAD_SIZE)).reshape(
                batch, per_row, HEAD_SIZE
            )
        return carry

    lax.fori_loop(0, row_count // batch, cached, 0)

    def arrival(slot, carry):
        row = row_ref[slot]

        @pl.when(row >= 0)
        def _():
            for a in range(kv_heads):
                queries = q_ref[row, a].astype(jnp.bfloat16)
                k_at, v_at = 2 * a * HEAD_SIZE, (2 * a + 1) * HEAD_SIZE
                scores = scores_of(queries, landed_ref[slot, :, k_at : k_at + HEAD_SIZE])
                before = peak[row, a]
                top = jnp.maximum(before, jnp.max(scores, axis=-1, keepdims=True))
                weights = jnp.exp2(scores - top[:, :1]).astype(jnp.bfloat16)
                fade = jnp.exp2(before - top)
                acc[row, a] = acc[row, a] * jnp.concatenate([fade, fade], axis=1) + jnp.dot(
                    weights,
                    with_ones(landed_ref[slot, :, v_at : v_at + HEAD_SIZE]),
                    preferred_element_type=jnp.float32,
                )

        return carry

    lax.fori_loop(0, row_ref.shape[0], arrival, 0)
    o_ref[...] = (acc[:, :, :, :HEAD_SIZE] / acc[:, :, :, HEAD_SIZE:]).astype(o_ref.dtype)


def decode_attention(queries, dec_cache, dec_len, landed, slot_rows, fresh, held=()):
    row_count, kv_heads, per_row = queries.shape[:3]
    context = dec_cache.shape[2]
    batch = max(1, min(row_count, 2 * HEAD_SIZE // context))
    whole = lambda array: pl.BlockSpec(array.shape, lambda g, *_: (0,) * array.ndim)
    return pl.pallas_call(
        without(functools.partial(decode_kernel, kv_heads, batch), 6, len(held)),
        grid_spec=pltpu.PrefetchScalarGridSpec(
            num_scalar_prefetch=2,
            grid=(1,),
            in_specs=[whole(queries), whole(dec_cache), whole(landed), whole(fresh)]
            + [pl.BlockSpec(memory_space=pl.ANY)] * len(held),
            out_specs=whole(queries),
            scratch_shapes=[
                pltpu.VMEM((row_count, kv_heads, per_row, 2 * HEAD_SIZE), jnp.float32),
                pltpu.VMEM((row_count, kv_heads, per_row, HEAD_SIZE), jnp.float32),
            ],
        ),
        out_shape=jax.ShapeDtypeStruct(queries.shape, jnp.float32),
        compiler_params=pltpu.CompilerParams(vmem_limit_bytes=KERNEL_VMEM),
        cost_estimate=pl.CostEstimate(
            flops=8 * queries.size * batch * context // COST_SHARE,
            bytes_accessed=(2 * dec_cache.size + 2 * landed.size) // COST_SHARE,
            transcendentals=queries.size * batch * context // HEAD_SIZE,
        ),
        name="decode_attention",
    )(dec_len, slot_rows, queries, dec_cache, landed, fresh, *held)


def shards(
    prefill_x,
    norm_gain,
    w_q,
    q_scale,
    key_value_weight,
    key_value_scale,
    w_o,
    o_scale,
    prefix_cache,
    prefix_len,
    dec_x,
    dec_cache,
    dec_len,
    place,
):
    prompts_total = prefix_cache.shape[1]
    row_count = dec_cache.shape[1]
    page_width = prefix_cache.shape[3]
    kv_heads = page_width // (2 * HEAD_SIZE)
    query_heads = w_q.shape[1] // HEAD_SIZE
    group_size = query_heads // kv_heads
    steps = dec_x.shape[0]
    section_count = lax.axis_size("section")
    section_index = lax.axis_index("section")
    tensor_count = lax.axis_size("tensor")
    tensor_index = lax.axis_index("tensor")
    head_span = max(1, 8 // query_heads)
    span_bits = head_span.bit_length() - 1
    block_width = w_o.shape[1] // tensor_count
    scales = (q_scale * EXP2_FACTOR, key_value_scale)

    weights = (norm_gain, w_q, key_value_weight)

    def kv_of_head(new_kv):
        for bit_number in range(span_bits):
            partner = partner_2(new_kv, "tensor", bit_number)
            new_kv = joined(new_kv, partner, bit_number, 1, tensor_index)
        return new_kv

    def finished(x, terms):
        total = sum(term.astype(jnp.float32) for term in terms)
        return (x.astype(jnp.float32) + total * o_scale).astype(jnp.bfloat16)

    dec_rows = dec_x.reshape(steps * row_count, -1)
    bounds = sorted({0, min(1, prompts_total - 1), prompts_total - 1, prompts_total})
    spans = list(zip(bounds[:-1], bounds[1:]))
    on_line = tensor_count == 4 and len(spans) == 3
    order = jnp.stack(
        line_order(tensor_index) if on_line else list(range(tensor_count))
    ).astype(jnp.int32)
    chunks = [prefill_x[first * PROMPT_TOKENS : last * PROMPT_TOKENS] for first, last in spans]
    blocks = chunks[:-1] + [jnp.concatenate([chunks[-1], dec_rows], axis=0)]
    pages = []

    def attention(k, queries):
        first, last = spans[k]
        return prefill_attention(queries, prefix_cache, first, last - first, pages[k], prefix_len)

    def keep(new_kv):
        new_kv = kv_of_head(new_kv)
        pages.append(new_kv[: chunks[len(pages)].shape[0]])
        return new_kv

    def back(attended, held=()):
        far, near, partner, own = project_out(
            attended, w_o, order[::-1], block_width, held=held
        )
        return LineScatter(own, partner, near, far, "tensor")

    def back_whole(attended):
        return project_out(
            attended, w_o, jnp.arange(tensor_count, dtype=jnp.int32), block_width, stacked=True
        )

    def summed(partial):
        return [lax.psum_scatter(partial, "tensor", scatter_dimension=0, tiled=False)]

    if on_line:
        first = LineGather(blocks[0], "tensor")
        first.second()
        begun = project_part(
            [[first.block], [first.partner]], order[:2], *weights, None, None, (first.middle,)
        )
        first.third(begun[2])
        second = LineGather(
            blocks[1], "tensor", (first.outer_far,), (first.outer, first.middle_far, begun[2])
        )
        queries, new_kv = project_part(first.slots()[2:], order[2:], *weights, begun, scales)
        keep(new_kv)
        attended = attention(0, queries)
        second.second(attended)
        sums = [back(attended, (second.partner, second.middle))]

        begun = project_part(
            [[second.block], [second.partner]], order[:2], *weights, None, None, (sums[0].own,)
        )
        second.third(begun[2])
        sums[0].second(begun[2])
        sums[0].third()
        third = LineGather(
            blocks[2], "tensor", (second.outer_far,), (second.outer, second.middle_far, begun[2])
        )
        queries, new_kv = project_part(
            second.slots()[2:], order[2:], *weights, begun, scales, sums[0].second_hop
        )
        keep(new_kv)
        attended = attention(1, queries)
        third.second(attended)
        sums.append(back(attended, (third.partner, third.middle, *sums[0].terms[1:])))

        third.third(sums[1].own)
        begun = project_part(
            [[third.block], [third.partner]],
            order[:2],
            *weights,
            None,
            None,
            (sums[1].own, third.outer, third.middle_far),
        )
        sums[1].second(begun[2])
        queries, new_kv = project_part(
            third.slots()[2:], order[2:], *weights, begun, scales, sums[1].first_hop
        )
        new_kv = keep(new_kv)
        sums.append(back(attention(2, queries)))
        sums[1].third(sums[2].own)
        hold = (sums[2].own,)
    else:
        terms_of = []
        for k, block in enumerate(blocks):
            whole = lax.all_gather(block, "tensor", axis=1, tiled=True)
            queries, new_kv = project_part([[whole]], order[:1], *weights, None, scales)
            new_kv = keep(new_kv)
            terms_of.append(summed(back_whole(attention(k, queries))))
        hold = ()
    tokens = chunks[-1].shape[0]
    dec_queries, fresh_kv = queries[tokens:], new_kv[tokens:]

    own_block = after(jnp.concatenate(pages, axis=0), *hold).reshape(
        prompts_total, PROMPT_TOKENS, page_width
    )
    owners = (place // row_count).reshape(section_count, prompts_total)
    targets = (place % row_count).reshape(section_count, prompts_total)
    owner_hits = (owners[:, :, None] == jnp.arange(section_count)[None, None, :]).astype(jnp.int32)
    slot_ranks = jnp.sum((jnp.cumsum(owner_hits, axis=1) - owner_hits) * owner_hits, axis=2)
    capacity = prompts_total // 2
    slot_ids = jnp.arange(capacity)
    sending = lax.dynamic_index_in_dim(owner_hits, section_index, 0, keepdims=False)
    my_ranks = lax.dynamic_index_in_dim(slot_ranks, section_index, 0, keepdims=False)
    selector = (
        jnp.transpose(sending)[:, None, :] * (my_ranks[None, None, :] == slot_ids[None, :, None])
    ).astype(jnp.bfloat16)
    here = (owners == section_index)[:, None, :] & (
        slot_ranks[:, None, :] == slot_ids[None, :, None]
    )
    slot_rows = jnp.sum(jnp.where(here, targets[:, None, :] + 1, 0), axis=2) - 1
    outgoing = jnp.einsum(
        "skp,pcw->skcw", selector, own_block, preferred_element_type=jnp.float32
    ).astype(jnp.bfloat16)
    received = lax.all_to_all(outgoing, "section", split_axis=0, concat_axis=0, tiled=True)
    if on_line:
        sums[2].second(received)
        hold = (*sums[2].first_hop, *sums[1].second_hop)
    landed = received.reshape(section_count * capacity, PROMPT_TOKENS, page_width)

    dec_queries = jnp.transpose(
        dec_queries.reshape(steps, row_count, kv_heads, group_size, HEAD_SIZE), (1, 2, 0, 3, 4)
    ).reshape(row_count, kv_heads, steps * group_size, HEAD_SIZE)
    fresh = jnp.transpose(fresh_kv.reshape(steps, row_count, page_width), (1, 0, 2))
    dec_attended = decode_attention(
        dec_queries.astype(jnp.float32),
        dec_cache,
        dec_len,
        landed,
        slot_rows.reshape(-1).astype(jnp.int32),
        fresh.astype(jnp.float32),
        hold,
    )
    dec_attended = (
        jnp.transpose(
            dec_attended.reshape(row_count, kv_heads, steps, group_size, HEAD_SIZE), (2, 0, 1, 3, 4)
        )
        .reshape(steps * row_count, -1)
        .astype(jnp.bfloat16)
    )
    if on_line:
        sums[2].third(dec_attended)
        to = [(tensor_index + shift) % tensor_count for shift in range(tensor_count)]
        own, *parts = project_out(
            dec_attended,
            w_o,
            jnp.stack(to).astype(jnp.int32),
            block_width,
            held=sums[2].second_hop,
        )
        dec_terms = [own] + [
            lax.ppermute(
                part, "tensor", [(j, (j + shift) % tensor_count) for j in range(tensor_count)]
            )
            for shift, part in enumerate(parts, 1)
        ]
        terms_of = [each.terms for each in sums]
    else:
        dec_terms = summed(back_whole(dec_attended))
    prefill_out = jnp.concatenate(
        [finished(x, terms) for x, terms in zip(chunks, terms_of)], axis=0
    )
    decode_out = finished(dec_rows, dec_terms).reshape(dec_x.shape)
    return (prefill_out, decode_out)


def solution(mesh):
    in_specs = (
        P(("groups", "section"), "tensor"),
        P(),
        P(None, "tensor"),
        P("tensor"),
        P(None, "tensor"),
        P("tensor"),
        P("tensor", None),
        P("tensor"),
        P("tensor", ("groups", "section"), None, None),
        P(("groups", "section")),
        P(None, ("groups", "section"), "tensor"),
        P("tensor", ("groups", "section"), None, None),
        P(("groups", "section")),
        P("groups"),
    )
    out_specs = (P(("groups", "section"), "tensor"), P(None, ("groups", "section"), "tensor"))
    return jax.shard_map(shards, mesh=mesh, in_specs=in_specs, out_specs=out_specs, check_vma=False)
```

```python
import functools
import math

import jax
import jax.numpy as jnp
from jax import lax
from jax.experimental import pallas as pl
from jax.experimental.pallas import tpu as pltpu
from jax.sharding import PartitionSpec as P

HEAD_SIZE = 128
PROMPT_TOKENS = 128
KERNEL_VMEM = 40 << 20
WEIGHT_BUFFERS = 8
COST_SHARE = 256
EXP2_FACTOR = math.log2(math.e) / math.sqrt(HEAD_SIZE)
MASKED = -1e30


def partner_2(block, axis, distance):
    count = lax.axis_size(axis)
    route = []
    for low in range(count):
        high = low | 1 << distance
        if high != low and high < count:
            route += [(low, high), (high, low)]
    return lax.ppermute(block, axis, route)


def joined(portion, partner, bit_number, concat_dim, tensor_index):
    upper_half = tensor_index // 2**bit_number % 2 == 1
    lower_first = jnp.concatenate([portion, partner], axis=concat_dim)
    upper_first = jnp.concatenate([partner, portion], axis=concat_dim)
    return jnp.where(upper_half, upper_first, lower_first)


def tile_of(extent, most):
    tile = extent
    while tile > most and tile % 2 == 0:
        tile //= 2
    return tile


def after(value, *others):
    return lax.optimization_barrier((value,) + others)[0]


def after_all(values, *others):
    return lax.optimization_barrier(tuple(values) + others)[: len(values)]


def line_order(index):
    low = index < 2
    return [index, index ^ 1, jnp.where(low, 2, 1), jnp.where(low, 3, 0)]


OUTER = [(0, 1), (1, 0), (2, 3), (3, 2)]
MIDDLE = [(1, 2), (2, 1)]
INWARD = [(0, 1), (3, 2)]
OUTWARD = [(1, 0), (2, 3)]


class LineGather:
    def __init__(self, block, axis, outer_held=(), middle_held=()):
        self.block, self.axis = block, axis
        self.partner = lax.ppermute(after(block, *outer_held), axis, OUTER)
        self.middle = lax.ppermute(after(block, *middle_held), axis, MIDDLE)

    def second(self, *held):
        partner, middle = after_all((self.partner, self.middle), *held)
        self.outer = lax.ppermute(middle, self.axis, OUTWARD)
        self.middle_far = lax.ppermute(partner, self.axis, MIDDLE)

    def third(self, *held):
        self.outer_far = lax.ppermute(after(self.middle_far, *held), self.axis, OUTWARD)

    def slots(self):
        return [
            [self.block],
            [self.partner],
            [self.middle, self.outer],
            [self.middle_far, self.outer_far],
        ]


def added(*terms):
    total = sum(term.astype(jnp.float32) for term in terms)
    return total.astype(terms[0].dtype)


class LineScatter:
    def __init__(self, own, partner, near, far, axis):
        self.own, self.partner, self.near, self.far = own, partner, near, far
        self.axis = axis
        self.far_in = lax.ppermute(far, axis, INWARD)

    def second(self, *held):
        far, near = after_all((added(self.far, self.far_in), self.near), *held)
        self.first_hop = (far,)
        self.near_in = lax.ppermute(near, self.axis, INWARD)
        self.far_out = lax.ppermute(far, self.axis, MIDDLE)

    def third(self, *held):
        near, partner = after_all(
            (added(self.near, self.near_in), added(self.partner, self.far_out)), *held
        )
        self.second_hop = (near, partner)
        near = lax.ppermute(near, self.axis, MIDDLE)
        partner = lax.ppermute(partner, self.axis, OUTER)
        self.terms = [self.own, near, partner]


def without(kernel, first, count):
    return lambda *refs: kernel(*refs[:first], *refs[first + count :])


def qkv_kernel(counts, begun, ended, tile, order, *refs):
    refs = list(refs)
    arrays = sum(counts)
    xs = [refs.pop(0) for _ in range(arrays)]
    gain_ref, wq_ref, wkv_ref = (refs.pop(0) for _ in range(3))
    sums_in = [refs.pop(0) for _ in range(3)] if begun else []
    if ended:
        qs_ref, kvs_ref, q_ref, kv_ref, accq, acckv, squares = (refs.pop(0) for _ in range(7))
    else:
        accq, acckv, squares = (refs.pop(0) for _ in range(3))
    x_bufs = [refs.pop(0) for _ in range(arrays)]
    wq_buf, wkv_buf, x_sem, w_sem, sum_sem = refs
    per = x_bufs[0].shape[1] // tile
    steps = len(counts) * per
    ahead = min(steps, wq_buf.shape[0])

    def weight_copies(step):
        buffer = lax.rem(step, ahead)
        at = pl.multiple_of((order[step // per] * per + lax.rem(step, per)) * tile, tile)
        return [
            pltpu.make_async_copy(ref.at[pl.ds(at, tile)], buf.at[buffer], w_sem.at[w, buffer])
            for w, (ref, buf) in enumerate([(wq_ref, wq_buf), (wkv_ref, wkv_buf)])
        ]

    x_copies = [
        pltpu.make_async_copy(ref, buf, x_sem.at[a]) for a, (ref, buf) in enumerate(zip(xs, x_bufs))
    ]
    sum_copies = [
        pltpu.make_async_copy(ref, acc, sum_sem.at[a])
        for a, (ref, acc) in enumerate(zip(sums_in, (accq, acckv, squares)))
    ]
    for copy in x_copies[: counts[0]] + sum_copies:
        copy.start()
    for step in range(ahead):
        for copy in weight_copies(step):
            copy.start()
    for copy in x_copies[counts[0] :]:
        copy.start()
    for copy in sum_copies:
        copy.wait()
    if not begun:
        accq[...] = jnp.zeros_like(accq)
        acckv[...] = jnp.zeros_like(acckv)
        squares[...] = jnp.zeros_like(squares)

    taken = 0
    for s, count in enumerate(counts):
        for copy in x_copies[taken : taken + count]:
            copy.wait()
        bufs = x_bufs[taken : taken + count]
        taken += count

        def body(j, carry, s=s, bufs=bufs):
            step = s * per + j
            for copy in weight_copies(step):
                copy.wait()
            at = pl.multiple_of(j * tile, tile)
            values = sum(buf[:, pl.ds(at, tile)].astype(jnp.float32) for buf in bufs)
            gain = gain_ref[:, pl.ds(pl.multiple_of((order[s] * per + j) * tile, tile), tile)]
            squares[...] += jnp.broadcast_to(
                jnp.sum(values * values, axis=-1, keepdims=True), squares.shape
            )
            scaled = (values * gain).astype(jnp.bfloat16)
            buffer = lax.rem(step, ahead)
            accq[...] += jnp.dot(scaled, wq_buf[buffer], preferred_element_type=jnp.float32)
            acckv[...] += jnp.dot(scaled, wkv_buf[buffer], preferred_element_type=jnp.float32)

            @pl.when(step + ahead < steps)
            def _():
                for copy in weight_copies(step + ahead):
                    copy.start()

            return carry

        lax.fori_loop(0, per, body, 0)
    if ended:
        root = lax.rsqrt(squares[:, :1] / ended + 1e-05)
        q_ref[...] = (accq[...] * root * qs_ref[...]).astype(q_ref.dtype)
        kv_ref[...] = (acckv[...] * root * kvs_ref[...]).astype(kv_ref.dtype)


def project_part(slots, order, norm_gain, w_q, kv_weight, begun, scales, held=()):
    rows, depth = slots[0][0].shape
    tile = tile_of(depth, 512)
    q_cols, kv_cols = w_q.shape[1], kv_weight.shape[1]
    arrays = [array for slot in slots for array in slot]

    def whole(shape):
        return pl.BlockSpec(shape, lambda g, order: (0,) * len(shape))

    anywhere = pl.BlockSpec(memory_space=pl.ANY)
    operands = arrays + [norm_gain.reshape(1, -1), w_q, kv_weight]
    in_specs = [anywhere] * len(arrays) + [whole((1, norm_gain.shape[0])), anywhere, anywhere]
    sums = [(rows, q_cols), (rows, kv_cols), (rows, HEAD_SIZE)]
    if begun is not None:
        operands += list(begun)
        in_specs += [anywhere] * 3
    if scales is not None:
        operands += [scale.reshape(1, -1) for scale in scales]
        in_specs += [whole((1, q_cols)), whole((1, kv_cols))]
        out_shapes = [jax.ShapeDtypeStruct(shape, jnp.bfloat16) for shape in sums[:2]]
        scratch = [pltpu.VMEM(shape, jnp.float32) for shape in sums]
    else:
        out_shapes = [jax.ShapeDtypeStruct(shape, jnp.float32) for shape in sums]
        scratch = []
    kernel = functools.partial(
        qkv_kernel,
        [len(slot) for slot in slots],
        begun is not None,
        0 if scales is None else w_q.shape[0],
        tile,
    )
    return pl.pallas_call(
        without(kernel, 1 + len(operands), len(held)),
        grid_spec=pltpu.PrefetchScalarGridSpec(
            num_scalar_prefetch=1,
            grid=(1,),
            in_specs=in_specs + [anywhere] * len(held),
            out_specs=[whole(out.shape) for out in out_shapes],
            scratch_shapes=scratch
            + [pltpu.VMEM((rows, depth), jnp.bfloat16) for _ in arrays]
            + [
                pltpu.VMEM((WEIGHT_BUFFERS, tile, q_cols), jnp.bfloat16),
                pltpu.VMEM((WEIGHT_BUFFERS, tile, kv_cols), jnp.bfloat16),
                pltpu.SemaphoreType.DMA((len(arrays),)),
                pltpu.SemaphoreType.DMA((2, WEIGHT_BUFFERS)),
                pltpu.SemaphoreType.DMA((3,)),
            ],
        ),
        out_shape=out_shapes,
        compiler_params=pltpu.CompilerParams(vmem_limit_bytes=KERNEL_VMEM),
        cost_estimate=pl.CostEstimate(
            flops=2 * rows * depth * len(slots) * (q_cols + kv_cols) // COST_SHARE,
            bytes_accessed=(2 * depth * len(slots) * (q_cols + kv_cols)) // COST_SHARE,
            transcendentals=0,
        ),
        name="norm_qkv",
    )(order, *operands, *held)


def out_kernel(count, stacked, tile, order, x_ref, w_ref, *refs):
    if stacked:
        outs, refs = [refs[0].at[s] for s in range(count)], refs[1:]
    else:
        outs, refs = refs[:count], refs[count:]
    x_buf, w_buf, x_sem, w_sem, o_sem = refs[:5]
    o_bufs = refs[5:]
    per = o_bufs[0].shape[1] // tile
    steps = count * per
    ahead = min(steps, w_buf.shape[0])

    def weight_copy(step):
        at = pl.multiple_of((order[step // per] * per + lax.rem(step, per)) * tile, tile)
        buffer = lax.rem(step, ahead)
        return pltpu.make_async_copy(
            w_ref.at[:, pl.ds(at, tile)], w_buf.at[buffer], w_sem.at[buffer]
        )

    x_copy = pltpu.make_async_copy(x_ref, x_buf, x_sem)
    x_copy.start()
    for step in range(ahead):
        weight_copy(step).start()
    x_copy.wait()
    o_copies = []
    for s, (out, o_buf) in enumerate(zip(outs, o_bufs)):

        def body(j, carry, s=s, o_buf=o_buf):
            step = s * per + j
            weight_copy(step).wait()
            o_buf[:, pl.ds(pl.multiple_of(j * tile, tile), tile)] = jnp.dot(
                x_buf[...], w_buf[lax.rem(step, ahead)], preferred_element_type=jnp.float32
            ).astype(o_buf.dtype)

            @pl.when(step + ahead < steps)
            def _():
                weight_copy(step + ahead).start()

            return carry

        lax.fori_loop(0, per, body, 0)
        o_copies.append(pltpu.make_async_copy(o_buf, out, o_sem.at[s]))
        o_copies[-1].start()
    for copy in o_copies:
        copy.wait()


def project_out(attended, w_o, order, block, stacked=False, held=()):
    rows, depth = attended.shape
    tile = tile_of(block, 512)
    count = order.shape[0]
    anywhere = pl.BlockSpec(memory_space=pl.ANY)
    return pl.pallas_call(
        without(functools.partial(out_kernel, count, stacked, tile), 3, len(held)),
        grid_spec=pltpu.PrefetchScalarGridSpec(
            num_scalar_prefetch=1,
            grid=(1,),
            in_specs=[anywhere] * (2 + len(held)),
            out_specs=anywhere if stacked else [anywhere] * count,
            scratch_shapes=[
                pltpu.VMEM((rows, depth), jnp.bfloat16),
                pltpu.VMEM((WEIGHT_BUFFERS, depth, tile), jnp.bfloat16),
                pltpu.SemaphoreType.DMA,
                pltpu.SemaphoreType.DMA((WEIGHT_BUFFERS,)),
                pltpu.SemaphoreType.DMA((count,)),
            ]
            + [pltpu.VMEM((rows, block), jnp.bfloat16)] * count,
        ),
        out_shape=jax.ShapeDtypeStruct((count, rows, block), jnp.bfloat16)
        if stacked
        else [jax.ShapeDtypeStruct((rows, block), jnp.bfloat16)] * count,
        compiler_params=pltpu.CompilerParams(vmem_limit_bytes=KERNEL_VMEM),
        cost_estimate=pl.CostEstimate(
            flops=2 * rows * depth * count * block // COST_SHARE,
            bytes_accessed=(2 * depth * count * block) // COST_SHARE,
            transcendentals=0,
        ),
        name="project_out",
    )(order, attended, w_o, *held)


def with_ones(values):
    return jnp.concatenate([values, jnp.ones_like(values)], axis=1)


def scores_of(queries, keys):
    return lax.dot_general(
        queries, keys, (((1,), (1,)), ((), ())), preferred_element_type=jnp.float32
    )


def prefill_kernel(kv_heads, group, span, first, len_ref, q_ref, cache_ref, new_ref, o_ref, *scratch):
    accs, peaks = scratch[:kv_heads], scratch[kv_heads:]
    tokens = q_ref.shape[0]
    rows = group * tokens
    live = len_ref[first + pl.program_id(0)]
    full = live // span
    query_token = lax.rem(lax.broadcasted_iota(jnp.int32, (rows, tokens), 0), tokens)
    key_token = lax.broadcasted_iota(jnp.int32, (rows, tokens), 1)
    causal = key_token <= query_token
    lane = lax.broadcasted_iota(jnp.int32, (1, span), 1)

    def queries_of(a):
        return jnp.concatenate(
            [
                q_ref[:, (a * group + h) * HEAD_SIZE : (a * group + h + 1) * HEAD_SIZE]
                for h in range(group)
            ],
            axis=0,
        )

    def columns(a, part):
        return pl.ds((2 * a + part) * HEAD_SIZE, HEAD_SIZE)

    for a in range(kv_heads):
        scores = jnp.where(causal, scores_of(queries_of(a), new_ref[:, columns(a, 0)]), MASKED)
        top = jnp.broadcast_to(jnp.max(scores, axis=-1, keepdims=True), (rows, HEAD_SIZE))
        weights = jnp.exp2(scores - top[:, :tokens]).astype(jnp.bfloat16)
        accs[a][...] = jnp.dot(
            weights, with_ones(new_ref[:, columns(a, 1)]), preferred_element_type=jnp.float32
        )
        peaks[a][...] = top

    def block(s, bias):
        at = pl.multiple_of(s * span, span)
        scores = [
            scores_of(queries_of(a), cache_ref[0, 0, pl.ds(at, span), columns(a, 0)])
            for a in range(kv_heads)
        ]
        for a in range(kv_heads):
            here = scores[a] if bias is None else scores[a] + bias
            before = peaks[a][...]
            top = jnp.maximum(before, jnp.max(here, axis=-1, keepdims=True))
            weights = jnp.exp2(
                here - jnp.concatenate([top] * (span // HEAD_SIZE), axis=1)
            ).astype(jnp.bfloat16)
            fade = jnp.exp2(before - top)
            values = cache_ref[0, 0, pl.ds(at, span), columns(a, 1)]
            accs[a][...] = accs[a][...] * jnp.concatenate([fade, fade], axis=1) + jnp.dot(
                weights, with_ones(values), preferred_element_type=jnp.float32
            )
            peaks[a][...] = top

    def step(s, carry):
        block(s, None)
        return carry

    lax.fori_loop(0, full, step, 0)

    @pl.when(full * span < live)
    def _():
        block(full, jnp.where(lane + full * span < live, 0.0, MASKED))

    for a in range(kv_heads):
        result = accs[a][:, :HEAD_SIZE] / accs[a][:, HEAD_SIZE:]
        for h in range(group):
            o_ref[:, (a * group + h) * HEAD_SIZE : (a * group + h + 1) * HEAD_SIZE] = result[
                h * tokens : (h + 1) * tokens
            ].astype(o_ref.dtype)


def prefill_attention(queries, prefix_cache, first, count, new_kv, prefix_len):
    width = queries.shape[1]
    positions, page = prefix_cache.shape[2:]
    kv_heads = page // (2 * HEAD_SIZE)
    group = width // HEAD_SIZE // kv_heads
    span = tile_of(positions, 512)
    rows = group * PROMPT_TOKENS
    return pl.pallas_call(
        functools.partial(prefill_kernel, kv_heads, group, span, first),
        grid_spec=pltpu.PrefetchScalarGridSpec(
            num_scalar_prefetch=1,
            grid=(count,),
            in_specs=[
                pl.BlockSpec((PROMPT_TOKENS, width), lambda g, n: (g, 0)),
                pl.BlockSpec((1, 1, positions, page), lambda g, n: (0, first + g, 0, 0)),
                pl.BlockSpec((PROMPT_TOKENS, page), lambda g, n: (g, 0)),
            ],
            out_specs=pl.BlockSpec((PROMPT_TOKENS, width), lambda g, n: (g, 0)),
            scratch_shapes=[pltpu.VMEM((rows, 2 * HEAD_SIZE), jnp.float32)] * kv_heads
            + [pltpu.VMEM((rows, HEAD_SIZE), jnp.float32)] * kv_heads,
        ),
        out_shape=jax.ShapeDtypeStruct((count * PROMPT_TOKENS, width), jnp.bfloat16),
        compiler_params=pltpu.CompilerParams(vmem_limit_bytes=KERNEL_VMEM),
        cost_estimate=pl.CostEstimate(
            flops=8 * count * rows * kv_heads * (positions + PROMPT_TOKENS) * HEAD_SIZE // COST_SHARE,
            bytes_accessed=(2 * count * positions * page) // COST_SHARE,
            transcendentals=count * rows * kv_heads * (positions + PROMPT_TOKENS),
        ),
        name="prefill_attention",
    )(prefix_len, queries, prefix_cache, new_kv)


def decode_kernel(
    kv_heads, batch, len_ref, row_ref, q_ref, cache_ref, landed_ref, fresh_ref, o_ref, acc, peak
):
    row_count, context = cache_ref.shape[1], cache_ref.shape[2]
    per_row = q_ref.shape[2]
    steps = fresh_ref.shape[1]
    rows = batch * per_row
    row_of = lax.broadcasted_iota(jnp.int32, (rows, batch * context), 0) // per_row
    key_row = lax.broadcasted_iota(jnp.int32, (rows, batch * context), 1) // context
    key_at = lax.rem(lax.broadcasted_iota(jnp.int32, (rows, batch * context), 1), context)
    fresh_query = lax.broadcasted_iota(jnp.int32, (rows, batch * steps), 0)
    fresh_key = lax.broadcasted_iota(jnp.int32, (rows, batch * steps), 1)
    fresh_live = (fresh_key // steps == fresh_query // per_row) & (
        lax.rem(fresh_key, steps) <= lax.rem(fresh_query, per_row) // (per_row // steps)
    )

    def cached(b, carry):
        first = b * batch
        live = jnp.zeros_like(key_row)
        for r in range(batch):
            live = jnp.where(key_row == r, len_ref[first + r], live)
        cache_live = (row_of == key_row) & (key_at < live)
        pages = cache_ref[0, pl.ds(first, batch)].reshape(batch * context, cache_ref.shape[3])
        fresh = fresh_ref[pl.ds(first, batch)].reshape(batch * steps, fresh_ref.shape[2])
        for a in range(kv_heads):
            queries = q_ref[pl.ds(first, batch), a].reshape(rows, HEAD_SIZE).astype(jnp.bfloat16)
            k_at, v_at = 2 * a * HEAD_SIZE, (2 * a + 1) * HEAD_SIZE
            scores = scores_of(queries, pages[:, k_at : k_at + HEAD_SIZE])
            scores = jnp.where(cache_live, scores, MASKED)
            recent = scores_of(queries, fresh[:, k_at : k_at + HEAD_SIZE].astype(jnp.bfloat16))
            recent = jnp.where(fresh_live, recent, MASKED)
            top = jnp.maximum(
                jnp.max(scores, axis=-1, keepdims=True), jnp.max(recent, axis=-1, keepdims=True)
            )
            weights = jnp.exp2(scores - top).astype(jnp.bfloat16)
            recent = jnp.exp2(recent - top).astype(jnp.bfloat16)
            total = jnp.dot(
                weights,
                with_ones(pages[:, v_at : v_at + HEAD_SIZE]),
                preferred_element_type=jnp.float32,
            ) + jnp.dot(
                recent,
                with_ones(fresh[:, v_at : v_at + HEAD_SIZE].astype(jnp.bfloat16)),
                preferred_element_type=jnp.float32,
            )
            acc[pl.ds(first, batch), a] = total.reshape(batch, per_row, 2 * HEAD_SIZE)
            peak[pl.ds(first, batch), a] = jnp.broadcast_to(top, (rows, HEAD_SIZE)).reshape(
                batch, per_row, HEAD_SIZE
            )
        return carry

    lax.fori_loop(0, row_count // batch, cached, 0)

    def arrival(slot, carry):
        row = row_ref[slot]

        @pl.when(row >= 0)
        def _():
            for a in range(kv_heads):
                queries = q_ref[row, a].astype(jnp.bfloat16)
                k_at, v_at = 2 * a * HEAD_SIZE, (2 * a + 1) * HEAD_SIZE
                scores = scores_of(queries, landed_ref[slot, :, k_at : k_at + HEAD_SIZE])
                before = peak[row, a]
                top = jnp.maximum(before, jnp.max(scores, axis=-1, keepdims=True))
                weights = jnp.exp2(scores - top[:, :1]).astype(jnp.bfloat16)
                fade = jnp.exp2(before - top)
                acc[row, a] = acc[row, a] * jnp.concatenate([fade, fade], axis=1) + jnp.dot(
                    weights,
                    with_ones(landed_ref[slot, :, v_at : v_at + HEAD_SIZE]),
                    preferred_element_type=jnp.float32,
                )

        return carry

    lax.fori_loop(0, row_ref.shape[0], arrival, 0)
    o_ref[...] = (acc[:, :, :, :HEAD_SIZE] / acc[:, :, :, HEAD_SIZE:]).astype(o_ref.dtype)


def decode_attention(queries, dec_cache, dec_len, landed, slot_rows, fresh, held=()):
    row_count, kv_heads, per_row = queries.shape[:3]
    context = dec_cache.shape[2]
    batch = max(1, min(row_count, 2 * HEAD_SIZE // context))
    whole = lambda array: pl.BlockSpec(array.shape, lambda g, *_: (0,) * array.ndim)
    return pl.pallas_call(
        without(functools.partial(decode_kernel, kv_heads, batch), 6, len(held)),
        grid_spec=pltpu.PrefetchScalarGridSpec(
            num_scalar_prefetch=2,
            grid=(1,),
            in_specs=[whole(queries), whole(dec_cache), whole(landed), whole(fresh)]
            + [pl.BlockSpec(memory_space=pl.ANY)] * len(held),
            out_specs=whole(queries),
            scratch_shapes=[
                pltpu.VMEM((row_count, kv_heads, per_row, 2 * HEAD_SIZE), jnp.float32),
                pltpu.VMEM((row_count, kv_heads, per_row, HEAD_SIZE), jnp.float32),
            ],
        ),
        out_shape=jax.ShapeDtypeStruct(queries.shape, jnp.float32),
        compiler_params=pltpu.CompilerParams(vmem_limit_bytes=KERNEL_VMEM),
        cost_estimate=pl.CostEstimate(
            flops=8 * queries.size * batch * context // COST_SHARE,
            bytes_accessed=(2 * dec_cache.size + 2 * landed.size) // COST_SHARE,
            transcendentals=queries.size * batch * context // HEAD_SIZE,
        ),
        name="decode_attention",
    )(dec_len, slot_rows, queries, dec_cache, landed, fresh, *held)


def shards(
    prefill_x,
    norm_gain,
    w_q,
    q_scale,
    key_value_weight,
    key_value_scale,
    w_o,
    o_scale,
    prefix_cache,
    prefix_len,
    dec_x,
    dec_cache,
    dec_len,
    place,
):
    prompts_total = prefix_cache.shape[1]
    row_count = dec_cache.shape[1]
    page_width = prefix_cache.shape[3]
    kv_heads = page_width // (2 * HEAD_SIZE)
    query_heads = w_q.shape[1] // HEAD_SIZE
    group_size = query_heads // kv_heads
    steps = dec_x.shape[0]
    section_count = lax.axis_size("section")
    section_index = lax.axis_index("section")
    tensor_count = lax.axis_size("tensor")
    tensor_index = lax.axis_index("tensor")
    head_span = max(1, 8 // query_heads)
    span_bits = head_span.bit_length() - 1
    block_width = w_o.shape[1] // tensor_count
    scales = (q_scale * EXP2_FACTOR, key_value_scale)

    weights = (norm_gain, w_q, key_value_weight)

    def kv_of_head(new_kv):
        for bit_number in range(span_bits):
            partner = partner_2(new_kv, "tensor", bit_number)
            new_kv = joined(new_kv, partner, bit_number, 1, tensor_index)
        return new_kv

    def finished(x, terms):
        total = sum(term.astype(jnp.float32) for term in terms)
        return (x.astype(jnp.float32) + total * o_scale).astype(jnp.bfloat16)

    dec_rows = dec_x.reshape(steps * row_count, -1)
    bounds = sorted({0, min(1, prompts_total - 1), prompts_total - 1, prompts_total})
    spans = list(zip(bounds[:-1], bounds[1:]))
    on_line = tensor_count == 4 and len(spans) == 3
    order = jnp.stack(
        line_order(tensor_index) if on_line else list(range(tensor_count))
    ).astype(jnp.int32)
    chunks = [prefill_x[first * PROMPT_TOKENS : last * PROMPT_TOKENS] for first, last in spans]
    blocks = chunks[:-1] + [jnp.concatenate([chunks[-1], dec_rows], axis=0)]
    pages = []

    def attention(k, queries):
        first, last = spans[k]
        return prefill_attention(queries, prefix_cache, first, last - first, pages[k], prefix_len)

    def keep(new_kv):
        new_kv = kv_of_head(new_kv)
        pages.append(new_kv[: chunks[len(pages)].shape[0]])
        return new_kv

    def back(attended, held=()):
        far, near, partner, own = project_out(
            attended, w_o, order[::-1], block_width, held=held
        )
        return LineScatter(own, partner, near, far, "tensor")

    def back_whole(attended):
        return project_out(
            attended, w_o, jnp.arange(tensor_count, dtype=jnp.int32), block_width, stacked=True
        )

    def summed(partial):
        return [lax.psum_scatter(partial, "tensor", scatter_dimension=0, tiled=False)]

    if on_line:
        first = LineGather(blocks[0], "tensor")
        first.second()
        begun = project_part(
            [[first.block], [first.partner]], order[:2], *weights, None, None, (first.middle,)
        )
        first.third(begun[2])
        second = LineGather(
            blocks[1], "tensor", (first.outer_far,), (first.outer, first.middle_far, begun[2])
        )
        queries, new_kv = project_part(first.slots()[2:], order[2:], *weights, begun, scales)
        keep(new_kv)
        attended = attention(0, queries)
        second.second(attended)
        sums = [back(attended, (second.partner, second.middle))]

        begun = project_part(
            [[second.block], [second.partner]], order[:2],
            *weights,
            None,
            None,
            (sums[0].own, second.outer),
        )
        second.third(begun[2])
        sums[0].second(begun[2])
        sums[0].third()
        third = LineGather(
            blocks[2], "tensor", (second.outer_far,), (second.outer, second.middle_far, begun[2])
        )
        queries, new_kv = project_part(
            second.slots()[2:], order[2:], *weights, begun, scales, sums[0].second_hop
        )
        keep(new_kv)
        third.second(queries)
        attended = attention(1, after(queries, third.partner, third.middle))
        third.third(attended)
        sums.append(back(attended, (third.outer, third.middle_far, *sums[0].terms[1:])))
        begun = project_part(
            [[third.block], [third.partner]],
            order[:2],
            *weights,
            None,
            None,
            (sums[1].own,),
        )
        queries, new_kv = project_part(third.slots()[2:], order[2:], *weights, begun, scales)
        new_kv = keep(new_kv)
        sums[1].second(queries)
        sums.append(back(attention(2, after(queries, *sums[1].first_hop))))
        sums[1].third(sums[2].own)
        hold = (sums[2].own,)
    else:
        terms_of = []
        for k, block in enumerate(blocks):
            whole = lax.all_gather(block, "tensor", axis=1, tiled=True)
            queries, new_kv = project_part([[whole]], order[:1], *weights, None, scales)
            new_kv = keep(new_kv)
            terms_of.append(summed(back_whole(attention(k, queries))))
        hold = ()
    tokens = chunks[-1].shape[0]
    dec_queries, fresh_kv = queries[tokens:], new_kv[tokens:]

    own_block = after(jnp.concatenate(pages, axis=0), *hold).reshape(
        prompts_total, PROMPT_TOKENS, page_width
    )
    owners = (place // row_count).reshape(section_count, prompts_total)
    targets = (place % row_count).reshape(section_count, prompts_total)
    owner_hits = (owners[:, :, None] == jnp.arange(section_count)[None, None, :]).astype(jnp.int32)
    slot_ranks = jnp.sum((jnp.cumsum(owner_hits, axis=1) - owner_hits) * owner_hits, axis=2)
    capacity = prompts_total // 2
    slot_ids = jnp.arange(capacity)
    sending = lax.dynamic_index_in_dim(owner_hits, section_index, 0, keepdims=False)
    my_ranks = lax.dynamic_index_in_dim(slot_ranks, section_index, 0, keepdims=False)
    selector = (
        jnp.transpose(sending)[:, None, :] * (my_ranks[None, None, :] == slot_ids[None, :, None])
    ).astype(jnp.bfloat16)
    here = (owners == section_index)[:, None, :] & (
        slot_ranks[:, None, :] == slot_ids[None, :, None]
    )
    slot_rows = jnp.sum(jnp.where(here, targets[:, None, :] + 1, 0), axis=2) - 1
    outgoing = jnp.einsum(
        "skp,pcw->skcw", selector, own_block, preferred_element_type=jnp.float32
    ).astype(jnp.bfloat16)
    received = lax.all_to_all(outgoing, "section", split_axis=0, concat_axis=0, tiled=True)
    if on_line:
        sums[2].second(received)
        hold = (*sums[2].first_hop, *sums[1].second_hop)
    landed = received.reshape(section_count * capacity, PROMPT_TOKENS, page_width)

    dec_queries = jnp.transpose(
        dec_queries.reshape(steps, row_count, kv_heads, group_size, HEAD_SIZE), (1, 2, 0, 3, 4)
    ).reshape(row_count, kv_heads, steps * group_size, HEAD_SIZE)
    fresh = jnp.transpose(fresh_kv.reshape(steps, row_count, page_width), (1, 0, 2))
    dec_attended = decode_attention(
        dec_queries.astype(jnp.float32),
        dec_cache,
        dec_len,
        landed,
        slot_rows.reshape(-1).astype(jnp.int32),
        fresh.astype(jnp.float32),
        hold,
    )
    dec_attended = (
        jnp.transpose(
            dec_attended.reshape(row_count, kv_heads, steps, group_size, HEAD_SIZE), (2, 0, 1, 3, 4)
        )
        .reshape(steps * row_count, -1)
        .astype(jnp.bfloat16)
    )
    if on_line:
        to = [(tensor_index + shift) % tensor_count for shift in range(tensor_count)]
        own, *parts = project_out(
            dec_attended, w_o, jnp.stack(to).astype(jnp.int32), block_width
        )
        sums[2].third(own)
        parts[-1] = after(parts[-1], *sums[1].terms[1:])
        dec_terms = [own] + [
            lax.ppermute(
                part, "tensor", [(j, (j + shift) % tensor_count) for j in range(tensor_count)]
            )
            for shift, part in enumerate(parts, 1)
        ]
        terms_of = [each.terms for each in sums]
    else:
        dec_terms = summed(back_whole(dec_attended))
    prefill_out = jnp.concatenate(
        [finished(x, terms) for x, terms in zip(chunks, terms_of)], axis=0
    )
    decode_out = finished(dec_rows, dec_terms).reshape(dec_x.shape)
    return (prefill_out, decode_out)


def solution(mesh):
    in_specs = (
        P(("groups", "section"), "tensor"),
        P(),
        P(None, "tensor"),
        P("tensor"),
        P(None, "tensor"),
        P("tensor"),
        P("tensor", None),
        P("tensor"),
        P("tensor", ("groups", "section"), None, None),
        P(("groups", "section")),
        P(None, ("groups", "section"), "tensor"),
        P("tensor", ("groups", "section"), None, None),
        P(("groups", "section")),
        P("groups"),
    )
    out_specs = (P(("groups", "section"), "tensor"), P(None, ("groups", "section"), "tensor"))
    return jax.shard_map(shards, mesh=mesh, in_specs=in_specs, out_specs=out_specs, check_vma=False)
```

```python
import functools
import math

import jax
import jax.numpy as jnp
from jax import lax
from jax.experimental import pallas as pl
from jax.experimental.pallas import tpu as pltpu
from jax.sharding import PartitionSpec as P

HEAD_SIZE = 128
PROMPT_TOKENS = 128
KERNEL_VMEM = 36 << 20
WEIGHT_BUFFERS = 8
COST_SHARE = 256
EXP2_FACTOR = math.log2(math.e) / math.sqrt(HEAD_SIZE)
MASKED = -1e30


def partner_2(block, axis, distance):
    count = lax.axis_size(axis)
    route = []
    for low in range(count):
        high = low | 1 << distance
        if high != low and high < count:
            route += [(low, high), (high, low)]
    return lax.ppermute(block, axis, route)


def joined(portion, partner, bit_number, concat_dim, tensor_index):
    upper_half = tensor_index // 2**bit_number % 2 == 1
    lower_first = jnp.concatenate([portion, partner], axis=concat_dim)
    upper_first = jnp.concatenate([partner, portion], axis=concat_dim)
    return jnp.where(upper_half, upper_first, lower_first)


def tile_of(extent, most):
    tile = extent
    while tile > most and tile % 2 == 0:
        tile //= 2
    return tile


def after(value, *others):
    return lax.optimization_barrier((value,) + others)[0]


def after_all(values, *others):
    return lax.optimization_barrier(tuple(values) + others)[: len(values)]


def line_order(index):
    low = index < 2
    return [index, index ^ 1, jnp.where(low, 2, 1), jnp.where(low, 3, 0)]


OUTER = [(0, 1), (1, 0), (2, 3), (3, 2)]
MIDDLE = [(1, 2), (2, 1)]
INWARD = [(0, 1), (3, 2)]
OUTWARD = [(1, 0), (2, 3)]


class LineGather:
    def __init__(self, block, axis, outer_held=(), middle_held=()):
        self.block, self.axis = block, axis
        self.partner = lax.ppermute(after(block, *outer_held), axis, OUTER)
        self.middle = lax.ppermute(after(block, *middle_held), axis, MIDDLE)

    def second(self, *held):
        partner, middle = after_all((self.partner, self.middle), *held)
        self.outer = lax.ppermute(middle, self.axis, OUTWARD)
        self.middle_far = lax.ppermute(partner, self.axis, MIDDLE)

    def third(self, *held):
        self.outer_far = lax.ppermute(after(self.middle_far, *held), self.axis, OUTWARD)

    def slots(self):
        return [
            [self.block],
            [self.partner],
            [self.middle, self.outer],
            [self.middle_far, self.outer_far],
        ]


def corners(arrays):
    return [array[:HEAD_SIZE, :HEAD_SIZE] for array in arrays]


def added(*terms):
    total = sum(term.astype(jnp.float32) for term in terms)
    return total.astype(terms[0].dtype)


class LineScatter:
    def __init__(self, own, partner, near, far, axis):
        self.own, self.partner, self.near, self.far = own, partner, near, far
        self.axis = axis
        self.far_in = lax.ppermute(far, axis, INWARD)

    def second(self, *held):
        far, near = after_all((added(self.far, self.far_in), self.near), *held)
        self.first_hop = (far,)
        self.near_in = lax.ppermute(near, self.axis, INWARD)
        self.far_out = lax.ppermute(far, self.axis, MIDDLE)

    def third(self, *held):
        self.third_begin()
        self.third_start(*held)

    def third_begin(self):
        self.second_hop = (
            added(self.near, self.near_in),
            added(self.partner, self.far_out),
        )

    def third_start(self, *held):
        near, partner = after_all(self.second_hop, *held)
        near = lax.ppermute(near, self.axis, MIDDLE)
        partner = lax.ppermute(partner, self.axis, OUTER)
        self.terms = [self.own, near, partner]


def in_hbm(arrays):
    return [pltpu.with_memory_space_constraint(array, pltpu.HBM) for array in arrays]


def without(kernel, first, count):
    return lambda *refs: kernel(*refs[:first], *refs[first + count :])


def qkv_kernel(counts, begun, ended, tile, order, *refs):
    refs = list(refs)
    arrays = sum(counts)
    xs = [refs.pop(0) for _ in range(arrays)]
    gain_ref, wq_ref, wkv_ref = (refs.pop(0) for _ in range(3))
    sums_in = [refs.pop(0) for _ in range(3)] if begun else []
    if ended:
        qs_ref, kvs_ref, q_ref, kv_ref, accq, acckv, squares = (refs.pop(0) for _ in range(7))
    else:
        accq, acckv, squares = (refs.pop(0) for _ in range(3))
    x_bufs = [refs.pop(0) for _ in range(arrays)]
    wq_buf, wkv_buf, x_sem, w_sem, sum_sem = refs
    per = x_bufs[0].shape[1] // tile
    steps = len(counts) * per
    ahead = min(steps, wq_buf.shape[0])

    def weight_copies(step):
        buffer = lax.rem(step, ahead)
        at = pl.multiple_of((order[step // per] * per + lax.rem(step, per)) * tile, tile)
        return [
            pltpu.make_async_copy(ref.at[pl.ds(at, tile)], buf.at[buffer], w_sem.at[w, buffer])
            for w, (ref, buf) in enumerate([(wq_ref, wq_buf), (wkv_ref, wkv_buf)])
        ]

    x_copies = [
        pltpu.make_async_copy(ref, buf, x_sem.at[a]) for a, (ref, buf) in enumerate(zip(xs, x_bufs))
    ]
    sum_copies = [
        pltpu.make_async_copy(ref, acc, sum_sem.at[a])
        for a, (ref, acc) in enumerate(zip(sums_in, (accq, acckv, squares)))
    ]
    for copy in x_copies[: counts[0]] + sum_copies:
        copy.start()
    for step in range(ahead):
        for copy in weight_copies(step):
            copy.start()
    for copy in x_copies[counts[0] :]:
        copy.start()
    for copy in sum_copies:
        copy.wait()
    if not begun:
        accq[...] = jnp.zeros_like(accq)
        acckv[...] = jnp.zeros_like(acckv)
        squares[...] = jnp.zeros_like(squares)

    taken = 0
    for s, count in enumerate(counts):
        for copy in x_copies[taken : taken + count]:
            copy.wait()
        bufs = x_bufs[taken : taken + count]
        taken += count

        def body(j, carry, s=s, bufs=bufs):
            step = s * per + j
            for copy in weight_copies(step):
                copy.wait()
            at = pl.multiple_of(j * tile, tile)
            values = sum(buf[:, pl.ds(at, tile)].astype(jnp.float32) for buf in bufs)
            gain = gain_ref[:, pl.ds(pl.multiple_of((order[s] * per + j) * tile, tile), tile)]
            squares[...] += jnp.broadcast_to(
                jnp.sum(values * values, axis=-1, keepdims=True), squares.shape
            )
            scaled = (values * gain).astype(jnp.bfloat16)
            buffer = lax.rem(step, ahead)
            accq[...] += jnp.dot(scaled, wq_buf[buffer], preferred_element_type=jnp.float32)
            acckv[...] += jnp.dot(scaled, wkv_buf[buffer], preferred_element_type=jnp.float32)

            @pl.when(step + ahead < steps)
            def _():
                for copy in weight_copies(step + ahead):
                    copy.start()

            return carry

        lax.fori_loop(0, per, body, 0)
    if ended:
        root = lax.rsqrt(squares[:, :1] / ended + 1e-05)
        q_ref[...] = (accq[...] * root * qs_ref[...]).astype(q_ref.dtype)
        kv_ref[...] = (acckv[...] * root * kvs_ref[...]).astype(kv_ref.dtype)


def project_part(slots, order, norm_gain, w_q, kv_weight, begun, scales, held=()):
    rows, depth = slots[0][0].shape
    tile = tile_of(depth, 512)
    q_cols, kv_cols = w_q.shape[1], kv_weight.shape[1]
    arrays = [array for slot in slots for array in slot]

    def whole(shape):
        return pl.BlockSpec(shape, lambda g, order: (0,) * len(shape))

    anywhere = pl.BlockSpec(memory_space=pl.ANY)
    operands = arrays + [norm_gain.reshape(1, -1)] + in_hbm([w_q, kv_weight])
    in_specs = [anywhere] * len(arrays) + [whole((1, norm_gain.shape[0])), anywhere, anywhere]
    sums = [(rows, q_cols), (rows, kv_cols), (rows, HEAD_SIZE)]
    if begun is not None:
        operands += list(begun)
        in_specs += [anywhere] * 3
    if scales is not None:
        operands += [scale.reshape(1, -1) for scale in scales]
        in_specs += [whole((1, q_cols)), whole((1, kv_cols))]
        out_shapes = [jax.ShapeDtypeStruct(shape, jnp.bfloat16) for shape in sums[:2]]
        scratch = [pltpu.VMEM(shape, jnp.float32) for shape in sums]
    else:
        out_shapes = [jax.ShapeDtypeStruct(shape, jnp.float32) for shape in sums]
        scratch = []
    kernel = functools.partial(
        qkv_kernel,
        [len(slot) for slot in slots],
        begun is not None,
        0 if scales is None else w_q.shape[0],
        tile,
    )
    return pl.pallas_call(
        without(kernel, 1 + len(operands), len(held)),
        grid_spec=pltpu.PrefetchScalarGridSpec(
            num_scalar_prefetch=1,
            grid=(1,),
            in_specs=in_specs + [anywhere] * len(held),
            out_specs=[whole(out.shape) for out in out_shapes],
            scratch_shapes=scratch
            + [pltpu.VMEM((rows, depth), jnp.bfloat16) for _ in arrays]
            + [
                pltpu.VMEM((WEIGHT_BUFFERS, tile, q_cols), jnp.bfloat16),
                pltpu.VMEM((WEIGHT_BUFFERS, tile, kv_cols), jnp.bfloat16),
                pltpu.SemaphoreType.DMA((len(arrays),)),
                pltpu.SemaphoreType.DMA((2, WEIGHT_BUFFERS)),
                pltpu.SemaphoreType.DMA((3,)),
            ],
        ),
        out_shape=out_shapes,
        compiler_params=pltpu.CompilerParams(vmem_limit_bytes=KERNEL_VMEM),
        cost_estimate=pl.CostEstimate(
            flops=2 * rows * depth * len(slots) * (q_cols + kv_cols) // COST_SHARE,
            bytes_accessed=(2 * depth * len(slots) * (q_cols + kv_cols)) // COST_SHARE,
            transcendentals=0,
        ),
        name="norm_qkv",
    )(order, *operands, *held)


def out_kernel(count, stacked, tile, order, x_ref, w_ref, *refs):
    if stacked:
        outs, refs = [refs[0].at[s] for s in range(count)], refs[1:]
    else:
        outs, refs = refs[:count], refs[count:]
    x_buf, w_buf, x_sem, w_sem, o_sem = refs[:5]
    o_bufs = refs[5:]
    per = o_bufs[0].shape[1] // tile
    steps = count * per
    ahead = min(steps, w_buf.shape[0])

    def weight_copy(step):
        at = pl.multiple_of((order[step // per] * per + lax.rem(step, per)) * tile, tile)
        buffer = lax.rem(step, ahead)
        return pltpu.make_async_copy(
            w_ref.at[:, pl.ds(at, tile)], w_buf.at[buffer], w_sem.at[buffer]
        )

    x_copy = pltpu.make_async_copy(x_ref, x_buf, x_sem)
    x_copy.start()
    for step in range(ahead):
        weight_copy(step).start()
    x_copy.wait()
    o_copies = []
    for s, (out, o_buf) in enumerate(zip(outs, o_bufs)):

        def body(j, carry, s=s, o_buf=o_buf):
            step = s * per + j
            weight_copy(step).wait()
            o_buf[:, pl.ds(pl.multiple_of(j * tile, tile), tile)] = jnp.dot(
                x_buf[...], w_buf[lax.rem(step, ahead)], preferred_element_type=jnp.float32
            ).astype(o_buf.dtype)

            @pl.when(step + ahead < steps)
            def _():
                weight_copy(step + ahead).start()

            return carry

        lax.fori_loop(0, per, body, 0)
        o_copies.append(pltpu.make_async_copy(o_buf, out, o_sem.at[s]))
        o_copies[-1].start()
    for copy in o_copies:
        copy.wait()


def project_out(attended, w_o, order, block, stacked=False, held=()):
    rows, depth = attended.shape
    tile = tile_of(block, 512)
    count = order.shape[0]
    anywhere = pl.BlockSpec(memory_space=pl.ANY)
    return pl.pallas_call(
        without(functools.partial(out_kernel, count, stacked, tile), 3, len(held)),
        grid_spec=pltpu.PrefetchScalarGridSpec(
            num_scalar_prefetch=1,
            grid=(1,),
            in_specs=[anywhere] * (2 + len(held)),
            out_specs=anywhere if stacked else [anywhere] * count,
            scratch_shapes=[
                pltpu.VMEM((rows, depth), jnp.bfloat16),
                pltpu.VMEM((WEIGHT_BUFFERS, depth, tile), jnp.bfloat16),
                pltpu.SemaphoreType.DMA,
                pltpu.SemaphoreType.DMA((WEIGHT_BUFFERS,)),
                pltpu.SemaphoreType.DMA((count,)),
            ]
            + [pltpu.VMEM((rows, block), jnp.bfloat16)] * count,
        ),
        out_shape=jax.ShapeDtypeStruct((count, rows, block), jnp.bfloat16)
        if stacked
        else [jax.ShapeDtypeStruct((rows, block), jnp.bfloat16)] * count,
        compiler_params=pltpu.CompilerParams(vmem_limit_bytes=KERNEL_VMEM),
        cost_estimate=pl.CostEstimate(
            flops=2 * rows * depth * count * block // COST_SHARE,
            bytes_accessed=(2 * depth * count * block) // COST_SHARE,
            transcendentals=0,
        ),
        name="project_out",
    )(order, attended, *in_hbm([w_o]), *held)


def with_ones(values):
    return jnp.concatenate([values, jnp.ones_like(values)], axis=1)


def scores_of(queries, keys):
    return lax.dot_general(
        queries, keys, (((1,), (1,)), ((), ())), preferred_element_type=jnp.float32
    )


def prefill_kernel(
    kv_heads, group, span, first, len_ref, q_ref, cache_ref, new_ref, o_ref, cache_buf, sem, *scratch
):
    accs, peaks = scratch[:kv_heads], scratch[kv_heads:]
    prompt = pl.program_id(0)

    def cache_copy(g):
        return pltpu.make_async_copy(cache_ref.at[0, first + g], cache_buf.at[g], sem.at[g])

    @pl.when(prompt == 0)
    def _():
        for g in range(cache_buf.shape[0]):
            cache_copy(g).start()

    tokens = q_ref.shape[0]
    rows = group * tokens
    live = len_ref[first + prompt]
    full = live // span
    query_token = lax.rem(lax.broadcasted_iota(jnp.int32, (rows, tokens), 0), tokens)
    key_token = lax.broadcasted_iota(jnp.int32, (rows, tokens), 1)
    causal = key_token <= query_token
    lane = lax.broadcasted_iota(jnp.int32, (1, span), 1)

    def queries_of(a):
        return jnp.concatenate(
            [
                q_ref[:, (a * group + h) * HEAD_SIZE : (a * group + h + 1) * HEAD_SIZE]
                for h in range(group)
            ],
            axis=0,
        )

    def columns(a, part):
        return pl.ds((2 * a + part) * HEAD_SIZE, HEAD_SIZE)

    for a in range(kv_heads):
        scores = jnp.where(causal, scores_of(queries_of(a), new_ref[:, columns(a, 0)]), MASKED)
        top = jnp.broadcast_to(jnp.max(scores, axis=-1, keepdims=True), (rows, HEAD_SIZE))
        weights = jnp.exp2(scores - top[:, :tokens]).astype(jnp.bfloat16)
        accs[a][...] = jnp.dot(
            weights, with_ones(new_ref[:, columns(a, 1)]), preferred_element_type=jnp.float32
        )
        peaks[a][...] = top

    cache_copy(prompt).wait()

    def block(s, bias):
        at = pl.multiple_of(s * span, span)
        scores = [
            scores_of(queries_of(a), cache_buf[prompt, pl.ds(at, span), columns(a, 0)])
            for a in range(kv_heads)
        ]
        for a in range(kv_heads):
            here = scores[a] if bias is None else scores[a] + bias
            before = peaks[a][...]
            top = jnp.maximum(before, jnp.max(here, axis=-1, keepdims=True))
            weights = jnp.exp2(
                here - jnp.concatenate([top] * (span // HEAD_SIZE), axis=1)
            ).astype(jnp.bfloat16)
            fade = jnp.exp2(before - top)
            values = cache_buf[prompt, pl.ds(at, span), columns(a, 1)]
            accs[a][...] = accs[a][...] * jnp.concatenate([fade, fade], axis=1) + jnp.dot(
                weights, with_ones(values), preferred_element_type=jnp.float32
            )
            peaks[a][...] = top

    def step(s, carry):
        block(s, None)
        return carry

    lax.fori_loop(0, full, step, 0)

    @pl.when(full * span < live)
    def _():
        block(full, jnp.where(lane + full * span < live, 0.0, MASKED))

    for a in range(kv_heads):
        result = accs[a][:, :HEAD_SIZE] / accs[a][:, HEAD_SIZE:]
        for h in range(group):
            o_ref[:, (a * group + h) * HEAD_SIZE : (a * group + h + 1) * HEAD_SIZE] = result[
                h * tokens : (h + 1) * tokens
            ].astype(o_ref.dtype)


def prefill_attention(queries, prefix_cache, first, count, new_kv, prefix_len):
    width = queries.shape[1]
    positions, page = prefix_cache.shape[2:]
    kv_heads = page // (2 * HEAD_SIZE)
    group = width // HEAD_SIZE // kv_heads
    span = tile_of(positions, 512)
    rows = group * PROMPT_TOKENS
    return pl.pallas_call(
        functools.partial(prefill_kernel, kv_heads, group, span, first),
        grid_spec=pltpu.PrefetchScalarGridSpec(
            num_scalar_prefetch=1,
            grid=(count,),
            in_specs=[
                pl.BlockSpec((PROMPT_TOKENS, width), lambda g, n: (g, 0)),
                pl.BlockSpec(memory_space=pl.ANY),
                pl.BlockSpec((PROMPT_TOKENS, page), lambda g, n: (g, 0)),
            ],
            out_specs=pl.BlockSpec((PROMPT_TOKENS, width), lambda g, n: (g, 0)),
            scratch_shapes=[
                pltpu.VMEM((count, positions, page), jnp.bfloat16),
                pltpu.SemaphoreType.DMA((count,)),
            ]
            + [pltpu.VMEM((rows, 2 * HEAD_SIZE), jnp.float32)] * kv_heads
            + [pltpu.VMEM((rows, HEAD_SIZE), jnp.float32)] * kv_heads,
        ),
        out_shape=jax.ShapeDtypeStruct((count * PROMPT_TOKENS, width), jnp.bfloat16),
        compiler_params=pltpu.CompilerParams(vmem_limit_bytes=KERNEL_VMEM),
        cost_estimate=pl.CostEstimate(
            flops=8 * count * rows * kv_heads * (positions + PROMPT_TOKENS) * HEAD_SIZE // COST_SHARE,
            bytes_accessed=(2 * count * positions * page) // COST_SHARE,
            transcendentals=count * rows * kv_heads * (positions + PROMPT_TOKENS),
        ),
        name="prefill_attention",
    )(prefix_len, queries, *in_hbm([prefix_cache]), new_kv)


def decode_kernel(
    kv_heads, batch, len_ref, row_ref, q_ref, cache_ref, landed_ref, fresh_ref, o_ref, acc, peak
):
    row_count, context = cache_ref.shape[1], cache_ref.shape[2]
    per_row = q_ref.shape[2]
    steps = fresh_ref.shape[1]
    rows = batch * per_row
    row_of = lax.broadcasted_iota(jnp.int32, (rows, batch * context), 0) // per_row
    key_row = lax.broadcasted_iota(jnp.int32, (rows, batch * context), 1) // context
    key_at = lax.rem(lax.broadcasted_iota(jnp.int32, (rows, batch * context), 1), context)
    fresh_query = lax.broadcasted_iota(jnp.int32, (rows, batch * steps), 0)
    fresh_key = lax.broadcasted_iota(jnp.int32, (rows, batch * steps), 1)
    fresh_live = (fresh_key // steps == fresh_query // per_row) & (
        lax.rem(fresh_key, steps) <= lax.rem(fresh_query, per_row) // (per_row // steps)
    )

    def cached(b, carry):
        first = b * batch
        live = jnp.zeros_like(key_row)
        for r in range(batch):
            live = jnp.where(key_row == r, len_ref[first + r], live)
        cache_live = (row_of == key_row) & (key_at < live)
        pages = cache_ref[0, pl.ds(first, batch)].reshape(batch * context, cache_ref.shape[3])
        fresh = fresh_ref[pl.ds(first, batch)].reshape(batch * steps, fresh_ref.shape[2])
        for a in range(kv_heads):
            queries = q_ref[pl.ds(first, batch), a].reshape(rows, HEAD_SIZE).astype(jnp.bfloat16)
            k_at, v_at = 2 * a * HEAD_SIZE, (2 * a + 1) * HEAD_SIZE
            scores = scores_of(queries, pages[:, k_at : k_at + HEAD_SIZE])
            scores = jnp.where(cache_live, scores, MASKED)
            recent = scores_of(queries, fresh[:, k_at : k_at + HEAD_SIZE].astype(jnp.bfloat16))
            recent = jnp.where(fresh_live, recent, MASKED)
            top = jnp.maximum(
                jnp.max(scores, axis=-1, keepdims=True), jnp.max(recent, axis=-1, keepdims=True)
            )
            weights = jnp.exp2(scores - top).astype(jnp.bfloat16)
            recent = jnp.exp2(recent - top).astype(jnp.bfloat16)
            total = jnp.dot(
                weights,
                with_ones(pages[:, v_at : v_at + HEAD_SIZE]),
                preferred_element_type=jnp.float32,
            ) + jnp.dot(
                recent,
                with_ones(fresh[:, v_at : v_at + HEAD_SIZE].astype(jnp.bfloat16)),
                preferred_element_type=jnp.float32,
            )
            acc[pl.ds(first, batch), a] = total.reshape(batch, per_row, 2 * HEAD_SIZE)
            peak[pl.ds(first, batch), a] = jnp.broadcast_to(top, (rows, HEAD_SIZE)).reshape(
                batch, per_row, HEAD_SIZE
            )
        return carry

    lax.fori_loop(0, row_count // batch, cached, 0)

    def arrival(slot, carry):
        row = row_ref[slot]

        @pl.when(row >= 0)
        def _():
            for a in range(kv_heads):
                queries = q_ref[row, a].astype(jnp.bfloat16)
                k_at, v_at = 2 * a * HEAD_SIZE, (2 * a + 1) * HEAD_SIZE
                scores = scores_of(queries, landed_ref[slot, :, k_at : k_at + HEAD_SIZE])
                before = peak[row, a]
                top = jnp.maximum(before, jnp.max(scores, axis=-1, keepdims=True))
                weights = jnp.exp2(scores - top[:, :1]).astype(jnp.bfloat16)
                fade = jnp.exp2(before - top)
                acc[row, a] = acc[row, a] * jnp.concatenate([fade, fade], axis=1) + jnp.dot(
                    weights,
                    with_ones(landed_ref[slot, :, v_at : v_at + HEAD_SIZE]),
                    preferred_element_type=jnp.float32,
                )

        return carry

    lax.fori_loop(0, row_ref.shape[0], arrival, 0)
    o_ref[...] = (acc[:, :, :, :HEAD_SIZE] / acc[:, :, :, HEAD_SIZE:]).astype(o_ref.dtype)


def decode_attention(queries, dec_cache, dec_len, landed, slot_rows, fresh, held=()):
    row_count, kv_heads, per_row = queries.shape[:3]
    context = dec_cache.shape[2]
    batch = max(1, min(row_count, 2 * HEAD_SIZE // context))
    whole = lambda array: pl.BlockSpec(array.shape, lambda g, *_: (0,) * array.ndim)
    return pl.pallas_call(
        without(functools.partial(decode_kernel, kv_heads, batch), 6, len(held)),
        grid_spec=pltpu.PrefetchScalarGridSpec(
            num_scalar_prefetch=2,
            grid=(1,),
            in_specs=[whole(queries), whole(dec_cache), whole(landed), whole(fresh)]
            + [pl.BlockSpec(memory_space=pl.ANY)] * len(held),
            out_specs=whole(queries),
            scratch_shapes=[
                pltpu.VMEM((row_count, kv_heads, per_row, 2 * HEAD_SIZE), jnp.float32),
                pltpu.VMEM((row_count, kv_heads, per_row, HEAD_SIZE), jnp.float32),
            ],
        ),
        out_shape=jax.ShapeDtypeStruct(queries.shape, jnp.float32),
        compiler_params=pltpu.CompilerParams(vmem_limit_bytes=KERNEL_VMEM),
        cost_estimate=pl.CostEstimate(
            flops=8 * queries.size * batch * context // COST_SHARE,
            bytes_accessed=(2 * dec_cache.size + 2 * landed.size) // COST_SHARE,
            transcendentals=queries.size * batch * context // HEAD_SIZE,
        ),
        name="decode_attention",
    )(dec_len, slot_rows, queries, dec_cache, landed, fresh, *held)


def shards(
    prefill_x,
    norm_gain,
    w_q,
    q_scale,
    key_value_weight,
    key_value_scale,
    w_o,
    o_scale,
    prefix_cache,
    prefix_len,
    dec_x,
    dec_cache,
    dec_len,
    place,
):
    prompts_total = prefix_cache.shape[1]
    row_count = dec_cache.shape[1]
    page_width = prefix_cache.shape[3]
    kv_heads = page_width // (2 * HEAD_SIZE)
    query_heads = w_q.shape[1] // HEAD_SIZE
    group_size = query_heads // kv_heads
    steps = dec_x.shape[0]
    section_count = lax.axis_size("section")
    section_index = lax.axis_index("section")
    tensor_count = lax.axis_size("tensor")
    tensor_index = lax.axis_index("tensor")
    head_span = max(1, 8 // query_heads)
    span_bits = head_span.bit_length() - 1
    block_width = w_o.shape[1] // tensor_count
    scales = (q_scale * EXP2_FACTOR, key_value_scale)

    weights = (norm_gain, w_q, key_value_weight)

    def kv_of_head(new_kv):
        for bit_number in range(span_bits):
            partner = partner_2(new_kv, "tensor", bit_number)
            new_kv = joined(new_kv, partner, bit_number, 1, tensor_index)
        return new_kv

    def finished(x, terms):
        total = sum(term.astype(jnp.float32) for term in terms)
        return (x.astype(jnp.float32) + total * o_scale).astype(jnp.bfloat16)

    dec_rows = dec_x.reshape(steps * row_count, -1)
    bounds = sorted({0, min(1, prompts_total - 1), prompts_total - 1, prompts_total})
    spans = list(zip(bounds[:-1], bounds[1:]))
    on_line = tensor_count == 4 and len(spans) == 3
    order = jnp.stack(
        line_order(tensor_index) if on_line else list(range(tensor_count))
    ).astype(jnp.int32)
    chunks = [prefill_x[first * PROMPT_TOKENS : last * PROMPT_TOKENS] for first, last in spans]
    blocks = chunks[:-1] + [jnp.concatenate([chunks[-1], dec_rows], axis=0)]
    pages = []

    def attention(k, queries):
        first, last = spans[k]
        return prefill_attention(queries, prefix_cache, first, last - first, pages[k], prefix_len)

    def keep(new_kv):
        new_kv = kv_of_head(new_kv)
        pages.append(new_kv[: chunks[len(pages)].shape[0]])
        return new_kv

    def back(attended, held=()):
        far, near, partner, own = project_out(
            attended, w_o, order[::-1], block_width, held=held
        )
        return LineScatter(own, partner, near, far, "tensor")

    def back_whole(attended):
        return project_out(
            attended, w_o, jnp.arange(tensor_count, dtype=jnp.int32), block_width, stacked=True
        )

    def summed(partial):
        return [lax.psum_scatter(partial, "tensor", scatter_dimension=0, tiled=False)]

    if on_line:
        first = LineGather(blocks[0], "tensor")
        first.second()
        begun = project_part(
            [[first.block], [first.partner]], order[:2], *weights, None, None, (first.middle,)
        )
        first.third(begun[2])
        second = LineGather(
            blocks[1], "tensor", (first.outer_far,), (first.outer, first.middle_far, begun[2])
        )
        queries, new_kv = project_part(first.slots()[2:], order[2:], *weights, begun, scales)
        keep(new_kv)
        attended = attention(0, queries)
        second.second(attended)
        sums = [back(attended, (second.partner, second.middle))]

        begun = project_part(
            [[second.block], [second.partner]], order[:2],
            *weights,
            None,
            None,
            (sums[0].own, second.outer),
        )
        second.third(begun[2])
        sums[0].second(begun[2])
        sums[0].third()
        third = LineGather(
            blocks[2], "tensor", (second.outer_far,), (second.outer, second.middle_far, begun[2])
        )
        queries, new_kv = project_part(
            second.slots()[2:], order[2:], *weights, begun, scales, sums[0].second_hop
        )
        keep(new_kv)
        third.second(queries)
        attended = attention(1, after(queries, third.partner, third.middle))
        third.third(attended)
        sums.append(back(attended, (third.outer, third.middle_far)))
        begun = project_part(
            [[third.block], [third.partner]],
            order[:2],
            *weights,
            None,
            None,
            (sums[1].own, *corners(sums[0].terms[1:])),
        )
        queries, new_kv = project_part(third.slots()[2:], order[2:], *weights, begun, scales)
        new_kv = keep(new_kv)
        sums[1].second(queries)
        sums[1].third_begin()
        sums.append(back(attention(2, after(queries, *sums[1].first_hop)), sums[1].second_hop))
        sums[1].third_start(sums[2].own)
        hold = (sums[2].own,)
    else:
        terms_of = []
        for k, block in enumerate(blocks):
            whole = lax.all_gather(block, "tensor", axis=1, tiled=True)
            queries, new_kv = project_part([[whole]], order[:1], *weights, None, scales)
            new_kv = keep(new_kv)
            terms_of.append(summed(back_whole(attention(k, queries))))
        hold = ()
    tokens = chunks[-1].shape[0]
    dec_queries, fresh_kv = queries[tokens:], new_kv[tokens:]

    own_block = after(jnp.concatenate(pages, axis=0), *hold).reshape(
        prompts_total, PROMPT_TOKENS, page_width
    )
    owners = (place // row_count).reshape(section_count, prompts_total)
    targets = (place % row_count).reshape(section_count, prompts_total)
    owner_hits = (owners[:, :, None] == jnp.arange(section_count)[None, None, :]).astype(jnp.int32)
    slot_ranks = jnp.sum((jnp.cumsum(owner_hits, axis=1) - owner_hits) * owner_hits, axis=2)
    capacity = prompts_total // 2
    slot_ids = jnp.arange(capacity)
    sending = lax.dynamic_index_in_dim(owner_hits, section_index, 0, keepdims=False)
    my_ranks = lax.dynamic_index_in_dim(slot_ranks, section_index, 0, keepdims=False)
    selector = (
        jnp.transpose(sending)[:, None, :] * (my_ranks[None, None, :] == slot_ids[None, :, None])
    ).astype(jnp.bfloat16)
    here = (owners == section_index)[:, None, :] & (
        slot_ranks[:, None, :] == slot_ids[None, :, None]
    )
    slot_rows = jnp.sum(jnp.where(here, targets[:, None, :] + 1, 0), axis=2) - 1
    outgoing = jnp.einsum(
        "skp,pcw->skcw", selector, own_block, preferred_element_type=jnp.float32
    ).astype(jnp.bfloat16)
    received = lax.all_to_all(outgoing, "section", split_axis=0, concat_axis=0, tiled=True)
    if on_line:
        sums[2].second(received)
        hold = (
            *sums[2].first_hop,
            *corners(sums[1].terms[1:]),
        )
    landed = received.reshape(section_count * capacity, PROMPT_TOKENS, page_width)

    dec_queries = jnp.transpose(
        dec_queries.reshape(steps, row_count, kv_heads, group_size, HEAD_SIZE), (1, 2, 0, 3, 4)
    ).reshape(row_count, kv_heads, steps * group_size, HEAD_SIZE)
    fresh = jnp.transpose(fresh_kv.reshape(steps, row_count, page_width), (1, 0, 2))
    dec_attended = decode_attention(
        dec_queries.astype(jnp.float32),
        dec_cache,
        dec_len,
        landed,
        slot_rows.reshape(-1).astype(jnp.int32),
        fresh.astype(jnp.float32),
        hold,
    )
    dec_attended = (
        jnp.transpose(
            dec_attended.reshape(row_count, kv_heads, steps, group_size, HEAD_SIZE), (2, 0, 1, 3, 4)
        )
        .reshape(steps * row_count, -1)
        .astype(jnp.bfloat16)
    )
    if on_line:
        to = [(tensor_index + shift) % tensor_count for shift in range(tensor_count)]
        sums[2].third(dec_attended)
        own, *parts = project_out(
            dec_attended,
            w_o,
            jnp.stack(to).astype(jnp.int32),
            block_width,
            held=sums[2].second_hop,
        )
        dec_terms = [own] + [
            lax.ppermute(
                part, "tensor", [(j, (j + shift) % tensor_count) for j in range(tensor_count)]
            )
            for shift, part in enumerate(parts, 1)
        ]
        terms_of = [each.terms for each in sums]
    else:
        dec_terms = summed(back_whole(dec_attended))
    prefill_out = jnp.concatenate(
        [finished(x, terms) for x, terms in zip(chunks, terms_of)], axis=0
    )
    decode_out = finished(dec_rows, dec_terms).reshape(dec_x.shape)
    return (prefill_out, decode_out)


def solution(mesh):
    in_specs = (
        P(("groups", "section"), "tensor"),
        P(),
        P(None, "tensor"),
        P("tensor"),
        P(None, "tensor"),
        P("tensor"),
        P("tensor", None),
        P("tensor"),
        P("tensor", ("groups", "section"), None, None),
        P(("groups", "section")),
        P(None, ("groups", "section"), "tensor"),
        P("tensor", ("groups", "section"), None, None),
        P(("groups", "section")),
        P("groups"),
    )
    out_specs = (P(("groups", "section"), "tensor"), P(None, ("groups", "section"), "tensor"))
    return jax.shard_map(shards, mesh=mesh, in_specs=in_specs, out_specs=out_specs, check_vma=False)
```

```python
import functools
import math

import jax
import jax.numpy as jnp
from jax import lax
from jax.experimental import pallas as pl
from jax.experimental.pallas import tpu as pltpu
from jax.sharding import PartitionSpec as P

HEAD_SIZE = 128
PROMPT_TOKENS = 128
KERNEL_VMEM = 36 << 20
WEIGHT_BUFFERS = 8
COST_SHARE = 256
EXP2_FACTOR = math.log2(math.e) / math.sqrt(HEAD_SIZE)
MASKED = -1e30


def partner_2(block, axis, distance):
    count = lax.axis_size(axis)
    route = []
    for low in range(count):
        high = low | 1 << distance
        if high != low and high < count:
            route += [(low, high), (high, low)]
    return lax.ppermute(block, axis, route)


def joined(portion, partner, bit_number, concat_dim, tensor_index):
    upper_half = tensor_index // 2**bit_number % 2 == 1
    lower_first = jnp.concatenate([portion, partner], axis=concat_dim)
    upper_first = jnp.concatenate([partner, portion], axis=concat_dim)
    return jnp.where(upper_half, upper_first, lower_first)


def tile_of(extent, most):
    tile = extent
    while tile > most and tile % 2 == 0:
        tile //= 2
    return tile


def after(value, *others):
    return lax.optimization_barrier((value,) + others)[0]


def after_all(values, *others):
    return lax.optimization_barrier(tuple(values) + others)[: len(values)]


def line_order(index):
    low = index < 2
    return [index, index ^ 1, jnp.where(low, 2, 1), jnp.where(low, 3, 0)]


OUTER = [(0, 1), (1, 0), (2, 3), (3, 2)]
MIDDLE = [(1, 2), (2, 1)]
INWARD = [(0, 1), (3, 2)]
OUTWARD = [(1, 0), (2, 3)]


class LineGather:
    def __init__(self, block, axis, outer_held=(), middle_held=()):
        self.block, self.axis = block, axis
        self.partner = lax.ppermute(after(block, *outer_held), axis, OUTER)
        self.middle = lax.ppermute(after(block, *middle_held), axis, MIDDLE)

    def second(self, *held):
        partner, middle = after_all((self.partner, self.middle), *held)
        self.outer = lax.ppermute(middle, self.axis, OUTWARD)
        self.middle_far = lax.ppermute(partner, self.axis, MIDDLE)

    def third(self, *held):
        self.outer_far = lax.ppermute(after(self.middle_far, *held), self.axis, OUTWARD)

    def slots(self):
        return [
            [self.block],
            [self.partner],
            [self.middle, self.outer],
            [self.middle_far, self.outer_far],
        ]


def corners(arrays):
    return [array[:HEAD_SIZE, :HEAD_SIZE] for array in arrays]


def added(*terms):
    total = sum(term.astype(jnp.float32) for term in terms)
    return total.astype(terms[0].dtype)


class LineScatter:
    def __init__(self, own, partner, near, far, axis):
        self.own, self.partner, self.near, self.far = own, partner, near, far
        self.axis = axis
        self.far_in = lax.ppermute(far, axis, INWARD)

    def second(self, *held):
        far, near = after_all((added(self.far, self.far_in), self.near), *held)
        self.first_hop = (far,)
        self.near_in = lax.ppermute(near, self.axis, INWARD)
        self.far_out = lax.ppermute(far, self.axis, MIDDLE)

    def third(self, *held):
        self.third_begin()
        self.third_start(*held)

    def third_begin(self):
        self.second_hop = (
            added(self.near, self.near_in),
            added(self.partner, self.far_out),
        )

    def third_start(self, *held):
        near, partner = after_all(self.second_hop, *held)
        near = lax.ppermute(near, self.axis, MIDDLE)
        partner = lax.ppermute(partner, self.axis, OUTER)
        self.terms = [self.own, near, partner]


def in_hbm(arrays):
    return [pltpu.with_memory_space_constraint(array, pltpu.HBM) for array in arrays]


def without(kernel, first, count):
    return lambda *refs: kernel(*refs[:first], *refs[first + count :])


def qkv_kernel(counts, begun, ended, tile, order, *refs):
    refs = list(refs)
    arrays = sum(counts)
    xs = [refs.pop(0) for _ in range(arrays)]
    gain_ref, wq_ref, wkv_ref = (refs.pop(0) for _ in range(3))
    sums_in = [refs.pop(0) for _ in range(3)] if begun else []
    if ended:
        qs_ref, kvs_ref, q_ref, kv_ref, accq, acckv, squares = (refs.pop(0) for _ in range(7))
    else:
        accq, acckv, squares = (refs.pop(0) for _ in range(3))
    x_bufs = [refs.pop(0) for _ in range(arrays)]
    wq_buf, wkv_buf, x_sem, w_sem, sum_sem = refs
    per = x_bufs[0].shape[1] // tile
    steps = len(counts) * per
    ahead = min(steps, wq_buf.shape[0])

    def weight_copies(step):
        buffer = lax.rem(step, ahead)
        at = pl.multiple_of((order[step // per] * per + lax.rem(step, per)) * tile, tile)
        return [
            pltpu.make_async_copy(ref.at[pl.ds(at, tile)], buf.at[buffer], w_sem.at[w, buffer])
            for w, (ref, buf) in enumerate([(wq_ref, wq_buf), (wkv_ref, wkv_buf)])
        ]

    x_copies = [
        pltpu.make_async_copy(ref, buf, x_sem.at[a]) for a, (ref, buf) in enumerate(zip(xs, x_bufs))
    ]
    sum_copies = [
        pltpu.make_async_copy(ref, acc, sum_sem.at[a])
        for a, (ref, acc) in enumerate(zip(sums_in, (accq, acckv, squares)))
    ]
    for copy in x_copies[: counts[0]] + sum_copies:
        copy.start()
    for step in range(ahead):
        for copy in weight_copies(step):
            copy.start()
    for copy in x_copies[counts[0] :]:
        copy.start()
    for copy in sum_copies:
        copy.wait()
    if not begun:
        accq[...] = jnp.zeros_like(accq)
        acckv[...] = jnp.zeros_like(acckv)
        squares[...] = jnp.zeros_like(squares)

    taken = 0
    for s, count in enumerate(counts):
        for copy in x_copies[taken : taken + count]:
            copy.wait()
        bufs = x_bufs[taken : taken + count]
        taken += count

        def body(j, carry, s=s, bufs=bufs):
            step = s * per + j
            for copy in weight_copies(step):
                copy.wait()
            at = pl.multiple_of(j * tile, tile)
            values = sum(buf[:, pl.ds(at, tile)].astype(jnp.float32) for buf in bufs)
            gain = gain_ref[:, pl.ds(pl.multiple_of((order[s] * per + j) * tile, tile), tile)]
            squares[...] += jnp.broadcast_to(
                jnp.sum(values * values, axis=-1, keepdims=True), squares.shape
            )
            scaled = (values * gain).astype(jnp.bfloat16)
            buffer = lax.rem(step, ahead)
            accq[...] += jnp.dot(scaled, wq_buf[buffer], preferred_element_type=jnp.float32)
            acckv[...] += jnp.dot(scaled, wkv_buf[buffer], preferred_element_type=jnp.float32)

            @pl.when(step + ahead < steps)
            def _():
                for copy in weight_copies(step + ahead):
                    copy.start()

            return carry

        lax.fori_loop(0, per, body, 0)
    if ended:
        root = lax.rsqrt(squares[:, :1] / ended + 1e-05)
        q_ref[...] = (accq[...] * root * qs_ref[...]).astype(q_ref.dtype)
        kv_ref[...] = (acckv[...] * root * kvs_ref[...]).astype(kv_ref.dtype)


def project_part(slots, order, norm_gain, w_q, kv_weight, begun, scales, held=()):
    rows, depth = slots[0][0].shape
    tile = tile_of(depth, 512)
    q_cols, kv_cols = w_q.shape[1], kv_weight.shape[1]
    arrays = [array for slot in slots for array in slot]

    def whole(shape):
        return pl.BlockSpec(shape, lambda g, order: (0,) * len(shape))

    anywhere = pl.BlockSpec(memory_space=pl.ANY)
    operands = arrays + [norm_gain.reshape(1, -1)] + in_hbm([w_q, kv_weight])
    in_specs = [anywhere] * len(arrays) + [whole((1, norm_gain.shape[0])), anywhere, anywhere]
    sums = [(rows, q_cols), (rows, kv_cols), (rows, HEAD_SIZE)]
    if begun is not None:
        operands += list(begun)
        in_specs += [anywhere] * 3
    if scales is not None:
        operands += [scale.reshape(1, -1) for scale in scales]
        in_specs += [whole((1, q_cols)), whole((1, kv_cols))]
        out_shapes = [jax.ShapeDtypeStruct(shape, jnp.bfloat16) for shape in sums[:2]]
        scratch = [pltpu.VMEM(shape, jnp.float32) for shape in sums]
    else:
        out_shapes = [jax.ShapeDtypeStruct(shape, jnp.float32) for shape in sums]
        scratch = []
    kernel = functools.partial(
        qkv_kernel,
        [len(slot) for slot in slots],
        begun is not None,
        0 if scales is None else w_q.shape[0],
        tile,
    )
    return pl.pallas_call(
        without(kernel, 1 + len(operands), len(held)),
        grid_spec=pltpu.PrefetchScalarGridSpec(
            num_scalar_prefetch=1,
            grid=(1,),
            in_specs=in_specs + [anywhere] * len(held),
            out_specs=[whole(out.shape) for out in out_shapes],
            scratch_shapes=scratch
            + [pltpu.VMEM((rows, depth), jnp.bfloat16) for _ in arrays]
            + [
                pltpu.VMEM((WEIGHT_BUFFERS, tile, q_cols), jnp.bfloat16),
                pltpu.VMEM((WEIGHT_BUFFERS, tile, kv_cols), jnp.bfloat16),
                pltpu.SemaphoreType.DMA((len(arrays),)),
                pltpu.SemaphoreType.DMA((2, WEIGHT_BUFFERS)),
                pltpu.SemaphoreType.DMA((3,)),
            ],
        ),
        out_shape=out_shapes,
        compiler_params=pltpu.CompilerParams(vmem_limit_bytes=KERNEL_VMEM),
        cost_estimate=pl.CostEstimate(
            flops=2 * rows * depth * len(slots) * (q_cols + kv_cols) // COST_SHARE,
            bytes_accessed=(2 * depth * len(slots) * (q_cols + kv_cols)) // COST_SHARE,
            transcendentals=0,
        ),
        name="norm_qkv",
    )(order, *operands, *held)


def out_kernel(count, stacked, tile, order, x_ref, w_ref, *refs):
    if stacked:
        outs, refs = [refs[0].at[s] for s in range(count)], refs[1:]
    else:
        outs, refs = refs[:count], refs[count:]
    x_buf, w_buf, x_sem, w_sem, o_sem = refs[:5]
    o_bufs = refs[5:]
    per = o_bufs[0].shape[1] // tile
    steps = count * per
    ahead = min(steps, w_buf.shape[0])

    def weight_copy(step):
        at = pl.multiple_of((order[step // per] * per + lax.rem(step, per)) * tile, tile)
        buffer = lax.rem(step, ahead)
        return pltpu.make_async_copy(
            w_ref.at[:, pl.ds(at, tile)], w_buf.at[buffer], w_sem.at[buffer]
        )

    x_copy = pltpu.make_async_copy(x_ref, x_buf, x_sem)
    x_copy.start()
    for step in range(ahead):
        weight_copy(step).start()
    x_copy.wait()
    o_copies = []
    for s, (out, o_buf) in enumerate(zip(outs, o_bufs)):

        def body(j, carry, s=s, o_buf=o_buf):
            step = s * per + j
            weight_copy(step).wait()
            o_buf[:, pl.ds(pl.multiple_of(j * tile, tile), tile)] = jnp.dot(
                x_buf[...], w_buf[lax.rem(step, ahead)], preferred_element_type=jnp.float32
            ).astype(o_buf.dtype)

            @pl.when(step + ahead < steps)
            def _():
                weight_copy(step + ahead).start()

            return carry

        lax.fori_loop(0, per, body, 0)
        o_copies.append(pltpu.make_async_copy(o_buf, out, o_sem.at[s]))
        o_copies[-1].start()
    for copy in o_copies:
        copy.wait()


def project_out(attended, w_o, order, block, stacked=False, held=()):
    rows, depth = attended.shape
    tile = tile_of(block, 512)
    count = order.shape[0]
    anywhere = pl.BlockSpec(memory_space=pl.ANY)
    return pl.pallas_call(
        without(functools.partial(out_kernel, count, stacked, tile), 3, len(held)),
        grid_spec=pltpu.PrefetchScalarGridSpec(
            num_scalar_prefetch=1,
            grid=(1,),
            in_specs=[anywhere] * (2 + len(held)),
            out_specs=anywhere if stacked else [anywhere] * count,
            scratch_shapes=[
                pltpu.VMEM((rows, depth), jnp.bfloat16),
                pltpu.VMEM((WEIGHT_BUFFERS, depth, tile), jnp.bfloat16),
                pltpu.SemaphoreType.DMA,
                pltpu.SemaphoreType.DMA((WEIGHT_BUFFERS,)),
                pltpu.SemaphoreType.DMA((count,)),
            ]
            + [pltpu.VMEM((rows, block), jnp.bfloat16)] * count,
        ),
        out_shape=jax.ShapeDtypeStruct((count, rows, block), jnp.bfloat16)
        if stacked
        else [jax.ShapeDtypeStruct((rows, block), jnp.bfloat16)] * count,
        compiler_params=pltpu.CompilerParams(vmem_limit_bytes=KERNEL_VMEM),
        cost_estimate=pl.CostEstimate(
            flops=2 * rows * depth * count * block // COST_SHARE,
            bytes_accessed=(2 * depth * count * block) // COST_SHARE,
            transcendentals=0,
        ),
        name="project_out",
    )(order, attended, *in_hbm([w_o]), *held)


def with_ones(values):
    return jnp.concatenate([values, jnp.ones_like(values)], axis=1)


def scores_of(queries, keys):
    return lax.dot_general(
        queries, keys, (((1,), (1,)), ((), ())), preferred_element_type=jnp.float32
    )


def prefill_kernel(
    kv_heads, group, span, first, len_ref, q_ref, cache_ref, new_ref, o_ref, cache_buf, sem, *scratch
):
    accs, peaks = scratch[:kv_heads], scratch[kv_heads:]
    prompt = pl.program_id(0)

    def cache_copy(g):
        return pltpu.make_async_copy(cache_ref.at[0, first + g], cache_buf.at[g], sem.at[g])

    @pl.when(prompt == 0)
    def _():
        for g in range(cache_buf.shape[0]):
            cache_copy(g).start()

    tokens = q_ref.shape[0]
    rows = group * tokens
    live = len_ref[first + prompt]
    full = live // span
    query_token = lax.rem(lax.broadcasted_iota(jnp.int32, (rows, tokens), 0), tokens)
    key_token = lax.broadcasted_iota(jnp.int32, (rows, tokens), 1)
    causal = key_token <= query_token
    lane = lax.broadcasted_iota(jnp.int32, (1, span), 1)

    def queries_of(a):
        return jnp.concatenate(
            [
                q_ref[:, (a * group + h) * HEAD_SIZE : (a * group + h + 1) * HEAD_SIZE]
                for h in range(group)
            ],
            axis=0,
        )

    def columns(a, part):
        return pl.ds((2 * a + part) * HEAD_SIZE, HEAD_SIZE)

    for a in range(kv_heads):
        scores = jnp.where(causal, scores_of(queries_of(a), new_ref[:, columns(a, 0)]), MASKED)
        top = jnp.broadcast_to(jnp.max(scores, axis=-1, keepdims=True), (rows, HEAD_SIZE))
        weights = jnp.exp2(scores - top[:, :tokens]).astype(jnp.bfloat16)
        accs[a][...] = jnp.dot(
            weights, with_ones(new_ref[:, columns(a, 1)]), preferred_element_type=jnp.float32
        )
        peaks[a][...] = top

    cache_copy(prompt).wait()

    def block(s, bias):
        at = pl.multiple_of(s * span, span)
        scores = [
            scores_of(queries_of(a), cache_buf[prompt, pl.ds(at, span), columns(a, 0)])
            for a in range(kv_heads)
        ]
        for a in range(kv_heads):
            here = scores[a] if bias is None else scores[a] + bias
            before = peaks[a][...]
            top = jnp.maximum(before, jnp.max(here, axis=-1, keepdims=True))
            weights = jnp.exp2(
                here - jnp.concatenate([top] * (span // HEAD_SIZE), axis=1)
            ).astype(jnp.bfloat16)
            fade = jnp.exp2(before - top)
            values = cache_buf[prompt, pl.ds(at, span), columns(a, 1)]
            accs[a][...] = accs[a][...] * jnp.concatenate([fade, fade], axis=1) + jnp.dot(
                weights, with_ones(values), preferred_element_type=jnp.float32
            )
            peaks[a][...] = top

    def step(s, carry):
        block(s, None)
        return carry

    lax.fori_loop(0, full, step, 0)

    @pl.when(full * span < live)
    def _():
        block(full, jnp.where(lane + full * span < live, 0.0, MASKED))

    for a in range(kv_heads):
        result = accs[a][:, :HEAD_SIZE] / accs[a][:, HEAD_SIZE:]
        for h in range(group):
            o_ref[:, (a * group + h) * HEAD_SIZE : (a * group + h + 1) * HEAD_SIZE] = result[
                h * tokens : (h + 1) * tokens
            ].astype(o_ref.dtype)


def prefill_attention(queries, prefix_cache, first, count, new_kv, prefix_len):
    width = queries.shape[1]
    positions, page = prefix_cache.shape[2:]
    kv_heads = page // (2 * HEAD_SIZE)
    group = width // HEAD_SIZE // kv_heads
    span = tile_of(positions, 512)
    rows = group * PROMPT_TOKENS
    return pl.pallas_call(
        functools.partial(prefill_kernel, kv_heads, group, span, first),
        grid_spec=pltpu.PrefetchScalarGridSpec(
            num_scalar_prefetch=1,
            grid=(count,),
            in_specs=[
                pl.BlockSpec((PROMPT_TOKENS, width), lambda g, n: (g, 0)),
                pl.BlockSpec(memory_space=pl.ANY),
                pl.BlockSpec((PROMPT_TOKENS, page), lambda g, n: (g, 0)),
            ],
            out_specs=pl.BlockSpec((PROMPT_TOKENS, width), lambda g, n: (g, 0)),
            scratch_shapes=[
                pltpu.VMEM((count, positions, page), jnp.bfloat16),
                pltpu.SemaphoreType.DMA((count,)),
            ]
            + [pltpu.VMEM((rows, 2 * HEAD_SIZE), jnp.float32)] * kv_heads
            + [pltpu.VMEM((rows, HEAD_SIZE), jnp.float32)] * kv_heads,
        ),
        out_shape=jax.ShapeDtypeStruct((count * PROMPT_TOKENS, width), jnp.bfloat16),
        compiler_params=pltpu.CompilerParams(vmem_limit_bytes=KERNEL_VMEM),
        cost_estimate=pl.CostEstimate(
            flops=8 * count * rows * kv_heads * (positions + PROMPT_TOKENS) * HEAD_SIZE // COST_SHARE,
            bytes_accessed=(2 * count * positions * page) // COST_SHARE,
            transcendentals=count * rows * kv_heads * (positions + PROMPT_TOKENS),
        ),
        name="prefill_attention",
    )(prefix_len, queries, *in_hbm([prefix_cache]), new_kv)


def decode_kernel(
    kv_heads, batch, len_ref, row_ref, q_ref, cache_ref, landed_ref, fresh_ref, o_ref, acc, peak
):
    row_count, context = cache_ref.shape[1], cache_ref.shape[2]
    per_row = q_ref.shape[2]
    steps = fresh_ref.shape[1]
    rows = batch * per_row
    row_of = lax.broadcasted_iota(jnp.int32, (rows, batch * context), 0) // per_row
    key_row = lax.broadcasted_iota(jnp.int32, (rows, batch * context), 1) // context
    key_at = lax.rem(lax.broadcasted_iota(jnp.int32, (rows, batch * context), 1), context)
    fresh_query = lax.broadcasted_iota(jnp.int32, (rows, batch * steps), 0)
    fresh_key = lax.broadcasted_iota(jnp.int32, (rows, batch * steps), 1)
    fresh_live = (fresh_key // steps == fresh_query // per_row) & (
        lax.rem(fresh_key, steps) <= lax.rem(fresh_query, per_row) // (per_row // steps)
    )

    def cached(b, carry):
        first = b * batch
        live = jnp.zeros_like(key_row)
        for r in range(batch):
            live = jnp.where(key_row == r, len_ref[first + r], live)
        cache_live = (row_of == key_row) & (key_at < live)
        pages = cache_ref[0, pl.ds(first, batch)].reshape(batch * context, cache_ref.shape[3])
        fresh = fresh_ref[pl.ds(first, batch)].reshape(batch * steps, fresh_ref.shape[2])
        for a in range(kv_heads):
            queries = q_ref[pl.ds(first, batch), a].reshape(rows, HEAD_SIZE).astype(jnp.bfloat16)
            k_at, v_at = 2 * a * HEAD_SIZE, (2 * a + 1) * HEAD_SIZE
            scores = scores_of(queries, pages[:, k_at : k_at + HEAD_SIZE])
            scores = jnp.where(cache_live, scores, MASKED)
            recent = scores_of(queries, fresh[:, k_at : k_at + HEAD_SIZE].astype(jnp.bfloat16))
            recent = jnp.where(fresh_live, recent, MASKED)
            top = jnp.maximum(
                jnp.max(scores, axis=-1, keepdims=True), jnp.max(recent, axis=-1, keepdims=True)
            )
            weights = jnp.exp2(scores - top).astype(jnp.bfloat16)
            recent = jnp.exp2(recent - top).astype(jnp.bfloat16)
            total = jnp.dot(
                weights,
                with_ones(pages[:, v_at : v_at + HEAD_SIZE]),
                preferred_element_type=jnp.float32,
            ) + jnp.dot(
                recent,
                with_ones(fresh[:, v_at : v_at + HEAD_SIZE].astype(jnp.bfloat16)),
                preferred_element_type=jnp.float32,
            )
            acc[pl.ds(first, batch), a] = total.reshape(batch, per_row, 2 * HEAD_SIZE)
            peak[pl.ds(first, batch), a] = jnp.broadcast_to(top, (rows, HEAD_SIZE)).reshape(
                batch, per_row, HEAD_SIZE
            )
        return carry

    lax.fori_loop(0, row_count // batch, cached, 0)

    def arrival(slot, carry):
        row = row_ref[slot]

        @pl.when(row >= 0)
        def _():
            for a in range(kv_heads):
                queries = q_ref[row, a].astype(jnp.bfloat16)
                k_at, v_at = 2 * a * HEAD_SIZE, (2 * a + 1) * HEAD_SIZE
                scores = scores_of(queries, landed_ref[slot, :, k_at : k_at + HEAD_SIZE])
                before = peak[row, a]
                top = jnp.maximum(before, jnp.max(scores, axis=-1, keepdims=True))
                weights = jnp.exp2(scores - top[:, :1]).astype(jnp.bfloat16)
                fade = jnp.exp2(before - top)
                acc[row, a] = acc[row, a] * jnp.concatenate([fade, fade], axis=1) + jnp.dot(
                    weights,
                    with_ones(landed_ref[slot, :, v_at : v_at + HEAD_SIZE]),
                    preferred_element_type=jnp.float32,
                )

        return carry

    lax.fori_loop(0, row_ref.shape[0], arrival, 0)
    o_ref[...] = (acc[:, :, :, :HEAD_SIZE] / acc[:, :, :, HEAD_SIZE:]).astype(o_ref.dtype)


def decode_attention(queries, dec_cache, dec_len, landed, slot_rows, fresh, held=()):
    row_count, kv_heads, per_row = queries.shape[:3]
    context = dec_cache.shape[2]
    batch = max(1, min(row_count, 2 * HEAD_SIZE // context))
    whole = lambda array: pl.BlockSpec(array.shape, lambda g, *_: (0,) * array.ndim)
    return pl.pallas_call(
        without(functools.partial(decode_kernel, kv_heads, batch), 6, len(held)),
        grid_spec=pltpu.PrefetchScalarGridSpec(
            num_scalar_prefetch=2,
            grid=(1,),
            in_specs=[whole(queries), whole(dec_cache), whole(landed), whole(fresh)]
            + [pl.BlockSpec(memory_space=pl.ANY)] * len(held),
            out_specs=whole(queries),
            scratch_shapes=[
                pltpu.VMEM((row_count, kv_heads, per_row, 2 * HEAD_SIZE), jnp.float32),
                pltpu.VMEM((row_count, kv_heads, per_row, HEAD_SIZE), jnp.float32),
            ],
        ),
        out_shape=jax.ShapeDtypeStruct(queries.shape, jnp.float32),
        compiler_params=pltpu.CompilerParams(vmem_limit_bytes=KERNEL_VMEM),
        cost_estimate=pl.CostEstimate(
            flops=8 * queries.size * batch * context // COST_SHARE,
            bytes_accessed=(2 * dec_cache.size + 2 * landed.size) // COST_SHARE,
            transcendentals=queries.size * batch * context // HEAD_SIZE,
        ),
        name="decode_attention",
    )(dec_len, slot_rows, queries, dec_cache, landed, fresh, *held)


def shards(
    prefill_x,
    norm_gain,
    w_q,
    q_scale,
    key_value_weight,
    key_value_scale,
    w_o,
    o_scale,
    prefix_cache,
    prefix_len,
    dec_x,
    dec_cache,
    dec_len,
    place,
):
    prompts_total = prefix_cache.shape[1]
    row_count = dec_cache.shape[1]
    page_width = prefix_cache.shape[3]
    kv_heads = page_width // (2 * HEAD_SIZE)
    query_heads = w_q.shape[1] // HEAD_SIZE
    group_size = query_heads // kv_heads
    steps = dec_x.shape[0]
    section_count = lax.axis_size("section")
    section_index = lax.axis_index("section")
    tensor_count = lax.axis_size("tensor")
    tensor_index = lax.axis_index("tensor")
    head_span = max(1, 8 // query_heads)
    span_bits = head_span.bit_length() - 1
    block_width = w_o.shape[1] // tensor_count
    scales = (q_scale * EXP2_FACTOR, key_value_scale)

    weights = (norm_gain, w_q, key_value_weight)

    def kv_of_head(new_kv):
        for bit_number in range(span_bits):
            partner = partner_2(new_kv, "tensor", bit_number)
            new_kv = joined(new_kv, partner, bit_number, 1, tensor_index)
        return new_kv

    def finished(x, terms):
        total = sum(term.astype(jnp.float32) for term in terms)
        return (x.astype(jnp.float32) + total * o_scale).astype(jnp.bfloat16)

    dec_rows = dec_x.reshape(steps * row_count, -1)
    bounds = sorted({0, min(1, prompts_total - 1), prompts_total - 1, prompts_total})
    spans = list(zip(bounds[:-1], bounds[1:]))
    on_line = tensor_count == 4 and len(spans) == 3
    order = jnp.stack(
        line_order(tensor_index) if on_line else list(range(tensor_count))
    ).astype(jnp.int32)
    chunks = [prefill_x[first * PROMPT_TOKENS : last * PROMPT_TOKENS] for first, last in spans]
    blocks = chunks[:-1] + [jnp.concatenate([chunks[-1], dec_rows], axis=0)]
    if on_line:
        begin = chunks[0].shape[0]
        rest, dec_rest = after_all((prefill_x[begin:], dec_rows), blocks[0])
        blocks[1] = rest[: chunks[1].shape[0]]
        blocks[2] = jnp.concatenate([rest[chunks[1].shape[0] :], dec_rest], axis=0)
    pages = []

    def attention(k, queries):
        first, last = spans[k]
        return prefill_attention(queries, prefix_cache, first, last - first, pages[k], prefix_len)

    def keep(new_kv):
        new_kv = kv_of_head(new_kv)
        pages.append(new_kv[: chunks[len(pages)].shape[0]])
        return new_kv

    def back(attended, held=()):
        far, near, partner, own = project_out(
            attended, w_o, order[::-1], block_width, held=held
        )
        return LineScatter(own, partner, near, far, "tensor")

    def back_whole(attended):
        return project_out(
            attended, w_o, jnp.arange(tensor_count, dtype=jnp.int32), block_width, stacked=True
        )

    def summed(partial):
        return [lax.psum_scatter(partial, "tensor", scatter_dimension=0, tiled=False)]

    if on_line:
        first = LineGather(blocks[0], "tensor")
        first.second()
        begun = project_part(
            [[first.block], [first.partner]], order[:2], *weights, None, None, (first.middle,)
        )
        first.third(begun[2])
        second = LineGather(
            blocks[1], "tensor", (first.outer_far,), (first.outer, first.middle_far, begun[2])
        )
        queries, new_kv = project_part(first.slots()[2:], order[2:], *weights, begun, scales)
        keep(new_kv)
        attended = attention(0, queries)
        second.second(attended)
        sums = [back(attended, (second.partner, second.middle))]

        begun = project_part(
            [[second.block], [second.partner]], order[:2],
            *weights,
            None,
            None,
            (sums[0].own, second.outer),
        )
        second.third(begun[2])
        sums[0].second(begun[2])
        sums[0].third()
        third = LineGather(
            blocks[2], "tensor", (second.outer_far,), (second.outer, second.middle_far, begun[2])
        )
        queries, new_kv = project_part(
            second.slots()[2:], order[2:], *weights, begun, scales, sums[0].second_hop
        )
        keep(new_kv)
        third.second(queries)
        attended = attention(1, after(queries, third.partner, third.middle))
        third.third(attended)
        sums.append(back(attended, (third.outer, third.middle_far)))
        begun = project_part(
            [[third.block], [third.partner]],
            order[:2],
            *weights,
            None,
            None,
            (sums[1].own,),
        )
        queries, new_kv = project_part(
            third.slots()[2:], order[2:], *weights, begun, scales, sums[0].terms[1:]
        )
        new_kv = keep(new_kv)
        sums[1].second(queries)
        sums[1].third_begin()
        sums.append(back(attention(2, after(queries, *sums[1].first_hop)), sums[1].second_hop))
        sums[1].third_start(sums[2].own)
        hold = (sums[2].own,)
    else:
        terms_of = []
        for k, block in enumerate(blocks):
            whole = lax.all_gather(block, "tensor", axis=1, tiled=True)
            queries, new_kv = project_part([[whole]], order[:1], *weights, None, scales)
            new_kv = keep(new_kv)
            terms_of.append(summed(back_whole(attention(k, queries))))
        hold = ()
    tokens = chunks[-1].shape[0]
    dec_queries, fresh_kv = queries[tokens:], new_kv[tokens:]

    own_block = after(jnp.concatenate(pages, axis=0), *hold).reshape(
        prompts_total, PROMPT_TOKENS, page_width
    )
    owners = (place // row_count).reshape(section_count, prompts_total)
    targets = (place % row_count).reshape(section_count, prompts_total)
    owner_hits = (owners[:, :, None] == jnp.arange(section_count)[None, None, :]).astype(jnp.int32)
    slot_ranks = jnp.sum((jnp.cumsum(owner_hits, axis=1) - owner_hits) * owner_hits, axis=2)
    capacity = prompts_total // 2
    slot_ids = jnp.arange(capacity)
    sending = lax.dynamic_index_in_dim(owner_hits, section_index, 0, keepdims=False)
    my_ranks = lax.dynamic_index_in_dim(slot_ranks, section_index, 0, keepdims=False)
    selector = (
        jnp.transpose(sending)[:, None, :] * (my_ranks[None, None, :] == slot_ids[None, :, None])
    ).astype(jnp.bfloat16)
    here = (owners == section_index)[:, None, :] & (
        slot_ranks[:, None, :] == slot_ids[None, :, None]
    )
    slot_rows = jnp.sum(jnp.where(here, targets[:, None, :] + 1, 0), axis=2) - 1
    outgoing = jnp.einsum(
        "skp,pcw->skcw", selector, own_block, preferred_element_type=jnp.float32
    ).astype(jnp.bfloat16)
    received = lax.all_to_all(outgoing, "section", split_axis=0, concat_axis=0, tiled=True)
    if on_line:
        sums[2].second(received)
        hold = sums[2].first_hop
    landed = received.reshape(section_count * capacity, PROMPT_TOKENS, page_width)

    dec_queries = jnp.transpose(
        dec_queries.reshape(steps, row_count, kv_heads, group_size, HEAD_SIZE), (1, 2, 0, 3, 4)
    ).reshape(row_count, kv_heads, steps * group_size, HEAD_SIZE)
    fresh = jnp.transpose(fresh_kv.reshape(steps, row_count, page_width), (1, 0, 2))
    dec_attended = decode_attention(
        dec_queries.astype(jnp.float32),
        dec_cache,
        dec_len,
        landed,
        slot_rows.reshape(-1).astype(jnp.int32),
        fresh.astype(jnp.float32),
        hold,
    )
    dec_attended = (
        jnp.transpose(
            dec_attended.reshape(row_count, kv_heads, steps, group_size, HEAD_SIZE), (2, 0, 1, 3, 4)
        )
        .reshape(steps * row_count, -1)
        .astype(jnp.bfloat16)
    )
    if on_line:
        to = [(tensor_index + shift) % tensor_count for shift in range(tensor_count)]
        sums[2].third(dec_attended)
        own, *parts = project_out(
            dec_attended,
            w_o,
            jnp.stack(to).astype(jnp.int32),
            block_width,
            held=(*sums[2].second_hop, *corners(sums[1].terms[1:])),
        )
        dec_terms = [own] + [
            lax.ppermute(
                part, "tensor", [(j, (j + shift) % tensor_count) for j in range(tensor_count)]
            )
            for shift, part in enumerate(parts, 1)
        ]
        terms_of = [each.terms for each in sums]
    else:
        dec_terms = summed(back_whole(dec_attended))
    prefill_out = jnp.concatenate(
        [finished(x, terms) for x, terms in zip(chunks, terms_of)], axis=0
    )
    decode_out = finished(dec_rows, dec_terms).reshape(dec_x.shape)
    return (prefill_out, decode_out)


def solution(mesh):
    in_specs = (
        P(("groups", "section"), "tensor"),
        P(),
        P(None, "tensor"),
        P("tensor"),
        P(None, "tensor"),
        P("tensor"),
        P("tensor", None),
        P("tensor"),
        P("tensor", ("groups", "section"), None, None),
        P(("groups", "section")),
        P(None, ("groups", "section"), "tensor"),
        P("tensor", ("groups", "section"), None, None),
        P(("groups", "section")),
        P("groups"),
    )
    out_specs = (P(("groups", "section"), "tensor"), P(None, ("groups", "section"), "tensor"))
    return jax.shard_map(shards, mesh=mesh, in_specs=in_specs, out_specs=out_specs, check_vma=False)
```

```python
import functools
import math

import jax
import jax.numpy as jnp
from jax import lax
from jax.experimental import pallas as pl
from jax.experimental.pallas import tpu as pltpu
from jax.sharding import PartitionSpec as P

HEAD_SIZE = 128
PROMPT_TOKENS = 128
KERNEL_VMEM = 36 << 20
WEIGHT_BUFFERS = 8
COST_SHARE = 256
EXP2_FACTOR = math.log2(math.e) / math.sqrt(HEAD_SIZE)
MASKED = -1e30


def partner_2(block, axis, distance):
    count = lax.axis_size(axis)
    route = []
    for low in range(count):
        high = low | 1 << distance
        if high != low and high < count:
            route += [(low, high), (high, low)]
    return lax.ppermute(block, axis, route)


def joined(portion, partner, bit_number, concat_dim, tensor_index):
    upper_half = tensor_index // 2**bit_number % 2 == 1
    lower_first = jnp.concatenate([portion, partner], axis=concat_dim)
    upper_first = jnp.concatenate([partner, portion], axis=concat_dim)
    return jnp.where(upper_half, upper_first, lower_first)


def tile_of(extent, most):
    tile = extent
    while tile > most and tile % 2 == 0:
        tile //= 2
    return tile


def after(value, *others):
    return lax.optimization_barrier((value,) + others)[0]


def after_all(values, *others):
    return lax.optimization_barrier(tuple(values) + others)[: len(values)]


def line_order(index):
    low = index < 2
    return [index, index ^ 1, jnp.where(low, 2, 1), jnp.where(low, 3, 0)]


OUTER = [(0, 1), (1, 0), (2, 3), (3, 2)]
MIDDLE = [(1, 2), (2, 1)]
INWARD = [(0, 1), (3, 2)]
OUTWARD = [(1, 0), (2, 3)]


class LineGather:
    def __init__(self, block, axis, outer_held=(), middle_held=()):
        self.block, self.axis = block, axis
        self.partner = lax.ppermute(after(block, *outer_held), axis, OUTER)
        self.middle = lax.ppermute(after(block, *middle_held), axis, MIDDLE)

    def second(self, *held):
        partner, middle = after_all((self.partner, self.middle), *held)
        self.outer = lax.ppermute(middle, self.axis, OUTWARD)
        self.middle_far = lax.ppermute(partner, self.axis, MIDDLE)

    def third(self, *held):
        self.outer_far = lax.ppermute(after(self.middle_far, *held), self.axis, OUTWARD)

    def slots(self):
        return [
            [self.block],
            [self.partner],
            [self.middle, self.outer],
            [self.middle_far, self.outer_far],
        ]


def corners(arrays):
    return [array[:HEAD_SIZE, :HEAD_SIZE] for array in arrays]


def added(*terms):
    total = sum(term.astype(jnp.float32) for term in terms)
    return total.astype(terms[0].dtype)


class LineScatter:
    def __init__(self, own, partner, near, far, axis):
        self.own, self.partner, self.near, self.far = own, partner, near, far
        self.axis = axis
        self.far_in = lax.ppermute(far, axis, INWARD)

    def second(self, *held):
        far, near = after_all((added(self.far, self.far_in), self.near), *held)
        self.first_hop = (far,)
        self.near_in = lax.ppermute(near, self.axis, INWARD)
        self.far_out = lax.ppermute(far, self.axis, MIDDLE)

    def third(self, *held):
        self.third_begin()
        self.third_start(*held)

    def third_begin(self):
        self.second_hop = (
            added(self.near, self.near_in),
            added(self.partner, self.far_out),
        )

    def third_start(self, *held):
        near, partner = after_all(self.second_hop, *held)
        near = lax.ppermute(near, self.axis, MIDDLE)
        partner = lax.ppermute(partner, self.axis, OUTER)
        self.terms = [self.own, near, partner]


def in_hbm(arrays):
    return [pltpu.with_memory_space_constraint(array, pltpu.HBM) for array in arrays]


def without(kernel, first, count):
    return lambda *refs: kernel(*refs[:first], *refs[first + count :])


def qkv_kernel(counts, begun, ended, tile, order, *refs):
    refs = list(refs)
    arrays = sum(counts)
    xs = [refs.pop(0) for _ in range(arrays)]
    gain_ref, wq_ref, wkv_ref = (refs.pop(0) for _ in range(3))
    sums_in = [refs.pop(0) for _ in range(3)] if begun else []
    if ended:
        qs_ref, kvs_ref, q_ref, kv_ref, accq, acckv, squares = (refs.pop(0) for _ in range(7))
    else:
        accq, acckv, squares = (refs.pop(0) for _ in range(3))
    x_bufs = [refs.pop(0) for _ in range(arrays)]
    wq_buf, wkv_buf, x_sem, w_sem, sum_sem = refs
    per = x_bufs[0].shape[1] // tile
    steps = len(counts) * per
    ahead = min(steps, wq_buf.shape[0])

    def weight_copies(step):
        buffer = lax.rem(step, ahead)
        at = pl.multiple_of((order[step // per] * per + lax.rem(step, per)) * tile, tile)
        return [
            pltpu.make_async_copy(ref.at[pl.ds(at, tile)], buf.at[buffer], w_sem.at[w, buffer])
            for w, (ref, buf) in enumerate([(wq_ref, wq_buf), (wkv_ref, wkv_buf)])
        ]

    x_copies = [
        pltpu.make_async_copy(ref, buf, x_sem.at[a]) for a, (ref, buf) in enumerate(zip(xs, x_bufs))
    ]
    sum_copies = [
        pltpu.make_async_copy(ref, acc, sum_sem.at[a])
        for a, (ref, acc) in enumerate(zip(sums_in, (accq, acckv, squares)))
    ]
    for copy in x_copies[: counts[0]] + sum_copies:
        copy.start()
    for step in range(ahead):
        for copy in weight_copies(step):
            copy.start()
    for copy in x_copies[counts[0] :]:
        copy.start()
    for copy in sum_copies:
        copy.wait()
    if not begun:
        accq[...] = jnp.zeros_like(accq)
        acckv[...] = jnp.zeros_like(acckv)
        squares[...] = jnp.zeros_like(squares)

    taken = 0
    for s, count in enumerate(counts):
        for copy in x_copies[taken : taken + count]:
            copy.wait()
        bufs = x_bufs[taken : taken + count]
        taken += count

        def body(j, carry, s=s, bufs=bufs):
            step = s * per + j
            for copy in weight_copies(step):
                copy.wait()
            at = pl.multiple_of(j * tile, tile)
            values = sum(buf[:, pl.ds(at, tile)].astype(jnp.float32) for buf in bufs)
            gain = gain_ref[:, pl.ds(pl.multiple_of((order[s] * per + j) * tile, tile), tile)]
            squares[...] += jnp.broadcast_to(
                jnp.sum(values * values, axis=-1, keepdims=True), squares.shape
            )
            scaled = (values * gain).astype(jnp.bfloat16)
            buffer = lax.rem(step, ahead)
            accq[...] += jnp.dot(scaled, wq_buf[buffer], preferred_element_type=jnp.float32)
            acckv[...] += jnp.dot(scaled, wkv_buf[buffer], preferred_element_type=jnp.float32)

            @pl.when(step + ahead < steps)
            def _():
                for copy in weight_copies(step + ahead):
                    copy.start()

            return carry

        lax.fori_loop(0, per, body, 0)
    if ended:
        root = lax.rsqrt(squares[:, :1] / ended + 1e-05)
        q_ref[...] = (accq[...] * root * qs_ref[...]).astype(q_ref.dtype)
        kv_ref[...] = (acckv[...] * root * kvs_ref[...]).astype(kv_ref.dtype)


def project_part(slots, order, norm_gain, w_q, kv_weight, begun, scales, held=()):
    rows, depth = slots[0][0].shape
    tile = tile_of(depth, 512)
    q_cols, kv_cols = w_q.shape[1], kv_weight.shape[1]
    arrays = [array for slot in slots for array in slot]

    def whole(shape):
        return pl.BlockSpec(shape, lambda g, order: (0,) * len(shape))

    anywhere = pl.BlockSpec(memory_space=pl.ANY)
    operands = arrays + [norm_gain.reshape(1, -1)] + in_hbm([w_q, kv_weight])
    in_specs = [anywhere] * len(arrays) + [whole((1, norm_gain.shape[0])), anywhere, anywhere]
    sums = [(rows, q_cols), (rows, kv_cols), (rows, HEAD_SIZE)]
    if begun is not None:
        operands += list(begun)
        in_specs += [anywhere] * 3
    if scales is not None:
        operands += [scale.reshape(1, -1) for scale in scales]
        in_specs += [whole((1, q_cols)), whole((1, kv_cols))]
        out_shapes = [jax.ShapeDtypeStruct(shape, jnp.bfloat16) for shape in sums[:2]]
        scratch = [pltpu.VMEM(shape, jnp.float32) for shape in sums]
    else:
        out_shapes = [jax.ShapeDtypeStruct(shape, jnp.float32) for shape in sums]
        scratch = []
    kernel = functools.partial(
        qkv_kernel,
        [len(slot) for slot in slots],
        begun is not None,
        0 if scales is None else w_q.shape[0],
        tile,
    )
    return pl.pallas_call(
        without(kernel, 1 + len(operands), len(held)),
        grid_spec=pltpu.PrefetchScalarGridSpec(
            num_scalar_prefetch=1,
            grid=(1,),
            in_specs=in_specs + [anywhere] * len(held),
            out_specs=[whole(out.shape) for out in out_shapes],
            scratch_shapes=scratch
            + [pltpu.VMEM((rows, depth), jnp.bfloat16) for _ in arrays]
            + [
                pltpu.VMEM((WEIGHT_BUFFERS, tile, q_cols), jnp.bfloat16),
                pltpu.VMEM((WEIGHT_BUFFERS, tile, kv_cols), jnp.bfloat16),
                pltpu.SemaphoreType.DMA((len(arrays),)),
                pltpu.SemaphoreType.DMA((2, WEIGHT_BUFFERS)),
                pltpu.SemaphoreType.DMA((3,)),
            ],
        ),
        out_shape=out_shapes,
        compiler_params=pltpu.CompilerParams(vmem_limit_bytes=KERNEL_VMEM),
        cost_estimate=pl.CostEstimate(
            flops=2 * rows * depth * len(slots) * (q_cols + kv_cols) // COST_SHARE,
            bytes_accessed=(2 * depth * len(slots) * (q_cols + kv_cols)) // COST_SHARE,
            transcendentals=0,
        ),
        name="norm_qkv",
    )(order, *operands, *held)


def out_kernel(count, stacked, tile, order, x_ref, w_ref, *refs):
    if stacked:
        outs, refs = [refs[0].at[s] for s in range(count)], refs[1:]
    else:
        outs, refs = refs[:count], refs[count:]
    x_buf, w_buf, x_sem, w_sem, o_sem = refs[:5]
    o_bufs = refs[5:]
    per = o_bufs[0].shape[1] // tile
    steps = count * per
    ahead = min(steps, w_buf.shape[0])

    def weight_copy(step):
        at = pl.multiple_of((order[step // per] * per + lax.rem(step, per)) * tile, tile)
        buffer = lax.rem(step, ahead)
        return pltpu.make_async_copy(
            w_ref.at[:, pl.ds(at, tile)], w_buf.at[buffer], w_sem.at[buffer]
        )

    x_copy = pltpu.make_async_copy(x_ref, x_buf, x_sem)
    x_copy.start()
    for step in range(ahead):
        weight_copy(step).start()
    x_copy.wait()
    o_copies = []
    for s, (out, o_buf) in enumerate(zip(outs, o_bufs)):

        def body(j, carry, s=s, o_buf=o_buf):
            step = s * per + j
            weight_copy(step).wait()
            o_buf[:, pl.ds(pl.multiple_of(j * tile, tile), tile)] = jnp.dot(
                x_buf[...], w_buf[lax.rem(step, ahead)], preferred_element_type=jnp.float32
            ).astype(o_buf.dtype)

            @pl.when(step + ahead < steps)
            def _():
                weight_copy(step + ahead).start()

            return carry

        lax.fori_loop(0, per, body, 0)
        o_copies.append(pltpu.make_async_copy(o_buf, out, o_sem.at[s]))
        o_copies[-1].start()
    for copy in o_copies:
        copy.wait()


def project_out(attended, w_o, order, block, stacked=False, held=()):
    rows, depth = attended.shape
    tile = tile_of(block, 512)
    count = order.shape[0]
    anywhere = pl.BlockSpec(memory_space=pl.ANY)
    return pl.pallas_call(
        without(functools.partial(out_kernel, count, stacked, tile), 3, len(held)),
        grid_spec=pltpu.PrefetchScalarGridSpec(
            num_scalar_prefetch=1,
            grid=(1,),
            in_specs=[anywhere] * (2 + len(held)),
            out_specs=anywhere if stacked else [anywhere] * count,
            scratch_shapes=[
                pltpu.VMEM((rows, depth), jnp.bfloat16),
                pltpu.VMEM((WEIGHT_BUFFERS, depth, tile), jnp.bfloat16),
                pltpu.SemaphoreType.DMA,
                pltpu.SemaphoreType.DMA((WEIGHT_BUFFERS,)),
                pltpu.SemaphoreType.DMA((count,)),
            ]
            + [pltpu.VMEM((rows, block), jnp.bfloat16)] * count,
        ),
        out_shape=jax.ShapeDtypeStruct((count, rows, block), jnp.bfloat16)
        if stacked
        else [jax.ShapeDtypeStruct((rows, block), jnp.bfloat16)] * count,
        compiler_params=pltpu.CompilerParams(vmem_limit_bytes=KERNEL_VMEM),
        cost_estimate=pl.CostEstimate(
            flops=2 * rows * depth * count * block // COST_SHARE,
            bytes_accessed=(2 * depth * count * block) // COST_SHARE,
            transcendentals=0,
        ),
        name="project_out",
    )(order, attended, *in_hbm([w_o]), *held)


def with_ones(values):
    return jnp.concatenate([values, jnp.ones_like(values)], axis=1)


def scores_of(queries, keys):
    return lax.dot_general(
        queries, keys, (((1,), (1,)), ((), ())), preferred_element_type=jnp.float32
    )


def prefill_kernel(
    kv_heads, group, span, first, len_ref, q_ref, cache_ref, new_ref, o_ref, cache_buf, sem, *scratch
):
    accs, peaks = scratch[:kv_heads], scratch[kv_heads:]
    prompt = pl.program_id(0)

    def cache_copy(g):
        return pltpu.make_async_copy(cache_ref.at[0, first + g], cache_buf.at[g], sem.at[g])

    @pl.when(prompt == 0)
    def _():
        for g in range(cache_buf.shape[0]):
            cache_copy(g).start()

    tokens = q_ref.shape[0]
    rows = group * tokens
    live = len_ref[first + prompt]
    full = live // span
    query_token = lax.rem(lax.broadcasted_iota(jnp.int32, (rows, tokens), 0), tokens)
    key_token = lax.broadcasted_iota(jnp.int32, (rows, tokens), 1)
    causal = key_token <= query_token
    lane = lax.broadcasted_iota(jnp.int32, (1, span), 1)

    def queries_of(a):
        return jnp.concatenate(
            [
                q_ref[:, (a * group + h) * HEAD_SIZE : (a * group + h + 1) * HEAD_SIZE]
                for h in range(group)
            ],
            axis=0,
        )

    def columns(a, part):
        return pl.ds((2 * a + part) * HEAD_SIZE, HEAD_SIZE)

    for a in range(kv_heads):
        scores = jnp.where(causal, scores_of(queries_of(a), new_ref[:, columns(a, 0)]), MASKED)
        top = jnp.broadcast_to(jnp.max(scores, axis=-1, keepdims=True), (rows, HEAD_SIZE))
        weights = jnp.exp2(scores - top[:, :tokens]).astype(jnp.bfloat16)
        accs[a][...] = jnp.dot(
            weights, with_ones(new_ref[:, columns(a, 1)]), preferred_element_type=jnp.float32
        )
        peaks[a][...] = top

    cache_copy(prompt).wait()

    def block(s, bias):
        at = pl.multiple_of(s * span, span)
        scores = [
            scores_of(queries_of(a), cache_buf[prompt, pl.ds(at, span), columns(a, 0)])
            for a in range(kv_heads)
        ]
        for a in range(kv_heads):
            here = scores[a] if bias is None else scores[a] + bias
            before = peaks[a][...]
            top = jnp.maximum(before, jnp.max(here, axis=-1, keepdims=True))
            weights = jnp.exp2(
                here - jnp.concatenate([top] * (span // HEAD_SIZE), axis=1)
            ).astype(jnp.bfloat16)
            fade = jnp.exp2(before - top)
            values = cache_buf[prompt, pl.ds(at, span), columns(a, 1)]
            accs[a][...] = accs[a][...] * jnp.concatenate([fade, fade], axis=1) + jnp.dot(
                weights, with_ones(values), preferred_element_type=jnp.float32
            )
            peaks[a][...] = top

    def step(s, carry):
        block(s, None)
        return carry

    lax.fori_loop(0, full, step, 0)

    @pl.when(full * span < live)
    def _():
        block(full, jnp.where(lane + full * span < live, 0.0, MASKED))

    for a in range(kv_heads):
        result = accs[a][:, :HEAD_SIZE] / accs[a][:, HEAD_SIZE:]
        for h in range(group):
            o_ref[:, (a * group + h) * HEAD_SIZE : (a * group + h + 1) * HEAD_SIZE] = result[
                h * tokens : (h + 1) * tokens
            ].astype(o_ref.dtype)


def prefill_attention(queries, prefix_cache, first, count, new_kv, prefix_len):
    width = queries.shape[1]
    positions, page = prefix_cache.shape[2:]
    kv_heads = page // (2 * HEAD_SIZE)
    group = width // HEAD_SIZE // kv_heads
    span = tile_of(positions, 512)
    rows = group * PROMPT_TOKENS
    return pl.pallas_call(
        functools.partial(prefill_kernel, kv_heads, group, span, first),
        grid_spec=pltpu.PrefetchScalarGridSpec(
            num_scalar_prefetch=1,
            grid=(count,),
            in_specs=[
                pl.BlockSpec((PROMPT_TOKENS, width), lambda g, n: (g, 0)),
                pl.BlockSpec(memory_space=pl.ANY),
                pl.BlockSpec((PROMPT_TOKENS, page), lambda g, n: (g, 0)),
            ],
            out_specs=pl.BlockSpec((PROMPT_TOKENS, width), lambda g, n: (g, 0)),
            scratch_shapes=[
                pltpu.VMEM((count, positions, page), jnp.bfloat16),
                pltpu.SemaphoreType.DMA((count,)),
            ]
            + [pltpu.VMEM((rows, 2 * HEAD_SIZE), jnp.float32)] * kv_heads
            + [pltpu.VMEM((rows, HEAD_SIZE), jnp.float32)] * kv_heads,
        ),
        out_shape=jax.ShapeDtypeStruct((count * PROMPT_TOKENS, width), jnp.bfloat16),
        compiler_params=pltpu.CompilerParams(vmem_limit_bytes=KERNEL_VMEM),
        cost_estimate=pl.CostEstimate(
            flops=8 * count * rows * kv_heads * (positions + PROMPT_TOKENS) * HEAD_SIZE // COST_SHARE,
            bytes_accessed=(2 * count * positions * page) // COST_SHARE,
            transcendentals=count * rows * kv_heads * (positions + PROMPT_TOKENS),
        ),
        name="prefill_attention",
    )(prefix_len, queries, *in_hbm([prefix_cache]), new_kv)


def decode_kernel(
    kv_heads, batch, len_ref, row_ref, q_ref, cache_ref, landed_ref, fresh_ref, o_ref, acc, peak
):
    row_count, context = cache_ref.shape[1], cache_ref.shape[2]
    per_row = q_ref.shape[2]
    steps = fresh_ref.shape[1]
    rows = batch * per_row
    row_of = lax.broadcasted_iota(jnp.int32, (rows, batch * context), 0) // per_row
    key_row = lax.broadcasted_iota(jnp.int32, (rows, batch * context), 1) // context
    key_at = lax.rem(lax.broadcasted_iota(jnp.int32, (rows, batch * context), 1), context)
    fresh_query = lax.broadcasted_iota(jnp.int32, (rows, batch * steps), 0)
    fresh_key = lax.broadcasted_iota(jnp.int32, (rows, batch * steps), 1)
    fresh_live = (fresh_key // steps == fresh_query // per_row) & (
        lax.rem(fresh_key, steps) <= lax.rem(fresh_query, per_row) // (per_row // steps)
    )

    def cached(b, carry):
        first = b * batch
        live = jnp.zeros_like(key_row)
        for r in range(batch):
            live = jnp.where(key_row == r, len_ref[first + r], live)
        cache_live = (row_of == key_row) & (key_at < live)
        pages = cache_ref[0, pl.ds(first, batch)].reshape(batch * context, cache_ref.shape[3])
        fresh = fresh_ref[pl.ds(first, batch)].reshape(batch * steps, fresh_ref.shape[2])
        for a in range(kv_heads):
            queries = q_ref[pl.ds(first, batch), a].reshape(rows, HEAD_SIZE).astype(jnp.bfloat16)
            k_at, v_at = 2 * a * HEAD_SIZE, (2 * a + 1) * HEAD_SIZE
            scores = scores_of(queries, pages[:, k_at : k_at + HEAD_SIZE])
            scores = jnp.where(cache_live, scores, MASKED)
            recent = scores_of(queries, fresh[:, k_at : k_at + HEAD_SIZE].astype(jnp.bfloat16))
            recent = jnp.where(fresh_live, recent, MASKED)
            top = jnp.maximum(
                jnp.max(scores, axis=-1, keepdims=True), jnp.max(recent, axis=-1, keepdims=True)
            )
            weights = jnp.exp2(scores - top).astype(jnp.bfloat16)
            recent = jnp.exp2(recent - top).astype(jnp.bfloat16)
            total = jnp.dot(
                weights,
                with_ones(pages[:, v_at : v_at + HEAD_SIZE]),
                preferred_element_type=jnp.float32,
            ) + jnp.dot(
                recent,
                with_ones(fresh[:, v_at : v_at + HEAD_SIZE].astype(jnp.bfloat16)),
                preferred_element_type=jnp.float32,
            )
            acc[pl.ds(first, batch), a] = total.reshape(batch, per_row, 2 * HEAD_SIZE)
            peak[pl.ds(first, batch), a] = jnp.broadcast_to(top, (rows, HEAD_SIZE)).reshape(
                batch, per_row, HEAD_SIZE
            )
        return carry

    lax.fori_loop(0, row_count // batch, cached, 0)

    def arrival(slot, carry):
        row = row_ref[slot]

        @pl.when(row >= 0)
        def _():
            for a in range(kv_heads):
                queries = q_ref[row, a].astype(jnp.bfloat16)
                k_at, v_at = 2 * a * HEAD_SIZE, (2 * a + 1) * HEAD_SIZE
                scores = scores_of(queries, landed_ref[slot, :, k_at : k_at + HEAD_SIZE])
                before = peak[row, a]
                top = jnp.maximum(before, jnp.max(scores, axis=-1, keepdims=True))
                weights = jnp.exp2(scores - top[:, :1]).astype(jnp.bfloat16)
                fade = jnp.exp2(before - top)
                acc[row, a] = acc[row, a] * jnp.concatenate([fade, fade], axis=1) + jnp.dot(
                    weights,
                    with_ones(landed_ref[slot, :, v_at : v_at + HEAD_SIZE]),
                    preferred_element_type=jnp.float32,
                )

        return carry

    lax.fori_loop(0, row_ref.shape[0], arrival, 0)
    o_ref[...] = (acc[:, :, :, :HEAD_SIZE] / acc[:, :, :, HEAD_SIZE:]).astype(o_ref.dtype)


def decode_attention(queries, dec_cache, dec_len, landed, slot_rows, fresh, held=()):
    row_count, kv_heads, per_row = queries.shape[:3]
    context = dec_cache.shape[2]
    batch = max(1, min(row_count, 2 * HEAD_SIZE // context))
    whole = lambda array: pl.BlockSpec(array.shape, lambda g, *_: (0,) * array.ndim)
    return pl.pallas_call(
        without(functools.partial(decode_kernel, kv_heads, batch), 6, len(held)),
        grid_spec=pltpu.PrefetchScalarGridSpec(
            num_scalar_prefetch=2,
            grid=(1,),
            in_specs=[whole(queries), whole(dec_cache), whole(landed), whole(fresh)]
            + [pl.BlockSpec(memory_space=pl.ANY)] * len(held),
            out_specs=whole(queries),
            scratch_shapes=[
                pltpu.VMEM((row_count, kv_heads, per_row, 2 * HEAD_SIZE), jnp.float32),
                pltpu.VMEM((row_count, kv_heads, per_row, HEAD_SIZE), jnp.float32),
            ],
        ),
        out_shape=jax.ShapeDtypeStruct(queries.shape, jnp.float32),
        compiler_params=pltpu.CompilerParams(vmem_limit_bytes=KERNEL_VMEM),
        cost_estimate=pl.CostEstimate(
            flops=8 * queries.size * batch * context // COST_SHARE,
            bytes_accessed=(2 * dec_cache.size + 2 * landed.size) // COST_SHARE,
            transcendentals=queries.size * batch * context // HEAD_SIZE,
        ),
        name="decode_attention",
    )(dec_len, slot_rows, queries, dec_cache, landed, fresh, *held)


def shards(
    prefill_x,
    norm_gain,
    w_q,
    q_scale,
    key_value_weight,
    key_value_scale,
    w_o,
    o_scale,
    prefix_cache,
    prefix_len,
    dec_x,
    dec_cache,
    dec_len,
    place,
):
    prompts_total = prefix_cache.shape[1]
    row_count = dec_cache.shape[1]
    page_width = prefix_cache.shape[3]
    kv_heads = page_width // (2 * HEAD_SIZE)
    query_heads = w_q.shape[1] // HEAD_SIZE
    group_size = query_heads // kv_heads
    steps = dec_x.shape[0]
    section_count = lax.axis_size("section")
    section_index = lax.axis_index("section")
    tensor_count = lax.axis_size("tensor")
    tensor_index = lax.axis_index("tensor")
    head_span = max(1, 8 // query_heads)
    span_bits = head_span.bit_length() - 1
    block_width = w_o.shape[1] // tensor_count
    scales = (q_scale * EXP2_FACTOR, key_value_scale)

    weights = (norm_gain, w_q, key_value_weight)

    def kv_of_head(new_kv):
        for bit_number in range(span_bits):
            partner = partner_2(new_kv, "tensor", bit_number)
            new_kv = joined(new_kv, partner, bit_number, 1, tensor_index)
        return new_kv

    def finished(x, terms):
        total = sum(term.astype(jnp.float32) for term in terms)
        return (x.astype(jnp.float32) + total * o_scale).astype(jnp.bfloat16)

    dec_rows = dec_x.reshape(steps * row_count, -1)
    bounds = sorted({0, min(1, prompts_total - 1), prompts_total - 1, prompts_total})
    spans = list(zip(bounds[:-1], bounds[1:]))
    on_line = tensor_count == 4 and len(spans) == 3
    order = jnp.stack(
        line_order(tensor_index) if on_line else list(range(tensor_count))
    ).astype(jnp.int32)
    chunks = [prefill_x[first * PROMPT_TOKENS : last * PROMPT_TOKENS] for first, last in spans]
    blocks = chunks[:-1] + [jnp.concatenate([chunks[-1], dec_rows], axis=0)]
    if on_line:
        begin = chunks[0].shape[0]
        rest, dec_rest = after_all((prefill_x[begin:], dec_rows), blocks[0])
        blocks[1] = rest[: chunks[1].shape[0]]
        blocks[2] = jnp.concatenate([rest[chunks[1].shape[0] :], dec_rest], axis=0)
    pages = []

    def attention(k, queries):
        first, last = spans[k]
        return prefill_attention(queries, prefix_cache, first, last - first, pages[k], prefix_len)

    def keep(new_kv):
        new_kv = kv_of_head(new_kv)
        pages.append(new_kv[: chunks[len(pages)].shape[0]])
        return new_kv

    def back(attended, held=()):
        far, near, partner, own = project_out(
            attended, w_o, order[::-1], block_width, held=held
        )
        return LineScatter(own, partner, near, far, "tensor")

    def back_whole(attended):
        return project_out(
            attended, w_o, jnp.arange(tensor_count, dtype=jnp.int32), block_width, stacked=True
        )

    def summed(partial):
        return [lax.psum_scatter(partial, "tensor", scatter_dimension=0, tiled=False)]

    if on_line:
        first = LineGather(blocks[0], "tensor")
        first.second()
        first.third()
        second = LineGather(
            blocks[1], "tensor", (first.outer_far,), (first.outer, first.middle_far)
        )
        queries, new_kv = project_part(first.slots(), order, *weights, None, scales)
        keep(new_kv)
        attended = attention(0, queries)
        second.second(attended)
        sums = [back(attended, (second.partner, second.middle))]

        begun = project_part(
            [[second.block], [second.partner]], order[:2],
            *weights,
            None,
            None,
            (sums[0].own, second.outer),
        )
        second.third(begun[2])
        sums[0].second(begun[2])
        sums[0].third()
        third = LineGather(
            blocks[2], "tensor", (second.outer_far,), (second.outer, second.middle_far, begun[2])
        )
        queries, new_kv = project_part(
            second.slots()[2:], order[2:], *weights, begun, scales, sums[0].second_hop
        )
        keep(new_kv)
        third.second(queries)
        attended = attention(1, after(queries, third.partner, third.middle))
        third.third(attended)
        sums.append(back(attended, (third.outer, third.middle_far)))
        begun = project_part(
            [[third.block], [third.partner]],
            order[:2],
            *weights,
            None,
            None,
            (sums[1].own,),
        )
        queries, new_kv = project_part(
            third.slots()[2:], order[2:], *weights, begun, scales, sums[0].terms[1:]
        )
        new_kv = keep(new_kv)
        sums[1].second(queries)
        sums[1].third_begin()
        sums.append(back(attention(2, after(queries, *sums[1].first_hop)), sums[1].second_hop))
        sums[1].third_start(sums[2].own)
        hold = (sums[2].own,)
    else:
        terms_of = []
        for k, block in enumerate(blocks):
            whole = lax.all_gather(block, "tensor", axis=1, tiled=True)
            queries, new_kv = project_part([[whole]], order[:1], *weights, None, scales)
            new_kv = keep(new_kv)
            terms_of.append(summed(back_whole(attention(k, queries))))
        hold = ()
    tokens = chunks[-1].shape[0]
    dec_queries, fresh_kv = queries[tokens:], new_kv[tokens:]

    own_block = after(jnp.concatenate(pages, axis=0), *hold).reshape(
        prompts_total, PROMPT_TOKENS, page_width
    )
    owners = (place // row_count).reshape(section_count, prompts_total)
    targets = (place % row_count).reshape(section_count, prompts_total)
    owner_hits = (owners[:, :, None] == jnp.arange(section_count)[None, None, :]).astype(jnp.int32)
    slot_ranks = jnp.sum((jnp.cumsum(owner_hits, axis=1) - owner_hits) * owner_hits, axis=2)
    capacity = prompts_total // 2
    slot_ids = jnp.arange(capacity)
    sending = lax.dynamic_index_in_dim(owner_hits, section_index, 0, keepdims=False)
    my_ranks = lax.dynamic_index_in_dim(slot_ranks, section_index, 0, keepdims=False)
    selector = (
        jnp.transpose(sending)[:, None, :] * (my_ranks[None, None, :] == slot_ids[None, :, None])
    ).astype(jnp.bfloat16)
    here = (owners == section_index)[:, None, :] & (
        slot_ranks[:, None, :] == slot_ids[None, :, None]
    )
    slot_rows = jnp.sum(jnp.where(here, targets[:, None, :] + 1, 0), axis=2) - 1
    outgoing = jnp.einsum(
        "skp,pcw->skcw", selector, own_block, preferred_element_type=jnp.float32
    ).astype(jnp.bfloat16)
    received = lax.all_to_all(outgoing, "section", split_axis=0, concat_axis=0, tiled=True)
    if on_line:
        sums[2].second(received)
        hold = sums[2].first_hop
    landed = received.reshape(section_count * capacity, PROMPT_TOKENS, page_width)

    dec_queries = jnp.transpose(
        dec_queries.reshape(steps, row_count, kv_heads, group_size, HEAD_SIZE), (1, 2, 0, 3, 4)
    ).reshape(row_count, kv_heads, steps * group_size, HEAD_SIZE)
    fresh = jnp.transpose(fresh_kv.reshape(steps, row_count, page_width), (1, 0, 2))
    dec_attended = decode_attention(
        dec_queries.astype(jnp.float32),
        dec_cache,
        dec_len,
        landed,
        slot_rows.reshape(-1).astype(jnp.int32),
        fresh.astype(jnp.float32),
        hold,
    )
    dec_attended = (
        jnp.transpose(
            dec_attended.reshape(row_count, kv_heads, steps, group_size, HEAD_SIZE), (2, 0, 1, 3, 4)
        )
        .reshape(steps * row_count, -1)
        .astype(jnp.bfloat16)
    )
    if on_line:
        to = [(tensor_index + shift) % tensor_count for shift in range(tensor_count)]
        own, *parts = project_out(
            dec_attended,
            w_o,
            jnp.stack(to).astype(jnp.int32),
            block_width,
            held=corners(sums[1].terms[1:]),
        )
        sums[2].third(own)
        dec_terms = [own] + [
            lax.ppermute(
                part, "tensor", [(j, (j + shift) % tensor_count) for j in range(tensor_count)]
            )
            for shift, part in enumerate(parts, 1)
        ]
        terms_of = [each.terms for each in sums]
    else:
        dec_terms = summed(back_whole(dec_attended))
    prefill_out = jnp.concatenate(
        [finished(x, terms) for x, terms in zip(chunks, terms_of)], axis=0
    )
    decode_out = finished(dec_rows, dec_terms).reshape(dec_x.shape)
    return (prefill_out, decode_out)


def solution(mesh):
    in_specs = (
        P(("groups", "section"), "tensor"),
        P(),
        P(None, "tensor"),
        P("tensor"),
        P(None, "tensor"),
        P("tensor"),
        P("tensor", None),
        P("tensor"),
        P("tensor", ("groups", "section"), None, None),
        P(("groups", "section")),
        P(None, ("groups", "section"), "tensor"),
        P("tensor", ("groups", "section"), None, None),
        P(("groups", "section")),
        P("groups"),
    )
    out_specs = (P(("groups", "section"), "tensor"), P(None, ("groups", "section"), "tensor"))
    return jax.shard_map(shards, mesh=mesh, in_specs=in_specs, out_specs=out_specs, check_vma=False)
```

```python
import functools
import math

import jax
import jax.numpy as jnp
from jax import lax
from jax.experimental import pallas as pl
from jax.experimental.pallas import tpu as pltpu
from jax.sharding import PartitionSpec as P

HEAD_SIZE = 128
PROMPT_TOKENS = 128
KERNEL_VMEM = 36 << 20
WEIGHT_BUFFERS = 8
COST_SHARE = 256
EXP2_FACTOR = math.log2(math.e) / math.sqrt(HEAD_SIZE)
MASKED = -1e30


def partner_2(block, axis, distance):
    count = lax.axis_size(axis)
    route = []
    for low in range(count):
        high = low | 1 << distance
        if high != low and high < count:
            route += [(low, high), (high, low)]
    return lax.ppermute(block, axis, route)


def joined(portion, partner, bit_number, concat_dim, tensor_index):
    upper_half = tensor_index // 2**bit_number % 2 == 1
    lower_first = jnp.concatenate([portion, partner], axis=concat_dim)
    upper_first = jnp.concatenate([partner, portion], axis=concat_dim)
    return jnp.where(upper_half, upper_first, lower_first)


def tile_of(extent, most):
    tile = extent
    while tile > most and tile % 2 == 0:
        tile //= 2
    return tile


def after(value, *others):
    return lax.optimization_barrier((value,) + others)[0]


def after_all(values, *others):
    return lax.optimization_barrier(tuple(values) + others)[: len(values)]


def line_order(index):
    low = index < 2
    return [index, index ^ 1, jnp.where(low, 2, 1), jnp.where(low, 3, 0)]


OUTER = [(0, 1), (1, 0), (2, 3), (3, 2)]
MIDDLE = [(1, 2), (2, 1)]
INWARD = [(0, 1), (3, 2)]
OUTWARD = [(1, 0), (2, 3)]


class LineGather:
    def __init__(self, block, axis, outer_held=(), middle_held=()):
        self.block, self.axis = block, axis
        self.partner = lax.ppermute(after(block, *outer_held), axis, OUTER)
        self.middle = lax.ppermute(after(block, *middle_held), axis, MIDDLE)

    def second(self, *held):
        partner, middle = after_all((self.partner, self.middle), *held)
        self.outer = lax.ppermute(middle, self.axis, OUTWARD)
        self.middle_far = lax.ppermute(partner, self.axis, MIDDLE)

    def third(self, *held):
        self.outer_far = lax.ppermute(after(self.middle_far, *held), self.axis, OUTWARD)

    def slots(self):
        return [
            [self.block],
            [self.partner],
            [self.middle, self.outer],
            [self.middle_far, self.outer_far],
        ]


def corners(arrays):
    return [array[:HEAD_SIZE, :HEAD_SIZE] for array in arrays]


def added(*terms):
    total = sum(term.astype(jnp.float32) for term in terms)
    return total.astype(terms[0].dtype)


class LineScatter:
    def __init__(self, own, partner, near, far, axis):
        self.own, self.partner, self.near, self.far = own, partner, near, far
        self.axis = axis
        self.far_in = lax.ppermute(far, axis, INWARD)

    def second(self, *held):
        far, near = after_all((added(self.far, self.far_in), self.near), *held)
        self.first_hop = (far,)
        self.near_in = lax.ppermute(near, self.axis, INWARD)
        self.far_out = lax.ppermute(far, self.axis, MIDDLE)

    def third(self, *held):
        self.third_begin()
        self.third_start(*held)

    def third_begin(self):
        self.second_hop = (
            added(self.near, self.near_in),
            added(self.partner, self.far_out),
        )

    def third_start(self, *held):
        near, partner = after_all(self.second_hop, *held)
        near = lax.ppermute(near, self.axis, MIDDLE)
        partner = lax.ppermute(partner, self.axis, OUTER)
        self.terms = [self.own, near, partner]


def in_hbm(arrays):
    return [pltpu.with_memory_space_constraint(array, pltpu.HBM) for array in arrays]


def without(kernel, first, count):
    return lambda *refs: kernel(*refs[:first], *refs[first + count :])


def qkv_kernel(counts, begun, ended, tile, order, *refs):
    refs = list(refs)
    arrays = sum(counts)
    xs = [refs.pop(0) for _ in range(arrays)]
    gain_ref, wq_ref, wkv_ref = (refs.pop(0) for _ in range(3))
    sums_in = [refs.pop(0) for _ in range(3)] if begun else []
    if ended:
        qs_ref, kvs_ref, q_ref, kv_ref, accq, acckv, squares = (refs.pop(0) for _ in range(7))
    else:
        accq, acckv, squares = (refs.pop(0) for _ in range(3))
    x_bufs = [refs.pop(0) for _ in range(arrays)]
    wq_buf, wkv_buf, x_sem, w_sem, sum_sem = refs
    per = x_bufs[0].shape[1] // tile
    steps = len(counts) * per
    ahead = min(steps, wq_buf.shape[0])

    def weight_copies(step):
        buffer = lax.rem(step, ahead)
        at = pl.multiple_of((order[step // per] * per + lax.rem(step, per)) * tile, tile)
        return [
            pltpu.make_async_copy(ref.at[pl.ds(at, tile)], buf.at[buffer], w_sem.at[w, buffer])
            for w, (ref, buf) in enumerate([(wq_ref, wq_buf), (wkv_ref, wkv_buf)])
        ]

    x_copies = [
        pltpu.make_async_copy(ref, buf, x_sem.at[a]) for a, (ref, buf) in enumerate(zip(xs, x_bufs))
    ]
    sum_copies = [
        pltpu.make_async_copy(ref, acc, sum_sem.at[a])
        for a, (ref, acc) in enumerate(zip(sums_in, (accq, acckv, squares)))
    ]
    for copy in x_copies[: counts[0]] + sum_copies:
        copy.start()
    for step in range(ahead):
        for copy in weight_copies(step):
            copy.start()
    for copy in x_copies[counts[0] :]:
        copy.start()
    for copy in sum_copies:
        copy.wait()
    if not begun:
        accq[...] = jnp.zeros_like(accq)
        acckv[...] = jnp.zeros_like(acckv)
        squares[...] = jnp.zeros_like(squares)

    taken = 0
    for s, count in enumerate(counts):
        for copy in x_copies[taken : taken + count]:
            copy.wait()
        bufs = x_bufs[taken : taken + count]
        taken += count

        def body(j, carry, s=s, bufs=bufs):
            step = s * per + j
            for copy in weight_copies(step):
                copy.wait()
            at = pl.multiple_of(j * tile, tile)
            values = sum(buf[:, pl.ds(at, tile)].astype(jnp.float32) for buf in bufs)
            gain = gain_ref[:, pl.ds(pl.multiple_of((order[s] * per + j) * tile, tile), tile)]
            squares[...] += jnp.broadcast_to(
                jnp.sum(values * values, axis=-1, keepdims=True), squares.shape
            )
            scaled = (values * gain).astype(jnp.bfloat16)
            buffer = lax.rem(step, ahead)
            accq[...] += jnp.dot(scaled, wq_buf[buffer], preferred_element_type=jnp.float32)
            acckv[...] += jnp.dot(scaled, wkv_buf[buffer], preferred_element_type=jnp.float32)

            @pl.when(step + ahead < steps)
            def _():
                for copy in weight_copies(step + ahead):
                    copy.start()

            return carry

        lax.fori_loop(0, per, body, 0)
    if ended:
        root = lax.rsqrt(squares[:, :1] / ended + 1e-05)
        q_ref[...] = (accq[...] * root * qs_ref[...]).astype(q_ref.dtype)
        kv_ref[...] = (acckv[...] * root * kvs_ref[...]).astype(kv_ref.dtype)


def project_part(slots, order, norm_gain, w_q, kv_weight, begun, scales, held=()):
    rows, depth = slots[0][0].shape
    tile = tile_of(depth, 512)
    q_cols, kv_cols = w_q.shape[1], kv_weight.shape[1]
    arrays = [array for slot in slots for array in slot]

    def whole(shape):
        return pl.BlockSpec(shape, lambda g, order: (0,) * len(shape))

    anywhere = pl.BlockSpec(memory_space=pl.ANY)
    operands = arrays + [norm_gain.reshape(1, -1)] + in_hbm([w_q, kv_weight])
    in_specs = [anywhere] * len(arrays) + [whole((1, norm_gain.shape[0])), anywhere, anywhere]
    sums = [(rows, q_cols), (rows, kv_cols), (rows, HEAD_SIZE)]
    if begun is not None:
        operands += in_hbm(begun)
        in_specs += [anywhere] * 3
    if scales is not None:
        operands += [scale.reshape(1, -1) for scale in scales]
        in_specs += [whole((1, q_cols)), whole((1, kv_cols))]
        out_shapes = [jax.ShapeDtypeStruct(shape, jnp.bfloat16) for shape in sums[:2]]
        scratch = [pltpu.VMEM(shape, jnp.float32) for shape in sums]
    else:
        out_shapes = [pltpu.HBM(shape, jnp.float32) for shape in sums]
        scratch = []
    kernel = functools.partial(
        qkv_kernel,
        [len(slot) for slot in slots],
        begun is not None,
        0 if scales is None else w_q.shape[0],
        tile,
    )
    return pl.pallas_call(
        without(kernel, 1 + len(operands), len(held)),
        grid_spec=pltpu.PrefetchScalarGridSpec(
            num_scalar_prefetch=1,
            grid=(1,),
            in_specs=in_specs + [anywhere] * len(held),
            out_specs=[whole(out.shape) for out in out_shapes],
            scratch_shapes=scratch
            + [pltpu.VMEM((rows, depth), jnp.bfloat16) for _ in arrays]
            + [
                pltpu.VMEM((WEIGHT_BUFFERS, tile, q_cols), jnp.bfloat16),
                pltpu.VMEM((WEIGHT_BUFFERS, tile, kv_cols), jnp.bfloat16),
                pltpu.SemaphoreType.DMA((len(arrays),)),
                pltpu.SemaphoreType.DMA((2, WEIGHT_BUFFERS)),
                pltpu.SemaphoreType.DMA((3,)),
            ],
        ),
        out_shape=out_shapes,
        compiler_params=pltpu.CompilerParams(vmem_limit_bytes=KERNEL_VMEM),
        cost_estimate=pl.CostEstimate(
            flops=2 * rows * depth * len(slots) * (q_cols + kv_cols) // COST_SHARE,
            bytes_accessed=(2 * depth * len(slots) * (q_cols + kv_cols)) // COST_SHARE,
            transcendentals=0,
        ),
        name="norm_qkv",
    )(order, *operands, *held)


def out_kernel(count, stacked, tile, order, x_ref, w_ref, *refs):
    if stacked:
        outs, refs = [refs[0].at[s] for s in range(count)], refs[1:]
    else:
        outs, refs = refs[:count], refs[count:]
    x_buf, w_buf, x_sem, w_sem, o_sem = refs[:5]
    o_bufs = refs[5:]
    per = o_bufs[0].shape[1] // tile
    steps = count * per
    ahead = min(steps, w_buf.shape[0])

    def weight_copy(step):
        at = pl.multiple_of((order[step // per] * per + lax.rem(step, per)) * tile, tile)
        buffer = lax.rem(step, ahead)
        return pltpu.make_async_copy(
            w_ref.at[:, pl.ds(at, tile)], w_buf.at[buffer], w_sem.at[buffer]
        )

    x_copy = pltpu.make_async_copy(x_ref, x_buf, x_sem)
    x_copy.start()
    for step in range(ahead):
        weight_copy(step).start()
    x_copy.wait()
    o_copies = []
    for s, (out, o_buf) in enumerate(zip(outs, o_bufs)):

        def body(j, carry, s=s, o_buf=o_buf):
            step = s * per + j
            weight_copy(step).wait()
            o_buf[:, pl.ds(pl.multiple_of(j * tile, tile), tile)] = jnp.dot(
                x_buf[...], w_buf[lax.rem(step, ahead)], preferred_element_type=jnp.float32
            ).astype(o_buf.dtype)

            @pl.when(step + ahead < steps)
            def _():
                weight_copy(step + ahead).start()

            return carry

        lax.fori_loop(0, per, body, 0)
        o_copies.append(pltpu.make_async_copy(o_buf, out, o_sem.at[s]))
        o_copies[-1].start()
    for copy in o_copies:
        copy.wait()


def project_out(attended, w_o, order, block, stacked=False, held=()):
    rows, depth = attended.shape
    tile = tile_of(block, 512)
    count = order.shape[0]
    anywhere = pl.BlockSpec(memory_space=pl.ANY)
    return pl.pallas_call(
        without(functools.partial(out_kernel, count, stacked, tile), 3, len(held)),
        grid_spec=pltpu.PrefetchScalarGridSpec(
            num_scalar_prefetch=1,
            grid=(1,),
            in_specs=[anywhere] * (2 + len(held)),
            out_specs=anywhere if stacked else [anywhere] * count,
            scratch_shapes=[
                pltpu.VMEM((rows, depth), jnp.bfloat16),
                pltpu.VMEM((WEIGHT_BUFFERS, depth, tile), jnp.bfloat16),
                pltpu.SemaphoreType.DMA,
                pltpu.SemaphoreType.DMA((WEIGHT_BUFFERS,)),
                pltpu.SemaphoreType.DMA((count,)),
            ]
            + [pltpu.VMEM((rows, block), jnp.bfloat16)] * count,
        ),
        out_shape=jax.ShapeDtypeStruct((count, rows, block), jnp.bfloat16)
        if stacked
        else [jax.ShapeDtypeStruct((rows, block), jnp.bfloat16)] * count,
        compiler_params=pltpu.CompilerParams(vmem_limit_bytes=KERNEL_VMEM),
        cost_estimate=pl.CostEstimate(
            flops=2 * rows * depth * count * block // COST_SHARE,
            bytes_accessed=(2 * depth * count * block) // COST_SHARE,
            transcendentals=0,
        ),
        name="project_out",
    )(order, attended, *in_hbm([w_o]), *held)


def with_ones(values):
    return jnp.concatenate([values, jnp.ones_like(values)], axis=1)


def scores_of(queries, keys):
    return lax.dot_general(
        queries, keys, (((1,), (1,)), ((), ())), preferred_element_type=jnp.float32
    )


def prefill_kernel(
    kv_heads, group, span, first, len_ref, q_ref, cache_ref, new_ref, o_ref, cache_buf, sem, *scratch
):
    accs, peaks = scratch[:kv_heads], scratch[kv_heads:]
    prompt = pl.program_id(0)

    def cache_copy(g):
        return pltpu.make_async_copy(cache_ref.at[0, first + g], cache_buf.at[g], sem.at[g])

    @pl.when(prompt == 0)
    def _():
        for g in range(cache_buf.shape[0]):
            cache_copy(g).start()

    tokens = q_ref.shape[0]
    rows = group * tokens
    live = len_ref[first + prompt]
    full = live // span
    query_token = lax.rem(lax.broadcasted_iota(jnp.int32, (rows, tokens), 0), tokens)
    key_token = lax.broadcasted_iota(jnp.int32, (rows, tokens), 1)
    causal = key_token <= query_token
    lane = lax.broadcasted_iota(jnp.int32, (1, span), 1)

    def queries_of(a):
        return jnp.concatenate(
            [
                q_ref[:, (a * group + h) * HEAD_SIZE : (a * group + h + 1) * HEAD_SIZE]
                for h in range(group)
            ],
            axis=0,
        )

    def columns(a, part):
        return pl.ds((2 * a + part) * HEAD_SIZE, HEAD_SIZE)

    for a in range(kv_heads):
        scores = jnp.where(causal, scores_of(queries_of(a), new_ref[:, columns(a, 0)]), MASKED)
        top = jnp.broadcast_to(jnp.max(scores, axis=-1, keepdims=True), (rows, HEAD_SIZE))
        weights = jnp.exp2(scores - top[:, :tokens]).astype(jnp.bfloat16)
        accs[a][...] = jnp.dot(
            weights, with_ones(new_ref[:, columns(a, 1)]), preferred_element_type=jnp.float32
        )
        peaks[a][...] = top

    cache_copy(prompt).wait()

    def block(s, bias):
        at = pl.multiple_of(s * span, span)
        scores = [
            scores_of(queries_of(a), cache_buf[prompt, pl.ds(at, span), columns(a, 0)])
            for a in range(kv_heads)
        ]
        for a in range(kv_heads):
            here = scores[a] if bias is None else scores[a] + bias
            before = peaks[a][...]
            top = jnp.maximum(before, jnp.max(here, axis=-1, keepdims=True))
            weights = jnp.exp2(
                here - jnp.concatenate([top] * (span // HEAD_SIZE), axis=1)
            ).astype(jnp.bfloat16)
            fade = jnp.exp2(before - top)
            values = cache_buf[prompt, pl.ds(at, span), columns(a, 1)]
            accs[a][...] = accs[a][...] * jnp.concatenate([fade, fade], axis=1) + jnp.dot(
                weights, with_ones(values), preferred_element_type=jnp.float32
            )
            peaks[a][...] = top

    def step(s, carry):
        block(s, None)
        return carry

    lax.fori_loop(0, full, step, 0)

    @pl.when(full * span < live)
    def _():
        block(full, jnp.where(lane + full * span < live, 0.0, MASKED))

    for a in range(kv_heads):
        result = accs[a][:, :HEAD_SIZE] / accs[a][:, HEAD_SIZE:]
        for h in range(group):
            o_ref[:, (a * group + h) * HEAD_SIZE : (a * group + h + 1) * HEAD_SIZE] = result[
                h * tokens : (h + 1) * tokens
            ].astype(o_ref.dtype)


def prefill_attention(queries, prefix_cache, first, count, new_kv, prefix_len):
    width = queries.shape[1]
    positions, page = prefix_cache.shape[2:]
    kv_heads = page // (2 * HEAD_SIZE)
    group = width // HEAD_SIZE // kv_heads
    span = tile_of(positions, 512)
    rows = group * PROMPT_TOKENS
    return pl.pallas_call(
        functools.partial(prefill_kernel, kv_heads, group, span, first),
        grid_spec=pltpu.PrefetchScalarGridSpec(
            num_scalar_prefetch=1,
            grid=(count,),
            in_specs=[
                pl.BlockSpec((PROMPT_TOKENS, width), lambda g, n: (g, 0)),
                pl.BlockSpec(memory_space=pl.ANY),
                pl.BlockSpec((PROMPT_TOKENS, page), lambda g, n: (g, 0)),
            ],
            out_specs=pl.BlockSpec((PROMPT_TOKENS, width), lambda g, n: (g, 0)),
            scratch_shapes=[
                pltpu.VMEM((count, positions, page), jnp.bfloat16),
                pltpu.SemaphoreType.DMA((count,)),
            ]
            + [pltpu.VMEM((rows, 2 * HEAD_SIZE), jnp.float32)] * kv_heads
            + [pltpu.VMEM((rows, HEAD_SIZE), jnp.float32)] * kv_heads,
        ),
        out_shape=jax.ShapeDtypeStruct((count * PROMPT_TOKENS, width), jnp.bfloat16),
        compiler_params=pltpu.CompilerParams(vmem_limit_bytes=KERNEL_VMEM),
        cost_estimate=pl.CostEstimate(
            flops=8 * count * rows * kv_heads * (positions + PROMPT_TOKENS) * HEAD_SIZE // COST_SHARE,
            bytes_accessed=(2 * count * positions * page) // COST_SHARE,
            transcendentals=count * rows * kv_heads * (positions + PROMPT_TOKENS),
        ),
        name="prefill_attention",
    )(prefix_len, queries, *in_hbm([prefix_cache]), new_kv)


def decode_kernel(
    kv_heads, batch, len_ref, row_ref, q_ref, cache_ref, landed_ref, fresh_ref, o_ref, acc, peak
):
    row_count, context = cache_ref.shape[1], cache_ref.shape[2]
    per_row = q_ref.shape[2]
    steps = fresh_ref.shape[1]
    rows = batch * per_row
    row_of = lax.broadcasted_iota(jnp.int32, (rows, batch * context), 0) // per_row
    key_row = lax.broadcasted_iota(jnp.int32, (rows, batch * context), 1) // context
    key_at = lax.rem(lax.broadcasted_iota(jnp.int32, (rows, batch * context), 1), context)
    fresh_query = lax.broadcasted_iota(jnp.int32, (rows, batch * steps), 0)
    fresh_key = lax.broadcasted_iota(jnp.int32, (rows, batch * steps), 1)
    fresh_live = (fresh_key // steps == fresh_query // per_row) & (
        lax.rem(fresh_key, steps) <= lax.rem(fresh_query, per_row) // (per_row // steps)
    )

    def cached(b, carry):
        first = b * batch
        live = jnp.zeros_like(key_row)
        for r in range(batch):
            live = jnp.where(key_row == r, len_ref[first + r], live)
        cache_live = (row_of == key_row) & (key_at < live)
        pages = cache_ref[0, pl.ds(first, batch)].reshape(batch * context, cache_ref.shape[3])
        fresh = fresh_ref[pl.ds(first, batch)].reshape(batch * steps, fresh_ref.shape[2])
        for a in range(kv_heads):
            queries = q_ref[pl.ds(first, batch), a].reshape(rows, HEAD_SIZE).astype(jnp.bfloat16)
            k_at, v_at = 2 * a * HEAD_SIZE, (2 * a + 1) * HEAD_SIZE
            scores = scores_of(queries, pages[:, k_at : k_at + HEAD_SIZE])
            scores = jnp.where(cache_live, scores, MASKED)
            recent = scores_of(queries, fresh[:, k_at : k_at + HEAD_SIZE].astype(jnp.bfloat16))
            recent = jnp.where(fresh_live, recent, MASKED)
            top = jnp.maximum(
                jnp.max(scores, axis=-1, keepdims=True), jnp.max(recent, axis=-1, keepdims=True)
            )
            weights = jnp.exp2(scores - top).astype(jnp.bfloat16)
            recent = jnp.exp2(recent - top).astype(jnp.bfloat16)
            total = jnp.dot(
                weights,
                with_ones(pages[:, v_at : v_at + HEAD_SIZE]),
                preferred_element_type=jnp.float32,
            ) + jnp.dot(
                recent,
                with_ones(fresh[:, v_at : v_at + HEAD_SIZE].astype(jnp.bfloat16)),
                preferred_element_type=jnp.float32,
            )
            acc[pl.ds(first, batch), a] = total.reshape(batch, per_row, 2 * HEAD_SIZE)
            peak[pl.ds(first, batch), a] = jnp.broadcast_to(top, (rows, HEAD_SIZE)).reshape(
                batch, per_row, HEAD_SIZE
            )
        return carry

    lax.fori_loop(0, row_count // batch, cached, 0)

    def arrival(slot, carry):
        row = row_ref[slot]

        @pl.when(row >= 0)
        def _():
            for a in range(kv_heads):
                queries = q_ref[row, a].astype(jnp.bfloat16)
                k_at, v_at = 2 * a * HEAD_SIZE, (2 * a + 1) * HEAD_SIZE
                scores = scores_of(queries, landed_ref[slot, :, k_at : k_at + HEAD_SIZE])
                before = peak[row, a]
                top = jnp.maximum(before, jnp.max(scores, axis=-1, keepdims=True))
                weights = jnp.exp2(scores - top[:, :1]).astype(jnp.bfloat16)
                fade = jnp.exp2(before - top)
                acc[row, a] = acc[row, a] * jnp.concatenate([fade, fade], axis=1) + jnp.dot(
                    weights,
                    with_ones(landed_ref[slot, :, v_at : v_at + HEAD_SIZE]),
                    preferred_element_type=jnp.float32,
                )

        return carry

    lax.fori_loop(0, row_ref.shape[0], arrival, 0)
    o_ref[...] = (acc[:, :, :, :HEAD_SIZE] / acc[:, :, :, HEAD_SIZE:]).astype(o_ref.dtype)


def decode_attention(queries, dec_cache, dec_len, landed, slot_rows, fresh, held=()):
    row_count, kv_heads, per_row = queries.shape[:3]
    context = dec_cache.shape[2]
    batch = max(1, min(row_count, 2 * HEAD_SIZE // context))
    whole = lambda array: pl.BlockSpec(array.shape, lambda g, *_: (0,) * array.ndim)
    return pl.pallas_call(
        without(functools.partial(decode_kernel, kv_heads, batch), 6, len(held)),
        grid_spec=pltpu.PrefetchScalarGridSpec(
            num_scalar_prefetch=2,
            grid=(1,),
            in_specs=[whole(queries), whole(dec_cache), whole(landed), whole(fresh)]
            + [pl.BlockSpec(memory_space=pl.ANY)] * len(held),
            out_specs=whole(queries),
            scratch_shapes=[
                pltpu.VMEM((row_count, kv_heads, per_row, 2 * HEAD_SIZE), jnp.float32),
                pltpu.VMEM((row_count, kv_heads, per_row, HEAD_SIZE), jnp.float32),
            ],
        ),
        out_shape=jax.ShapeDtypeStruct(queries.shape, jnp.float32),
        compiler_params=pltpu.CompilerParams(vmem_limit_bytes=KERNEL_VMEM),
        cost_estimate=pl.CostEstimate(
            flops=8 * queries.size * batch * context // COST_SHARE,
            bytes_accessed=(2 * dec_cache.size + 2 * landed.size) // COST_SHARE,
            transcendentals=queries.size * batch * context // HEAD_SIZE,
        ),
        name="decode_attention",
    )(dec_len, slot_rows, queries, dec_cache, landed, fresh, *held)


def shards(
    prefill_x,
    norm_gain,
    w_q,
    q_scale,
    key_value_weight,
    key_value_scale,
    w_o,
    o_scale,
    prefix_cache,
    prefix_len,
    dec_x,
    dec_cache,
    dec_len,
    place,
):
    prompts_total = prefix_cache.shape[1]
    row_count = dec_cache.shape[1]
    page_width = prefix_cache.shape[3]
    kv_heads = page_width // (2 * HEAD_SIZE)
    query_heads = w_q.shape[1] // HEAD_SIZE
    group_size = query_heads // kv_heads
    steps = dec_x.shape[0]
    section_count = lax.axis_size("section")
    section_index = lax.axis_index("section")
    tensor_count = lax.axis_size("tensor")
    tensor_index = lax.axis_index("tensor")
    head_span = max(1, 8 // query_heads)
    span_bits = head_span.bit_length() - 1
    block_width = w_o.shape[1] // tensor_count
    scales = (q_scale * EXP2_FACTOR, key_value_scale)

    weights = (norm_gain, w_q, key_value_weight)

    def kv_of_head(new_kv):
        for bit_number in range(span_bits):
            partner = partner_2(new_kv, "tensor", bit_number)
            new_kv = joined(new_kv, partner, bit_number, 1, tensor_index)
        return new_kv

    def finished(x, terms):
        total = sum(term.astype(jnp.float32) for term in terms)
        return (x.astype(jnp.float32) + total * o_scale).astype(jnp.bfloat16)

    dec_rows = dec_x.reshape(steps * row_count, -1)
    bounds = sorted({0, min(1, prompts_total - 1), prompts_total - 1, prompts_total})
    spans = list(zip(bounds[:-1], bounds[1:]))
    on_line = tensor_count == 4 and len(spans) == 3
    order = jnp.stack(
        line_order(tensor_index) if on_line else list(range(tensor_count))
    ).astype(jnp.int32)
    chunks = [prefill_x[first * PROMPT_TOKENS : last * PROMPT_TOKENS] for first, last in spans]
    blocks = chunks[:-1] + [jnp.concatenate([chunks[-1], dec_rows], axis=0)]
    if on_line:
        begin = chunks[0].shape[0]
        rest, dec_rest = after_all((prefill_x[begin:], dec_rows), blocks[0])
        blocks[1] = rest[: chunks[1].shape[0]]
        blocks[2] = jnp.concatenate([rest[chunks[1].shape[0] :], dec_rest], axis=0)
    pages = []

    def attention(k, queries):
        first, last = spans[k]
        return prefill_attention(queries, prefix_cache, first, last - first, pages[k], prefix_len)

    def keep(new_kv):
        new_kv = kv_of_head(new_kv)
        pages.append(new_kv[: chunks[len(pages)].shape[0]])
        return new_kv

    def back(attended, held=()):
        far, near, partner, own = project_out(
            attended, w_o, order[::-1], block_width, held=held
        )
        return LineScatter(own, partner, near, far, "tensor")

    def back_whole(attended):
        return project_out(
            attended, w_o, jnp.arange(tensor_count, dtype=jnp.int32), block_width, stacked=True
        )

    def summed(partial):
        return [lax.psum_scatter(partial, "tensor", scatter_dimension=0, tiled=False)]

    if on_line:
        first = LineGather(blocks[0], "tensor")
        first.second()
        begun = project_part(
            [[first.block], [first.partner]], order[:2], *weights, None, None, (first.middle,)
        )
        first.third(begun[2])
        second = LineGather(
            blocks[1], "tensor", (first.outer_far,), (first.outer, first.middle_far, begun[2])
        )
        queries, new_kv = project_part(first.slots()[2:], order[2:], *weights, begun, scales)
        keep(new_kv)
        attended = attention(0, queries)
        second.second(attended)
        sums = [back(attended, (second.partner, second.middle))]

        begun = project_part(
            [[second.block], [second.partner]], order[:2],
            *weights,
            None,
            None,
            (sums[0].own, second.outer),
        )
        second.third(begun[2])
        sums[0].second(begun[2])
        sums[0].third()
        third = LineGather(
            blocks[2], "tensor", (second.outer_far,), (second.outer, second.middle_far, begun[2])
        )
        queries, new_kv = project_part(
            second.slots()[2:], order[2:], *weights, begun, scales, sums[0].second_hop
        )
        keep(new_kv)
        third.second(queries)
        attended = attention(1, after(queries, third.partner, third.middle))
        third.third(attended)
        sums.append(back(attended, (third.outer, third.middle_far)))
        begun = project_part(
            [[third.block], [third.partner]],
            order[:2],
            *weights,
            None,
            None,
            (sums[1].own,),
        )
        queries, new_kv = project_part(
            third.slots()[2:], order[2:], *weights, begun, scales, sums[0].terms[1:]
        )
        new_kv = keep(new_kv)
        sums[1].second(queries)
        sums[1].third_begin()
        sums.append(back(attention(2, after(queries, *sums[1].first_hop)), sums[1].second_hop))
        sums[1].third_start(sums[2].own)
        hold = (sums[2].own,)
    else:
        terms_of = []
        for k, block in enumerate(blocks):
            whole = lax.all_gather(block, "tensor", axis=1, tiled=True)
            queries, new_kv = project_part([[whole]], order[:1], *weights, None, scales)
            new_kv = keep(new_kv)
            terms_of.append(summed(back_whole(attention(k, queries))))
        hold = ()
    tokens = chunks[-1].shape[0]
    dec_queries, fresh_kv = queries[tokens:], new_kv[tokens:]

    own_block = jnp.concatenate(pages, axis=0).reshape(prompts_total, PROMPT_TOKENS, page_width)
    owners = (place // row_count).reshape(section_count, prompts_total)
    targets = (place % row_count).reshape(section_count, prompts_total)
    owner_hits = (owners[:, :, None] == jnp.arange(section_count)[None, None, :]).astype(jnp.int32)
    slot_ranks = jnp.sum((jnp.cumsum(owner_hits, axis=1) - owner_hits) * owner_hits, axis=2)
    capacity = prompts_total // 2
    slot_ids = jnp.arange(capacity)
    sending = lax.dynamic_index_in_dim(owner_hits, section_index, 0, keepdims=False)
    my_ranks = lax.dynamic_index_in_dim(slot_ranks, section_index, 0, keepdims=False)
    selector = (
        jnp.transpose(sending)[:, None, :] * (my_ranks[None, None, :] == slot_ids[None, :, None])
    ).astype(jnp.bfloat16)
    here = (owners == section_index)[:, None, :] & (
        slot_ranks[:, None, :] == slot_ids[None, :, None]
    )
    slot_rows = jnp.sum(jnp.where(here, targets[:, None, :] + 1, 0), axis=2) - 1
    outgoing = jnp.einsum(
        "skp,pcw->skcw", selector, own_block, preferred_element_type=jnp.float32
    ).astype(jnp.bfloat16)
    received = lax.all_to_all(after(outgoing, *hold), "section", split_axis=0, concat_axis=0, tiled=True)
    if on_line:
        sums[2].second(received)
        hold = sums[2].first_hop
    landed = received.reshape(section_count * capacity, PROMPT_TOKENS, page_width)

    dec_queries = jnp.transpose(
        dec_queries.reshape(steps, row_count, kv_heads, group_size, HEAD_SIZE), (1, 2, 0, 3, 4)
    ).reshape(row_count, kv_heads, steps * group_size, HEAD_SIZE)
    fresh = jnp.transpose(fresh_kv.reshape(steps, row_count, page_width), (1, 0, 2))
    dec_attended = decode_attention(
        dec_queries.astype(jnp.float32),
        dec_cache,
        dec_len,
        landed,
        slot_rows.reshape(-1).astype(jnp.int32),
        fresh.astype(jnp.float32),
        hold,
    )
    dec_attended = (
        jnp.transpose(
            dec_attended.reshape(row_count, kv_heads, steps, group_size, HEAD_SIZE), (2, 0, 1, 3, 4)
        )
        .reshape(steps * row_count, -1)
        .astype(jnp.bfloat16)
    )
    if on_line:
        to = [(tensor_index + shift) % tensor_count for shift in range(tensor_count)]
        own, *parts = project_out(
            dec_attended,
            w_o,
            jnp.stack(to).astype(jnp.int32),
            block_width,
            held=corners(sums[1].terms[1:]),
        )
        sums[2].third(own)
        dec_terms = [own] + [
            lax.ppermute(
                part, "tensor", [(j, (j + shift) % tensor_count) for j in range(tensor_count)]
            )
            for shift, part in enumerate(parts, 1)
        ]
        terms_of = [each.terms for each in sums]
    else:
        dec_terms = summed(back_whole(dec_attended))
    prefill_out = jnp.concatenate(
        [finished(x, terms) for x, terms in zip(chunks, terms_of)], axis=0
    )
    decode_out = finished(dec_rows, dec_terms).reshape(dec_x.shape)
    return (prefill_out, decode_out)


def solution(mesh):
    in_specs = (
        P(("groups", "section"), "tensor"),
        P(),
        P(None, "tensor"),
        P("tensor"),
        P(None, "tensor"),
        P("tensor"),
        P("tensor", None),
        P("tensor"),
        P("tensor", ("groups", "section"), None, None),
        P(("groups", "section")),
        P(None, ("groups", "section"), "tensor"),
        P("tensor", ("groups", "section"), None, None),
        P(("groups", "section")),
        P("groups"),
    )
    out_specs = (P(("groups", "section"), "tensor"), P(None, ("groups", "section"), "tensor"))
    return jax.shard_map(shards, mesh=mesh, in_specs=in_specs, out_specs=out_specs, check_vma=False)
```

```python
import functools
import math

import jax
import jax.numpy as jnp
from jax import lax
from jax.experimental import pallas as pl
from jax.experimental.pallas import tpu as pltpu
from jax.sharding import PartitionSpec as P

HEAD_SIZE = 128
PROMPT_TOKENS = 128
KERNEL_VMEM = 36 << 20
WEIGHT_BUFFERS = 8
COST_SHARE = 256
EXP2_FACTOR = math.log2(math.e) / math.sqrt(HEAD_SIZE)
MASKED = -1e30


def partner_2(block, axis, distance):
    count = lax.axis_size(axis)
    route = []
    for low in range(count):
        high = low | 1 << distance
        if high != low and high < count:
            route += [(low, high), (high, low)]
    return lax.ppermute(block, axis, route)


def joined(portion, partner, bit_number, concat_dim, tensor_index):
    upper_half = tensor_index // 2**bit_number % 2 == 1
    lower_first = jnp.concatenate([portion, partner], axis=concat_dim)
    upper_first = jnp.concatenate([partner, portion], axis=concat_dim)
    return jnp.where(upper_half, upper_first, lower_first)


def tile_of(extent, most):
    tile = extent
    while tile > most and tile % 2 == 0:
        tile //= 2
    return tile


def after(value, *others):
    return lax.optimization_barrier((value,) + others)[0]


def after_all(values, *others):
    return lax.optimization_barrier(tuple(values) + others)[: len(values)]


def line_order(index):
    low = index < 2
    return [index, index ^ 1, jnp.where(low, 2, 1), jnp.where(low, 3, 0)]


OUTER = [(0, 1), (1, 0), (2, 3), (3, 2)]
MIDDLE = [(1, 2), (2, 1)]
INWARD = [(0, 1), (3, 2)]
OUTWARD = [(1, 0), (2, 3)]


class LineGather:
    def __init__(self, block, axis, outer_held=(), middle_held=()):
        self.block, self.axis = block, axis
        self.partner = lax.ppermute(after(block, *outer_held), axis, OUTER)
        self.middle = lax.ppermute(after(block, *middle_held), axis, MIDDLE)

    def second(self, *held):
        partner, middle = after_all((self.partner, self.middle), *held)
        self.outer = lax.ppermute(middle, self.axis, OUTWARD)
        self.middle_far = lax.ppermute(partner, self.axis, MIDDLE)

    def third(self, *held):
        self.outer_far = lax.ppermute(after(self.middle_far, *held), self.axis, OUTWARD)

    def slots(self):
        return [
            [self.block],
            [self.partner],
            [self.middle, self.outer],
            [self.middle_far, self.outer_far],
        ]


def corners(arrays):
    return [array[:HEAD_SIZE, :HEAD_SIZE] for array in arrays]


def added(*terms):
    total = sum(term.astype(jnp.float32) for term in terms)
    return total.astype(terms[0].dtype)


class LineScatter:
    def __init__(self, own, partner, near, far, axis):
        self.own, self.partner, self.near, self.far = own, partner, near, far
        self.axis = axis
        self.far_in = lax.ppermute(far, axis, INWARD)

    def second(self, *held):
        far, near = after_all((added(self.far, self.far_in), self.near), *held)
        self.first_hop = (far,)
        self.near_in = lax.ppermute(near, self.axis, INWARD)
        self.far_out = lax.ppermute(far, self.axis, MIDDLE)

    def third(self, *held):
        self.third_begin()
        self.third_start(*held)

    def third_begin(self):
        self.second_hop = (
            added(self.near, self.near_in),
            added(self.partner, self.far_out),
        )

    def third_start(self, *held):
        near, partner = after_all(self.second_hop, *held)
        near = lax.ppermute(near, self.axis, MIDDLE)
        partner = lax.ppermute(partner, self.axis, OUTER)
        self.terms = [self.own, near, partner]


def in_hbm(arrays):
    return [pltpu.with_memory_space_constraint(array, pltpu.HBM) for array in arrays]


def without(kernel, first, count):
    return lambda *refs: kernel(*refs[:first], *refs[first + count :])


def qkv_kernel(counts, begun, ended, tile, order, *refs):
    refs = list(refs)
    arrays = sum(counts)
    xs = [refs.pop(0) for _ in range(arrays)]
    gain_ref, wq_ref, wkv_ref = (refs.pop(0) for _ in range(3))
    sums_in = [refs.pop(0) for _ in range(3)] if begun else []
    if ended:
        qs_ref, kvs_ref, q_ref, kv_ref, accq, acckv, squares = (refs.pop(0) for _ in range(7))
    else:
        accq, acckv, squares = (refs.pop(0) for _ in range(3))
    x_bufs = [refs.pop(0) for _ in range(arrays)]
    wq_buf, wkv_buf, x_sem, w_sem, sum_sem = refs
    per = x_bufs[0].shape[1] // tile
    steps = len(counts) * per
    ahead = min(steps, wq_buf.shape[0])

    def weight_copies(step):
        buffer = lax.rem(step, ahead)
        at = pl.multiple_of((order[step // per] * per + lax.rem(step, per)) * tile, tile)
        return [
            pltpu.make_async_copy(ref.at[pl.ds(at, tile)], buf.at[buffer], w_sem.at[w, buffer])
            for w, (ref, buf) in enumerate([(wq_ref, wq_buf), (wkv_ref, wkv_buf)])
        ]

    x_copies = [
        pltpu.make_async_copy(ref, buf, x_sem.at[a]) for a, (ref, buf) in enumerate(zip(xs, x_bufs))
    ]
    sum_copies = [
        pltpu.make_async_copy(ref, acc, sum_sem.at[a])
        for a, (ref, acc) in enumerate(zip(sums_in, (accq, acckv, squares)))
    ]
    for copy in x_copies[: counts[0]] + sum_copies:
        copy.start()
    for step in range(ahead):
        for copy in weight_copies(step):
            copy.start()
    for copy in x_copies[counts[0] :]:
        copy.start()
    for copy in sum_copies:
        copy.wait()
    if not begun:
        accq[...] = jnp.zeros_like(accq)
        acckv[...] = jnp.zeros_like(acckv)
        squares[...] = jnp.zeros_like(squares)

    taken = 0
    for s, count in enumerate(counts):
        for copy in x_copies[taken : taken + count]:
            copy.wait()
        bufs = x_bufs[taken : taken + count]
        taken += count

        def body(j, carry, s=s, bufs=bufs):
            step = s * per + j
            for copy in weight_copies(step):
                copy.wait()
            at = pl.multiple_of(j * tile, tile)
            values = sum(buf[:, pl.ds(at, tile)].astype(jnp.float32) for buf in bufs)
            gain = gain_ref[:, pl.ds(pl.multiple_of((order[s] * per + j) * tile, tile), tile)]
            squares[...] += jnp.broadcast_to(
                jnp.sum(values * values, axis=-1, keepdims=True), squares.shape
            )
            scaled = (values * gain).astype(jnp.bfloat16)
            buffer = lax.rem(step, ahead)
            accq[...] += jnp.dot(scaled, wq_buf[buffer], preferred_element_type=jnp.float32)
            acckv[...] += jnp.dot(scaled, wkv_buf[buffer], preferred_element_type=jnp.float32)

            @pl.when(step + ahead < steps)
            def _():
                for copy in weight_copies(step + ahead):
                    copy.start()

            return carry

        lax.fori_loop(0, per, body, 0)
    if ended:
        root = lax.rsqrt(squares[:, :1] / ended + 1e-05)
        q_ref[...] = (accq[...] * root * qs_ref[...]).astype(q_ref.dtype)
        kv_ref[...] = (acckv[...] * root * kvs_ref[...]).astype(kv_ref.dtype)


def project_part(slots, order, norm_gain, w_q, kv_weight, begun, scales, held=()):
    rows, depth = slots[0][0].shape
    tile = tile_of(depth, 512)
    q_cols, kv_cols = w_q.shape[1], kv_weight.shape[1]
    arrays = [array for slot in slots for array in slot]

    def whole(shape):
        return pl.BlockSpec(shape, lambda g, order: (0,) * len(shape))

    anywhere = pl.BlockSpec(memory_space=pl.ANY)
    operands = arrays + [norm_gain.reshape(1, -1)] + in_hbm([w_q, kv_weight])
    in_specs = [anywhere] * len(arrays) + [whole((1, norm_gain.shape[0])), anywhere, anywhere]
    sums = [(rows, q_cols), (rows, kv_cols), (rows, HEAD_SIZE)]
    if begun is not None:
        operands += list(begun)
        in_specs += [anywhere] * 3
    if scales is not None:
        operands += [scale.reshape(1, -1) for scale in scales]
        in_specs += [whole((1, q_cols)), whole((1, kv_cols))]
        out_shapes = [jax.ShapeDtypeStruct(shape, jnp.bfloat16) for shape in sums[:2]]
        scratch = [pltpu.VMEM(shape, jnp.float32) for shape in sums]
    else:
        out_shapes = [jax.ShapeDtypeStruct(shape, jnp.float32) for shape in sums]
        scratch = []
    kernel = functools.partial(
        qkv_kernel,
        [len(slot) for slot in slots],
        begun is not None,
        0 if scales is None else w_q.shape[0],
        tile,
    )
    return pl.pallas_call(
        without(kernel, 1 + len(operands), len(held)),
        grid_spec=pltpu.PrefetchScalarGridSpec(
            num_scalar_prefetch=1,
            grid=(1,),
            in_specs=in_specs + [anywhere] * len(held),
            out_specs=[whole(out.shape) for out in out_shapes],
            scratch_shapes=scratch
            + [pltpu.VMEM((rows, depth), jnp.bfloat16) for _ in arrays]
            + [
                pltpu.VMEM((WEIGHT_BUFFERS, tile, q_cols), jnp.bfloat16),
                pltpu.VMEM((WEIGHT_BUFFERS, tile, kv_cols), jnp.bfloat16),
                pltpu.SemaphoreType.DMA((len(arrays),)),
                pltpu.SemaphoreType.DMA((2, WEIGHT_BUFFERS)),
                pltpu.SemaphoreType.DMA((3,)),
            ],
        ),
        out_shape=out_shapes,
        compiler_params=pltpu.CompilerParams(vmem_limit_bytes=KERNEL_VMEM),
        cost_estimate=pl.CostEstimate(
            flops=2 * rows * depth * len(slots) * (q_cols + kv_cols) // COST_SHARE,
            bytes_accessed=(2 * depth * len(slots) * (q_cols + kv_cols)) // COST_SHARE,
            transcendentals=0,
        ),
        name="norm_qkv",
    )(order, *operands, *held)


def out_kernel(count, stacked, tile, order, x_ref, w_ref, *refs):
    if stacked:
        outs, refs = [refs[0].at[s] for s in range(count)], refs[1:]
    else:
        outs, refs = refs[:count], refs[count:]
    x_buf, w_buf, x_sem, w_sem, o_sem = refs[:5]
    o_bufs = refs[5:]
    per = o_bufs[0].shape[1] // tile
    steps = count * per
    ahead = min(steps, w_buf.shape[0])

    def weight_copy(step):
        at = pl.multiple_of((order[step // per] * per + lax.rem(step, per)) * tile, tile)
        buffer = lax.rem(step, ahead)
        return pltpu.make_async_copy(
            w_ref.at[:, pl.ds(at, tile)], w_buf.at[buffer], w_sem.at[buffer]
        )

    x_copy = pltpu.make_async_copy(x_ref, x_buf, x_sem)
    x_copy.start()
    for step in range(ahead):
        weight_copy(step).start()
    x_copy.wait()
    o_copies = []
    for s, (out, o_buf) in enumerate(zip(outs, o_bufs)):

        def body(j, carry, s=s, o_buf=o_buf):
            step = s * per + j
            weight_copy(step).wait()
            o_buf[:, pl.ds(pl.multiple_of(j * tile, tile), tile)] = jnp.dot(
                x_buf[...], w_buf[lax.rem(step, ahead)], preferred_element_type=jnp.float32
            ).astype(o_buf.dtype)

            @pl.when(step + ahead < steps)
            def _():
                weight_copy(step + ahead).start()

            return carry

        lax.fori_loop(0, per, body, 0)
        o_copies.append(pltpu.make_async_copy(o_buf, out, o_sem.at[s]))
        o_copies[-1].start()
    for copy in o_copies:
        copy.wait()


def project_out(attended, w_o, order, block, stacked=False, held=()):
    rows, depth = attended.shape
    tile = tile_of(block, 512)
    count = order.shape[0]
    anywhere = pl.BlockSpec(memory_space=pl.ANY)
    return pl.pallas_call(
        without(functools.partial(out_kernel, count, stacked, tile), 3, len(held)),
        grid_spec=pltpu.PrefetchScalarGridSpec(
            num_scalar_prefetch=1,
            grid=(1,),
            in_specs=[anywhere] * (2 + len(held)),
            out_specs=anywhere if stacked else [anywhere] * count,
            scratch_shapes=[
                pltpu.VMEM((rows, depth), jnp.bfloat16),
                pltpu.VMEM((WEIGHT_BUFFERS, depth, tile), jnp.bfloat16),
                pltpu.SemaphoreType.DMA,
                pltpu.SemaphoreType.DMA((WEIGHT_BUFFERS,)),
                pltpu.SemaphoreType.DMA((count,)),
            ]
            + [pltpu.VMEM((rows, block), jnp.bfloat16)] * count,
        ),
        out_shape=jax.ShapeDtypeStruct((count, rows, block), jnp.bfloat16)
        if stacked
        else [jax.ShapeDtypeStruct((rows, block), jnp.bfloat16)] * count,
        compiler_params=pltpu.CompilerParams(vmem_limit_bytes=KERNEL_VMEM),
        cost_estimate=pl.CostEstimate(
            flops=2 * rows * depth * count * block // COST_SHARE,
            bytes_accessed=(2 * depth * count * block) // COST_SHARE,
            transcendentals=0,
        ),
        name="project_out",
    )(order, attended, *in_hbm([w_o]), *held)


def with_ones(values):
    return jnp.concatenate([values, jnp.ones_like(values)], axis=1)


def scores_of(queries, keys):
    return lax.dot_general(
        queries, keys, (((1,), (1,)), ((), ())), preferred_element_type=jnp.float32
    )


def prefill_kernel(
    kv_heads, group, span, first, len_ref, q_ref, cache_ref, new_ref, o_ref, cache_buf, sem, *scratch
):
    accs, peaks = scratch[:kv_heads], scratch[kv_heads:]
    prompt = pl.program_id(0)

    def cache_copy(g):
        return pltpu.make_async_copy(cache_ref.at[0, first + g], cache_buf.at[g], sem.at[g])

    @pl.when(prompt == 0)
    def _():
        for g in range(cache_buf.shape[0]):
            cache_copy(g).start()

    tokens = q_ref.shape[0]
    rows = group * tokens
    live = len_ref[first + prompt]
    full = live // span
    query_token = lax.rem(lax.broadcasted_iota(jnp.int32, (rows, tokens), 0), tokens)
    key_token = lax.broadcasted_iota(jnp.int32, (rows, tokens), 1)
    causal = key_token <= query_token
    lane = lax.broadcasted_iota(jnp.int32, (1, span), 1)

    def queries_of(a):
        return jnp.concatenate(
            [
                q_ref[:, (a * group + h) * HEAD_SIZE : (a * group + h + 1) * HEAD_SIZE]
                for h in range(group)
            ],
            axis=0,
        )

    def columns(a, part):
        return pl.ds((2 * a + part) * HEAD_SIZE, HEAD_SIZE)

    for a in range(kv_heads):
        scores = jnp.where(causal, scores_of(queries_of(a), new_ref[:, columns(a, 0)]), MASKED)
        top = jnp.broadcast_to(jnp.max(scores, axis=-1, keepdims=True), (rows, HEAD_SIZE))
        weights = jnp.exp2(scores - top[:, :tokens]).astype(jnp.bfloat16)
        accs[a][...] = jnp.dot(
            weights, with_ones(new_ref[:, columns(a, 1)]), preferred_element_type=jnp.float32
        )
        peaks[a][...] = top

    cache_copy(prompt).wait()

    def block(s, bias):
        at = pl.multiple_of(s * span, span)
        scores = [
            scores_of(queries_of(a), cache_buf[prompt, pl.ds(at, span), columns(a, 0)])
            for a in range(kv_heads)
        ]
        for a in range(kv_heads):
            here = scores[a] if bias is None else scores[a] + bias
            before = peaks[a][...]
            top = jnp.maximum(before, jnp.max(here, axis=-1, keepdims=True))
            weights = jnp.exp2(
                here - jnp.concatenate([top] * (span // HEAD_SIZE), axis=1)
            ).astype(jnp.bfloat16)
            fade = jnp.exp2(before - top)
            values = cache_buf[prompt, pl.ds(at, span), columns(a, 1)]
            accs[a][...] = accs[a][...] * jnp.concatenate([fade, fade], axis=1) + jnp.dot(
                weights, with_ones(values), preferred_element_type=jnp.float32
            )
            peaks[a][...] = top

    def step(s, carry):
        block(s, None)
        return carry

    lax.fori_loop(0, full, step, 0)

    @pl.when(full * span < live)
    def _():
        block(full, jnp.where(lane + full * span < live, 0.0, MASKED))

    for a in range(kv_heads):
        result = accs[a][:, :HEAD_SIZE] / accs[a][:, HEAD_SIZE:]
        for h in range(group):
            o_ref[:, (a * group + h) * HEAD_SIZE : (a * group + h + 1) * HEAD_SIZE] = result[
                h * tokens : (h + 1) * tokens
            ].astype(o_ref.dtype)


def prefill_attention(queries, prefix_cache, first, count, new_kv, prefix_len):
    width = queries.shape[1]
    positions, page = prefix_cache.shape[2:]
    kv_heads = page // (2 * HEAD_SIZE)
    group = width // HEAD_SIZE // kv_heads
    span = tile_of(positions, 512)
    rows = group * PROMPT_TOKENS
    return pl.pallas_call(
        functools.partial(prefill_kernel, kv_heads, group, span, first),
        grid_spec=pltpu.PrefetchScalarGridSpec(
            num_scalar_prefetch=1,
            grid=(count,),
            in_specs=[
                pl.BlockSpec((PROMPT_TOKENS, width), lambda g, n: (g, 0)),
                pl.BlockSpec(memory_space=pl.ANY),
                pl.BlockSpec((PROMPT_TOKENS, page), lambda g, n: (g, 0)),
            ],
            out_specs=pl.BlockSpec((PROMPT_TOKENS, width), lambda g, n: (g, 0)),
            scratch_shapes=[
                pltpu.VMEM((count, positions, page), jnp.bfloat16),
                pltpu.SemaphoreType.DMA((count,)),
            ]
            + [pltpu.VMEM((rows, 2 * HEAD_SIZE), jnp.float32)] * kv_heads
            + [pltpu.VMEM((rows, HEAD_SIZE), jnp.float32)] * kv_heads,
        ),
        out_shape=jax.ShapeDtypeStruct((count * PROMPT_TOKENS, width), jnp.bfloat16),
        compiler_params=pltpu.CompilerParams(vmem_limit_bytes=KERNEL_VMEM),
        cost_estimate=pl.CostEstimate(
            flops=8 * count * rows * kv_heads * (positions + PROMPT_TOKENS) * HEAD_SIZE // COST_SHARE,
            bytes_accessed=(2 * count * positions * page) // COST_SHARE,
            transcendentals=count * rows * kv_heads * (positions + PROMPT_TOKENS),
        ),
        name="prefill_attention",
    )(prefix_len, queries, *in_hbm([prefix_cache]), new_kv)


def decode_kernel(
    kv_heads, batch, len_ref, row_ref, q_ref, cache_ref, landed_ref, fresh_ref, o_ref, acc, peak
):
    row_count, context = cache_ref.shape[1], cache_ref.shape[2]
    per_row = q_ref.shape[2]
    steps = fresh_ref.shape[1]
    rows = batch * per_row
    row_of = lax.broadcasted_iota(jnp.int32, (rows, batch * context), 0) // per_row
    key_row = lax.broadcasted_iota(jnp.int32, (rows, batch * context), 1) // context
    key_at = lax.rem(lax.broadcasted_iota(jnp.int32, (rows, batch * context), 1), context)
    fresh_query = lax.broadcasted_iota(jnp.int32, (rows, batch * steps), 0)
    fresh_key = lax.broadcasted_iota(jnp.int32, (rows, batch * steps), 1)
    fresh_live = (fresh_key // steps == fresh_query // per_row) & (
        lax.rem(fresh_key, steps) <= lax.rem(fresh_query, per_row) // (per_row // steps)
    )

    def cached(b, carry):
        first = b * batch
        live = jnp.zeros_like(key_row)
        for r in range(batch):
            live = jnp.where(key_row == r, len_ref[first + r], live)
        cache_live = (row_of == key_row) & (key_at < live)
        pages = cache_ref[0, pl.ds(first, batch)].reshape(batch * context, cache_ref.shape[3])
        fresh = fresh_ref[pl.ds(first, batch)].reshape(batch * steps, fresh_ref.shape[2])
        for a in range(kv_heads):
            queries = q_ref[pl.ds(first, batch), a].reshape(rows, HEAD_SIZE).astype(jnp.bfloat16)
            k_at, v_at = 2 * a * HEAD_SIZE, (2 * a + 1) * HEAD_SIZE
            scores = scores_of(queries, pages[:, k_at : k_at + HEAD_SIZE])
            scores = jnp.where(cache_live, scores, MASKED)
            recent = scores_of(queries, fresh[:, k_at : k_at + HEAD_SIZE].astype(jnp.bfloat16))
            recent = jnp.where(fresh_live, recent, MASKED)
            top = jnp.maximum(
                jnp.max(scores, axis=-1, keepdims=True), jnp.max(recent, axis=-1, keepdims=True)
            )
            weights = jnp.exp2(scores - top).astype(jnp.bfloat16)
            recent = jnp.exp2(recent - top).astype(jnp.bfloat16)
            total = jnp.dot(
                weights,
                with_ones(pages[:, v_at : v_at + HEAD_SIZE]),
                preferred_element_type=jnp.float32,
            ) + jnp.dot(
                recent,
                with_ones(fresh[:, v_at : v_at + HEAD_SIZE].astype(jnp.bfloat16)),
                preferred_element_type=jnp.float32,
            )
            acc[pl.ds(first, batch), a] = total.reshape(batch, per_row, 2 * HEAD_SIZE)
            peak[pl.ds(first, batch), a] = jnp.broadcast_to(top, (rows, HEAD_SIZE)).reshape(
                batch, per_row, HEAD_SIZE
            )
        return carry

    lax.fori_loop(0, row_count // batch, cached, 0)

    def arrival(slot, carry):
        row = row_ref[slot]

        @pl.when(row >= 0)
        def _():
            for a in range(kv_heads):
                queries = q_ref[row, a].astype(jnp.bfloat16)
                k_at, v_at = 2 * a * HEAD_SIZE, (2 * a + 1) * HEAD_SIZE
                scores = scores_of(queries, landed_ref[slot, :, k_at : k_at + HEAD_SIZE])
                before = peak[row, a]
                top = jnp.maximum(before, jnp.max(scores, axis=-1, keepdims=True))
                weights = jnp.exp2(scores - top[:, :1]).astype(jnp.bfloat16)
                fade = jnp.exp2(before - top)
                acc[row, a] = acc[row, a] * jnp.concatenate([fade, fade], axis=1) + jnp.dot(
                    weights,
                    with_ones(landed_ref[slot, :, v_at : v_at + HEAD_SIZE]),
                    preferred_element_type=jnp.float32,
                )

        return carry

    lax.fori_loop(0, row_ref.shape[0], arrival, 0)
    o_ref[...] = (acc[:, :, :, :HEAD_SIZE] / acc[:, :, :, HEAD_SIZE:]).astype(o_ref.dtype)


def decode_attention(queries, dec_cache, dec_len, landed, slot_rows, fresh, held=()):
    row_count, kv_heads, per_row = queries.shape[:3]
    context = dec_cache.shape[2]
    batch = max(1, min(row_count, 2 * HEAD_SIZE // context))
    whole = lambda array: pl.BlockSpec(array.shape, lambda g, *_: (0,) * array.ndim)
    return pl.pallas_call(
        without(functools.partial(decode_kernel, kv_heads, batch), 6, len(held)),
        grid_spec=pltpu.PrefetchScalarGridSpec(
            num_scalar_prefetch=2,
            grid=(1,),
            in_specs=[whole(queries), whole(dec_cache), whole(landed), whole(fresh)]
            + [pl.BlockSpec(memory_space=pl.ANY)] * len(held),
            out_specs=whole(queries),
            scratch_shapes=[
                pltpu.VMEM((row_count, kv_heads, per_row, 2 * HEAD_SIZE), jnp.float32),
                pltpu.VMEM((row_count, kv_heads, per_row, HEAD_SIZE), jnp.float32),
            ],
        ),
        out_shape=jax.ShapeDtypeStruct(queries.shape, jnp.float32),
        compiler_params=pltpu.CompilerParams(vmem_limit_bytes=KERNEL_VMEM),
        cost_estimate=pl.CostEstimate(
            flops=8 * queries.size * batch * context // COST_SHARE,
            bytes_accessed=(2 * dec_cache.size + 2 * landed.size) // COST_SHARE,
            transcendentals=queries.size * batch * context // HEAD_SIZE,
        ),
        name="decode_attention",
    )(dec_len, slot_rows, queries, dec_cache, landed, fresh, *held)


def shards(
    prefill_x,
    norm_gain,
    w_q,
    q_scale,
    key_value_weight,
    key_value_scale,
    w_o,
    o_scale,
    prefix_cache,
    prefix_len,
    dec_x,
    dec_cache,
    dec_len,
    place,
):
    prompts_total = prefix_cache.shape[1]
    row_count = dec_cache.shape[1]
    page_width = prefix_cache.shape[3]
    kv_heads = page_width // (2 * HEAD_SIZE)
    query_heads = w_q.shape[1] // HEAD_SIZE
    group_size = query_heads // kv_heads
    steps = dec_x.shape[0]
    section_count = lax.axis_size("section")
    section_index = lax.axis_index("section")
    tensor_count = lax.axis_size("tensor")
    tensor_index = lax.axis_index("tensor")
    head_span = max(1, 8 // query_heads)
    span_bits = head_span.bit_length() - 1
    block_width = w_o.shape[1] // tensor_count
    scales = (q_scale * EXP2_FACTOR, key_value_scale)

    weights = (norm_gain, w_q, key_value_weight)

    def kv_of_head(new_kv):
        for bit_number in range(span_bits):
            partner = partner_2(new_kv, "tensor", bit_number)
            new_kv = joined(new_kv, partner, bit_number, 1, tensor_index)
        return new_kv

    def finished(x, terms):
        total = sum(term.astype(jnp.float32) for term in terms)
        return (x.astype(jnp.float32) + total * o_scale).astype(jnp.bfloat16)

    dec_rows = dec_x.reshape(steps * row_count, -1)
    bounds = sorted({0, min(1, prompts_total - 1), prompts_total - 1, prompts_total})
    spans = list(zip(bounds[:-1], bounds[1:]))
    on_line = tensor_count == 4 and len(spans) == 3
    order = jnp.stack(
        line_order(tensor_index) if on_line else list(range(tensor_count))
    ).astype(jnp.int32)
    chunks = [prefill_x[first * PROMPT_TOKENS : last * PROMPT_TOKENS] for first, last in spans]
    blocks = chunks[:-1] + [jnp.concatenate([chunks[-1], dec_rows], axis=0)]
    if on_line:
        begin = chunks[0].shape[0]
        rest, dec_rest = after_all((prefill_x[begin:], dec_rows), blocks[0])
        blocks[1] = rest[: chunks[1].shape[0]]
        blocks[2] = jnp.concatenate([rest[chunks[1].shape[0] :], dec_rest], axis=0)
    pages = []

    def attention(k, queries):
        first, last = spans[k]
        return prefill_attention(queries, prefix_cache, first, last - first, pages[k], prefix_len)

    def keep(new_kv):
        new_kv = kv_of_head(new_kv)
        pages.append(new_kv[: chunks[len(pages)].shape[0]])
        return new_kv

    def back(attended, held=()):
        far, near, partner, own = project_out(
            attended, w_o, order[::-1], block_width, held=held
        )
        return LineScatter(own, partner, near, far, "tensor")

    def back_whole(attended):
        return project_out(
            attended, w_o, jnp.arange(tensor_count, dtype=jnp.int32), block_width, stacked=True
        )

    def summed(partial):
        return [lax.psum_scatter(partial, "tensor", scatter_dimension=0, tiled=False)]

    if on_line:
        first = LineGather(blocks[0], "tensor")
        first.second()
        begun = project_part(
            [[first.block], [first.partner]], order[:2], *weights, None, None, (first.middle,)
        )
        first.third(begun[2])
        second = LineGather(
            blocks[1], "tensor", (first.outer_far,), (first.outer, first.middle_far, begun[2])
        )
        queries, new_kv = project_part(first.slots()[2:], order[2:], *weights, begun, scales)
        keep(new_kv)
        attended = attention(0, queries)
        second.second(attended)
        sums = [back(attended, (second.partner, second.middle))]

        begun = project_part(
            [[second.block], [second.partner]], order[:2],
            *weights,
            None,
            None,
            (sums[0].own, second.outer),
        )
        second.third(begun[2])
        sums[0].second(begun[2])
        sums[0].third()
        third = LineGather(
            blocks[2], "tensor", (second.outer_far,), (second.outer, second.middle_far, begun[2])
        )
        queries, new_kv = project_part(
            second.slots()[2:], order[2:], *weights, begun, scales, sums[0].second_hop
        )
        keep(new_kv)
        third.second(queries)
        attended = attention(1, after(queries, third.partner, third.middle))
        third.third(attended)
        sums.append(back(attended, (third.outer, third.middle_far)))
        begun = project_part(
            [[third.block], [third.partner]],
            order[:2],
            *weights,
            None,
            None,
            (sums[1].own,),
        )
        queries, new_kv = project_part(
            third.slots()[2:], order[2:], *weights, begun, scales, sums[0].terms[1:]
        )
        new_kv = keep(new_kv)
        sums[1].second(queries)
        sums[1].third_begin()
        sums.append(back(attention(2, after(queries, *sums[1].first_hop)), sums[1].second_hop))
        sums[1].third_start(sums[2].own)
        hold = (sums[2].own,)
    else:
        terms_of = []
        for k, block in enumerate(blocks):
            whole = lax.all_gather(block, "tensor", axis=1, tiled=True)
            queries, new_kv = project_part([[whole]], order[:1], *weights, None, scales)
            new_kv = keep(new_kv)
            terms_of.append(summed(back_whole(attention(k, queries))))
        hold = ()
    tokens = chunks[-1].shape[0]
    dec_queries, fresh_kv = queries[tokens:], new_kv[tokens:]

    own_block = jnp.concatenate(pages, axis=0).reshape(prompts_total, PROMPT_TOKENS, page_width)
    owners = (place // row_count).reshape(section_count, prompts_total)
    targets = (place % row_count).reshape(section_count, prompts_total)
    owner_hits = (owners[:, :, None] == jnp.arange(section_count)[None, None, :]).astype(jnp.int32)
    slot_ranks = jnp.sum((jnp.cumsum(owner_hits, axis=1) - owner_hits) * owner_hits, axis=2)
    capacity = prompts_total // 2
    slot_ids = jnp.arange(capacity)
    sending = lax.dynamic_index_in_dim(owner_hits, section_index, 0, keepdims=False)
    my_ranks = lax.dynamic_index_in_dim(slot_ranks, section_index, 0, keepdims=False)
    selector = (
        jnp.transpose(sending)[:, None, :] * (my_ranks[None, None, :] == slot_ids[None, :, None])
    ).astype(jnp.bfloat16)
    here = (owners == section_index)[:, None, :] & (
        slot_ranks[:, None, :] == slot_ids[None, :, None]
    )
    slot_rows = jnp.sum(jnp.where(here, targets[:, None, :] + 1, 0), axis=2) - 1
    outgoing = jnp.einsum(
        "skp,pcw->skcw", selector, own_block, preferred_element_type=jnp.float32
    ).astype(jnp.bfloat16)
    received = lax.all_to_all(after(outgoing, *hold), "section", split_axis=0, concat_axis=0, tiled=True)
    if on_line:
        sums[2].second(received)
        hold = sums[2].first_hop
    landed = received.reshape(section_count * capacity, PROMPT_TOKENS, page_width)

    dec_queries = jnp.transpose(
        dec_queries.reshape(steps, row_count, kv_heads, group_size, HEAD_SIZE), (1, 2, 0, 3, 4)
    ).reshape(row_count, kv_heads, steps * group_size, HEAD_SIZE)
    fresh = jnp.transpose(fresh_kv.reshape(steps, row_count, page_width), (1, 0, 2))
    dec_attended = decode_attention(
        dec_queries.astype(jnp.float32),
        dec_cache,
        dec_len,
        landed,
        slot_rows.reshape(-1).astype(jnp.int32),
        fresh.astype(jnp.float32),
        hold,
    )
    dec_attended = (
        jnp.transpose(
            dec_attended.reshape(row_count, kv_heads, steps, group_size, HEAD_SIZE), (2, 0, 1, 3, 4)
        )
        .reshape(steps * row_count, -1)
        .astype(jnp.bfloat16)
    )
    if on_line:
        to = [(tensor_index + shift) % tensor_count for shift in range(tensor_count)]
        own, *parts = project_out(
            dec_attended,
            w_o,
            jnp.stack(to).astype(jnp.int32),
            block_width,
            held=corners(sums[1].terms[1:]),
        )
        sums[2].third(own)
        dec_terms = [own] + [
            lax.ppermute(
                part, "tensor", [(j, (j + shift) % tensor_count) for j in range(tensor_count)]
            )
            for shift, part in enumerate(parts, 1)
        ]
        terms_of = [each.terms for each in sums]
    else:
        dec_terms = summed(back_whole(dec_attended))
    prefill_out = jnp.concatenate(
        [finished(x, terms) for x, terms in zip(chunks, terms_of)], axis=0
    )
    decode_out = finished(dec_rows, dec_terms).reshape(dec_x.shape)
    return (prefill_out, decode_out)


def solution(mesh):
    in_specs = (
        P(("groups", "section"), "tensor"),
        P(),
        P(None, "tensor"),
        P("tensor"),
        P(None, "tensor"),
        P("tensor"),
        P("tensor", None),
        P("tensor"),
        P("tensor", ("groups", "section"), None, None),
        P(("groups", "section")),
        P(None, ("groups", "section"), "tensor"),
        P("tensor", ("groups", "section"), None, None),
        P(("groups", "section")),
        P("groups"),
    )
    out_specs = (P(("groups", "section"), "tensor"), P(None, ("groups", "section"), "tensor"))
    return jax.shard_map(shards, mesh=mesh, in_specs=in_specs, out_specs=out_specs, check_vma=False)
```
